32 devices in a mesh: grp: 2 (over x), ty: 4 (over y, core), tx: 4 (over z).
Axes of the slice: x: 2, y: 2, z: 4, core: 2. Of those that a mesh axis runs over, the one named last changes fastest.
Arguments:
- adjoint_state: float32 [2, 5, 50, 48, 1536], P('grp', None, None, 'tx', 'ty'), may hold values from -6 to 6
- land_mask: int32 [2, 48, 1536], P('grp', 'tx', 'ty'), may hold values 0 or 1
- diffusivity: float32 [2, 48, 1536], P('grp', 'tx', 'ty'), may hold values from 0.02 to 0.24
- mixing: float32 [2, 5, 50, 50], P('grp'), may hold values from -0.875 to 0.875
- nudging: float32 [48, 1536], P('tx', 'ty'), may hold values from 0.1 to 1
- nest_x: int32 [16], P(('ty', 'tx')), may hold values from 0 to 8
- nest_y: int32 [16], P(('ty', 'tx')), may hold values from 0 to 256
- obs_forcing: float32 [2, 16, 16, 16], P('grp', ('ty', 'tx')), may hold values from -6 to 6
- obs_cell: int32 [2, 16, 16, 16], P('grp', None, None, ('ty', 'tx')), may hold values from 0 to 1151999
- obs_count: int32 [2, 16, 16], P('grp', None, ('ty', 'tx')), may hold values from 0 to 16, as said below
Outputs:
- updated_state: float32 [2, 5, 50, 48, 1536], P('grp', None, None, 'tx', 'ty')
The draws below stay inside these ranges and needn't reach their ends.
Inputs may be any that keep to these rules, and one draw needn't show every extreme that they name: `obs_count`: in every draw some destination tile of each grid receives 16 live slots from every source tile; which one is drawn.
All inputs are finite; a program needn't handle non-finite values. No bound on the sum of `land_mask` on one device may be relied on, other than what follows from the above.
Results may differ from the reference program's by a relative error of at most 0.0003.
Values sent between devices are 32-bit elements; how exact they have to be, the bound alone decides.
No kernel may reach another device: no remote copies, remote signals or barrier semaphores. Data moves between devices by JAX's collectives and lax.ppermute only.
A program may use at most 128 MiB of HBM per device.

```python
import math
import jax
import jax.numpy as jnp
from jax import lax

F = 5
L = 50
CX = 12
CY = 384
SLOT = 16
NT = 16
NX = 48
NY = 1536


def draw_obs_count(key, part):
    first, second = jax.random.split(key)
    base = jax.random.randint(first, (2, NT, NT), 0, SLOT + 1)
    hottest = jax.random.randint(second, (2, 1, 1), 0, NT)
    dest = lax.broadcasted_iota(jnp.int32, (2, NT, NT), 2)
    return jnp.where(dest == hottest, SLOT, base).astype(jnp.int32)


def place_ends(drawn, stream_key, least, top_value):
    place = [jax.random.randint(jax.random.fold_in(stream_key, axis), (), 0, length) for axis, length in enumerate(drawn.shape)]
    widest = drawn.shape.index(max(drawn.shape))
    beside = place[:widest] + [(place[widest] + 1) % drawn.shape[widest]] + place[widest + 1:]
    return drawn.at[tuple(place)].set(least).at[tuple(beside)].set(top_value)


def levels(own_key, shape, pieces, least, largest):
    def one(position, parts):
        heights = jax.random.uniform(jax.random.fold_in(jax.random.fold_in(own_key, 6), position), (parts,), jnp.float32, least / len(pieces), largest / len(pieces))
        return jnp.repeat(jnp.exp(heights), shape[position] // parts).reshape((-1,) + (1,) * (len(shape) - position - 1))

    factor_of = one(*pieces[0])
    for cut in pieces[1:]:
        factor_of = factor_of * one(*cut)
    return factor_of


def noise(rng, dims, scale, limit, shards=(), held_as=jnp.bfloat16):
    entries = jax.random.normal(rng, dims, jnp.float32) * scale
    if len(shards) > 0:
        entries = levels(rng, dims, shards, -0.22, 0.18) * entries
    return jnp.clip(entries, min=-limit, max=limit).astype(held_as)


def setup_inputs(seed: int = 0) -> dict:
    seeds = jax.random.split(jax.random.key(seed), 11)
    adjoint_state = noise(seeds[0], (2, F, L, NX, NY), 1.0, 6.0, ((0, 2), (3, 4), (4, 4)), jnp.float32)
    land_mask = place_ends((jax.random.randint(seeds[1], (2, NX, NY), 0, 5) < 4).astype(jnp.int32), jax.random.fold_in(seeds[1], 1), 0, 1)
    diffusivity = jnp.clip(jnp.exp(math.log(0.24) - 2.4849066 * jax.random.uniform(seeds[2], (2, NX, NY), jnp.float32) ** levels(seeds[2], (2, NX, NY), ((0, 2), (1, 4), (2, 4)), -0.2, 0.2)), 0.02, 0.24)
    mixing = noise(seeds[3], (2, F, L, L), L ** -0.5, 0.875, ((0, 2),), jnp.float32)
    nudging = jnp.clip(jnp.exp(math.log(1.0) - 2.3025851 * jax.random.uniform(seeds[4], (NX, NY), jnp.float32) ** levels(seeds[4], (NX, NY), ((0, 4), (1, 4)), -0.2, 0.2)), 0.1, 1.0)
    nest_x = place_ends(jax.random.randint(seeds[5], (NT,), 0, CX - CX // 3 + 1), jax.random.fold_in(seeds[5], 1), 0, (CX - CX // 3 + 1) - 1).astype(jnp.int32)
    nest_y = place_ends(jax.random.randint(seeds[6], (NT,), 0, CY - CY // 3 + 1), jax.random.fold_in(seeds[6], 1), 0, (CY - CY // 3 + 1) - 1).astype(jnp.int32)
    obs_forcing = noise(seeds[7], (2, NT, SLOT, NT), 1.0, 6.0, ((0, 2), (1, 16)), jnp.float32)
    obs_cell = place_ends(jax.random.randint(seeds[8], (2, NT, SLOT, NT), 0, F * L * CX * CY), jax.random.fold_in(seeds[8], 1), 0, (F * L * CX * CY) - 1).astype(jnp.int32)
    obs_count = draw_obs_count(jax.random.fold_in(seeds[10], 71), 0)
    return dict(adjoint_state=adjoint_state, land_mask=land_mask, diffusivity=diffusivity, mixing=mixing, nudging=nudging, nest_x=nest_x, nest_y=nest_y, obs_forcing=obs_forcing, obs_cell=obs_cell, obs_count=obs_count)


def spread_field(field, kappa):
    padded = jnp.pad(field, ((0, 0), (0, 0), (1, 1), (1, 1)))
    beside_all = padded[:, :, 2:, 1:-1] + padded[:, :, :-2, 1:-1]
    beside_all = beside_all + padded[:, :, 1:-1, 2:] + padded[:, :, 1:-1, :-2]
    return field + kappa * (beside_all - 4.0 * field)


def grid_step(inputs):
    state, mask_int, kappa, matrix, values, cells, counts, weight = inputs
    mask = mask_int.astype(jnp.float32)
    masked = state * mask[None, None]
    spread = spread_field(masked, kappa)
    flat = spread.reshape(F, L, NX * NY)
    mixed = jnp.einsum("fkl,flc->fkc", matrix.astype(jnp.float32), flat.astype(jnp.float32), precision=lax.Precision.HIGHEST).reshape(F, L, NX, NY)
    tiles_x = NX // CX
    live = jnp.arange(SLOT, dtype=jnp.int32)[None, :, None] < counts[:, None, :]
    dest = jnp.arange(NT, dtype=jnp.int32)[None, None, :]
    tile_y = dest // tiles_x
    tile_x = dest % tiles_x
    field_idx = cells // (L * CX * CY)
    level_idx = (cells // (CX * CY)) % L
    x_idx = tile_x * CX + (cells // CY) % CX
    y_idx = tile_y * CY + cells % CY
    forced = mixed.at[field_idx, level_idx, x_idx, y_idx].add(jnp.where(live, values, jnp.zeros_like(values)))
    reduced = (weight * mixed).reshape(F, L, tiles_x, CX // 3, 3, NY // CY, CY // 3, 3).sum(axis=(4, 7))
    return forced, reduced, mixed


def reference(adjoint_state, land_mask, diffusivity, mixing, nudging, nest_x, nest_y, obs_forcing, obs_cell, obs_count):
    weights = jnp.stack([nudging, nudging])
    forced, reduced, mixed = lax.map(grid_step, (adjoint_state, land_mask, diffusivity, mixing, obs_forcing, obs_cell, obs_count, weights))
    tiles_x = NX // CX
    tiles_y = NY // CY
    off_x = nest_x.reshape(tiles_y, tiles_x)
    off_y = nest_y.reshape(tiles_y, tiles_x)
    tx_grid = jnp.arange(tiles_x, dtype=jnp.int32)[None, :]
    ty_grid = jnp.arange(tiles_y, dtype=jnp.int32)[:, None]
    x_rows = (tx_grid * CX + off_x)[:, :, None] + jnp.arange(CX // 3, dtype=jnp.int32)[None, None, :]
    y_rows = (ty_grid * CY + off_y)[:, :, None] + jnp.arange(CY // 3, dtype=jnp.int32)[None, None, :]
    xi = x_rows[:, :, :, None]
    yi = y_rows[:, :, None, :]
    block = mixed[1][:, :, xi, yi]
    child_red = jnp.transpose(reduced[0], (0, 1, 4, 2, 3, 5))
    parent = forced[1].at[:, :, xi, yi].add(child_red - block)
    block_t = jnp.transpose(block, (0, 1, 3, 4, 2, 5))
    spread_back = jnp.repeat(jnp.repeat(block_t, 3, axis=3), 3, axis=5).reshape(F, L, NX, NY) / 9.0
    child = forced[0] + spread_back
    masks = land_mask.astype(jnp.float32)
    return jnp.stack([child * masks[0][None, None], parent * masks[1][None, None]])
```

```python
import functools

import jax
import jax.numpy as jnp
from jax import lax
from jax.experimental import pallas as pl
from jax.experimental.pallas import tpu as pltpu
from jax.sharding import PartitionSpec as P

LANE = 128
DEPTH = 64
MIB = 1 << 20
ANY = pl.BlockSpec(memory_space=pl.ANY)
SMEM = pl.BlockSpec(memory_space=pltpu.SMEM)


def whole(shape):
    return pl.BlockSpec(shape, lambda f: (0,) * len(shape))


def per_field(shape):
    return pl.BlockSpec((1,) + shape, lambda f: (f,) + (0,) * len(shape))


def lane_ids(shape):
    return lax.broadcasted_iota(jnp.int32, shape, len(shape) - 1)


def mask_row(mask_ref, x):
    return mask_ref[x].astype(jnp.float32)


def x_edges_kernel(state, mask, low, high, buf, sems):
    cols = state.shape[2]
    copies = [
        pltpu.make_async_copy(state.at[:, :, x], buf.at[n], sems.at[n])
        for n, x in enumerate((0, cols - 1))
    ]
    for copy in copies:
        copy.start()
    for n, (x, out) in enumerate(((0, low), (cols - 1, high))):
        copies[n].wait()
        out[...] = buf[n] * mask_row(mask, x)[None, None]


def x_edges(state5, mask):
    fields, levels, cols, _, rows = state5.shape
    edge = (fields, levels, 1, rows)
    return pl.pallas_call(
        x_edges_kernel,
        in_specs=[ANY, pl.BlockSpec(memory_space=pltpu.VMEM)],
        out_shape=[jax.ShapeDtypeStruct(edge, jnp.float32)] * 2,
        scratch_shapes=[pltpu.VMEM((2,) + edge, jnp.float32), pltpu.SemaphoreType.DMA((2,))],
        compiler_params=pltpu.CompilerParams(vmem_limit_bytes=16 * MIB),
        name="x_edges",
    )(state5, mask)


def y_edges_kernel(levels, cols, chunks, state, mask, low, high):
    f = pl.program_id(0)
    step = cols * chunks
    lanes = lane_ids((levels, LANE))
    first = jnp.zeros((levels, LANE), jnp.float32)
    last = jnp.zeros((levels, LANE), jnp.float32)
    for x in range(cols):
        row = mask_row(mask, x)
        v = state[0, pl.ds(x * chunks, levels, stride=step), :] * row[:, :LANE]
        first = jnp.where(lanes == x, pltpu.roll(v, x, 1) if x else v, first)
        v = state[0, pl.ds(x * chunks + chunks - 1, levels, stride=step), :] * row[:, -LANE:]
        last = jnp.where(lanes == x, pltpu.roll(v, x + 1, 1), last)

    @pl.when(f == 0)
    def _():
        low[...] = jnp.zeros_like(low)
        high[...] = jnp.zeros_like(high)

    low[:levels, :] += pltpu.roll(first, f * cols, 1)
    high[:levels, :] += pltpu.roll(last, f * cols, 1)


def y_edges(state2, mask, levels, cols, chunks):
    fields = state2.shape[0]
    edge = (DEPTH, LANE)
    return pl.pallas_call(
        functools.partial(y_edges_kernel, levels, cols, chunks),
        grid=(fields,),
        in_specs=[per_field(state2.shape[1:]), whole(mask.shape)],
        out_specs=[whole(edge)] * 2,
        out_shape=[jax.ShapeDtypeStruct(edge, jnp.float32)] * 2,
        compiler_params=pltpu.CompilerParams(vmem_limit_bytes=16 * MIB),
        name="y_edges",
    )(state2, mask)


def fill_padded(levels, cols, chunks, state, mask, x_low, x_high, padded):
    step = cols * chunks
    padded[0, :levels, :] = x_low[0, :, 0, :]
    padded[cols + 1, :levels, :] = x_high[0, :, 0, :]
    for x in range(cols):
        row = mask_row(mask, x)
        for c in range(chunks):
            part = slice(c * LANE, (c + 1) * LANE)
            padded[x + 1, :levels, part] = (
                state[0, pl.ds(x * chunks + c, levels, stride=step), :] * row[:, part]
            )


def spread_row(padded, kappa, y_low, y_high, f, cols, x):
    here = padded[x + 1]
    rows = here.shape[1]
    k = f * cols + x
    lanes = lane_ids((DEPTH, LANE))
    before = pltpu.roll(here, 1, 1)
    after = pltpu.roll(here, rows - 1, 1)
    edge = pltpu.roll(y_low[...], lax.rem(LANE - k, LANE), 1)
    before = jnp.concatenate([jnp.where(lanes == 0, edge, before[:, :LANE]), before[:, LANE:]], 1)
    edge = pltpu.roll(y_high[...], LANE - 1 - k, 1)
    after = jnp.concatenate(
        [after[:, :-LANE], jnp.where(lanes == LANE - 1, edge, after[:, -LANE:])], 1
    )
    beside = padded[x] + padded[x + 2] + before + after
    return here + kappa[x] * (beside - 4.0 * here)


def halves(value):
    high = value.astype(jnp.bfloat16)
    return high, (value - high.astype(jnp.float32)).astype(jnp.bfloat16)


def fill_matrix(levels, mixing, square, matrix):
    square[:levels, :levels] = mixing[0, :, 0, :]
    value = square[...]
    high = value.astype(jnp.bfloat16).astype(jnp.float32)
    low = value - high
    matrix[:, :LANE] = (high + pltpu.roll(high, DEPTH, 1)).astype(jnp.bfloat16)
    matrix[:, LANE:] = (low + pltpu.roll(low, DEPTH, 1)).astype(jnp.bfloat16)


def fill_stack(stack, part, value):
    high, low = halves(value)
    for n, half in enumerate((high, low, high, low)):
        stack[n * DEPTH : (n + 1) * DEPTH, part] = half


def payload_kernel(
    levels, cols, chunks, is_child, nest_x, nest_y,
    state, mask, kappa, nudging, mixing, x_low, x_high, y_low, y_high,
    out, padded, square, matrix, stack, group,
):
    f = pl.program_id(0)
    rows = chunks * LANE
    blocks = cols // 3

    @pl.when(f == 0)
    def _():
        padded[...] = jnp.zeros_like(padded)
        square[...] = jnp.zeros_like(square)
        group[...] = jnp.where(
            lax.broadcasted_iota(jnp.int32, group.shape, 0) // 3 == lane_ids(group.shape), 1.0, 0.0
        ).astype(jnp.bfloat16)

    fill_padded(levels, cols, chunks, state, mask, x_low, x_high, padded)
    fill_matrix(levels, mixing, square, matrix)
    spread = functools.partial(spread_row, padded, kappa, y_low, y_high, f, cols)

    @pl.when(is_child[0] == 1)
    def _():
        for i in range(blocks):
            total = None
            for x in range(3 * i, 3 * i + 3):
                term = nudging[x : x + 1, :] * spread(x)
                total = term if total is None else total + term
            high, low = halves(total)
            value = jnp.dot(high, group[...], preferred_element_type=jnp.float32)
            value = value + jnp.dot(low, group[...], preferred_element_type=jnp.float32)
            fill_stack(stack, slice(i * LANE, (i + 1) * LANE), value)

    @pl.when(is_child[0] == 0)
    def _():
        back = lax.rem(rows - nest_y[0], rows)
        for i in range(blocks):
            value = pltpu.roll(spread(nest_x[0] + i), back, 1)[:, :LANE]
            fill_stack(stack, slice(i * LANE, (i + 1) * LANE), value)

    mixed = jnp.dot(matrix[...], stack[...], preferred_element_type=jnp.float32)
    for i in range(blocks):
        out[0, pl.ds(i, levels, stride=blocks), :] = mixed[:levels, i * LANE : (i + 1) * LANE]


def payload_of(is_child, nest_x, nest_y, state2, mask, kappa, nudging, mixing, halos, dims):
    levels, cols, chunks = dims
    fields = state2.shape[0]
    rows = chunks * LANE
    blocks = cols // 3
    x_low, x_high, y_low, y_high = halos
    return pl.pallas_call(
        functools.partial(payload_kernel, levels, cols, chunks),
        grid=(fields,),
        in_specs=[SMEM, SMEM, SMEM]
        + [per_field(state2.shape[1:]), whole(mask.shape), whole(kappa.shape)]
        + [whole(nudging.shape), per_field(mixing.shape[1:])]
        + [per_field(x_low.shape[1:])] * 2
        + [whole(y_low.shape)] * 2,
        out_specs=per_field((levels * blocks, LANE)),
        out_shape=jax.ShapeDtypeStruct((fields, levels * blocks, LANE), jnp.float32),
        scratch_shapes=[
            pltpu.VMEM((cols + 2, DEPTH, rows), jnp.float32),
            pltpu.VMEM((DEPTH, LANE), jnp.float32),
            pltpu.VMEM((DEPTH, 4 * DEPTH), jnp.bfloat16),
            pltpu.VMEM((4 * DEPTH, blocks * LANE), jnp.bfloat16),
            pltpu.VMEM((rows, LANE), jnp.bfloat16),
        ],
        compiler_params=pltpu.CompilerParams(vmem_limit_bytes=24 * MIB),
        name="payload",
    )(is_child, nest_x, nest_y, state2, mask, kappa, nudging, mixing, *halos)


def tile_kernel(
    levels, cols, chunks, cells, counts, values,
    state, mask, mask_rows, kappa, mixing, x_low, x_high, y_low, y_high,
    out, padded, square, matrix, stack,
):
    f = pl.program_id(0)
    rows = chunks * LANE
    step = cols * chunks

    @pl.when(f == 0)
    def _():
        padded[...] = jnp.zeros_like(padded)
        square[...] = jnp.zeros_like(square)

    fill_padded(levels, cols, chunks, state, mask, x_low, x_high, padded)
    fill_matrix(levels, mixing, square, matrix)
    pair = 2
    for x0 in range(0, cols, pair):
        for n in range(pair):
            value = spread_row(padded, kappa, y_low, y_high, f, cols, x0 + n)
            fill_stack(stack, slice(n * rows, (n + 1) * rows), value)
        mixed = jnp.dot(matrix[...], stack[...], preferred_element_type=jnp.float32)
        for n in range(pair):
            row = mask_row(mask, x0 + n)
            for c in range(chunks):
                part = mixed[:levels, n * rows + c * LANE : n * rows + (c + 1) * LANE]
                start = f * (levels * step) + (x0 + n) * chunks + c
                out[pl.ds(start, levels, stride=step), :] = (
                    part * row[:, c * LANE : (c + 1) * LANE]
                )

    @pl.when(f == pl.num_programs(0) - 1)
    def _():
        lanes = lane_ids((1, LANE))

        def source(s, carry):
            def slot(k, carry):
                cell = cells[s, k]
                column = lax.div(cell, cols * rows)
                inside = cell - column * (cols * rows)
                piece = lax.div(inside, LANE)
                lane = inside - piece * LANE
                at = pl.ds(column * step + piece, 1)
                add = jnp.where(lanes == lane, values[s, k], 0.0)
                out[at, :] = out[at, :] + add * mask_rows[piece].astype(jnp.float32)
                return carry

            return lax.fori_loop(0, counts[0, s], slot, carry)

        lax.fori_loop(0, cells.shape[0], source, 0)


def tile_of(cells, counts, values, state2, mask, mask_rows, kappa, mixing, halos, dims):
    levels, cols, chunks = dims
    fields = state2.shape[0]
    rows = chunks * LANE
    x_low, x_high, y_low, y_high = halos
    size = (fields * levels * cols * chunks, LANE)
    return pl.pallas_call(
        functools.partial(tile_kernel, levels, cols, chunks),
        grid=(fields,),
        in_specs=[SMEM, SMEM, SMEM]
        + [per_field(state2.shape[1:]), whole(mask.shape), whole(mask_rows.shape)]
        + [whole(kappa.shape), per_field(mixing.shape[1:])]
        + [per_field(x_low.shape[1:])] * 2
        + [whole(y_low.shape)] * 2,
        out_specs=whole(size),
        out_shape=jax.ShapeDtypeStruct(size, jnp.float32),
        scratch_shapes=[
            pltpu.VMEM((cols + 2, DEPTH, rows), jnp.float32),
            pltpu.VMEM((DEPTH, LANE), jnp.float32),
            pltpu.VMEM((DEPTH, 4 * DEPTH), jnp.bfloat16),
            pltpu.VMEM((4 * DEPTH, 2 * rows), jnp.bfloat16),
        ],
        compiler_params=pltpu.CompilerParams(vmem_limit_bytes=40 * MIB),
        cost_estimate=pl.CostEstimate(
            flops=8 * fields * levels * levels * cols * rows,
            bytes_accessed=12 * fields * levels * cols * rows,
            transcendentals=0,
        ),
        name="tile",
    )(cells, counts, values, state2, mask, mask_rows, kappa, mixing, *halos)


def finish_kernel(
    levels, cols, chunks, is_child, nest_x, nest_y, tile, mask, arrived, sent, out, group
):
    f = pl.program_id(0)
    rows = chunks * LANE
    step = cols * chunks
    blocks = cols // 3

    @pl.when(is_child[0] == 1)
    def _():
        @pl.when(f == 0)
        def _():
            ids = lax.broadcasted_iota(jnp.int32, group.shape, 0)
            ids = jnp.where(ids < LANE, ids, ids - LANE)
            group[...] = jnp.where(lane_ids(group.shape) // 3 == ids, 1.0, 0.0).astype(jnp.bfloat16)

        for i in range(blocks):
            high, low = halves(arrived[0, pl.ds(i, levels, stride=blocks), :])
            both = jnp.concatenate([high, low], axis=1)
            value = jnp.dot(both, group[...], preferred_element_type=jnp.float32) * (1.0 / 9.0)
            for x in range(3 * i, 3 * i + 3):
                row = mask_row(mask, x)
                for c in range(chunks):
                    part = slice(c * LANE, (c + 1) * LANE)
                    at = pl.ds(x * chunks + c, levels, stride=step)
                    out[0, at, :] = tile[0, at, :] + value[:, part] * row[:, part]

    @pl.when(is_child[0] == 0)
    def _():
        out[...] = tile[...]
        for i in range(blocks):
            at = pl.ds(i, levels, stride=blocks)
            delta = arrived[0, at, :] - sent[0, at, :]
            wide = jnp.concatenate([delta, jnp.zeros((levels, rows - LANE), jnp.float32)], 1)
            value = pltpu.roll(wide, nest_y[0], 1) * mask_row(mask, nest_x[0] + i)
            for c in range(chunks):
                at = pl.ds((nest_x[0] + i) * chunks + c, levels, stride=step)
                out[0, at, :] = out[0, at, :] + value[:, c * LANE : (c + 1) * LANE]


def finish(is_child, nest_x, nest_y, tile, mask, arrived, sent, dims):
    levels, cols, chunks = dims
    fields = tile.shape[0]
    return pl.pallas_call(
        functools.partial(finish_kernel, levels, cols, chunks),
        grid=(fields,),
        in_specs=[SMEM, SMEM, SMEM]
        + [per_field(tile.shape[1:]), whole(mask.shape)]
        + [per_field(arrived.shape[1:])] * 2,
        out_specs=per_field(tile.shape[1:]),
        out_shape=jax.ShapeDtypeStruct(tile.shape, jnp.float32),
        scratch_shapes=[pltpu.VMEM((2 * LANE, chunks * LANE), jnp.bfloat16)],
        compiler_params=pltpu.CompilerParams(vmem_limit_bytes=24 * MIB),
        name="finish",
    )(is_child, nest_x, nest_y, tile, mask, arrived, sent)


def from_neighbours(low, high, axis):
    ends = lax.axis_size(axis) - 1
    before = lax.ppermute(high, axis, [(i, i + 1) for i in range(ends)])
    after = lax.ppermute(low, axis, [(i + 1, i) for i in range(ends)])
    return before, after


def local(
    adjoint_state,
    land_mask,
    diffusivity,
    mixing,
    nudging,
    nest_x,
    nest_y,
    obs_forcing,
    obs_cell,
    obs_count,
):
    _, fields, levels, cols, rows = adjoint_state.shape
    chunks = rows // LANE
    dims = (levels, cols, chunks)
    state5 = adjoint_state.reshape(fields, levels, cols, 1, rows)
    state2 = adjoint_state.reshape(fields, levels * cols * chunks, LANE)
    mask = land_mask.reshape(cols, 1, rows)
    mask_rows = land_mask.reshape(cols * chunks, 1, LANE)
    kappa = diffusivity.reshape(cols, 1, rows)
    matrices = mixing.reshape(fields, levels, 1, levels)
    is_child = (lax.axis_index("grp") == 0).astype(jnp.int32).reshape(1)

    gathered = lax.all_gather(obs_forcing[0, 0], ("ty", "tx"), axis=0)
    me = lax.axis_index("ty") * lax.axis_size("tx") + lax.axis_index("tx")
    values = lax.dynamic_index_in_dim(gathered, me, axis=2, keepdims=False)

    x_low, x_high = x_edges(state5, mask)
    x_halos = from_neighbours(x_low, x_high, "tx")
    y_low, y_high = y_edges(state2, mask, levels, cols, chunks)
    y_halos = from_neighbours(y_low, y_high, "ty")
    halos = x_halos + y_halos

    sent = payload_of(
        is_child, nest_x, nest_y, state2, mask, kappa, nudging, matrices, halos, dims
    )
    arrived = lax.ppermute(sent, "grp", [(0, 1), (1, 0)])
    tile = tile_of(
        obs_cell[0, :, :, 0],
        obs_count.reshape(1, -1),
        values,
        state2,
        mask,
        mask_rows,
        kappa,
        matrices,
        halos,
        dims,
    ).reshape(state2.shape)
    out = finish(is_child, nest_x, nest_y, tile, mask, arrived, sent, dims)
    return out.reshape(adjoint_state.shape)


def solution(mesh):
    in_specs = (
        P("grp", None, None, "tx", "ty"),
        P("grp", "tx", "ty"),
        P("grp", "tx", "ty"),
        P("grp", None, None, None),
        P("tx", "ty"),
        P(("ty", "tx")),
        P(("ty", "tx")),
        P("grp", ("ty", "tx"), None, None),
        P("grp", None, None, ("ty", "tx")),
        P("grp", None, ("ty", "tx")),
    )
    out_specs = P("grp", None, None, "tx", "ty")
    return jax.shard_map(local, mesh=mesh, in_specs=in_specs, out_specs=out_specs, check_vma=False)
```

```python
import functools

import jax
import jax.numpy as jnp
from jax import lax
from jax.experimental import pallas as pl
from jax.experimental.pallas import tpu as pltpu
from jax.sharding import PartitionSpec as P

LANE = 128
PAD = 56
DEPTH = 64
MIB = 1 << 20
HBM = pl.BlockSpec(memory_space=pltpu.HBM)
SMEM = pl.BlockSpec(memory_space=pltpu.SMEM)
VMEM = pl.BlockSpec(memory_space=pltpu.VMEM)
F32 = jnp.float32


def lane_ids(shape):
    return lax.broadcasted_iota(jnp.int32, shape, len(shape) - 1)


def row_of(ref, x):
    return ref[x].astype(F32)


def chunk(c):
    return slice(c * LANE, (c + 1) * LANE)


def x_edges_kernel(state, mask, forcing, low, high, parcel, buf, mask_buf, sems):
    cols = state.shape[2]
    copies = [pltpu.make_async_copy(mask, mask_buf, sems.at[2])]
    for n, x in enumerate((0, cols - 1)):
        copies.append(pltpu.make_async_copy(state.at[:, :, x], buf.at[n], sems.at[n]))
    for copy in copies:
        copy.start()
    slots, dests = forcing.shape
    parcel[...] = jnp.zeros_like(parcel)
    for t in range(parcel.shape[0]):
        parcel[t, :, :dests] = forcing[...]
    for copy in copies:
        copy.wait()
    for n, (x, out) in enumerate(((0, low), (cols - 1, high))):
        out[...] = buf[n] * row_of(mask_buf, x)[None, None]


def x_edges(state5, mask, forcing, peers):
    fields, levels, cols, _, rows = state5.shape
    edge = (fields, levels, 1, rows)
    return pl.pallas_call(
        x_edges_kernel,
        in_specs=[HBM, HBM, VMEM],
        out_specs=[VMEM] * 3,
        out_shape=[jax.ShapeDtypeStruct(edge, F32)] * 2
        + [jax.ShapeDtypeStruct((peers, forcing.shape[0], LANE), F32)],
        scratch_shapes=[
            pltpu.VMEM((2,) + edge, F32),
            pltpu.VMEM(mask.shape, jnp.int32),
            pltpu.SemaphoreType.DMA((3,)),
        ],
        compiler_params=pltpu.CompilerParams(vmem_limit_bytes=61 * MIB),
        name="x_edges",
    )(state5, mask, forcing)


def spread_of(here, above, below, kappa, y_low, y_high):
    rows = here.shape[1]
    lanes = lane_ids((here.shape[0], LANE))
    before = pltpu.roll(here, 1, 1)
    after = pltpu.roll(here, rows - 1, 1)
    before = jnp.concatenate([jnp.where(lanes == 0, y_low, before[:, :LANE]), before[:, LANE:]], 1)
    after = jnp.concatenate(
        [after[:, :-LANE], jnp.where(lanes == LANE - 1, y_high, after[:, -LANE:])], 1
    )
    return here + kappa * (above + below + before + after - 4.0 * here)


def halves(value):
    high = value.astype(jnp.bfloat16)
    return high, (value - high.astype(F32)).astype(jnp.bfloat16)


def fill_matrix(levels, mixing, square, matrix):
    square[:levels, :levels] = mixing
    value = square[...]
    high = value.astype(jnp.bfloat16).astype(F32)
    low = value - high
    matrix[:, :LANE] = (high + pltpu.roll(high, DEPTH, 1)).astype(jnp.bfloat16)
    matrix[:, LANE:] = (low + pltpu.roll(low, DEPTH, 1)).astype(jnp.bfloat16)


def fill_stack(stack, part, value):
    wide = jnp.concatenate([value, jnp.zeros((DEPTH - PAD, value.shape[1]), F32)], 0)
    high, low = halves(wide)
    for n, half in enumerate((high, low, high, low)):
        stack[n * DEPTH : (n + 1) * DEPTH, part] = half


def mix(matrix, stack):
    return jnp.dot(matrix, stack, preferred_element_type=F32)


def fill_group(group):
    ids = lax.broadcasted_iota(jnp.int32, group.shape, 0) // 3
    group[...] = jnp.where(ids == lane_ids(group.shape), 1.0, 0.0).astype(jnp.bfloat16)


def grouped(value, group):
    high, low = halves(value)
    total = jnp.dot(high, group, preferred_element_type=F32)
    return total + jnp.dot(low, group, preferred_element_type=F32)


def inner_kernel(
    levels, is_child, nest_x, nest_y, state, mask, kappa, nudging, mixing,
    out, masked, matrices, square, stack, group,
):
    fields, cols, _, rows = masked.shape
    chunks = rows // LANE
    step = cols * chunks
    size = levels * step
    blocks = cols // 3
    inner = blocks - 2
    square[...] = jnp.zeros_like(square)
    fill_group(group)

    def field(f, carry):
        fill_matrix(levels, mixing[f, :, 0, :], square, matrices.at[f])
        for x in range(cols):
            row = row_of(mask, x)
            masked[f, x, PAD - 8 :, :] = jnp.zeros((8, rows), F32)
            for c in range(chunks):
                at = pl.ds(f * size + x * chunks + c, levels, stride=step)
                masked[f, x, :levels, chunk(c)] = state[at, :] * row[:, chunk(c)]

        def spread(x):
            return spread_of(masked[f, x], masked[f, x - 1], masked[f, x + 1], kappa[x], 0.0, 0.0)

        @pl.when(is_child[0] == 1)
        def _():
            for b in range(inner):
                total = None
                for x in range(3 * b + 3, 3 * b + 6):
                    term = nudging[x : x + 1, :] * spread(x)
                    total = term if total is None else total + term
                fill_stack(stack, chunk(b), grouped(total, group[...]))

        @pl.when(is_child[0] == 0)
        def _():
            back = lax.rem(rows - nest_y[0], rows)
            for b in range(inner):
                value = pltpu.roll(spread(nest_x[0] + b + 1), back, 1)[:, :LANE]
                fill_stack(stack, chunk(b), value)

        mixed = mix(matrices[f], stack[...])
        for b in range(inner):
            at = pl.ds(f * (levels * inner) + b, levels, stride=inner)
            out[at, :] = mixed[:levels, chunk(b)]
        return carry

    lax.fori_loop(0, fields, field, 0)


def inner_part(scalars, state2, mask, kappa, nudging, mixing, dims):
    fields, levels, cols, chunks = dims
    rows = chunks * LANE
    inner = cols // 3 - 2
    return pl.pallas_call(
        functools.partial(inner_kernel, levels),
        in_specs=[SMEM] * 3 + [VMEM] * 5,
        out_specs=[VMEM] * 3,
        out_shape=[
            jax.ShapeDtypeStruct((fields * levels * inner, LANE), F32),
            jax.ShapeDtypeStruct((fields, cols, PAD, rows), F32),
            jax.ShapeDtypeStruct((fields, DEPTH, 4 * DEPTH), jnp.bfloat16),
        ],
        scratch_shapes=[
            pltpu.VMEM((DEPTH, LANE), F32),
            pltpu.VMEM((4 * DEPTH, inner * LANE), jnp.bfloat16),
            pltpu.VMEM((rows, LANE), jnp.bfloat16),
        ],
        compiler_params=pltpu.CompilerParams(vmem_limit_bytes=24 * MIB),
        name="inner_part",
    )(*scalars, state2, mask, kappa, nudging, mixing)


def y_edges_kernel(ty, masked, arrived, parcel):
    fields, cols, _, rows = masked.shape
    lanes = lane_ids((PAD, LANE))

    def field(f, carry):
        low, high = carry
        first = jnp.zeros((PAD, LANE), F32)
        last = jnp.zeros((PAD, LANE), F32)
        for x in range(cols):
            v = masked[f, x, :, :LANE]
            first = jnp.where(lanes == x, pltpu.roll(v, x, 1) if x else v, first)
            v = masked[f, x, :, rows - LANE :]
            last = jnp.where(lanes == x, pltpu.roll(v, x + 1, 1), last)
        return low + pltpu.roll(first, f * cols, 1), high + pltpu.roll(last, f * cols, 1)

    zero = jnp.zeros((PAD, LANE), F32)
    low, high = lax.fori_loop(0, fields, field, (zero, zero))
    sources, slots, _ = arrived.shape
    for t in range(parcel.shape[0]):
        for s in range(sources):
            parcel[t, s * slots : (s + 1) * slots, :] = arrived[s]
        before = (ty[0] == t + 1).astype(F32)
        after = (ty[0] == t - 1).astype(F32)
        parcel[t, sources * slots :, :] = low * before + high * after


def y_edges(ty, masked, arrived, peers):
    sources, slots, _ = arrived.shape
    return pl.pallas_call(
        y_edges_kernel,
        in_specs=[SMEM, VMEM, VMEM],
        out_specs=VMEM,
        out_shape=jax.ShapeDtypeStruct((peers, sources * slots + PAD, LANE), F32),
        compiler_params=pltpu.CompilerParams(vmem_limit_bytes=20 * MIB),
        name="y_edges",
    )(ty, masked, arrived)


def fill_halos(ty, parcel, y_low, y_high):
    peers, height, _ = parcel.shape
    before = parcel[jnp.maximum(ty[0] - 1, 0), height - PAD :, :]
    after = parcel[jnp.minimum(ty[0] + 1, peers - 1), height - PAD :, :]
    y_low[...] = jnp.where(ty[0] > 0, before, 0.0)
    y_high[...] = jnp.where(ty[0] < peers - 1, after, 0.0)


def at_first(y_low, k):
    return pltpu.roll(y_low[...], lax.rem(LANE - k, LANE), 1)


def at_last(y_high, k):
    return pltpu.roll(y_high[...], LANE - 1 - k, 1)


def outer_kernel(
    levels, is_child, nest_x, nest_y, ty, masked, matrices, kappa, nudging, x_low, x_high, parcel,
    out, sides, y_low, y_high, stack, group,
):
    fields, cols, _, rows = masked.shape
    blocks = cols // 3
    inner = blocks - 2
    lanes = lane_ids((PAD, LANE))
    sides[...] = jnp.zeros_like(sides)
    fill_group(group)
    fill_halos(ty, parcel, y_low, y_high)

    def field(f, fixes):
        sides[0, :levels, :] = x_low[f, :, 0, :]
        sides[1, :levels, :] = x_high[f, :, 0, :]

        @pl.when(is_child[0] == 1)
        def _():
            for n, b in enumerate((0, blocks - 1)):
                total = None
                for x in range(3 * b, 3 * b + 3):
                    above = masked[f, x - 1] if x > 0 else sides[0]
                    below = masked[f, x + 1] if x < cols - 1 else sides[1]
                    k = f * cols + x
                    value = spread_of(
                        masked[f, x], above, below, kappa[x], at_first(y_low, k), at_last(y_high, k)
                    )
                    term = nudging[x : x + 1, :] * value
                    total = term if total is None else total + term
                fill_stack(stack, chunk(n), grouped(total, group[...]))
            fix = jnp.zeros((PAD, LANE), F32)
            for b in range(inner):
                part = jnp.zeros((PAD, LANE), F32)
                for x in range(3 * b + 3, 3 * b + 6):
                    weight = nudging[x : x + 1, :] * kappa[x]
                    k = f * cols + x
                    first = at_first(y_low, k) * weight[:, :LANE]
                    last = at_last(y_high, k) * weight[:, rows - LANE :]
                    part = part + jnp.where(lanes == 0, first, 0.0)
                    part = part + jnp.where(lanes == LANE - 1, last, 0.0)
                fix = fix + (pltpu.roll(part, 2 * b, 1) if b else part)
            fill_stack(stack, chunk(2), fix)

        @pl.when(is_child[0] == 0)
        def _():
            back = lax.rem(rows - nest_y[0], rows)
            for n, b in enumerate((0, blocks - 1)):
                x = nest_x[0] + b
                above = masked[f, jnp.maximum(x - 1, 0)]
                above = jnp.where(x == 0, sides[0], above)
                below = masked[f, jnp.minimum(x + 1, cols - 1)]
                below = jnp.where(x == cols - 1, sides[1], below)
                k = f * cols + x
                value = spread_of(
                    masked[f, x], above, below, kappa[x], at_first(y_low, k), at_last(y_high, k)
                )
                fill_stack(stack, chunk(n), pltpu.roll(value, back, 1)[:, :LANE])
            starts = (nest_y[0] == 0).astype(F32)
            ends = (nest_y[0] == rows - LANE).astype(F32)
            fix = jnp.zeros((PAD, LANE), F32)
            for b in range(inner):
                x = nest_x[0] + b + 1
                k = f * cols + x
                weight = kappa[x]
                first = at_first(y_low, k) * (weight[:, :LANE] * starts)
                last = at_last(y_high, k) * (weight[:, rows - LANE :] * ends)
                part = jnp.where(lanes == 0, first, jnp.where(lanes == LANE - 1, last, 0.0))
                fix = fix + (pltpu.roll(part, 2 * b, 1) if b else part)
            fill_stack(stack, chunk(2), fix)

        mixed = mix(matrices[f], stack[...])
        for n in range(2):
            at = pl.ds(f * (2 * levels) + n, levels, stride=2)
            out[at, :] = mixed[:levels, chunk(n)]
        return fixes + pltpu.roll(mixed[:PAD, chunk(2)], 2 * inner * f, 1)

    fixes = lax.fori_loop(0, fields, field, jnp.zeros((PAD, LANE), F32))
    out[out.shape[0] - PAD :, :] = fixes


def outer_part(scalars, ty, masked, matrices, kappa, nudging, x_halos, parcel, dims):
    fields, levels, cols, chunks = dims
    rows = chunks * LANE
    height = -(-fields * 2 * levels // 8) * 8 + PAD
    return pl.pallas_call(
        functools.partial(outer_kernel, levels),
        in_specs=[SMEM] * 4 + [VMEM] * 7,
        out_specs=VMEM,
        out_shape=jax.ShapeDtypeStruct((height, LANE), F32),
        scratch_shapes=[
            pltpu.VMEM((2, PAD, rows), F32),
            pltpu.VMEM((PAD, LANE), F32),
            pltpu.VMEM((PAD, LANE), F32),
            pltpu.VMEM((4 * DEPTH, 3 * LANE), jnp.bfloat16),
            pltpu.VMEM((rows, LANE), jnp.bfloat16),
        ],
        compiler_params=pltpu.CompilerParams(vmem_limit_bytes=20 * MIB),
        name="outer_part",
    )(*scalars, ty, masked, matrices, kappa, nudging, *x_halos, parcel)


def tile_kernel(
    levels, cells, counts, ty, me, masked, matrices, kappa, x_low, x_high, parcel,
    out, sides, y_low, y_high, stack,
):
    fields, cols, _, rows = masked.shape
    chunks = rows // LANE
    sides[...] = jnp.zeros_like(sides)
    fill_halos(ty, parcel, y_low, y_high)
    pair = 2

    def field(f, carry):
        sides[0, :levels, :] = x_low[f, :, 0, :]
        sides[1, :levels, :] = x_high[f, :, 0, :]
        for x0 in range(0, cols, pair):
            for x in range(x0, x0 + pair):
                above = masked[f, x - 1] if x > 0 else sides[0]
                below = masked[f, x + 1] if x < cols - 1 else sides[1]
                k = f * cols + x
                value = spread_of(
                    masked[f, x], above, below, kappa[x], at_first(y_low, k), at_last(y_high, k)
                )
                fill_stack(stack, slice((x - x0) * rows, (x - x0 + 1) * rows), value)
            mixed = mix(matrices[f], stack[...])
            for n in range(pair * chunks):
                out[(f * cols + x0) * chunks + n, :, :] = mixed[:PAD, chunk(n)]
        return carry

    lax.fori_loop(0, fields, field, 0)
    lanes = lane_ids((1, LANE))
    peers = parcel.shape[0]
    slots = cells.shape[1]
    sources = cells.shape[0] // peers

    def source(s, carry):
        group = lax.div(s, sources)
        first = (s - group * sources) * slots

        def slot(k, carry):
            cell = cells[s, k]
            column = lax.div(cell, cols * rows)
            inside = cell - column * (cols * rows)
            f = lax.div(column, levels)
            level = column - f * levels
            piece = lax.div(inside, LANE)
            lane = inside - piece * LANE
            value = parcel[group, pl.ds(first + k, 1), :]
            value = pltpu.roll(value, lax.rem(lane + LANE - me[0], LANE), 1)
            at = f * (cols * chunks) + piece
            old = out[at, pl.ds(level, 1), :]
            out[at, pl.ds(level, 1), :] = old + jnp.where(lanes == lane, value, 0.0)
            return carry

        return lax.fori_loop(0, counts[0, s], slot, carry)

    lax.fori_loop(0, cells.shape[0], source, 0)


def tile_of(cells, counts, ty, me, masked, matrices, kappa, x_halos, parcel, dims):
    fields, levels, cols, chunks = dims
    rows = chunks * LANE
    return pl.pallas_call(
        functools.partial(tile_kernel, levels),
        in_specs=[SMEM] * 4 + [VMEM] * 6,
        out_specs=VMEM,
        out_shape=jax.ShapeDtypeStruct((fields * cols * chunks, PAD, LANE), F32),
        scratch_shapes=[
            pltpu.VMEM((2, PAD, rows), F32),
            pltpu.VMEM((PAD, LANE), F32),
            pltpu.VMEM((PAD, LANE), F32),
            pltpu.VMEM((4 * DEPTH, 2 * rows), jnp.bfloat16),
        ],
        compiler_params=pltpu.CompilerParams(vmem_limit_bytes=24 * MIB),
        cost_estimate=pl.CostEstimate(
            flops=8 * fields * levels * levels * cols * rows,
            bytes_accessed=12 * fields * levels * cols * rows,
            transcendentals=0,
        ),
        name="tile",
    )(cells, counts, ty, me, masked, matrices, kappa, *x_halos, parcel)


def finish_kernel(
    levels, is_child, nest_x, nest_y, tile, mask, in_arrived, out_arrived, in_sent, out_sent,
    out, buf, group, sems,
):
    cols = mask.shape[0]
    rows = mask.shape[2]
    chunks = rows // LANE
    step = cols * chunks
    size = levels * step
    fields = out.shape[0] // size
    blocks = cols // 3
    inner = blocks - 2
    lanes = lane_ids((levels, LANE))
    ends = jnp.logical_or(lanes == 0, lanes == LANE - 1)
    height = out_arrived.shape[0]

    def copy(f):
        at = pl.ds(f * size, size)
        return pltpu.make_async_copy(buf.at[at], out.at[at], sems.at[f])

    def payload(f, b, inner_ref, outer_ref):
        if b in (0, blocks - 1):
            return outer_ref[pl.ds(f * (2 * levels) + min(b, 1), levels, stride=2), :]
        value = inner_ref[pl.ds(f * (levels * inner) + b - 1, levels, stride=inner), :]
        fixes = outer_ref[height - PAD : height - PAD + levels, :]
        shift = lax.rem(2 * LANE - 2 * inner * f - 2 * (b - 1), LANE)
        return value + jnp.where(ends, pltpu.roll(fixes, shift, 1), 0.0)

    def plain(f, x):
        row = row_of(mask, x)
        for c in range(chunks):
            piece = x * chunks + c
            at = pl.ds(f * size + piece, levels, stride=step)
            buf[at, :] = tile[f * step + piece, :levels, :] * row[:, chunk(c)]

    def fill_child(f, carry):
        for b in range(blocks):
            high, low = halves(payload(f, b, in_arrived, out_arrived))
            both = jnp.concatenate([high, low], axis=1)
            value = jnp.dot(both, group[...], preferred_element_type=F32) * (1.0 / 9.0)
            for x in range(3 * b, 3 * b + 3):
                row = row_of(mask, x)
                for c in range(chunks):
                    piece = x * chunks + c
                    at = pl.ds(f * size + piece, levels, stride=step)
                    total = tile[f * step + piece, :levels, :] + value[:, chunk(c)]
                    buf[at, :] = total * row[:, chunk(c)]
        copy(f).start()
        return carry

    def fill_parent(f, carry):
        for x in range(cols):
            plain(f, x)
        for b in range(blocks):
            delta = payload(f, b, in_arrived, out_arrived) - payload(f, b, in_sent, out_sent)
            wide = jnp.concatenate([delta, jnp.zeros((levels, rows - LANE), F32)], 1)
            x = nest_x[0] + b
            value = pltpu.roll(wide, nest_y[0], 1) * row_of(mask, x)
            for c in range(chunks):
                at = pl.ds(f * size + x * chunks + c, levels, stride=step)
                buf[at, :] = buf[at, :] + value[:, chunk(c)]
        copy(f).start()
        return carry

    @pl.when(is_child[0] == 1)
    def _():
        ids = lax.broadcasted_iota(jnp.int32, group.shape, 0)
        ids = jnp.where(ids < LANE, ids, ids - LANE)
        group[...] = jnp.where(lane_ids(group.shape) // 3 == ids, 1.0, 0.0).astype(jnp.bfloat16)
        lax.fori_loop(0, fields, fill_child, 0)

    @pl.when(is_child[0] == 0)
    def _():
        lax.fori_loop(0, fields, fill_parent, 0)

    for f in range(fields):
        copy(f).wait()


def finish(scalars, tile, mask, arrived, sent, dims):
    fields, levels, cols, chunks = dims
    rows = chunks * LANE
    size = (fields * levels * cols * chunks, LANE)
    return pl.pallas_call(
        functools.partial(finish_kernel, levels),
        in_specs=[SMEM] * 3 + [VMEM] * 6,
        out_specs=HBM,
        out_shape=jax.ShapeDtypeStruct(size, F32),
        scratch_shapes=[
            pltpu.VMEM(size, F32),
            pltpu.VMEM((2 * LANE, rows), jnp.bfloat16),
            pltpu.SemaphoreType.DMA((fields,)),
        ],
        compiler_params=pltpu.CompilerParams(vmem_limit_bytes=24 * MIB),
        name="finish",
    )(*scalars, tile, mask, *arrived, *sent)


def from_neighbours(low, high, axis):
    ends = lax.axis_size(axis) - 1
    before = lax.ppermute(high, axis, [(i, i + 1) for i in range(ends)])
    after = lax.ppermute(low, axis, [(i + 1, i) for i in range(ends)])
    return before, after


def to_all(parcel, axis):
    return lax.all_to_all(parcel, axis, split_axis=0, concat_axis=0, tiled=True)


def swapped(value):
    return lax.ppermute(value, "grp", [(0, 1), (1, 0)])


def local(
    adjoint_state,
    land_mask,
    diffusivity,
    mixing,
    nudging,
    nest_x,
    nest_y,
    obs_forcing,
    obs_cell,
    obs_count,
):
    _, fields, levels, cols, rows = adjoint_state.shape
    chunks = rows // LANE
    dims = (fields, levels, cols, chunks)
    state5 = adjoint_state.reshape(fields, levels, cols, 1, rows)
    state2 = adjoint_state.reshape(fields * levels * cols * chunks, LANE)
    mask = land_mask.reshape(cols, 1, rows)
    kappa = diffusivity.reshape(cols, 1, rows)
    mixing = mixing.reshape(fields, levels, 1, levels)
    ty = lax.axis_index("ty").astype(jnp.int32)
    me = ty * lax.axis_size("tx") + lax.axis_index("tx").astype(jnp.int32)
    is_child = (lax.axis_index("grp") == 0).astype(jnp.int32)
    ty, me, is_child = ty.reshape(1), me.reshape(1), is_child.reshape(1)
    scalars = (is_child, nest_x, nest_y)

    x_low, x_high, parcel = x_edges(state5, mask, obs_forcing[0, 0], lax.axis_size("tx"))
    x_halos = from_neighbours(x_low, x_high, "tx")
    parcel = to_all(parcel, "tx")
    in_sent, masked, matrices = inner_part(scalars, state2, mask, kappa, nudging, mixing, dims)
    in_arrived = swapped(in_sent)
    parcel = to_all(y_edges(ty, masked, parcel, lax.axis_size("ty")), "ty")
    out_sent = outer_part(scalars, ty, masked, matrices, kappa, nudging, x_halos, parcel, dims)
    out_arrived = swapped(out_sent)
    cells = obs_cell[0, :, :, 0]
    counts = obs_count.reshape(1, -1)
    tile = tile_of(cells, counts, ty, me, masked, matrices, kappa, x_halos, parcel, dims)
    out = finish(scalars, tile, mask, (in_arrived, out_arrived), (in_sent, out_sent), dims)
    return out.reshape(adjoint_state.shape)


def solution(mesh):
    in_specs = (
        P("grp", None, None, "tx", "ty"),
        P("grp", "tx", "ty"),
        P("grp", "tx", "ty"),
        P("grp", None, None, None),
        P("tx", "ty"),
        P(("ty", "tx")),
        P(("ty", "tx")),
        P("grp", ("ty", "tx"), None, None),
        P("grp", None, None, ("ty", "tx")),
        P("grp", None, ("ty", "tx")),
    )
    out_specs = P("grp", None, None, "tx", "ty")
    return jax.shard_map(local, mesh=mesh, in_specs=in_specs, out_specs=out_specs, check_vma=False)
```

```python
import functools

import jax
import jax.numpy as jnp
from jax import lax
from jax.experimental import pallas as pl
from jax.experimental.pallas import tpu as pltpu
from jax.sharding import PartitionSpec as P

LANE = 128
PAD = 56
DEPTH = 64
MIB = 1 << 20
HBM = pl.BlockSpec(memory_space=pltpu.HBM)
SMEM = pl.BlockSpec(memory_space=pltpu.SMEM)
VMEM = pl.BlockSpec(memory_space=pltpu.VMEM)
F32 = jnp.float32


def lane_ids(shape):
    return lax.broadcasted_iota(jnp.int32, shape, len(shape) - 1)


def row_of(ref, x):
    return ref[x].astype(F32)


def chunk(c):
    return slice(c * LANE, (c + 1) * LANE)


def in_hbm(value):
    return pltpu.with_memory_space_constraint(value, pltpu.HBM)


def in_vmem(value):
    return pltpu.with_memory_space_constraint(value, pltpu.VMEM)


def x_edges_kernel(state, mask, low, high, buf, mask_buf, sems):
    fields, _, cols = state.shape[:3]
    copies = [pltpu.make_async_copy(mask, mask_buf, sems.at[2 * fields])]
    for n, x in enumerate((0, cols - 1)):
        for f in range(fields):
            copies.append(
                pltpu.make_async_copy(state.at[f, :, x], buf.at[n, f], sems.at[n * fields + f])
            )
    for copy in copies:
        copy.start()
    copies[0].wait()
    for n, (x, out) in enumerate(((0, low), (cols - 1, high))):
        for f in range(fields):
            copies[1 + n * fields + f].wait()
            out[f] = buf[n, f] * row_of(mask_buf, x)[None]


def x_edges(state5, mask):
    fields, levels, cols, _, rows = state5.shape
    edge = (fields, levels, 1, rows)
    return pl.pallas_call(
        x_edges_kernel,
        in_specs=[HBM, HBM],
        out_specs=[VMEM] * 2,
        out_shape=[pltpu.VMEM(edge, F32)] * 2,
        scratch_shapes=[
            pltpu.VMEM((2,) + edge, F32),
            pltpu.VMEM(mask.shape, jnp.int32),
            pltpu.SemaphoreType.DMA((2 * fields + 1,)),
        ],
        compiler_params=pltpu.CompilerParams(vmem_limit_bytes=8 * MIB),
        name="x_edges",
    )(in_hbm(state5), in_hbm(mask))


def spread_of(here, above, below, kappa, y_low=0.0, y_high=0.0):
    rows = here.shape[1]
    lanes = lane_ids((here.shape[0], LANE))
    before = pltpu.roll(here, 1, 1)
    after = pltpu.roll(here, rows - 1, 1)
    before = jnp.concatenate([jnp.where(lanes == 0, y_low, before[:, :LANE]), before[:, LANE:]], 1)
    after = jnp.concatenate(
        [after[:, :-LANE], jnp.where(lanes == LANE - 1, y_high, after[:, -LANE:])], 1
    )
    beside = before + after
    if above is not None:
        beside = beside + above
    if below is not None:
        beside = beside + below
    return here + kappa * (beside - 4.0 * here)


def halves(value):
    high = value.astype(jnp.bfloat16)
    return high, (value - high.astype(F32)).astype(jnp.bfloat16)


def deepened(value):
    return jnp.concatenate([value, jnp.zeros((DEPTH - value.shape[0], value.shape[1]), F32)], 0)


def fill_matrix(levels, mixing, square, matrix):
    square[:levels, :levels] = mixing
    value = square[...]
    high = value.astype(jnp.bfloat16).astype(F32)
    low = value - high
    matrix[:, :LANE] = (high + pltpu.roll(high, DEPTH, 1)).astype(jnp.bfloat16)
    matrix[:, LANE:] = (low + pltpu.roll(low, DEPTH, 1)).astype(jnp.bfloat16)


def fill_stack(stack, part, value):
    high, low = halves(value)
    for n, half in enumerate((high, low, high, low)):
        stack[n * DEPTH : (n + 1) * DEPTH, part] = half


def mix(matrix, stack):
    return jnp.dot(matrix, stack, preferred_element_type=F32)


def fill_group(group):
    ids = lax.broadcasted_iota(jnp.int32, group.shape, 0) // 3
    group[...] = jnp.where(ids == lane_ids(group.shape), 1.0, 0.0).astype(jnp.bfloat16)


def grouped(high, low, group):
    total = jnp.dot(high, group, preferred_element_type=F32)
    return total + jnp.dot(low, group, preferred_element_type=F32)


def aligned(index, size):
    return pl.ds(pl.multiple_of(index * size, size), size)


def front_kernel(
    levels, is_child, nest_x, nest_y, ty, state, mask, kappa, nudging, mixing, forcing,
    masked, matrices, first_edge, second_edge, inner, base,
    buf, mask_buf, kappa_buf, nudging_buf, mixing_buf, forcing_buf, square, wide, stack, group, sems,
):
    fields, cols, _, rows = masked.shape
    chunks = rows // LANE
    step = cols * chunks
    size = levels * step
    blocks = cols // 3

    def copy(f):
        at = pl.ds(f * size, size)
        return pltpu.make_async_copy(state.at[at], buf.at[at], sems.at[f])

    smalls = [
        pltpu.make_async_copy(source, target, sems.at[fields + n])
        for n, (source, target) in enumerate(
            (
                (mask, mask_buf),
                (kappa, kappa_buf),
                (nudging, nudging_buf),
                (mixing, mixing_buf),
                (forcing, forcing_buf),
            )
        )
    ]
    copy(0).start()
    for small in smalls:
        small.start()
    for f in range(1, fields):
        copy(f).start()
    square[...] = jnp.zeros_like(square)
    fill_group(group)
    for small in smalls:
        small.wait()
    lanes = lane_ids((PAD, LANE))

    def field(f, carry):
        copy(f).wait()
        fill_matrix(levels, mixing_buf[f, :, 0, :], square, matrices.at[f])
        for x in range(cols):
            row = row_of(mask_buf, x)
            masked[f, x, PAD - 8 :, :] = jnp.zeros((8, rows), F32)
            for c in range(chunks):
                at = pl.ds(f * size + x * chunks + c, levels, stride=step)
                masked[f, x, :levels, chunk(c)] = buf[at, :] * row[:, chunk(c)]

        low, high = carry
        start = jnp.zeros((PAD, LANE), F32)
        end = jnp.zeros((PAD, LANE), F32)
        for x in range(cols):
            v = masked[f, x, :, :LANE]
            start = jnp.where(lanes == x, pltpu.roll(v, x, 1) if x else v, start)
            v = masked[f, x, :, rows - LANE :]
            end = jnp.where(lanes == x, pltpu.roll(v, x + 1, 1), end)

        @pl.when(is_child[0] == 1)
        def _():
            for b in range(blocks):
                total = None
                for x in range(3 * b, 3 * b + 3):
                    above = masked[f, x - 1] if x > 0 else None
                    below = masked[f, x + 1] if x < cols - 1 else None
                    value = spread_of(masked[f, x], above, below, kappa_buf[x])
                    term = nudging_buf[x : x + 1, :] * value
                    total = term if total is None else total + term
                at = aligned(f * blocks + b, DEPTH)
                wide[0, at, :], wide[1, at, :] = halves(deepened(total))

        @pl.when(is_child[0] == 0)
        def _():
            back = lax.rem(rows - nest_y[0], rows)
            for b in range(blocks):
                x = nest_x[0] + b
                above = masked[f, jnp.maximum(x - 1, 0)]
                below = masked[f, jnp.minimum(x + 1, cols - 1)]
                if b == 0:
                    above = jnp.where(x == 0, 0.0, above)
                if b == blocks - 1:
                    below = jnp.where(x == cols - 1, 0.0, below)
                value = spread_of(masked[f, x], above, below, kappa_buf[x])
                value = deepened(pltpu.roll(value, back, 1)[:, :LANE])
                fill_stack(stack.at[f], chunk(b), value)

        return low + pltpu.roll(start, f * cols, 1), high + pltpu.roll(end, f * cols, 1)

    zero = jnp.zeros((PAD, LANE), F32)
    low, high = lax.fori_loop(0, fields, field, (zero, zero))
    slots, dests = forcing_buf.shape
    even = (lax.rem(ty[0], 2) == 0).astype(F32)
    second = (ty[0] == 1).astype(F32)
    first_edge[:PAD, :] = high * even + low * (1.0 - even)
    first_edge[PAD:, :] = jnp.zeros((slots, LANE), F32)
    first_edge[PAD:, :dests] = forcing_buf[...]
    second_edge[...] = high * second + low * (1.0 - second)

    @pl.when(is_child[0] == 1)
    def _():
        value = grouped(wide[0], wide[1], group[...])
        for f in range(fields):
            for b in range(blocks):
                at = (f * blocks + b) * DEPTH
                fill_stack(stack.at[f], chunk(b), value[at : at + DEPTH])

    for f in range(fields):
        mixed = mix(matrices[f], stack[f])
        for b in range(1, blocks - 1):
            at = pl.ds(f * levels * (blocks - 2) + b - 1, levels, stride=blocks - 2)
            inner[at, :] = mixed[:levels, chunk(b)]
        base[f, :, :LANE] = mixed[:PAD, :LANE]
        base[f, :, LANE:] = mixed[:PAD, chunk(blocks - 1)]


def front(scalars, ty, state2, mask, kappa, nudging, mixing, forcing, dims):
    fields, levels, cols, chunks = dims
    rows = chunks * LANE
    blocks = cols // 3
    slots = forcing.shape[0]
    large = (state2, mask, kappa, nudging, mixing, forcing)
    return pl.pallas_call(
        functools.partial(front_kernel, levels),
        in_specs=[SMEM] * 4 + [HBM] * 6,
        out_specs=[VMEM] * 6,
        out_shape=[
            pltpu.VMEM((fields, cols, PAD, rows), F32),
            pltpu.VMEM((fields, DEPTH, 4 * DEPTH), jnp.bfloat16),
            pltpu.VMEM((PAD + slots, LANE), F32),
            pltpu.VMEM((PAD, LANE), F32),
            pltpu.VMEM((fields * levels * (blocks - 2), LANE), F32),
            pltpu.VMEM((fields, PAD, 2 * LANE), F32),
        ],
        scratch_shapes=[
            pltpu.VMEM(state2.shape, F32),
            pltpu.VMEM(mask.shape, jnp.int32),
            pltpu.VMEM(kappa.shape, F32),
            pltpu.VMEM(nudging.shape, F32),
            pltpu.VMEM(mixing.shape, F32),
            pltpu.VMEM(forcing.shape, F32),
            pltpu.VMEM((DEPTH, LANE), F32),
            pltpu.VMEM((2, fields * blocks * DEPTH, rows), jnp.bfloat16),
            pltpu.VMEM((fields, 4 * DEPTH, blocks * LANE), jnp.bfloat16),
            pltpu.VMEM((rows, LANE), jnp.bfloat16),
            pltpu.SemaphoreType.DMA((fields + 5,)),
        ],
        compiler_params=pltpu.CompilerParams(vmem_limit_bytes=20 * MIB),
        name="front",
    )(*scalars, ty, *map(in_hbm, large))


def y_halos(ty, peers, first, second):
    one, two = first[:PAD, :], second[:PAD, :]
    even = (lax.rem(ty[0], 2) == 0).astype(F32)
    inside_low = (ty[0] > 0).astype(F32)
    inside_high = (ty[0] < peers - 1).astype(F32)
    low = (two * even + one * (1.0 - even)) * inside_low
    high = (one * even + two * (1.0 - even)) * inside_high
    return low, high


def outer_kernel(
    levels, peers, is_child, nest_x, nest_y, ty,
    matrices, base, kappa, nudging, x_low, x_high, first, second,
    out, sides, wide, stack, group,
):
    fields = matrices.shape[0]
    cols, _, rows = kappa.shape
    blocks = cols // 3
    lanes = lane_ids((PAD, LANE))
    ends = ((0, x_low), (cols - 1, x_high))
    sides[...] = jnp.zeros_like(sides)
    low, high = y_halos(ty, peers, first, second)

    def weights(row_at):
        start = jnp.zeros((1, LANE), F32)
        end = jnp.zeros((1, LANE), F32)
        ids = lane_ids((1, LANE))
        for x in range(cols):
            row = row_at(x)
            start = jnp.where(ids == x, pltpu.roll(row[:, :LANE], x, 1) if x else row[:, :LANE], start)
            end = jnp.where(ids == x, pltpu.roll(row[:, rows - LANE :], x + 1, 1), end)
        starts, finals = start, end
        for f in range(1, fields):
            starts = starts + pltpu.roll(start, f * cols, 1)
            finals = finals + pltpu.roll(end, f * cols, 1)
        return starts, finals

    def fill_fix(begin, finish):
        value = jnp.where(lax.rem(lanes, 3) == 0, begin, 0.0)
        value = jnp.where(lax.rem(lanes, 3) == 1, pltpu.roll(finish, 1, 1), value)
        value = jnp.where(lanes < fields * cols, value, 0.0)
        for f in range(fields):
            fill_stack(stack.at[f], chunk(2), deepened(value))

    @pl.when(is_child[0] == 1)
    def _():
        fill_group(group)
        for n, (x, halo) in enumerate(ends):
            weight = nudging[x : x + 1, :] * kappa[x]
            for f in range(fields):
                at = (f * 2 + n) * DEPTH
                sides[at : at + levels, :] = halo[f, :, 0, :] * weight
        wide[0], wide[1] = halves(sides[...])
        value = grouped(wide[0], wide[1], group[...])
        for f in range(fields):
            for n in range(2):
                at = (f * 2 + n) * DEPTH
                fill_stack(stack.at[f], chunk(n), value[at : at + DEPTH])
        starts, finals = weights(lambda x: nudging[x : x + 1, :] * kappa[x])
        begin = low * starts
        finish = high * finals
        begin = begin + pltpu.roll(begin, LANE - 1, 1) + pltpu.roll(begin, LANE - 2, 1)
        finish = finish + pltpu.roll(finish, LANE - 1, 1) + pltpu.roll(finish, LANE - 2, 1)
        fill_fix(begin, finish)

    @pl.when(is_child[0] == 0)
    def _():
        back = lax.rem(rows - nest_y[0], rows)
        reached = (nest_x[0] == 0, nest_x[0] + blocks == cols)
        for n, (x, halo) in enumerate(ends):
            weight = kappa[x] * reached[n].astype(F32)
            for f in range(fields):
                at = (f * 2 + n) * DEPTH
                sides[at : at + levels, :] = halo[f, :, 0, :] * weight
                value = pltpu.roll(sides[at : at + DEPTH, :], back, 1)[:, :LANE]
                fill_stack(stack.at[f], chunk(n), value)
        starts, finals = weights(lambda x: kappa[x])
        begin = low * (starts * (nest_y[0] == 0).astype(F32))
        finish = high * (finals * (nest_y[0] == rows - LANE).astype(F32))
        parts = [jnp.zeros((PAD, LANE), F32)] * 2
        for b in range(blocks):
            shift = lax.rem(LANE + 2 * b - nest_x[0], LANE)
            here = lax.rem(lanes, cols) == 3 * b
            for n, value in enumerate((begin, finish)):
                parts[n] = jnp.where(here, pltpu.roll(value, shift, 1), parts[n])
        fill_fix(*parts)

    fixes = jnp.zeros((PAD, LANE), F32)
    for f in range(fields):
        mixed = mix(matrices[f], stack[f])
        for n in range(2):
            at = pl.ds(f * (2 * levels) + n, levels, stride=2)
            out[at, :] = base[f, :levels, chunk(n)] + mixed[:levels, chunk(n)]
        own = jnp.logical_and(lanes >= f * cols, lanes < (f + 1) * cols)
        fixes = jnp.where(own, mixed[:PAD, chunk(2)], fixes)
    out[out.shape[0] - PAD :, :] = fixes


def outer(scalars, ty, matrices, base, kappa, nudging, x_halos, firsts, dims, peers):
    fields, levels, cols, chunks = dims
    rows = chunks * LANE
    height = -(-fields * 2 * levels // 8) * 8 + PAD
    return pl.pallas_call(
        functools.partial(outer_kernel, levels, peers),
        in_specs=[SMEM] * 4 + [VMEM] * 8,
        out_specs=VMEM,
        out_shape=pltpu.VMEM((height, LANE), F32),
        scratch_shapes=[
            pltpu.VMEM((fields * 2 * DEPTH, rows), F32),
            pltpu.VMEM((2, fields * 2 * DEPTH, rows), jnp.bfloat16),
            pltpu.VMEM((fields, 4 * DEPTH, 3 * LANE), jnp.bfloat16),
            pltpu.VMEM((rows, LANE), jnp.bfloat16),
        ],
        compiler_params=pltpu.CompilerParams(vmem_limit_bytes=12 * MIB),
        name="outer",
    )(*scalars, ty, matrices, base, kappa, nudging, *x_halos, *firsts)


def tile_kernel(
    levels, peers, places, values, ty, masked, matrices, kappa, x_low, x_high, first, second,
    out, sides, y_low, y_high, stack,
):
    fields, cols, _, rows = masked.shape
    chunks = rows // LANE
    sides[...] = jnp.zeros_like(sides)
    y_low[...], y_high[...] = y_halos(ty, peers, first, second)
    pair = 2

    def field(f, carry):
        sides[0, :levels, :] = x_low[f, :, 0, :]
        sides[1, :levels, :] = x_high[f, :, 0, :]
        for x0 in range(0, cols, pair):
            for x in range(x0, x0 + pair):
                above = masked[f, x - 1] if x > 0 else sides[0]
                below = masked[f, x + 1] if x < cols - 1 else sides[1]
                k = f * cols + x
                start = pltpu.roll(y_low[...], lax.rem(LANE - k, LANE), 1)
                end = pltpu.roll(y_high[...], LANE - 1 - k, 1)
                value = spread_of(masked[f, x], above, below, kappa[x], start, end)
                part = slice((x - x0) * rows, (x - x0 + 1) * rows)
                fill_stack(stack, part, deepened(value))
            mixed = mix(matrices[f], stack[...])
            for n in range(pair * chunks):
                out[(f * cols + x0) * chunks + n, :, :] = mixed[:PAD, chunk(n)]
        return carry

    lax.fori_loop(0, fields, field, 0)
    lanes = lane_ids((1, LANE))
    sources, slots = places.shape

    def source(s, carry):
        for k in range(slots):
            place = places[s, k]
            at = place >> 13
            level = (place >> 7) & (DEPTH - 1)
            lane = place & (LANE - 1)
            old = out[at, pl.ds(level, 1), :]
            out[at, pl.ds(level, 1), :] = old + jnp.where(lanes == lane, values[s, k], 0.0)
        return carry

    lax.fori_loop(0, sources, source, 0)


def tile_of(places, values, ty, masked, matrices, kappa, x_halos, firsts, dims, peers):
    fields, levels, cols, chunks = dims
    rows = chunks * LANE
    return pl.pallas_call(
        functools.partial(tile_kernel, levels, peers),
        in_specs=[SMEM] * 3 + [VMEM] * 7,
        out_specs=VMEM,
        out_shape=pltpu.VMEM((fields * cols * chunks, PAD, LANE), F32),
        scratch_shapes=[
            pltpu.VMEM((2, PAD, rows), F32),
            pltpu.VMEM((PAD, LANE), F32),
            pltpu.VMEM((PAD, LANE), F32),
            pltpu.VMEM((4 * DEPTH, 2 * rows), jnp.bfloat16),
        ],
        compiler_params=pltpu.CompilerParams(vmem_limit_bytes=12 * MIB),
        name="tile",
    )(places, values, ty, in_vmem(masked), matrices, kappa, *x_halos, *firsts)


def finish_kernel(
    levels, is_child, nest_x, nest_y, tile, mask, in_arrived, out_arrived, in_sent, out_sent,
    out, buf, group, sems,
):
    cols = mask.shape[0]
    rows = mask.shape[2]
    chunks = rows // LANE
    step = cols * chunks
    size = levels * step
    fields = out.shape[0] // size
    blocks = cols // 3
    inner = blocks - 2
    lanes = lane_ids((levels, LANE))
    height = out_arrived.shape[0]

    def copy(f):
        at = pl.ds(f * size, size)
        return pltpu.make_async_copy(buf.at[at], out.at[at], sems.at[f])

    def payload(f, b, inner_ref, outer_ref):
        if b in (0, blocks - 1):
            value = outer_ref[pl.ds(f * (2 * levels) + min(b, 1), levels, stride=2), :]
        else:
            value = inner_ref[pl.ds(f * (levels * inner) + b - 1, levels, stride=inner), :]
        fixes = outer_ref[height - PAD : height - PAD + levels, :]
        k = f * cols + 3 * b
        value = value + jnp.where(lanes == 0, pltpu.roll(fixes, lax.rem(LANE - k, LANE), 1), 0.0)
        return value + jnp.where(lanes == LANE - 1, pltpu.roll(fixes, LANE - 2 - k, 1), 0.0)

    def fill_child(f, carry):
        for b in range(blocks):
            high, low = halves(payload(f, b, in_arrived, out_arrived))
            both = jnp.concatenate([high, low], axis=1)
            value = jnp.dot(both, group[...], preferred_element_type=F32) * (1.0 / 9.0)
            for x in range(3 * b, 3 * b + 3):
                row = row_of(mask, x)
                for c in range(chunks):
                    piece = x * chunks + c
                    at = pl.ds(f * size + piece, levels, stride=step)
                    total = tile[f * step + piece, :levels, :] + value[:, chunk(c)]
                    buf[at, :] = total * row[:, chunk(c)]
        copy(f).start()
        return carry

    def fill_parent(f, carry):
        for x in range(cols):
            row = row_of(mask, x)
            for c in range(chunks):
                piece = x * chunks + c
                at = pl.ds(f * size + piece, levels, stride=step)
                buf[at, :] = tile[f * step + piece, :levels, :] * row[:, chunk(c)]
        for b in range(blocks):
            delta = payload(f, b, in_arrived, out_arrived) - payload(f, b, in_sent, out_sent)
            wide = jnp.concatenate([delta, jnp.zeros((levels, rows - LANE), F32)], 1)
            x = nest_x[0] + b
            value = pltpu.roll(wide, nest_y[0], 1) * row_of(mask, x)
            for c in range(chunks):
                at = pl.ds(f * size + x * chunks + c, levels, stride=step)
                buf[at, :] = buf[at, :] + value[:, chunk(c)]
        copy(f).start()
        return carry

    @pl.when(is_child[0] == 1)
    def _():
        ids = lax.broadcasted_iota(jnp.int32, group.shape, 0)
        ids = jnp.where(ids < LANE, ids, ids - LANE)
        group[...] = jnp.where(lane_ids(group.shape) // 3 == ids, 1.0, 0.0).astype(jnp.bfloat16)
        lax.fori_loop(0, fields, fill_child, 0)

    @pl.when(is_child[0] == 0)
    def _():
        lax.fori_loop(0, fields, fill_parent, 0)

    for f in range(fields):
        copy(f).wait()


def finish(scalars, tile, mask, arrived, sent, dims):
    fields, levels, cols, chunks = dims
    rows = chunks * LANE
    size = (fields * levels * cols * chunks, LANE)
    return pl.pallas_call(
        functools.partial(finish_kernel, levels),
        in_specs=[SMEM] * 3 + [VMEM] * 6,
        out_specs=HBM,
        out_shape=pltpu.HBM(size, F32),
        scratch_shapes=[
            pltpu.VMEM(size, F32),
            pltpu.VMEM((2 * LANE, rows), jnp.bfloat16),
            pltpu.SemaphoreType.DMA((fields,)),
        ],
        compiler_params=pltpu.CompilerParams(vmem_limit_bytes=16 * MIB),
        name="finish",
    )(*scalars, in_vmem(tile), mask, *arrived, *sent)


def from_neighbours(low, high, axis):
    ends = lax.axis_size(axis) - 1
    before = lax.ppermute(high, axis, [(i, i + 1) for i in range(ends)])
    after = lax.ppermute(low, axis, [(i + 1, i) for i in range(ends)])
    return before, after


def swapped(value, axis, mask):
    return lax.ppermute(value, axis, [(i, i ^ mask) for i in range(lax.axis_size(axis))])


def observed(cells, counts, gathered, ty, tx, dims):
    _, levels, cols, chunks = dims
    rows = chunks * LANE
    peers, across = lax.axis_size("ty"), lax.axis_size("tx")
    slots = cells.shape[1]
    order = lax.broadcasted_iota(jnp.int32, (across, peers), 1)
    order = order ^ (order >> 1) ^ ty
    sources = order * across + (lax.broadcasted_iota(jnp.int32, (across, peers), 0) ^ tx)
    sources = sources.reshape(-1)
    cells = jnp.take(cells, sources, axis=0)
    counts = jnp.take(counts, sources, axis=0)
    column, inside = cells // (cols * rows), cells % (cols * rows)
    at = (column // levels) * (cols * chunks) + inside // LANE
    places = (at << 13) | ((column % levels) << 7) | (inside % LANE)
    values = lax.dynamic_slice_in_dim(gathered, ty * across + tx, 1, axis=1).reshape(-1, slots)
    live = lax.broadcasted_iota(jnp.int32, values.shape, 1) < counts[:, None]
    return places, jnp.where(live, values, 0.0)


def local(
    adjoint_state,
    land_mask,
    diffusivity,
    mixing,
    nudging,
    nest_x,
    nest_y,
    obs_forcing,
    obs_cell,
    obs_count,
):
    _, fields, levels, cols, rows = adjoint_state.shape
    chunks = rows // LANE
    dims = (fields, levels, cols, chunks)
    state5 = adjoint_state.reshape(fields, levels, cols, 1, rows)
    state2 = adjoint_state.reshape(fields * levels * cols * chunks, LANE)
    mask = land_mask.reshape(cols, 1, rows)
    kappa = diffusivity.reshape(cols, 1, rows)
    mixing = mixing.reshape(fields, levels, 1, levels)
    peers = lax.axis_size("ty")
    assert peers == 4 and lax.axis_size("tx") & (lax.axis_size("tx") - 1) == 0
    row = lax.axis_index("ty").astype(jnp.int32)
    column = lax.axis_index("tx").astype(jnp.int32)
    ty = row.reshape(1)
    is_child = (lax.axis_index("grp") == 0).astype(jnp.int32).reshape(1)
    scalars = (is_child, nest_x, nest_y)

    x_low, x_high = x_edges(state5, mask)
    x_halos = from_neighbours(x_low, x_high, "tx")
    masked, matrices, first, second, in_sent, base = front(
        scalars, ty, state2, mask, kappa, nudging, mixing, obs_forcing[0, 0], dims
    )
    first_arrived = swapped(first, "ty", 1)
    in_arrived = swapped(in_sent, "grp", 1)
    gathered = jnp.concatenate([first[PAD:], first_arrived[PAD:]])
    second = jnp.concatenate([second, gathered])
    second_arrived = swapped(second, "ty", 3)
    firsts = (first_arrived, second_arrived)
    out_sent = outer(
        scalars, ty, matrices, base, kappa, nudging, x_halos, firsts, dims, peers
    )
    out_arrived = swapped(out_sent, "grp", 1)
    gathered = jnp.concatenate([gathered, second_arrived[PAD:]])
    mask_bit = 1
    while mask_bit < lax.axis_size("tx"):
        gathered = jnp.concatenate([gathered, swapped(gathered, "tx", mask_bit)])
        mask_bit *= 2
    places, values = observed(
        obs_cell[0, :, :, 0], obs_count.reshape(-1), gathered, row, column, dims
    )
    tile = tile_of(places, values, ty, masked, matrices, kappa, x_halos, firsts, dims, peers)
    out = finish(scalars, tile, mask, (in_arrived, out_arrived), (in_sent, out_sent), dims)
    return out.reshape(adjoint_state.shape)


def solution(mesh):
    in_specs = (
        P("grp", None, None, "tx", "ty"),
        P("grp", "tx", "ty"),
        P("grp", "tx", "ty"),
        P("grp", None, None, None),
        P("tx", "ty"),
        P(("ty", "tx")),
        P(("ty", "tx")),
        P("grp", ("ty", "tx"), None, None),
        P("grp", None, None, ("ty", "tx")),
        P("grp", None, ("ty", "tx")),
    )
    out_specs = P("grp", None, None, "tx", "ty")
    return jax.shard_map(local, mesh=mesh, in_specs=in_specs, out_specs=out_specs, check_vma=False)
```

```python
import functools

import jax
import jax.numpy as jnp
from jax import lax
from jax.experimental import pallas as pl
from jax.experimental.pallas import tpu as pltpu
from jax.sharding import PartitionSpec as P

LANE = 128
PAD = 56
DEPTH = 64
MIB = 1 << 20
HBM = pl.BlockSpec(memory_space=pltpu.HBM)
SMEM = pl.BlockSpec(memory_space=pltpu.SMEM)
VMEM = pl.BlockSpec(memory_space=pltpu.VMEM)
F32 = jnp.float32


def lane_ids(shape):
    return lax.broadcasted_iota(jnp.int32, shape, len(shape) - 1)


def row_of(ref, x):
    return ref[x].astype(F32)


def chunk(c):
    return slice(c * LANE, (c + 1) * LANE)


def in_hbm(value):
    return pltpu.with_memory_space_constraint(value, pltpu.HBM)


def in_vmem(value):
    return pltpu.with_memory_space_constraint(value, pltpu.VMEM)


def x_edges_kernel(state, mask, low, high, buf, mask_buf, sems):
    fields, _, cols = state.shape[:3]
    copies = [pltpu.make_async_copy(mask, mask_buf, sems.at[2 * fields])]
    for n, x in enumerate((0, cols - 1)):
        for f in range(fields):
            copies.append(
                pltpu.make_async_copy(state.at[f, :, x], buf.at[n, f], sems.at[n * fields + f])
            )
    for copy in copies:
        copy.start()
    copies[0].wait()
    for n, (x, out) in enumerate(((0, low), (cols - 1, high))):
        for f in range(fields):
            copies[1 + n * fields + f].wait()
            out[f] = buf[n, f] * row_of(mask_buf, x)[None]


def x_edges(state5, mask):
    fields, levels, cols, _, rows = state5.shape
    edge = (fields, levels, 1, rows)
    return pl.pallas_call(
        x_edges_kernel,
        in_specs=[HBM, HBM],
        out_specs=[VMEM] * 2,
        out_shape=[pltpu.VMEM(edge, F32)] * 2,
        scratch_shapes=[
            pltpu.VMEM((2,) + edge, F32),
            pltpu.VMEM(mask.shape, jnp.int32),
            pltpu.SemaphoreType.DMA((2 * fields + 1,)),
        ],
        compiler_params=pltpu.CompilerParams(vmem_limit_bytes=8 * MIB),
        name="x_edges",
    )(in_hbm(state5), in_hbm(mask))


def spread_of(here, above, below, kappa, edge=None):
    rows = here.shape[1]
    lanes = lane_ids((here.shape[0], LANE))
    edge = 0.0 if edge is None else edge
    before = pltpu.roll(here, 1, 1)
    after = pltpu.roll(here, rows - 1, 1)
    before = jnp.concatenate([jnp.where(lanes == 0, edge, before[:, :LANE]), before[:, LANE:]], 1)
    after = jnp.concatenate(
        [after[:, :-LANE], jnp.where(lanes == LANE - 1, edge, after[:, -LANE:])], 1
    )
    return here + kappa * (above + below + before + after - 4.0 * here)


def halves(value):
    high = value.astype(jnp.bfloat16)
    return high, (value - high.astype(F32)).astype(jnp.bfloat16)


def deepened(value):
    return jnp.concatenate([value, jnp.zeros((DEPTH - value.shape[0], value.shape[1]), F32)], 0)


def fill_matrix(levels, mixing, square, matrix):
    square[:levels, :levels] = mixing
    value = square[...]
    high = value.astype(jnp.bfloat16).astype(F32)
    matrix[:DEPTH, :] = (high + pltpu.roll(high, DEPTH, 1)).astype(jnp.bfloat16)
    matrix[DEPTH:, :] = (value - high).astype(jnp.bfloat16)


def fill_stack(stack, part, value):
    high, low = halves(value)
    stack[:DEPTH, part] = high
    stack[DEPTH:, part] = low


def mix(matrix, stack):
    both = jnp.dot(matrix, stack, preferred_element_type=F32)
    return both[:DEPTH] + both[DEPTH:]


def fill_group(group):
    rows = group.shape[0] // 2
    ids = lax.broadcasted_iota(jnp.int32, group.shape, 0)
    ids = jnp.where(ids < rows, ids, ids - rows) // 3
    group[...] = jnp.where(ids == lane_ids(group.shape), 1.0, 0.0).astype(jnp.bfloat16)


def grouped(wide, group):
    return jnp.dot(wide, group, preferred_element_type=F32)


def aligned(index, size):
    return pl.ds(pl.multiple_of(index * size, size), size)


def packed(rows_of, cols):
    parts = []
    for x in range(cols):
        first, last = rows_of(x)
        lanes = lane_ids(first.shape)
        parts.append(jnp.where(lanes == 0, first, jnp.where(lanes == LANE - 1, last, 0.0)))
    shift = 2
    while len(parts) > 1:
        pairs = [parts[n : n + 2] for n in range(0, len(parts), 2)]
        parts = [p[0] + pltpu.roll(p[1], shift, 1) if len(p) == 2 else p[0] for p in pairs]
        shift *= 2
    return parts[0]


def front_kernel(
    levels, is_child, state, mask, kappa, nudging, mixing, nest_x, nest_y,
    masked_out, matrices, edges, inner, base,
    buf, masked, mask_buf, kappa_buf, nudging_buf, mixing_buf, square, weights,
    wide, stack, group, sems, out_sems,
):
    fields, cols, _, rows = masked.shape
    chunks = rows // LANE
    step = cols * chunks
    size = levels * step
    blocks = cols // 3
    terms = 11

    def copy(f):
        at = pl.ds(f * size, size)
        return pltpu.make_async_copy(state.at[at], buf.at[at], sems.at[f])

    def copy_out(f):
        return pltpu.make_async_copy(masked.at[f], masked_out.at[f], out_sems.at[f])

    pairs = (
        (mask, mask_buf),
        (kappa, kappa_buf),
        (nudging, nudging_buf),
        (mixing, mixing_buf),
    )
    smalls = [
        pltpu.make_async_copy(source, target, sems.at[fields + n])
        for n, (source, target) in enumerate(pairs)
    ]
    copy(0).start()
    for small in smalls:
        small.start()
    for f in range(1, fields):
        copy(f).start()
    square[...] = jnp.zeros_like(square)
    for small in smalls:
        small.wait()

    @pl.when(is_child[0] == 1)
    def _():
        fill_group(group)
        ids = lane_ids((1, rows))
        for b in range(blocks):
            own = range(3 * b, 3 * b + 3)
            both = {x: nudging_buf[x : x + 1, :] * kappa_buf[x] for x in own}
            for n, x in enumerate(range(3 * b - 1, 3 * b + 4)):
                total = None
                for near in (x - 1, x + 1):
                    if near in both:
                        total = both[near] if total is None else total + both[near]
                if x in both:
                    total = total + (nudging_buf[x : x + 1, :] - 4.0 * both[x])
                weights[b * terms + n : b * terms + n + 1, :] = total
            for n, x in enumerate(own):
                at = b * terms + 5 + n
                value = jnp.where(ids == rows - 1, 0.0, pltpu.roll(both[x], rows - 1, 1))
                weights[at : at + 1, :] = value
                value = jnp.where(ids == 0, 0.0, pltpu.roll(both[x], 1, 1))
                weights[at + 3 : at + 4, :] = value

    def weight(b, n):
        return weights[b * terms + n : b * terms + n + 1, :]

    def field(f, total_edges):
        copy(f).wait()
        fill_matrix(levels, mixing_buf[f, :, 0, :], square, matrices.at[f])
        for x in range(cols):
            row = row_of(mask_buf, x)
            masked[f, x, PAD - 8 :, :] = jnp.zeros((8, rows), F32)
            for c in range(chunks):
                at = pl.ds(f * size + x * chunks + c, levels, stride=step)
                masked[f, x, :levels, chunk(c)] = buf[at, :] * row[:, chunk(c)]
        copy_out(f).start()
        own_edges = packed(
            lambda x: (masked[f, x, :, :LANE], masked[f, x, :, rows - LANE :]), cols
        )

        @pl.when(is_child[0] == 1)
        def _():
            for b in range(blocks):
                total = None
                for n, x in enumerate(range(3 * b - 1, 3 * b + 4)):
                    if 0 <= x < cols:
                        term = weight(b, n) * masked[f, x]
                        total = term if total is None else total + term
                for side, shift in ((0, 1), (3, rows - 1)):
                    value = None
                    for n in range(3):
                        term = weight(b, 5 + side + n) * masked[f, 3 * b + n]
                        value = term if value is None else value + term
                    total = total + pltpu.roll(value, shift, 1)
                at = aligned(f * blocks + b, DEPTH)
                wide[at, :rows], wide[at, rows:] = halves(deepened(total))

        @pl.when(is_child[0] == 0)
        def _():
            back = lax.rem(rows - nest_y[0], rows)
            for b in range(blocks):
                x = nest_x[0] + b
                above = masked[f, jnp.maximum(x - 1, 0)]
                below = masked[f, jnp.minimum(x + 1, cols - 1)]
                if b == 0:
                    above = jnp.where(x == 0, 0.0, above)
                if b == blocks - 1:
                    below = jnp.where(x == cols - 1, 0.0, below)
                value = spread_of(masked[f, x], above, below, kappa_buf[x])
                value = deepened(pltpu.roll(value, back, 1)[:, :LANE])
                fill_stack(stack.at[f], chunk(b), value)

        return total_edges + pltpu.roll(own_edges, 2 * f * cols, 1)

    edges[...] = lax.fori_loop(0, fields, field, jnp.zeros((PAD, LANE), F32))

    @pl.when(is_child[0] == 1)
    def _():
        value = grouped(wide[...], group[...])
        for f in range(fields):
            for b in range(blocks):
                at = (f * blocks + b) * DEPTH
                fill_stack(stack.at[f], chunk(b), value[at : at + DEPTH])

    for f in range(fields):
        mixed = mix(matrices[f], stack[f])
        for b in range(1, blocks - 1):
            at = pl.ds(f * levels * (blocks - 2) + b - 1, levels, stride=blocks - 2)
            inner[at, :] = mixed[:levels, chunk(b)]
        base[f, :, :LANE] = mixed[:PAD, :LANE]
        base[f, :, LANE:] = mixed[:PAD, chunk(blocks - 1)]
    for f in range(fields):
        copy_out(f).wait()


def front(is_child, state2, mask, kappa, nudging, mixing, nests, dims):
    fields, levels, cols, chunks = dims
    rows = chunks * LANE
    blocks = cols // 3
    arrays = (state2, mask, kappa, nudging, mixing)
    tile = (fields, cols, PAD, rows)
    return pl.pallas_call(
        functools.partial(front_kernel, levels),
        in_specs=[SMEM] + [HBM] * 5 + [SMEM] * 2,
        out_specs=[HBM] + [VMEM] * 4,
        out_shape=[
            pltpu.HBM(tile, F32),
            pltpu.VMEM((fields, 2 * DEPTH, 2 * DEPTH), jnp.bfloat16),
            pltpu.VMEM((PAD, LANE), F32),
            pltpu.VMEM((fields * levels * (blocks - 2), LANE), F32),
            pltpu.VMEM((fields, PAD, 2 * LANE), F32),
        ],
        scratch_shapes=[
            pltpu.VMEM(state2.shape, F32),
            pltpu.VMEM(tile, F32),
            pltpu.VMEM(mask.shape, jnp.int32),
            pltpu.VMEM(kappa.shape, F32),
            pltpu.VMEM(nudging.shape, F32),
            pltpu.VMEM(mixing.shape, F32),
            pltpu.VMEM((DEPTH, LANE), F32),
            pltpu.VMEM((-(-blocks * 11 // 8) * 8, rows), F32),
            pltpu.VMEM((fields * blocks * DEPTH, 2 * rows), jnp.bfloat16),
            pltpu.VMEM((fields, 2 * DEPTH, blocks * LANE), jnp.bfloat16),
            pltpu.VMEM((2 * rows, LANE), jnp.bfloat16),
            pltpu.SemaphoreType.DMA((fields + 4,)),
            pltpu.SemaphoreType.DMA((fields,)),
        ],
        compiler_params=pltpu.CompilerParams(vmem_limit_bytes=28 * MIB),
        name="front",
    )(is_child, *map(in_hbm, arrays), *nests)


def y_halos(ty, peers, first, second):
    one, two = first[:PAD, :], second[:PAD, :]
    even = (lax.rem(ty[0], 2) == 0).astype(F32)
    odd = 1.0 - even
    before = (two * even + one * odd) * (ty[0] > 0).astype(F32)
    after = (one * even + two * odd) * (ty[0] < peers - 1).astype(F32)
    low = lax.rem(lane_ids((PAD, LANE)), 2) == 0
    return jnp.where(low, pltpu.roll(before, 1, 1), pltpu.roll(after, LANE - 1, 1))


def outer_kernel(
    levels, peers, is_child, ty, matrices, base, kappa, nudging, x_low, x_high, first, second,
    nest_x, nest_y, out, sides, wide, stack, group,
):
    fields = matrices.shape[0]
    cols, _, rows = kappa.shape
    blocks = cols // 3
    lanes = lane_ids((PAD, LANE))
    turned = lax.rem(lanes + 1, LANE)
    ends = ((0, x_low), (cols - 1, x_high))
    sides[...] = jnp.zeros_like(sides)
    halo = y_halos(ty, peers, first, second)

    def weighted(row_of_x):
        one = packed(lambda x: (row_of_x(x)[:, :LANE], row_of_x(x)[:, rows - LANE :]), cols)
        total = one
        for f in range(1, fields):
            total = total + pltpu.roll(one, 2 * f * cols, 1)
        return halo * total

    def fill_fix(value):
        for f in range(fields):
            fill_stack(stack.at[f], chunk(2), deepened(value))

    @pl.when(is_child[0] == 1)
    def _():
        fill_group(group)
        for n, (x, side) in enumerate(ends):
            weight = nudging[x : x + 1, :] * kappa[x]
            for f in range(fields):
                at = (f * 2 + n) * DEPTH
                sides[at : at + levels, :] = side[f, :, 0, :] * weight
        wide[:, :rows], wide[:, rows:] = halves(sides[...])
        value = grouped(wide[...], group[...])
        for f in range(fields):
            for n in range(2):
                at = (f * 2 + n) * DEPTH
                fill_stack(stack.at[f], chunk(n), value[at : at + DEPTH])
        part = weighted(lambda x: nudging[x : x + 1, :] * kappa[x])
        fill_fix(part + pltpu.roll(part, LANE - 2, 1) + pltpu.roll(part, LANE - 4, 1))

    @pl.when(is_child[0] == 0)
    def _():
        back = lax.rem(rows - nest_y[0], rows)
        reached = (nest_x[0] == 0, nest_x[0] + blocks == cols)
        for n, (x, side) in enumerate(ends):
            weight = kappa[x] * reached[n].astype(F32)
            for f in range(fields):
                at = (f * 2 + n) * DEPTH
                sides[at : at + levels, :] = side[f, :, 0, :] * weight
                value = pltpu.roll(sides[at : at + DEPTH, :], back, 1)[:, :LANE]
                fill_stack(stack.at[f], chunk(n), value)
        starts = (nest_y[0] == 0).astype(F32)
        finals = (nest_y[0] == rows - LANE).astype(F32)
        part = weighted(lambda x: kappa[x])
        part = part * jnp.where(lax.rem(lanes, 2) == 0, starts, finals)
        value = jnp.zeros((PAD, LANE), F32)
        for b in range(blocks):
            shift = lax.rem(LANE + 4 * b - 2 * nest_x[0], LANE)
            here = lax.rem(turned, 2 * cols) // 2 == 3 * b
            value = jnp.where(here, pltpu.roll(part, shift, 1), value)
        fill_fix(value)

    fixes = jnp.zeros((PAD, LANE), F32)
    for f in range(fields):
        mixed = mix(matrices[f], stack[f])
        for n in range(2):
            at = pl.ds(f * (2 * levels) + n, levels, stride=2)
            out[at, :] = base[f, :levels, chunk(n)] + mixed[:levels, chunk(n)]
        fixes = jnp.where(turned // (2 * cols) == f, mixed[:PAD, chunk(2)], fixes)
    out[out.shape[0] - PAD :, :] = fixes


def outer(is_child, ty, matrices, base, kappa, nudging, x_halos, firsts, nests, dims, peers):
    fields, levels, cols, chunks = dims
    rows = chunks * LANE
    height = -(-fields * 2 * levels // 8) * 8 + PAD
    return pl.pallas_call(
        functools.partial(outer_kernel, levels, peers),
        in_specs=[SMEM] * 2 + [VMEM] * 8 + [SMEM] * 2,
        out_specs=VMEM,
        out_shape=pltpu.VMEM((height, LANE), F32),
        scratch_shapes=[
            pltpu.VMEM((fields * 2 * DEPTH, rows), F32),
            pltpu.VMEM((fields * 2 * DEPTH, 2 * rows), jnp.bfloat16),
            pltpu.VMEM((fields, 2 * DEPTH, 3 * LANE), jnp.bfloat16),
            pltpu.VMEM((2 * rows, LANE), jnp.bfloat16),
        ],
        compiler_params=pltpu.CompilerParams(vmem_limit_bytes=12 * MIB),
        name="outer",
    )(is_child, ty, matrices, base, kappa, nudging, *x_halos, *firsts, *nests)


def tile_kernel(
    levels, peers, across, places, counts, values, ty, tx,
    masked_in, matrices, kappa, x_low, x_high, first, second, _,
    out, masked, sides, halo, stack, sems,
):
    fields, cols, _, rows = masked.shape
    chunks = rows // LANE

    def copy(f):
        return pltpu.make_async_copy(masked_in.at[f], masked.at[f], sems.at[f])

    for f in range(fields):
        copy(f).start()
    sides[...] = jnp.zeros_like(sides)
    halo[...] = y_halos(ty, peers, first, second)
    pair = 2

    def field(f, carry):
        copy(f).wait()
        sides[0, :levels, :] = x_low[f, :, 0, :]
        sides[1, :levels, :] = x_high[f, :, 0, :]
        for x0 in range(0, cols, pair):
            for x in range(x0, x0 + pair):
                above = masked[f, x - 1] if x > 0 else sides[0]
                below = masked[f, x + 1] if x < cols - 1 else sides[1]
                shift = lax.rem(LANE - 2 * (f * cols + x), LANE)
                edge = pltpu.roll(halo[...], lax.rem(LANE + shift, LANE), 1)
                value = spread_of(masked[f, x], above, below, kappa[x], edge)
                part = slice((x - x0) * rows, (x - x0 + 1) * rows)
                fill_stack(stack, part, deepened(value))
            mixed = mix(matrices[f], stack[...])
            for n in range(pair * chunks):
                out[(f * cols + x0) * chunks + n, :, :] = mixed[:PAD, chunk(n)]
        return carry

    lax.fori_loop(0, fields, field, 0)
    lanes = lane_ids((1, LANE))
    sources, slots = places.shape
    batch = 4

    def source(s, carry):
        row, column = lax.div(s, across), lax.rem(s, across)
        origin = (row ^ (row >> 1) ^ ty[0]) * across + (column ^ tx[0])
        count = counts[0, origin]
        for k0 in range(0, slots, batch):
            where, adds, olds = [], [], []
            for k in range(k0, k0 + batch):
                place = places[origin, k]
                value = jnp.where(k < count, values[s, k], 0.0)
                where.append(place >> 7)
                adds.append(jnp.where(lanes == (place & (LANE - 1)), value, 0.0))
                at, level = place >> 13, (place >> 7) & (DEPTH - 1)
                olds.append((at, level, out[at, pl.ds(level, 1), :]))
            for k in range(batch):
                at, level, total = olds[k]
                total = total + adds[k]
                for j in range(k):
                    total = total + jnp.where(where[j] == where[k], adds[j], 0.0)
                out[at, pl.ds(level, 1), :] = total
        return carry

    lax.fori_loop(0, sources, source, 0)


def tile_of(scalars, masked, matrices, kappa, x_halos, firsts, arrived, dims, peers, across):
    fields, levels, cols, chunks = dims
    rows = chunks * LANE
    return pl.pallas_call(
        functools.partial(tile_kernel, levels, peers, across),
        in_specs=[SMEM] * 5 + [HBM] + [VMEM] * 6 + [pl.BlockSpec(memory_space=pl.ANY)],
        out_specs=VMEM,
        out_shape=pltpu.VMEM((fields * cols * chunks, PAD, LANE), F32),
        scratch_shapes=[
            pltpu.VMEM(masked.shape, F32),
            pltpu.VMEM((2, PAD, rows), F32),
            pltpu.VMEM((PAD, LANE), F32),
            pltpu.VMEM((2 * DEPTH, 2 * rows), jnp.bfloat16),
            pltpu.SemaphoreType.DMA((fields,)),
        ],
        compiler_params=pltpu.CompilerParams(vmem_limit_bytes=16 * MIB),
        cost_estimate=pl.CostEstimate(flops=1, bytes_accessed=1, transcendentals=0),
        name="tile",
    )(*scalars, in_hbm(masked), matrices, kappa, *x_halos, *firsts, arrived)


def finish_kernel(
    levels, is_child, tile, mask, in_arrived, out_arrived, in_sent, out_sent, nest_x, nest_y,
    out, buf, group, sems,
):
    cols = mask.shape[0]
    rows = mask.shape[2]
    chunks = rows // LANE
    step = cols * chunks
    size = levels * step
    fields = out.shape[0] // size
    blocks = cols // 3
    inner = blocks - 2
    lanes = lane_ids((levels, LANE))
    ends = jnp.logical_or(lanes == 0, lanes == LANE - 1)
    height = out_arrived.shape[0]

    def copy(f):
        at = pl.ds(f * size, size)
        return pltpu.make_async_copy(buf.at[at], out.at[at], sems.at[f])

    def payload(f, b, inner_ref, outer_ref):
        if b in (0, blocks - 1):
            value = outer_ref[pl.ds(f * (2 * levels) + min(b, 1), levels, stride=2), :]
        else:
            value = inner_ref[pl.ds(f * (levels * inner) + b - 1, levels, stride=inner), :]
        fixes = outer_ref[height - PAD : height - PAD + levels, :]
        shift = lax.rem(LANE - 2 * (f * cols + 3 * b), LANE)
        fixes = pltpu.roll(fixes, lax.rem(LANE + shift, LANE), 1)
        return value + jnp.where(ends, fixes, 0.0)

    def fill_child(f, carry):
        for b in range(blocks):
            high, low = halves(payload(f, b, in_arrived, out_arrived))
            both = jnp.concatenate([high, low], axis=1)
            value = jnp.dot(both, group[...], preferred_element_type=F32) * (1.0 / 9.0)
            for x in range(3 * b, 3 * b + 3):
                row = row_of(mask, x)
                for c in range(chunks):
                    piece = x * chunks + c
                    at = pl.ds(f * size + piece, levels, stride=step)
                    total = tile[f * step + piece, :levels, :] + value[:, chunk(c)]
                    buf[at, :] = total * row[:, chunk(c)]
        copy(f).start()
        return carry

    def fill_plain(f, carry):
        for x in range(cols):
            row = row_of(mask, x)
            for c in range(chunks):
                piece = x * chunks + c
                at = pl.ds(f * size + piece, levels, stride=step)
                buf[at, :] = tile[f * step + piece, :levels, :] * row[:, chunk(c)]
        return carry

    def fill_parent(f, carry):
        fill_plain(f, carry)
        for b in range(blocks):
            delta = payload(f, b, in_arrived, out_arrived) - payload(f, b, in_sent, out_sent)
            wide = jnp.concatenate([delta, jnp.zeros((levels, rows - LANE), F32)], 1)
            x = nest_x[0] + b
            value = pltpu.roll(wide, nest_y[0], 1) * row_of(mask, x)
            for c in range(chunks):
                at = pl.ds(f * size + x * chunks + c, levels, stride=step)
                buf[at, :] = buf[at, :] + value[:, chunk(c)]
        copy(f).start()
        return carry

    @pl.when(is_child[0] == 1)
    def _():
        ids = lax.broadcasted_iota(jnp.int32, group.shape, 0)
        ids = jnp.where(ids < LANE, ids, ids - LANE)
        group[...] = jnp.where(lane_ids(group.shape) // 3 == ids, 1.0, 0.0).astype(jnp.bfloat16)
        lax.fori_loop(0, fields, fill_child, 0)

    @pl.when(is_child[0] == 0)
    def _():
        lax.fori_loop(0, fields, fill_parent, 0)

    for f in range(fields):
        copy(f).wait()


def finish(is_child, tile, mask, arrived, sent, nests, dims):
    fields, levels, cols, chunks = dims
    rows = chunks * LANE
    size = (fields * levels * cols * chunks, LANE)
    return pl.pallas_call(
        functools.partial(finish_kernel, levels),
        in_specs=[SMEM] + [VMEM] * 6 + [SMEM] * 2,
        out_specs=HBM,
        out_shape=pltpu.HBM(size, F32),
        scratch_shapes=[
            pltpu.VMEM(size, F32),
            pltpu.VMEM((2 * LANE, rows), jnp.bfloat16),
            pltpu.SemaphoreType.DMA((fields,)),
        ],
        compiler_params=pltpu.CompilerParams(vmem_limit_bytes=16 * MIB),
        name="finish",
    )(is_child, in_vmem(tile), mask, *arrived, *sent, *nests)


def from_neighbours(low, high, axis):
    ends = lax.axis_size(axis) - 1
    before = lax.ppermute(high, axis, [(i, i + 1) for i in range(ends)])
    after = lax.ppermute(low, axis, [(i + 1, i) for i in range(ends)])
    return before, after


def swapped(value, axis, mask):
    return lax.ppermute(value, axis, [(i, i ^ mask) for i in range(lax.axis_size(axis))])


def places_of(cells, dims):
    _, levels, cols, chunks = dims
    rows = chunks * LANE
    column, inside = cells // (cols * rows), cells % (cols * rows)
    at = (column // levels) * (cols * chunks) + inside // LANE
    return (at << 13) | ((column % levels) << 7) | (inside % LANE)


def local(
    adjoint_state,
    land_mask,
    diffusivity,
    mixing,
    nudging,
    nest_x,
    nest_y,
    obs_forcing,
    obs_cell,
    obs_count,
):
    _, fields, levels, cols, rows = adjoint_state.shape
    chunks = rows // LANE
    dims = (fields, levels, cols, chunks)
    state5 = adjoint_state.reshape(fields, levels, cols, 1, rows)
    state2 = adjoint_state.reshape(fields * levels * cols * chunks, LANE)
    mask = land_mask.reshape(cols, 1, rows)
    kappa = diffusivity.reshape(cols, 1, rows)
    mixing = mixing.reshape(fields, levels, 1, levels)
    peers, across = lax.axis_size("ty"), lax.axis_size("tx")
    assert peers == 4 and across & (across - 1) == 0 and 2 * fields * cols <= LANE
    assert levels <= PAD and cols % 3 == 0 and rows == 3 * LANE
    row = lax.axis_index("ty").astype(jnp.int32)
    column = lax.axis_index("tx").astype(jnp.int32)
    ty, tx = row.reshape(1), column.reshape(1)
    is_child = (lax.axis_index("grp") == 0).astype(jnp.int32).reshape(1)
    nests = (nest_x, nest_y)

    gathered = obs_forcing[0, 0]
    slots, dests = gathered.shape
    bit = 1
    while bit < across:
        gathered = jnp.concatenate([gathered, swapped(gathered, "tx", bit)])
        bit *= 2
    x_low, x_high = x_edges(state5, mask)
    x_halos = from_neighbours(x_low, x_high, "tx")
    masked, matrices, edges, in_sent, base = front(
        is_child, state2, mask, kappa, nudging, mixing, nests, dims
    )
    gathered = jnp.pad(gathered, ((0, 0), (0, LANE - dests)))
    first = swapped(jnp.concatenate([edges, gathered]), "ty", 1)
    in_arrived = swapped(in_sent, "grp", 1)
    gathered = jnp.concatenate([gathered, first[PAD:]])
    second = swapped(jnp.concatenate([edges, gathered]), "ty", 3)
    firsts = (first, second)
    out_sent = outer(
        is_child, ty, matrices, base, kappa, nudging, x_halos, firsts, nests, dims, peers
    )
    out_arrived = swapped(out_sent, "grp", 1)
    gathered = jnp.concatenate([gathered, second[PAD:]])
    values = lax.dynamic_slice_in_dim(gathered, row * across + column, 1, axis=1)
    scalars = (
        places_of(obs_cell[0, :, :, 0], dims),
        obs_count.reshape(1, -1),
        values.reshape(-1, slots),
        ty,
        tx,
    )
    tile = tile_of(
        scalars, masked, matrices, kappa, x_halos, firsts, in_arrived, dims, peers, across
    )
    out = finish(is_child, tile, mask, (in_arrived, out_arrived), (in_sent, out_sent), nests, dims)
    return out.reshape(adjoint_state.shape)


def solution(mesh):
    in_specs = (
        P("grp", None, None, "tx", "ty"),
        P("grp", "tx", "ty"),
        P("grp", "tx", "ty"),
        P("grp", None, None, None),
        P("tx", "ty"),
        P(("ty", "tx")),
        P(("ty", "tx")),
        P("grp", ("ty", "tx"), None, None),
        P("grp", None, None, ("ty", "tx")),
        P("grp", None, ("ty", "tx")),
    )
    out_specs = P("grp", None, None, "tx", "ty")
    return jax.shard_map(local, mesh=mesh, in_specs=in_specs, out_specs=out_specs, check_vma=False)
```

```python
import functools

import jax
import jax.numpy as jnp
from jax import lax
from jax.experimental import pallas as pl
from jax.experimental.pallas import tpu as pltpu
from jax.sharding import PartitionSpec as P

LANE = 128
PAD = 56
DEPTH = 64
MIB = 1 << 20
HBM = pl.BlockSpec(memory_space=pltpu.HBM)
SMEM = pl.BlockSpec(memory_space=pltpu.SMEM)
VMEM = pl.BlockSpec(memory_space=pltpu.VMEM)
F32 = jnp.float32
COST = pl.CostEstimate(flops=10**10, bytes_accessed=10**8, transcendentals=0)


def lane_ids(shape):
    return lax.broadcasted_iota(jnp.int32, shape, len(shape) - 1)


def row_of(ref, x):
    return ref[x].astype(F32)


def chunk(c):
    return slice(c * LANE, (c + 1) * LANE)


def in_hbm(value):
    return pltpu.with_memory_space_constraint(value, pltpu.HBM)


def in_vmem(value):
    return pltpu.with_memory_space_constraint(value, pltpu.VMEM)


def x_edges_kernel(state, mask, low, high, buf, mask_buf, sems):
    fields, _, cols = state.shape[:3]
    copies = [pltpu.make_async_copy(mask, mask_buf, sems.at[2 * fields])]
    for n, x in enumerate((0, cols - 1)):
        for f in range(fields):
            copies.append(
                pltpu.make_async_copy(state.at[f, :, x], buf.at[n, f], sems.at[n * fields + f])
            )
    for copy in copies:
        copy.start()
    copies[0].wait()
    for n, (x, out) in enumerate(((0, low), (cols - 1, high))):
        for f in range(fields):
            copies[1 + n * fields + f].wait()
            out[f] = buf[n, f] * row_of(mask_buf, x)[None]


def x_edges(state5, mask):
    fields, levels, cols, _, rows = state5.shape
    edge = (fields, levels, 1, rows)
    return pl.pallas_call(
        x_edges_kernel,
        in_specs=[HBM, HBM],
        out_specs=[VMEM] * 2,
        out_shape=[pltpu.VMEM(edge, F32)] * 2,
        scratch_shapes=[
            pltpu.VMEM((2,) + edge, F32),
            pltpu.VMEM(mask.shape, jnp.int32),
            pltpu.SemaphoreType.DMA((2 * fields + 1,)),
        ],
        compiler_params=pltpu.CompilerParams(vmem_limit_bytes=8 * MIB),
        cost_estimate=COST,
        name="x_edges",
    )(in_hbm(state5), in_hbm(mask))


def spread_of(here, above, below, kappa, edge=None):
    rows = here.shape[1]
    lanes = lane_ids((here.shape[0], LANE))
    edge = 0.0 if edge is None else edge
    before = pltpu.roll(here, 1, 1)
    after = pltpu.roll(here, rows - 1, 1)
    before = jnp.concatenate([jnp.where(lanes == 0, edge, before[:, :LANE]), before[:, LANE:]], 1)
    after = jnp.concatenate(
        [after[:, :-LANE], jnp.where(lanes == LANE - 1, edge, after[:, -LANE:])], 1
    )
    return here + kappa * (above + below + before + after - 4.0 * here)


def halves(value):
    high = value.astype(jnp.bfloat16)
    return high, (value - high.astype(F32)).astype(jnp.bfloat16)


def deepened(value):
    return jnp.concatenate([value, jnp.zeros((DEPTH - value.shape[0], value.shape[1]), F32)], 0)


def fill_matrix(levels, mixing, square, matrix):
    square[:levels, :levels] = mixing
    value = square[...]
    high = value.astype(jnp.bfloat16).astype(F32)
    matrix[:DEPTH, :] = (high + pltpu.roll(high, DEPTH, 1)).astype(jnp.bfloat16)
    matrix[DEPTH:, :] = (value - high).astype(jnp.bfloat16)


def fill_stack(stack, part, value):
    high, low = halves(value)
    stack[:DEPTH, part] = high
    stack[DEPTH:, part] = low


def mix(matrix, stack):
    both = jnp.dot(matrix, stack, preferred_element_type=F32)
    return both[:DEPTH] + both[DEPTH:]


def fill_group(group):
    rows = group.shape[0] // 2
    ids = lax.broadcasted_iota(jnp.int32, group.shape, 0)
    ids = jnp.where(ids < rows, ids, ids - rows) // 3
    group[...] = jnp.where(ids == lane_ids(group.shape), 1.0, 0.0).astype(jnp.bfloat16)


def grouped(wide, group):
    return jnp.dot(wide, group, preferred_element_type=F32)


def aligned(index, size):
    return pl.ds(pl.multiple_of(index * size, size), size)


def packed(rows_of, cols):
    parts = []
    for x in range(cols):
        first, last = rows_of(x)
        lanes = lane_ids(first.shape)
        parts.append(jnp.where(lanes == 0, first, jnp.where(lanes == LANE - 1, last, 0.0)))
    shift = 2
    while len(parts) > 1:
        pairs = [parts[n : n + 2] for n in range(0, len(parts), 2)]
        parts = [p[0] + pltpu.roll(p[1], shift, 1) if len(p) == 2 else p[0] for p in pairs]
        shift *= 2
    return parts[0]


def fill_masked(levels, state, f, mask, masked):
    cols, _, rows = masked.shape
    chunks = rows // LANE
    step = cols * chunks
    for x in range(cols):
        row = row_of(mask, x)
        masked[x, PAD - 8 :, :] = jnp.zeros((8, rows), F32)
        for c in range(chunks):
            at = pl.ds(f * (levels * step) + x * chunks + c, levels, stride=step)
            masked[x, :levels, chunk(c)] = state[at, :] * row[:, chunk(c)]


def front_kernel(
    levels, is_child, state, mask, kappa, nudging, mixing, nest_x, nest_y,
    matrices, edges, inner, base,
    buf, masked, mask_buf, kappa_buf, nudging_buf, mixing_buf, square, weights,
    wide, stack, group, sems,
):
    fields, cols, _, rows = masked.shape
    chunks = rows // LANE
    step = cols * chunks
    size = levels * step
    blocks = cols // 3
    terms = 11

    def copy(f):
        at = pl.ds(f * size, size)
        return pltpu.make_async_copy(state.at[at], buf.at[at], sems.at[f])

    pairs = (
        (mask, mask_buf),
        (kappa, kappa_buf),
        (nudging, nudging_buf),
        (mixing, mixing_buf),
    )
    smalls = [
        pltpu.make_async_copy(source, target, sems.at[fields + n])
        for n, (source, target) in enumerate(pairs)
    ]
    copy(0).start()
    for small in smalls:
        small.start()
    for f in range(1, fields):
        copy(f).start()
    square[...] = jnp.zeros_like(square)
    for small in smalls:
        small.wait()

    @pl.when(is_child[0] == 1)
    def _():
        fill_group(group)
        ids = lane_ids((1, rows))
        for b in range(blocks):
            own = range(3 * b, 3 * b + 3)
            both = {x: nudging_buf[x : x + 1, :] * kappa_buf[x] for x in own}
            for n, x in enumerate(range(3 * b - 1, 3 * b + 4)):
                total = None
                for near in (x - 1, x + 1):
                    if near in both:
                        total = both[near] if total is None else total + both[near]
                if x in both:
                    total = total + (nudging_buf[x : x + 1, :] - 4.0 * both[x])
                weights[b * terms + n : b * terms + n + 1, :] = total
            for n, x in enumerate(own):
                at = b * terms + 5 + n
                value = jnp.where(ids == rows - 1, 0.0, pltpu.roll(both[x], rows - 1, 1))
                weights[at : at + 1, :] = value
                value = jnp.where(ids == 0, 0.0, pltpu.roll(both[x], 1, 1))
                weights[at + 3 : at + 4, :] = value

    def weight(b, n):
        return weights[b * terms + n : b * terms + n + 1, :]

    def field(f, total_edges):
        copy(f).wait()
        fill_matrix(levels, mixing_buf[f, :, 0, :], square, matrices.at[f])
        fill_masked(levels, buf, f, mask_buf, masked.at[f])
        own_edges = packed(
            lambda x: (masked[f, x, :, :LANE], masked[f, x, :, rows - LANE :]), cols
        )

        @pl.when(is_child[0] == 1)
        def _():
            for b in range(blocks):
                total = None
                for n, x in enumerate(range(3 * b - 1, 3 * b + 4)):
                    if 0 <= x < cols:
                        term = weight(b, n) * masked[f, x]
                        total = term if total is None else total + term
                for side, shift in ((0, 1), (3, rows - 1)):
                    value = None
                    for n in range(3):
                        term = weight(b, 5 + side + n) * masked[f, 3 * b + n]
                        value = term if value is None else value + term
                    total = total + pltpu.roll(value, shift, 1)
                at = aligned(f * blocks + b, DEPTH)
                wide[at, :rows], wide[at, rows:] = halves(deepened(total))

        @pl.when(is_child[0] == 0)
        def _():
            back = lax.rem(rows - nest_y[0], rows)
            for b in range(blocks):
                x = nest_x[0] + b
                above = masked[f, jnp.maximum(x - 1, 0)]
                below = masked[f, jnp.minimum(x + 1, cols - 1)]
                if b == 0:
                    above = jnp.where(x == 0, 0.0, above)
                if b == blocks - 1:
                    below = jnp.where(x == cols - 1, 0.0, below)
                value = spread_of(masked[f, x], above, below, kappa_buf[x])
                value = deepened(pltpu.roll(value, back, 1)[:, :LANE])
                fill_stack(stack.at[f], chunk(b), value)

        return total_edges + pltpu.roll(own_edges, 2 * f * cols, 1)

    edges[...] = lax.fori_loop(0, fields, field, jnp.zeros((PAD, LANE), F32))

    @pl.when(is_child[0] == 1)
    def _():
        value = grouped(wide[...], group[...])
        for f in range(fields):
            for b in range(blocks):
                at = (f * blocks + b) * DEPTH
                fill_stack(stack.at[f], chunk(b), value[at : at + DEPTH])

    for f in range(fields):
        mixed = mix(matrices[f], stack[f])
        for b in range(1, blocks - 1):
            at = pl.ds(f * levels * (blocks - 2) + b - 1, levels, stride=blocks - 2)
            inner[at, :] = mixed[:levels, chunk(b)]
        base[f, :, :LANE] = mixed[:PAD, :LANE]
        base[f, :, LANE:] = mixed[:PAD, chunk(blocks - 1)]


def front(is_child, state2, mask, kappa, nudging, mixing, nests, dims):
    fields, levels, cols, chunks = dims
    rows = chunks * LANE
    blocks = cols // 3
    arrays = (state2, mask, kappa, nudging, mixing)
    tile = (fields, cols, PAD, rows)
    return pl.pallas_call(
        functools.partial(front_kernel, levels),
        in_specs=[SMEM] + [HBM] * 5 + [SMEM] * 2,
        out_specs=[VMEM] * 4,
        out_shape=[
            pltpu.VMEM((fields, 2 * DEPTH, 2 * DEPTH), jnp.bfloat16),
            pltpu.VMEM((PAD, LANE), F32),
            pltpu.VMEM((fields * levels * (blocks - 2), LANE), F32),
            pltpu.VMEM((fields, PAD, 2 * LANE), F32),
        ],
        scratch_shapes=[
            pltpu.VMEM(state2.shape, F32),
            pltpu.VMEM(tile, F32),
            pltpu.VMEM(mask.shape, jnp.int32),
            pltpu.VMEM(kappa.shape, F32),
            pltpu.VMEM(nudging.shape, F32),
            pltpu.VMEM(mixing.shape, F32),
            pltpu.VMEM((DEPTH, LANE), F32),
            pltpu.VMEM((-(-blocks * 11 // 8) * 8, rows), F32),
            pltpu.VMEM((fields * blocks * DEPTH, 2 * rows), jnp.bfloat16),
            pltpu.VMEM((fields, 2 * DEPTH, blocks * LANE), jnp.bfloat16),
            pltpu.VMEM((2 * rows, LANE), jnp.bfloat16),
            pltpu.SemaphoreType.DMA((fields + 4,)),
        ],
        compiler_params=pltpu.CompilerParams(vmem_limit_bytes=28 * MIB),
        cost_estimate=COST,
        name="front",
    )(is_child, *map(in_hbm, arrays), *nests)


def y_halos(ty, peers, first, second):
    one, two = first[:PAD, :], second[:PAD, :]
    even = (lax.rem(ty[0], 2) == 0).astype(F32)
    odd = 1.0 - even
    before = (two * even + one * odd) * (ty[0] > 0).astype(F32)
    after = (one * even + two * odd) * (ty[0] < peers - 1).astype(F32)
    low = lax.rem(lane_ids((PAD, LANE)), 2) == 0
    return jnp.where(low, pltpu.roll(before, 1, 1), pltpu.roll(after, LANE - 1, 1))


def outer_kernel(
    levels, peers, is_child, ty, matrices, base, kappa, nudging, x_low, x_high, first, second,
    nest_x, nest_y, out, sides, wide, stack, group,
):
    fields = matrices.shape[0]
    cols, _, rows = kappa.shape
    blocks = cols // 3
    lanes = lane_ids((PAD, LANE))
    turned = lax.rem(lanes + 1, LANE)
    ends = ((0, x_low), (cols - 1, x_high))
    sides[...] = jnp.zeros_like(sides)
    halo = y_halos(ty, peers, first, second)

    def weighted(row_of_x):
        one = packed(lambda x: (row_of_x(x)[:, :LANE], row_of_x(x)[:, rows - LANE :]), cols)
        total = one
        for f in range(1, fields):
            total = total + pltpu.roll(one, 2 * f * cols, 1)
        return halo * total

    def fill_fix(value):
        for f in range(fields):
            fill_stack(stack.at[f], chunk(2), deepened(value))

    @pl.when(is_child[0] == 1)
    def _():
        fill_group(group)
        for n, (x, side) in enumerate(ends):
            weight = nudging[x : x + 1, :] * kappa[x]
            for f in range(fields):
                at = (f * 2 + n) * DEPTH
                sides[at : at + levels, :] = side[f, :, 0, :] * weight
        wide[:, :rows], wide[:, rows:] = halves(sides[...])
        value = grouped(wide[...], group[...])
        for f in range(fields):
            for n in range(2):
                at = (f * 2 + n) * DEPTH
                fill_stack(stack.at[f], chunk(n), value[at : at + DEPTH])
        part = weighted(lambda x: nudging[x : x + 1, :] * kappa[x])
        fill_fix(part + pltpu.roll(part, LANE - 2, 1) + pltpu.roll(part, LANE - 4, 1))

    @pl.when(is_child[0] == 0)
    def _():
        back = lax.rem(rows - nest_y[0], rows)
        reached = (nest_x[0] == 0, nest_x[0] + blocks == cols)
        for n, (x, side) in enumerate(ends):
            weight = kappa[x] * reached[n].astype(F32)
            for f in range(fields):
                at = (f * 2 + n) * DEPTH
                sides[at : at + levels, :] = side[f, :, 0, :] * weight
                value = pltpu.roll(sides[at : at + DEPTH, :], back, 1)[:, :LANE]
                fill_stack(stack.at[f], chunk(n), value)
        starts = (nest_y[0] == 0).astype(F32)
        finals = (nest_y[0] == rows - LANE).astype(F32)
        part = weighted(lambda x: kappa[x])
        part = part * jnp.where(lax.rem(lanes, 2) == 0, starts, finals)
        value = jnp.zeros((PAD, LANE), F32)
        for b in range(blocks):
            shift = lax.rem(LANE + 4 * b - 2 * nest_x[0], LANE)
            here = lax.rem(turned, 2 * cols) // 2 == 3 * b
            value = jnp.where(here, pltpu.roll(part, shift, 1), value)
        fill_fix(value)

    fixes = jnp.zeros((PAD, LANE), F32)
    for f in range(fields):
        mixed = mix(matrices[f], stack[f])
        for n in range(2):
            at = pl.ds(f * (2 * levels) + n, levels, stride=2)
            out[at, :] = base[f, :levels, chunk(n)] + mixed[:levels, chunk(n)]
        fixes = jnp.where(turned // (2 * cols) == f, mixed[:PAD, chunk(2)], fixes)
    out[out.shape[0] - PAD :, :] = fixes


def outer(is_child, ty, matrices, base, kappa, nudging, x_halos, firsts, nests, dims, peers):
    fields, levels, cols, chunks = dims
    rows = chunks * LANE
    height = -(-fields * 2 * levels // 8) * 8 + PAD
    return pl.pallas_call(
        functools.partial(outer_kernel, levels, peers),
        in_specs=[SMEM] * 2 + [VMEM] * 8 + [SMEM] * 2,
        out_specs=VMEM,
        out_shape=pltpu.VMEM((height, LANE), F32),
        scratch_shapes=[
            pltpu.VMEM((fields * 2 * DEPTH, rows), F32),
            pltpu.VMEM((fields * 2 * DEPTH, 2 * rows), jnp.bfloat16),
            pltpu.VMEM((fields, 2 * DEPTH, 3 * LANE), jnp.bfloat16),
            pltpu.VMEM((2 * rows, LANE), jnp.bfloat16),
        ],
        compiler_params=pltpu.CompilerParams(vmem_limit_bytes=12 * MIB),
        cost_estimate=COST,
        name="outer",
    )(is_child, ty, matrices, base, kappa, nudging, *x_halos, *firsts, *nests)


def tile_kernel(
    levels, peers, ty, state, mask, matrices, kappa, x_low, x_high, first, second,
    out, buf, masked, sides, halo, stack, sems,
):
    cols, _, rows = masked.shape
    chunks = rows // LANE
    size = levels * cols * chunks
    fields = state.shape[0] // size

    def copy(f):
        at = pl.ds(f * size, size)
        return pltpu.make_async_copy(state.at[at], buf.at[at], sems.at[f])

    for f in range(fields):
        copy(f).start()
    sides[...] = jnp.zeros_like(sides)
    halo[...] = y_halos(ty, peers, first, second)
    pair = 2

    def field(f, carry):
        copy(f).wait()
        fill_masked(levels, buf, f, mask, masked)
        sides[0, :levels, :] = x_low[f, :, 0, :]
        sides[1, :levels, :] = x_high[f, :, 0, :]
        for x0 in range(0, cols, pair):
            for x in range(x0, x0 + pair):
                above = masked[x - 1] if x > 0 else sides[0]
                below = masked[x + 1] if x < cols - 1 else sides[1]
                shift = lax.rem(LANE - 2 * (f * cols + x), LANE)
                edge = pltpu.roll(halo[...], lax.rem(LANE + shift, LANE), 1)
                value = spread_of(masked[x], above, below, kappa[x], edge)
                part = slice((x - x0) * rows, (x - x0 + 1) * rows)
                fill_stack(stack, part, deepened(value))
            mixed = mix(matrices[f], stack[...])
            for n in range(pair * chunks):
                out[aligned((f * cols + x0) * chunks + n, PAD), :] = mixed[:PAD, chunk(n)]
        return carry

    lax.fori_loop(0, fields, field, 0)


def tile_of(ty, state2, mask, matrices, kappa, x_halos, firsts, dims, peers):
    fields, levels, cols, chunks = dims
    rows = chunks * LANE
    return pl.pallas_call(
        functools.partial(tile_kernel, levels, peers),
        in_specs=[SMEM] + [HBM] + [VMEM] * 7,
        out_specs=VMEM,
        out_shape=pltpu.VMEM((fields * cols * chunks * PAD, LANE), F32),
        scratch_shapes=[
            pltpu.VMEM(state2.shape, F32),
            pltpu.VMEM((cols, PAD, rows), F32),
            pltpu.VMEM((2, PAD, rows), F32),
            pltpu.VMEM((PAD, LANE), F32),
            pltpu.VMEM((2 * DEPTH, 2 * rows), jnp.bfloat16),
            pltpu.SemaphoreType.DMA((fields,)),
        ],
        compiler_params=pltpu.CompilerParams(vmem_limit_bytes=16 * MIB),
        cost_estimate=COST,
        name="tile",
    )(ty, in_hbm(state2), mask, matrices, kappa, *x_halos, *firsts)


def observe_kernel(places, values, _, out):
    lanes = lane_ids((1, LANE))
    sources, slots = places.shape

    def source(s, carry):
        for k in range(0, slots, 2):
            ats, adds = [], []
            for n in range(2):
                place = places[s, k + n]
                ats.append(place >> 7)
                adds.append(jnp.where(lanes == (place & (LANE - 1)), values[s, k + n], 0.0))
            olds = [out[pl.ds(at, 1), :] for at in ats]
            also = jnp.where(ats[0] == ats[1], adds[0], 0.0)
            out[pl.ds(ats[0], 1), :] = olds[0] + adds[0]
            out[pl.ds(ats[1], 1), :] = olds[1] + adds[1] + also
        return carry

    lax.fori_loop(0, sources, source, 0)


def observe(places, values, tile):
    return pl.pallas_call(
        observe_kernel,
        in_specs=[SMEM] * 2 + [VMEM],
        out_specs=VMEM,
        out_shape=pltpu.VMEM(tile.shape, F32),
        input_output_aliases={2: 0},
        compiler_params=pltpu.CompilerParams(vmem_limit_bytes=4 * MIB),
        cost_estimate=COST,
        name="observe",
    )(places, values, in_vmem(tile))


def finish_kernel(
    levels, is_child, tile, mask, in_arrived, out_arrived, in_sent, out_sent, nest_x, nest_y,
    out, buf, group, sems,
):
    cols = mask.shape[0]
    rows = mask.shape[2]
    chunks = rows // LANE
    step = cols * chunks
    size = levels * step
    fields = out.shape[0] // size
    blocks = cols // 3
    inner = blocks - 2
    lanes = lane_ids((levels, LANE))
    ends = jnp.logical_or(lanes == 0, lanes == LANE - 1)
    height = out_arrived.shape[0]

    def copy(f):
        at = pl.ds(f * size, size)
        return pltpu.make_async_copy(buf.at[at], out.at[at], sems.at[f])

    def piece_of(f, piece):
        return tile[pl.ds(pl.multiple_of((f * step + piece) * PAD, 8), levels), :]

    def payload(f, b, inner_ref, outer_ref):
        if b in (0, blocks - 1):
            value = outer_ref[pl.ds(f * (2 * levels) + min(b, 1), levels, stride=2), :]
        else:
            value = inner_ref[pl.ds(f * (levels * inner) + b - 1, levels, stride=inner), :]
        fixes = outer_ref[height - PAD : height - PAD + levels, :]
        shift = lax.rem(LANE - 2 * (f * cols + 3 * b), LANE)
        fixes = pltpu.roll(fixes, lax.rem(LANE + shift, LANE), 1)
        return value + jnp.where(ends, fixes, 0.0)

    def fill_child(f, carry):
        for b in range(blocks):
            high, low = halves(payload(f, b, in_arrived, out_arrived))
            both = jnp.concatenate([high, low], axis=1)
            value = jnp.dot(both, group[...], preferred_element_type=F32) * (1.0 / 9.0)
            for x in range(3 * b, 3 * b + 3):
                row = row_of(mask, x)
                for c in range(chunks):
                    piece = x * chunks + c
                    at = pl.ds(f * size + piece, levels, stride=step)
                    total = piece_of(f, piece) + value[:, chunk(c)]
                    buf[at, :] = total * row[:, chunk(c)]
        copy(f).start()
        return carry

    def fill_plain(f, carry):
        for x in range(cols):
            row = row_of(mask, x)
            for c in range(chunks):
                piece = x * chunks + c
                at = pl.ds(f * size + piece, levels, stride=step)
                buf[at, :] = piece_of(f, piece) * row[:, chunk(c)]
        return carry

    def fill_parent(f, carry):
        fill_plain(f, carry)
        for b in range(blocks):
            delta = payload(f, b, in_arrived, out_arrived) - payload(f, b, in_sent, out_sent)
            wide = jnp.concatenate([delta, jnp.zeros((levels, rows - LANE), F32)], 1)
            x = nest_x[0] + b
            value = pltpu.roll(wide, nest_y[0], 1) * row_of(mask, x)
            for c in range(chunks):
                at = pl.ds(f * size + x * chunks + c, levels, stride=step)
                buf[at, :] = buf[at, :] + value[:, chunk(c)]
        copy(f).start()
        return carry

    @pl.when(is_child[0] == 1)
    def _():
        ids = lax.broadcasted_iota(jnp.int32, group.shape, 0)
        ids = jnp.where(ids < LANE, ids, ids - LANE)
        group[...] = jnp.where(lane_ids(group.shape) // 3 == ids, 1.0, 0.0).astype(jnp.bfloat16)
        lax.fori_loop(0, fields, fill_child, 0)

    @pl.when(is_child[0] == 0)
    def _():
        lax.fori_loop(0, fields, fill_parent, 0)

    for f in range(fields):
        copy(f).wait()


def finish(is_child, tile, mask, arrived, sent, nests, dims):
    fields, levels, cols, chunks = dims
    rows = chunks * LANE
    size = (fields * levels * cols * chunks, LANE)
    return pl.pallas_call(
        functools.partial(finish_kernel, levels),
        in_specs=[SMEM] + [VMEM] * 6 + [SMEM] * 2,
        out_specs=HBM,
        out_shape=pltpu.HBM(size, F32),
        scratch_shapes=[
            pltpu.VMEM(size, F32),
            pltpu.VMEM((2 * LANE, rows), jnp.bfloat16),
            pltpu.SemaphoreType.DMA((fields,)),
        ],
        compiler_params=pltpu.CompilerParams(vmem_limit_bytes=16 * MIB),
        cost_estimate=COST,
        name="finish",
    )(is_child, in_vmem(tile), mask, *arrived, *sent, *nests)


def from_neighbours(low, high, axis):
    ends = lax.axis_size(axis) - 1
    before = lax.ppermute(high, axis, [(i, i + 1) for i in range(ends)])
    after = lax.ppermute(low, axis, [(i + 1, i) for i in range(ends)])
    return before, after


def swapped(value, axis, mask):
    return lax.ppermute(value, axis, [(i, i ^ mask) for i in range(lax.axis_size(axis))])


def doubled(own, other, bit):
    return jnp.concatenate([jnp.where(bit, other, own), jnp.where(bit, own, other)])


def places_of(cells, dims):
    _, levels, cols, chunks = dims
    rows = chunks * LANE
    column, inside = cells // (cols * rows), cells % (cols * rows)
    at = (column // levels) * (cols * chunks) + inside // LANE
    return ((at * PAD + column % levels) << 7) | (inside % LANE)


def local(
    adjoint_state,
    land_mask,
    diffusivity,
    mixing,
    nudging,
    nest_x,
    nest_y,
    obs_forcing,
    obs_cell,
    obs_count,
):
    _, fields, levels, cols, rows = adjoint_state.shape
    chunks = rows // LANE
    dims = (fields, levels, cols, chunks)
    state5 = adjoint_state.reshape(fields, levels, cols, 1, rows)
    state2 = adjoint_state.reshape(fields * levels * cols * chunks, LANE)
    mask = land_mask.reshape(cols, 1, rows)
    kappa = diffusivity.reshape(cols, 1, rows)
    mixing = mixing.reshape(fields, levels, 1, levels)
    peers, across = lax.axis_size("ty"), lax.axis_size("tx")
    assert peers == 4 and across & (across - 1) == 0 and 2 * fields * cols <= LANE
    assert levels <= PAD and cols % 3 == 0 and rows == 3 * LANE
    row = lax.axis_index("ty").astype(jnp.int32)
    column = lax.axis_index("tx").astype(jnp.int32)
    ty = row.reshape(1)
    is_child = (lax.axis_index("grp") == 0).astype(jnp.int32).reshape(1)
    nests = (nest_x, nest_y)

    forcing = obs_forcing[0, 0]
    slots, dests = forcing.shape
    width = ((0, 0), (0, LANE - dests))
    other = jnp.pad(swapped(forcing, "tx", 1), width)
    gathered = doubled(jnp.pad(forcing, width), other, column & 1)
    x_low, x_high = x_edges(state5, mask)
    x_halos = from_neighbours(x_low, x_high, "tx")
    matrices, edges, in_sent, base = front(
        is_child, state2, mask, kappa, nudging, mixing, nests, dims
    )
    first = swapped(jnp.concatenate([edges, gathered]), "ty", 1)
    in_arrived = swapped(in_sent, "grp", 1)
    gathered = doubled(gathered, first[PAD:], row & 1)
    gathered, x_halos = lax.optimization_barrier((gathered, x_halos))
    second = swapped(jnp.concatenate([edges, gathered]), "ty", 3)
    firsts = (first, second)
    out_sent = outer(
        is_child, ty, matrices, base, kappa, nudging, x_halos, firsts, nests, dims, peers
    )
    out_arrived = swapped(out_sent, "grp", 1)
    gathered = doubled(gathered, second[PAD:], row >> 1)
    tile = tile_of(ty, state2, mask, matrices, kappa, x_halos, firsts, dims, peers)
    for n in range(1, across.bit_length() - 1):
        other = swapped(gathered, "tx", 1 << n)
        gathered = doubled(gathered, other, (column >> n) & 1)
    values = lax.dynamic_slice_in_dim(gathered, row * across + column, 1, axis=1)
    values = values.reshape(across // 2, peers, 2, slots).swapaxes(0, 1).reshape(-1, slots)
    live = lax.broadcasted_iota(jnp.int32, values.shape, 1) < obs_count[0]
    values = jnp.where(live, values, 0.0)
    tile = observe(places_of(obs_cell[0, :, :, 0], dims), values, tile)
    out = finish(is_child, tile, mask, (in_arrived, out_arrived), (in_sent, out_sent), nests, dims)
    return out.reshape(adjoint_state.shape)


def solution(mesh):
    in_specs = (
        P("grp", None, None, "tx", "ty"),
        P("grp", "tx", "ty"),
        P("grp", "tx", "ty"),
        P("grp", None, None, None),
        P("tx", "ty"),
        P(("ty", "tx")),
        P(("ty", "tx")),
        P("grp", ("ty", "tx"), None, None),
        P("grp", None, None, ("ty", "tx")),
        P("grp", None, ("ty", "tx")),
    )
    out_specs = P("grp", None, None, "tx", "ty")
    return jax.shard_map(local, mesh=mesh, in_specs=in_specs, out_specs=out_specs, check_vma=False)
```

```python
import functools

import jax
import jax.numpy as jnp
from jax import lax
from jax.experimental import pallas as pl
from jax.experimental.pallas import tpu as pltpu
from jax.sharding import PartitionSpec as P

LANE = 128
PAD = 56
DEPTH = 64
MIB = 1 << 20
HBM = pl.BlockSpec(memory_space=pltpu.HBM)
SMEM = pl.BlockSpec(memory_space=pltpu.SMEM)
VMEM = pl.BlockSpec(memory_space=pltpu.VMEM)
F32 = jnp.float32
COST = pl.CostEstimate(flops=10**10, bytes_accessed=10**8, transcendentals=0)


def lane_ids(shape):
    return lax.broadcasted_iota(jnp.int32, shape, len(shape) - 1)


def row_of(ref, x):
    return ref[x].astype(F32)


def chunk(c):
    return slice(c * LANE, (c + 1) * LANE)


def in_hbm(value):
    return pltpu.with_memory_space_constraint(value, pltpu.HBM)


def in_vmem(value):
    return pltpu.with_memory_space_constraint(value, pltpu.VMEM)


def x_edges_kernel(state, mask, low, high, buf, mask_buf, sems):
    fields, _, cols = state.shape[:3]
    copies = [pltpu.make_async_copy(mask, mask_buf, sems.at[2 * fields])]
    for n, x in enumerate((0, cols - 1)):
        for f in range(fields):
            copies.append(
                pltpu.make_async_copy(state.at[f, :, x], buf.at[n, f], sems.at[n * fields + f])
            )
    for copy in copies:
        copy.start()
    copies[0].wait()
    for n, (x, out) in enumerate(((0, low), (cols - 1, high))):
        for f in range(fields):
            copies[1 + n * fields + f].wait()
            out[f] = buf[n, f] * row_of(mask_buf, x)[None]


def x_edges(state5, mask):
    fields, levels, cols, _, rows = state5.shape
    edge = (fields, levels, 1, rows)
    return pl.pallas_call(
        x_edges_kernel,
        in_specs=[HBM, HBM],
        out_specs=[VMEM] * 2,
        out_shape=[pltpu.VMEM(edge, F32)] * 2,
        scratch_shapes=[
            pltpu.VMEM((2,) + edge, F32),
            pltpu.VMEM(mask.shape, jnp.int32),
            pltpu.SemaphoreType.DMA((2 * fields + 1,)),
        ],
        compiler_params=pltpu.CompilerParams(vmem_limit_bytes=8 * MIB),
        cost_estimate=COST,
        name="x_edges",
    )(in_hbm(state5), in_hbm(mask))


def spread_of(here, above, below, kappa, edge=None):
    rows = here.shape[1]
    lanes = lane_ids((here.shape[0], LANE))
    edge = 0.0 if edge is None else edge
    before = pltpu.roll(here, 1, 1)
    after = pltpu.roll(here, rows - 1, 1)
    before = jnp.concatenate([jnp.where(lanes == 0, edge, before[:, :LANE]), before[:, LANE:]], 1)
    after = jnp.concatenate(
        [after[:, :-LANE], jnp.where(lanes == LANE - 1, edge, after[:, -LANE:])], 1
    )
    return here + kappa * (above + below + before + after - 4.0 * here)


def halves(value):
    high = value.astype(jnp.bfloat16)
    return high, (value - high.astype(F32)).astype(jnp.bfloat16)


def deepened(value):
    return jnp.concatenate([value, jnp.zeros((DEPTH - value.shape[0], value.shape[1]), F32)], 0)


def fill_matrix(levels, mixing, square, matrix):
    square[:levels, :levels] = mixing
    value = square[...]
    high = value.astype(jnp.bfloat16).astype(F32)
    matrix[:DEPTH, :] = (high + pltpu.roll(high, DEPTH, 1)).astype(jnp.bfloat16)
    matrix[DEPTH:, :] = (value - high).astype(jnp.bfloat16)


def fill_stack(stack, part, value):
    high, low = halves(value)
    stack[:DEPTH, part] = high
    stack[DEPTH:, part] = low


def mix(matrix, stack):
    both = jnp.dot(matrix, stack, preferred_element_type=F32)
    return both[:DEPTH] + both[DEPTH:]


def fill_group(group):
    rows = group.shape[0] // 2
    ids = lax.broadcasted_iota(jnp.int32, group.shape, 0)
    ids = jnp.where(ids < rows, ids, ids - rows) // 3
    group[...] = jnp.where(ids == lane_ids(group.shape), 1.0, 0.0).astype(jnp.bfloat16)


def grouped(wide, group):
    return jnp.dot(wide, group, preferred_element_type=F32)


def aligned(index, size):
    return pl.ds(pl.multiple_of(index * size, size), size)


def packed(rows_of, cols):
    parts = []
    for x in range(cols):
        first, last = rows_of(x)
        lanes = lane_ids(first.shape)
        parts.append(jnp.where(lanes == 0, first, jnp.where(lanes == LANE - 1, last, 0.0)))
    shift = 2
    while len(parts) > 1:
        pairs = [parts[n : n + 2] for n in range(0, len(parts), 2)]
        parts = [p[0] + pltpu.roll(p[1], shift, 1) if len(p) == 2 else p[0] for p in pairs]
        shift *= 2
    return parts[0]


def fill_masked(levels, state, f, mask, masked):
    cols, _, rows = masked.shape
    chunks = rows // LANE
    step = cols * chunks
    for x in range(cols):
        row = row_of(mask, x)
        masked[x, PAD - 8 :, :] = jnp.zeros((8, rows), F32)
        for c in range(chunks):
            at = pl.ds(f * (levels * step) + x * chunks + c, levels, stride=step)
            masked[x, :levels, chunk(c)] = state[at, :] * row[:, chunk(c)]


def front_kernel(
    levels, is_child, state, mask, kappa, nudging, mixing, nest_x, nest_y,
    matrices, edges, inner, base,
    buf, masked, mask_buf, kappa_buf, nudging_buf, mixing_buf, square, weights,
    wide, stack, group, sems,
):
    fields, cols, _, rows = masked.shape
    chunks = rows // LANE
    step = cols * chunks
    size = levels * step
    blocks = cols // 3
    terms = 11

    def copy(f):
        at = pl.ds(f * size, size)
        return pltpu.make_async_copy(state.at[at], buf.at[at], sems.at[f])

    pairs = (
        (mask, mask_buf),
        (kappa, kappa_buf),
        (nudging, nudging_buf),
        (mixing, mixing_buf),
    )
    smalls = [
        pltpu.make_async_copy(source, target, sems.at[fields + n])
        for n, (source, target) in enumerate(pairs)
    ]
    copy(0).start()
    for small in smalls:
        small.start()
    for f in range(1, fields):
        copy(f).start()
    square[...] = jnp.zeros_like(square)
    for small in smalls:
        small.wait()

    @pl.when(is_child[0] == 1)
    def _():
        fill_group(group)
        ids = lane_ids((1, rows))
        for b in range(blocks):
            own = range(3 * b, 3 * b + 3)
            both = {x: nudging_buf[x : x + 1, :] * kappa_buf[x] for x in own}
            for n, x in enumerate(range(3 * b - 1, 3 * b + 4)):
                total = None
                for near in (x - 1, x + 1):
                    if near in both:
                        total = both[near] if total is None else total + both[near]
                if x in both:
                    total = total + (nudging_buf[x : x + 1, :] - 4.0 * both[x])
                weights[b * terms + n : b * terms + n + 1, :] = total
            for n, x in enumerate(own):
                at = b * terms + 5 + n
                value = jnp.where(ids == rows - 1, 0.0, pltpu.roll(both[x], rows - 1, 1))
                weights[at : at + 1, :] = value
                value = jnp.where(ids == 0, 0.0, pltpu.roll(both[x], 1, 1))
                weights[at + 3 : at + 4, :] = value

    def weight(b, n):
        return weights[b * terms + n : b * terms + n + 1, :]

    def field(f, total_edges):
        copy(f).wait()
        fill_matrix(levels, mixing_buf[f, :, 0, :], square, matrices.at[f])
        fill_masked(levels, buf, f, mask_buf, masked.at[f])
        own_edges = packed(
            lambda x: (masked[f, x, :, :LANE], masked[f, x, :, rows - LANE :]), cols
        )

        @pl.when(is_child[0] == 1)
        def _():
            for b in range(blocks):
                total = None
                for n, x in enumerate(range(3 * b - 1, 3 * b + 4)):
                    if 0 <= x < cols:
                        term = weight(b, n) * masked[f, x]
                        total = term if total is None else total + term
                for side, shift in ((0, 1), (3, rows - 1)):
                    value = None
                    for n in range(3):
                        term = weight(b, 5 + side + n) * masked[f, 3 * b + n]
                        value = term if value is None else value + term
                    total = total + pltpu.roll(value, shift, 1)
                at = aligned(f * blocks + b, DEPTH)
                wide[at, :rows], wide[at, rows:] = halves(deepened(total))

        @pl.when(is_child[0] == 0)
        def _():
            back = lax.rem(rows - nest_y[0], rows)
            for b in range(blocks):
                x = nest_x[0] + b
                above = masked[f, jnp.maximum(x - 1, 0)]
                below = masked[f, jnp.minimum(x + 1, cols - 1)]
                if b == 0:
                    above = jnp.where(x == 0, 0.0, above)
                if b == blocks - 1:
                    below = jnp.where(x == cols - 1, 0.0, below)
                value = spread_of(masked[f, x], above, below, kappa_buf[x])
                value = deepened(pltpu.roll(value, back, 1)[:, :LANE])
                fill_stack(stack.at[f], chunk(b), value)

        return total_edges + pltpu.roll(own_edges, 2 * f * cols, 1)

    edges[...] = lax.fori_loop(0, fields, field, jnp.zeros((PAD, LANE), F32))

    @pl.when(is_child[0] == 1)
    def _():
        value = grouped(wide[...], group[...])
        for f in range(fields):
            for b in range(blocks):
                at = (f * blocks + b) * DEPTH
                fill_stack(stack.at[f], chunk(b), value[at : at + DEPTH])

    for f in range(fields):
        mixed = mix(matrices[f], stack[f])
        for b in range(1, blocks - 1):
            at = pl.ds(f * levels * (blocks - 2) + b - 1, levels, stride=blocks - 2)
            inner[at, :] = mixed[:levels, chunk(b)]
        base[f, :, :LANE] = mixed[:PAD, :LANE]
        base[f, :, LANE:] = mixed[:PAD, chunk(blocks - 1)]


def front(is_child, state2, mask, kappa, nudging, mixing, nests, dims):
    fields, levels, cols, chunks = dims
    rows = chunks * LANE
    blocks = cols // 3
    arrays = (state2, mask, kappa, nudging, mixing)
    tile = (fields, cols, PAD, rows)
    return pl.pallas_call(
        functools.partial(front_kernel, levels),
        in_specs=[SMEM] + [HBM] * 5 + [SMEM] * 2,
        out_specs=[VMEM] * 4,
        out_shape=[
            pltpu.VMEM((fields, 2 * DEPTH, 2 * DEPTH), jnp.bfloat16),
            pltpu.VMEM((PAD, LANE), F32),
            pltpu.VMEM((fields * levels * (blocks - 2), LANE), F32),
            pltpu.VMEM((fields, PAD, 2 * LANE), F32),
        ],
        scratch_shapes=[
            pltpu.VMEM(state2.shape, F32),
            pltpu.VMEM(tile, F32),
            pltpu.VMEM(mask.shape, jnp.int32),
            pltpu.VMEM(kappa.shape, F32),
            pltpu.VMEM(nudging.shape, F32),
            pltpu.VMEM(mixing.shape, F32),
            pltpu.VMEM((DEPTH, LANE), F32),
            pltpu.VMEM((-(-blocks * 11 // 8) * 8, rows), F32),
            pltpu.VMEM((fields * blocks * DEPTH, 2 * rows), jnp.bfloat16),
            pltpu.VMEM((fields, 2 * DEPTH, blocks * LANE), jnp.bfloat16),
            pltpu.VMEM((2 * rows, LANE), jnp.bfloat16),
            pltpu.SemaphoreType.DMA((fields + 4,)),
        ],
        compiler_params=pltpu.CompilerParams(vmem_limit_bytes=28 * MIB),
        cost_estimate=COST,
        name="front",
    )(is_child, *map(in_hbm, arrays), *nests)


def y_halos(ty, peers, first, second):
    one, two = first[:PAD, :], second[:PAD, :]
    even = (lax.rem(ty[0], 2) == 0).astype(F32)
    odd = 1.0 - even
    before = (two * even + one * odd) * (ty[0] > 0).astype(F32)
    after = (one * even + two * odd) * (ty[0] < peers - 1).astype(F32)
    low = lax.rem(lane_ids((PAD, LANE)), 2) == 0
    return jnp.where(low, pltpu.roll(before, 1, 1), pltpu.roll(after, LANE - 1, 1))


def outer_kernel(
    levels, peers, is_child, ty, matrices, base, kappa, nudging, x_low, x_high, first, second,
    nest_x, nest_y, out, sides, wide, stack, group,
):
    fields = matrices.shape[0]
    cols, _, rows = kappa.shape
    blocks = cols // 3
    lanes = lane_ids((PAD, LANE))
    turned = lax.rem(lanes + 1, LANE)
    ends = ((0, x_low), (cols - 1, x_high))
    sides[...] = jnp.zeros_like(sides)
    halo = y_halos(ty, peers, first, second)

    def weighted(row_of_x):
        one = packed(lambda x: (row_of_x(x)[:, :LANE], row_of_x(x)[:, rows - LANE :]), cols)
        total = one
        for f in range(1, fields):
            total = total + pltpu.roll(one, 2 * f * cols, 1)
        return halo * total

    def fill_fix(value):
        for f in range(fields):
            fill_stack(stack.at[f], chunk(2), deepened(value))

    @pl.when(is_child[0] == 1)
    def _():
        fill_group(group)
        for n, (x, side) in enumerate(ends):
            weight = nudging[x : x + 1, :] * kappa[x]
            for f in range(fields):
                at = (f * 2 + n) * DEPTH
                sides[at : at + levels, :] = side[f, :, 0, :] * weight
        wide[:, :rows], wide[:, rows:] = halves(sides[...])
        value = grouped(wide[...], group[...])
        for f in range(fields):
            for n in range(2):
                at = (f * 2 + n) * DEPTH
                fill_stack(stack.at[f], chunk(n), value[at : at + DEPTH])
        part = weighted(lambda x: nudging[x : x + 1, :] * kappa[x])
        fill_fix(part + pltpu.roll(part, LANE - 2, 1) + pltpu.roll(part, LANE - 4, 1))

    @pl.when(is_child[0] == 0)
    def _():
        back = lax.rem(rows - nest_y[0], rows)
        reached = (nest_x[0] == 0, nest_x[0] + blocks == cols)
        for n, (x, side) in enumerate(ends):
            weight = kappa[x] * reached[n].astype(F32)
            for f in range(fields):
                at = (f * 2 + n) * DEPTH
                sides[at : at + levels, :] = side[f, :, 0, :] * weight
                value = pltpu.roll(sides[at : at + DEPTH, :], back, 1)[:, :LANE]
                fill_stack(stack.at[f], chunk(n), value)
        starts = (nest_y[0] == 0).astype(F32)
        finals = (nest_y[0] == rows - LANE).astype(F32)
        part = weighted(lambda x: kappa[x])
        part = part * jnp.where(lax.rem(lanes, 2) == 0, starts, finals)
        value = jnp.zeros((PAD, LANE), F32)
        for b in range(blocks):
            shift = lax.rem(LANE + 4 * b - 2 * nest_x[0], LANE)
            here = lax.rem(turned, 2 * cols) // 2 == 3 * b
            value = jnp.where(here, pltpu.roll(part, shift, 1), value)
        fill_fix(value)

    fixes = jnp.zeros((PAD, LANE), F32)
    for f in range(fields):
        mixed = mix(matrices[f], stack[f])
        for n in range(2):
            at = pl.ds(f * (2 * levels) + n, levels, stride=2)
            out[at, :] = base[f, :levels, chunk(n)] + mixed[:levels, chunk(n)]
        fixes = jnp.where(turned // (2 * cols) == f, mixed[:PAD, chunk(2)], fixes)
    out[out.shape[0] - PAD :, :] = fixes


def outer(is_child, ty, matrices, base, kappa, nudging, x_halos, firsts, nests, dims, peers):
    fields, levels, cols, chunks = dims
    rows = chunks * LANE
    height = -(-fields * 2 * levels // 8) * 8 + PAD
    return pl.pallas_call(
        functools.partial(outer_kernel, levels, peers),
        in_specs=[SMEM] * 2 + [VMEM] * 8 + [SMEM] * 2,
        out_specs=VMEM,
        out_shape=pltpu.VMEM((height, LANE), F32),
        scratch_shapes=[
            pltpu.VMEM((fields * 2 * DEPTH, rows), F32),
            pltpu.VMEM((fields * 2 * DEPTH, 2 * rows), jnp.bfloat16),
            pltpu.VMEM((fields, 2 * DEPTH, 3 * LANE), jnp.bfloat16),
            pltpu.VMEM((2 * rows, LANE), jnp.bfloat16),
        ],
        compiler_params=pltpu.CompilerParams(vmem_limit_bytes=12 * MIB),
        cost_estimate=COST,
        name="outer",
    )(is_child, ty, matrices, base, kappa, nudging, *x_halos, *firsts, *nests)


def tile_kernel(
    levels, peers, ty, places, counts, values, own, state, mask, matrices, kappa, x_low, x_high,
    first, second,
    out, buf, masked, sides, halo, stack, sems,
):
    cols, _, rows = masked.shape
    chunks = rows // LANE
    size = levels * cols * chunks
    fields = state.shape[0] // size

    def copy(f):
        at = pl.ds(f * size, size)
        return pltpu.make_async_copy(state.at[at], buf.at[at], sems.at[f])

    for f in range(fields):
        copy(f).start()
    sides[...] = jnp.zeros_like(sides)
    halo[...] = y_halos(ty, peers, first, second)
    pair = 2

    def field(f, carry):
        copy(f).wait()
        fill_masked(levels, buf, f, mask, masked)
        sides[0, :levels, :] = x_low[f, :, 0, :]
        sides[1, :levels, :] = x_high[f, :, 0, :]
        for x0 in range(0, cols, pair):
            for x in range(x0, x0 + pair):
                above = masked[x - 1] if x > 0 else sides[0]
                below = masked[x + 1] if x < cols - 1 else sides[1]
                shift = lax.rem(LANE - 2 * (f * cols + x), LANE)
                edge = pltpu.roll(halo[...], lax.rem(LANE + shift, LANE), 1)
                value = spread_of(masked[x], above, below, kappa[x], edge)
                part = slice((x - x0) * rows, (x - x0 + 1) * rows)
                fill_stack(stack, part, deepened(value))
            mixed = mix(matrices[f], stack[...])
            for n in range(pair * chunks):
                out[aligned((f * cols + x0) * chunks + n, PAD), :] = mixed[:PAD, chunk(n)]
        return carry

    lax.fori_loop(0, fields, field, 0)
    lanes = lane_ids((1, LANE))
    sources, slots = places.shape

    def source(s, carry):
        row, column = lax.div(s, sources // peers), lax.rem(s, sources // peers)
        at_values = (((column >> 1) * peers + row) * 2 + (column & 1)) ^ own[0]
        count = counts[0, s]
        for k in range(0, slots, 2):
            ats, adds = [], []
            for n in range(k, k + 2):
                place = places[s, n]
                value = jnp.where(n < count, values[n, at_values], 0.0)
                ats.append(place >> 7)
                adds.append(jnp.where(lanes == (place & (LANE - 1)), value, 0.0))
            olds = [out[pl.ds(at, 1), :] for at in ats]
            also = jnp.where(ats[0] == ats[1], adds[0], 0.0)
            out[pl.ds(ats[0], 1), :] = olds[0] + adds[0]
            out[pl.ds(ats[1], 1), :] = olds[1] + adds[1] + also
        return carry

    lax.fori_loop(0, sources, source, 0)


def tile_of(ty, seen, state2, mask, matrices, kappa, x_halos, firsts, dims, peers):
    fields, levels, cols, chunks = dims
    rows = chunks * LANE
    return pl.pallas_call(
        functools.partial(tile_kernel, levels, peers),
        in_specs=[SMEM] * 5 + [HBM] + [VMEM] * 7,
        out_specs=VMEM,
        out_shape=pltpu.VMEM((fields * cols * chunks * PAD, LANE), F32),
        scratch_shapes=[
            pltpu.VMEM(state2.shape, F32),
            pltpu.VMEM((cols, PAD, rows), F32),
            pltpu.VMEM((2, PAD, rows), F32),
            pltpu.VMEM((PAD, LANE), F32),
            pltpu.VMEM((2 * DEPTH, 2 * rows), jnp.bfloat16),
            pltpu.SemaphoreType.DMA((fields,)),
        ],
        compiler_params=pltpu.CompilerParams(vmem_limit_bytes=16 * MIB),
        cost_estimate=COST,
        name="tile",
    )(ty, *seen, in_hbm(state2), mask, matrices, kappa, *x_halos, *firsts)


def finish_kernel(
    levels, is_child, tile, mask, in_arrived, out_arrived, in_sent, out_sent, nest_x, nest_y,
    out, buf, group, sems,
):
    cols = mask.shape[0]
    rows = mask.shape[2]
    chunks = rows // LANE
    step = cols * chunks
    size = levels * step
    fields = out.shape[0] // size
    blocks = cols // 3
    inner = blocks - 2
    lanes = lane_ids((levels, LANE))
    ends = jnp.logical_or(lanes == 0, lanes == LANE - 1)
    height = out_arrived.shape[0]

    def copy(f):
        at = pl.ds(f * size, size)
        return pltpu.make_async_copy(buf.at[at], out.at[at], sems.at[f])

    def piece_of(f, piece):
        return tile[pl.ds(pl.multiple_of((f * step + piece) * PAD, 8), levels), :]

    def payload(f, b, inner_ref, outer_ref):
        if b in (0, blocks - 1):
            value = outer_ref[pl.ds(f * (2 * levels) + min(b, 1), levels, stride=2), :]
        else:
            value = inner_ref[pl.ds(f * (levels * inner) + b - 1, levels, stride=inner), :]
        fixes = outer_ref[height - PAD : height - PAD + levels, :]
        shift = lax.rem(LANE - 2 * (f * cols + 3 * b), LANE)
        fixes = pltpu.roll(fixes, lax.rem(LANE + shift, LANE), 1)
        return value + jnp.where(ends, fixes, 0.0)

    def fill_child(f, carry):
        for b in range(blocks):
            high, low = halves(payload(f, b, in_arrived, out_arrived))
            both = jnp.concatenate([high, low], axis=1)
            value = jnp.dot(both, group[...], preferred_element_type=F32) * (1.0 / 9.0)
            for x in range(3 * b, 3 * b + 3):
                row = row_of(mask, x)
                for c in range(chunks):
                    piece = x * chunks + c
                    at = pl.ds(f * size + piece, levels, stride=step)
                    total = piece_of(f, piece) + value[:, chunk(c)]
                    buf[at, :] = total * row[:, chunk(c)]
        copy(f).start()
        return carry

    def fill_plain(f, carry):
        for x in range(cols):
            row = row_of(mask, x)
            for c in range(chunks):
                piece = x * chunks + c
                at = pl.ds(f * size + piece, levels, stride=step)
                buf[at, :] = piece_of(f, piece) * row[:, chunk(c)]
        return carry

    def fill_parent(f, carry):
        fill_plain(f, carry)
        for b in range(blocks):
            delta = payload(f, b, in_arrived, out_arrived) - payload(f, b, in_sent, out_sent)
            wide = jnp.concatenate([delta, jnp.zeros((levels, rows - LANE), F32)], 1)
            x = nest_x[0] + b
            value = pltpu.roll(wide, nest_y[0], 1) * row_of(mask, x)
            for c in range(chunks):
                at = pl.ds(f * size + x * chunks + c, levels, stride=step)
                buf[at, :] = buf[at, :] + value[:, chunk(c)]
        copy(f).start()
        return carry

    @pl.when(is_child[0] == 1)
    def _():
        ids = lax.broadcasted_iota(jnp.int32, group.shape, 0)
        ids = jnp.where(ids < LANE, ids, ids - LANE)
        group[...] = jnp.where(lane_ids(group.shape) // 3 == ids, 1.0, 0.0).astype(jnp.bfloat16)
        lax.fori_loop(0, fields, fill_child, 0)

    @pl.when(is_child[0] == 0)
    def _():
        lax.fori_loop(0, fields, fill_parent, 0)

    for f in range(fields):
        copy(f).wait()


def finish(is_child, tile, mask, arrived, sent, nests, dims):
    fields, levels, cols, chunks = dims
    rows = chunks * LANE
    size = (fields * levels * cols * chunks, LANE)
    return pl.pallas_call(
        functools.partial(finish_kernel, levels),
        in_specs=[SMEM] + [VMEM] * 6 + [SMEM] * 2,
        out_specs=HBM,
        out_shape=pltpu.HBM(size, F32),
        scratch_shapes=[
            pltpu.VMEM(size, F32),
            pltpu.VMEM((2 * LANE, rows), jnp.bfloat16),
            pltpu.SemaphoreType.DMA((fields,)),
        ],
        compiler_params=pltpu.CompilerParams(vmem_limit_bytes=16 * MIB),
        cost_estimate=COST,
        name="finish",
    )(is_child, in_vmem(tile), mask, *arrived, *sent, *nests)


def from_neighbours(low, high, axis):
    ends = lax.axis_size(axis) - 1
    before = lax.ppermute(high, axis, [(i, i + 1) for i in range(ends)])
    after = lax.ppermute(low, axis, [(i + 1, i) for i in range(ends)])
    return before, after


def swapped(value, axis, mask):
    return lax.ppermute(value, axis, [(i, i ^ mask) for i in range(lax.axis_size(axis))])


def stacked(blocks):
    width = blocks.shape[1]
    blocks = jnp.pad(blocks, ((0, 0), (0, -width % LANE)))
    return jnp.concatenate([blocks[:, chunk(n)] for n in range(blocks.shape[1] // LANE)])


def unstacked(rows, slots, width):
    parts = [rows[n : n + slots] for n in range(0, rows.shape[0], slots)]
    return jnp.concatenate(parts, axis=1)[:, :width]


def places_of(cells, dims):
    _, levels, cols, chunks = dims
    rows = chunks * LANE
    column, inside = cells // (cols * rows), cells % (cols * rows)
    at = (column // levels) * (cols * chunks) + inside // LANE
    return ((at * PAD + column % levels) << 7) | (inside % LANE)


def local(
    adjoint_state,
    land_mask,
    diffusivity,
    mixing,
    nudging,
    nest_x,
    nest_y,
    obs_forcing,
    obs_cell,
    obs_count,
):
    _, fields, levels, cols, rows = adjoint_state.shape
    chunks = rows // LANE
    dims = (fields, levels, cols, chunks)
    state5 = adjoint_state.reshape(fields, levels, cols, 1, rows)
    state2 = adjoint_state.reshape(fields * levels * cols * chunks, LANE)
    mask = land_mask.reshape(cols, 1, rows)
    kappa = diffusivity.reshape(cols, 1, rows)
    mixing = mixing.reshape(fields, levels, 1, levels)
    peers, across = lax.axis_size("ty"), lax.axis_size("tx")
    assert peers == 4 and across & (across - 1) == 0 and 2 * fields * cols <= LANE
    assert levels <= PAD and cols % 3 == 0 and rows == 3 * LANE
    row = lax.axis_index("ty").astype(jnp.int32)
    column = lax.axis_index("tx").astype(jnp.int32)
    ty = row.reshape(1)
    is_child = (lax.axis_index("grp") == 0).astype(jnp.int32).reshape(1)
    nests = (nest_x, nest_y)

    forcing = obs_forcing[0, 0]
    slots, dests = forcing.shape
    pair = jnp.concatenate([forcing, swapped(forcing, "tx", 1)], axis=1)
    x_low, x_high = x_edges(state5, mask)
    x_halos = from_neighbours(x_low, x_high, "tx")
    matrices, edges, in_sent, base = front(
        is_child, state2, mask, kappa, nudging, mixing, nests, dims
    )
    parcel = jnp.concatenate([edges, stacked(pair)])
    first = swapped(parcel, "ty", 1)
    second = swapped(parcel, "ty", 3)
    third = swapped(parcel[PAD:], "ty", 2)
    in_arrived = swapped(in_sent, "grp", 1)
    firsts = (first, second)
    width = pair.shape[1]
    others = [unstacked(rows, slots, width) for rows in (first[PAD:], third, second[PAD:])]
    gathered = jnp.concatenate([pair, *others], axis=1)
    gathered, x_halos = lax.optimization_barrier((gathered, x_halos))
    out_sent = outer(
        is_child, ty, matrices, base, kappa, nudging, x_halos, firsts, nests, dims, peers
    )
    out_arrived = swapped(out_sent, "grp", 1)
    for n in range(1, across.bit_length() - 1):
        gathered = jnp.concatenate([gathered, swapped(gathered, "tx", 1 << n)], axis=1)
    values = gathered.reshape(slots, -1, dests)
    values = lax.dynamic_slice_in_dim(values, row * across + column, 1, axis=2)[..., 0]
    own = ((column >> 1) * peers + row) * 2 + (column & 1)
    places = places_of(obs_cell[0, :, :, 0], dims)
    seen = (places, obs_count.reshape(1, -1), values, own.reshape(1))
    tile = tile_of(ty, seen, state2, mask, matrices, kappa, x_halos, firsts, dims, peers)
    out = finish(is_child, tile, mask, (in_arrived, out_arrived), (in_sent, out_sent), nests, dims)
    return out.reshape(adjoint_state.shape)


def solution(mesh):
    in_specs = (
        P("grp", None, None, "tx", "ty"),
        P("grp", "tx", "ty"),
        P("grp", "tx", "ty"),
        P("grp", None, None, None),
        P("tx", "ty"),
        P(("ty", "tx")),
        P(("ty", "tx")),
        P("grp", ("ty", "tx"), None, None),
        P("grp", None, None, ("ty", "tx")),
        P("grp", None, ("ty", "tx")),
    )
    out_specs = P("grp", None, None, "tx", "ty")
    return jax.shard_map(local, mesh=mesh, in_specs=in_specs, out_specs=out_specs, check_vma=False)
```

```python
import functools

import jax
import jax.numpy as jnp
from jax import lax
from jax.experimental import pallas as pl
from jax.experimental.pallas import tpu as pltpu
from jax.sharding import PartitionSpec as P

LANE = 128
PAD = 56
DEPTH = 64
MIB = 1 << 20
HBM = pl.BlockSpec(memory_space=pltpu.HBM)
SMEM = pl.BlockSpec(memory_space=pltpu.SMEM)
VMEM = pl.BlockSpec(memory_space=pltpu.VMEM)
F32 = jnp.float32
COST = pl.CostEstimate(flops=10**10, bytes_accessed=10**8, transcendentals=0)


def lane_ids(shape):
    return lax.broadcasted_iota(jnp.int32, shape, len(shape) - 1)


def row_of(ref, x):
    return ref[x].astype(F32)


def chunk(c):
    return slice(c * LANE, (c + 1) * LANE)


def in_hbm(value):
    return pltpu.with_memory_space_constraint(value, pltpu.HBM)


def in_vmem(value):
    return pltpu.with_memory_space_constraint(value, pltpu.VMEM)


def x_edges_kernel(state, mask, low, high, buf, mask_buf, sems):
    fields, _, cols = state.shape[:3]
    copies = [pltpu.make_async_copy(mask, mask_buf, sems.at[2 * fields])]
    for n, x in enumerate((0, cols - 1)):
        for f in range(fields):
            copies.append(
                pltpu.make_async_copy(state.at[f, :, x], buf.at[n, f], sems.at[n * fields + f])
            )
    for copy in copies:
        copy.start()
    copies[0].wait()
    for n, (x, out) in enumerate(((0, low), (cols - 1, high))):
        for f in range(fields):
            copies[1 + n * fields + f].wait()
            out[f] = buf[n, f] * row_of(mask_buf, x)[None]


def x_edges(state5, mask):
    fields, levels, cols, _, rows = state5.shape
    edge = (fields, levels, 1, rows)
    return pl.pallas_call(
        x_edges_kernel,
        in_specs=[HBM, HBM],
        out_specs=[VMEM] * 2,
        out_shape=[pltpu.VMEM(edge, F32)] * 2,
        scratch_shapes=[
            pltpu.VMEM((2,) + edge, F32),
            pltpu.VMEM(mask.shape, jnp.int32),
            pltpu.SemaphoreType.DMA((2 * fields + 1,)),
        ],
        compiler_params=pltpu.CompilerParams(vmem_limit_bytes=8 * MIB),
        cost_estimate=COST,
        name="x_edges",
    )(in_hbm(state5), in_hbm(mask))


def spread_of(here, above, below, kappa, edge=None):
    rows = here.shape[1]
    lanes = lane_ids((here.shape[0], LANE))
    edge = 0.0 if edge is None else edge
    before = pltpu.roll(here, 1, 1)
    after = pltpu.roll(here, rows - 1, 1)
    before = jnp.concatenate([jnp.where(lanes == 0, edge, before[:, :LANE]), before[:, LANE:]], 1)
    after = jnp.concatenate(
        [after[:, :-LANE], jnp.where(lanes == LANE - 1, edge, after[:, -LANE:])], 1
    )
    return here + kappa * (above + below + before + after - 4.0 * here)


def halves(value):
    high = value.astype(jnp.bfloat16)
    return high, (value - high.astype(F32)).astype(jnp.bfloat16)


def deepened(value):
    return jnp.concatenate([value, jnp.zeros((DEPTH - value.shape[0], value.shape[1]), F32)], 0)


def fill_matrix(levels, mixing, square, matrix):
    square[:levels, :levels] = mixing
    value = square[...]
    high = value.astype(jnp.bfloat16).astype(F32)
    matrix[:DEPTH, :] = (high + pltpu.roll(high, DEPTH, 1)).astype(jnp.bfloat16)
    matrix[DEPTH:, :] = (value - high).astype(jnp.bfloat16)


def fill_stack(stack, part, value):
    high, low = halves(value)
    stack[:DEPTH, part] = high
    stack[DEPTH:, part] = low


def mix(matrix, stack):
    both = jnp.dot(matrix, stack, preferred_element_type=F32)
    return both[:DEPTH] + both[DEPTH:]


def fill_group(group):
    rows = group.shape[0] // 2
    ids = lax.broadcasted_iota(jnp.int32, group.shape, 0)
    ids = jnp.where(ids < rows, ids, ids - rows) // 3
    group[...] = jnp.where(ids == lane_ids(group.shape), 1.0, 0.0).astype(jnp.bfloat16)


def grouped(wide, group):
    return jnp.dot(wide, group, preferred_element_type=F32)


def aligned(index, size):
    return pl.ds(pl.multiple_of(index * size, size), size)


def packed(rows_of, cols):
    parts = []
    for x in range(cols):
        first, last = rows_of(x)
        lanes = lane_ids(first.shape)
        parts.append(jnp.where(lanes == 0, first, jnp.where(lanes == LANE - 1, last, 0.0)))
    shift = 2
    while len(parts) > 1:
        pairs = [parts[n : n + 2] for n in range(0, len(parts), 2)]
        parts = [p[0] + pltpu.roll(p[1], shift, 1) if len(p) == 2 else p[0] for p in pairs]
        shift *= 2
    return parts[0]


def fill_masked(levels, state, f, mask, masked):
    cols, _, rows = masked.shape
    chunks = rows // LANE
    step = cols * chunks
    for x in range(cols):
        row = row_of(mask, x)
        masked[x, PAD - 8 :, :] = jnp.zeros((8, rows), F32)
        for c in range(chunks):
            at = pl.ds(f * (levels * step) + x * chunks + c, levels, stride=step)
            masked[x, :levels, chunk(c)] = state[at, :] * row[:, chunk(c)]


def front_kernel(
    levels, is_child, state, mask_buf, kappa_buf, nudging_buf, mixing_buf, nest_x, nest_y,
    matrices, edges, inner, base, masked, square, weights, wide, stack, group,
):
    fields, cols, _, rows = masked.shape
    chunks = rows // LANE
    step = cols * chunks
    size = levels * step
    blocks = cols // 3
    terms = 11

    square[...] = jnp.zeros_like(square)

    @pl.when(is_child[0] == 1)
    def _():
        fill_group(group)
        ids = lane_ids((1, rows))
        for b in range(blocks):
            own = range(3 * b, 3 * b + 3)
            both = {x: nudging_buf[x : x + 1, :] * kappa_buf[x] for x in own}
            for n, x in enumerate(range(3 * b - 1, 3 * b + 4)):
                total = None
                for near in (x - 1, x + 1):
                    if near in both:
                        total = both[near] if total is None else total + both[near]
                if x in both:
                    total = total + (nudging_buf[x : x + 1, :] - 4.0 * both[x])
                weights[b * terms + n : b * terms + n + 1, :] = total
            for n, x in enumerate(own):
                at = b * terms + 5 + n
                value = jnp.where(ids == rows - 1, 0.0, pltpu.roll(both[x], rows - 1, 1))
                weights[at : at + 1, :] = value
                value = jnp.where(ids == 0, 0.0, pltpu.roll(both[x], 1, 1))
                weights[at + 3 : at + 4, :] = value

    def weight(b, n):
        return weights[b * terms + n : b * terms + n + 1, :]

    def field(f, total_edges):
        fill_matrix(levels, mixing_buf[f, :, 0, :], square, matrices.at[f])
        fill_masked(levels, state, f, mask_buf, masked.at[f])
        own_edges = packed(
            lambda x: (masked[f, x, :, :LANE], masked[f, x, :, rows - LANE :]), cols
        )

        @pl.when(is_child[0] == 1)
        def _():
            for b in range(blocks):
                total = None
                for n, x in enumerate(range(3 * b - 1, 3 * b + 4)):
                    if 0 <= x < cols:
                        term = weight(b, n) * masked[f, x]
                        total = term if total is None else total + term
                for side, shift in ((0, 1), (3, rows - 1)):
                    value = None
                    for n in range(3):
                        term = weight(b, 5 + side + n) * masked[f, 3 * b + n]
                        value = term if value is None else value + term
                    total = total + pltpu.roll(value, shift, 1)
                at = aligned(f * blocks + b, DEPTH)
                wide[at, :rows], wide[at, rows:] = halves(deepened(total))

        @pl.when(is_child[0] == 0)
        def _():
            back = lax.rem(rows - nest_y[0], rows)
            for b in range(blocks):
                x = nest_x[0] + b
                above = masked[f, jnp.maximum(x - 1, 0)]
                below = masked[f, jnp.minimum(x + 1, cols - 1)]
                if b == 0:
                    above = jnp.where(x == 0, 0.0, above)
                if b == blocks - 1:
                    below = jnp.where(x == cols - 1, 0.0, below)
                value = spread_of(masked[f, x], above, below, kappa_buf[x])
                value = deepened(pltpu.roll(value, back, 1)[:, :LANE])
                fill_stack(stack.at[f], chunk(b), value)

        return total_edges + pltpu.roll(own_edges, 2 * f * cols, 1)

    edges[...] = lax.fori_loop(0, fields, field, jnp.zeros((PAD, LANE), F32))

    @pl.when(is_child[0] == 1)
    def _():
        value = grouped(wide[...], group[...])
        for f in range(fields):
            for b in range(blocks):
                at = (f * blocks + b) * DEPTH
                fill_stack(stack.at[f], chunk(b), value[at : at + DEPTH])

    for f in range(fields):
        mixed = mix(matrices[f], stack[f])
        for b in range(1, blocks - 1):
            at = pl.ds(f * levels * (blocks - 2) + b - 1, levels, stride=blocks - 2)
            inner[at, :] = mixed[:levels, chunk(b)]
        base[f, :, :LANE] = mixed[:PAD, :LANE]
        base[f, :, LANE:] = mixed[:PAD, chunk(blocks - 1)]


def front(is_child, state2, mask, kappa, nudging, mixing, nests, dims):
    fields, levels, cols, chunks = dims
    rows = chunks * LANE
    blocks = cols // 3
    arrays = (state2, mask, kappa, nudging, mixing)
    tile = (fields, cols, PAD, rows)
    return pl.pallas_call(
        functools.partial(front_kernel, levels),
        in_specs=[SMEM] + [VMEM] * 5 + [SMEM] * 2,
        out_specs=[VMEM] * 4,
        out_shape=[
            pltpu.VMEM((fields, 2 * DEPTH, 2 * DEPTH), jnp.bfloat16),
            pltpu.VMEM((PAD, LANE), F32),
            pltpu.VMEM((fields * levels * (blocks - 2), LANE), F32),
            pltpu.VMEM((fields, PAD, 2 * LANE), F32),
        ],
        scratch_shapes=[
            pltpu.VMEM(tile, F32),
            pltpu.VMEM((DEPTH, LANE), F32),
            pltpu.VMEM((-(-blocks * 11 // 8) * 8, rows), F32),
            pltpu.VMEM((fields * blocks * DEPTH, 2 * rows), jnp.bfloat16),
            pltpu.VMEM((fields, 2 * DEPTH, blocks * LANE), jnp.bfloat16),
            pltpu.VMEM((2 * rows, LANE), jnp.bfloat16),
        ],
        compiler_params=pltpu.CompilerParams(vmem_limit_bytes=28 * MIB),
        cost_estimate=COST,
        name="front",
    )(is_child, *arrays, *nests)


def y_halos(ty, peers, first, second):
    one, two = first[:PAD, :], second[:PAD, :]
    even = (lax.rem(ty[0], 2) == 0).astype(F32)
    odd = 1.0 - even
    before = (two * even + one * odd) * (ty[0] > 0).astype(F32)
    after = (one * even + two * odd) * (ty[0] < peers - 1).astype(F32)
    low = lax.rem(lane_ids((PAD, LANE)), 2) == 0
    return jnp.where(low, pltpu.roll(before, 1, 1), pltpu.roll(after, LANE - 1, 1))


def outer_kernel(
    levels, peers, is_child, ty, matrices, base, kappa, nudging, x_low, x_high, first, second,
    nest_x, nest_y, out, sides, wide, stack, group,
):
    fields = matrices.shape[0]
    cols, _, rows = kappa.shape
    blocks = cols // 3
    lanes = lane_ids((PAD, LANE))
    turned = lax.rem(lanes + 1, LANE)
    ends = ((0, x_low), (cols - 1, x_high))
    sides[...] = jnp.zeros_like(sides)
    halo = y_halos(ty, peers, first, second)

    def weighted(row_of_x):
        one = packed(lambda x: (row_of_x(x)[:, :LANE], row_of_x(x)[:, rows - LANE :]), cols)
        total = one
        for f in range(1, fields):
            total = total + pltpu.roll(one, 2 * f * cols, 1)
        return halo * total

    def fill_fix(value):
        for f in range(fields):
            fill_stack(stack.at[f], chunk(2), deepened(value))

    @pl.when(is_child[0] == 1)
    def _():
        fill_group(group)
        for n, (x, side) in enumerate(ends):
            weight = nudging[x : x + 1, :] * kappa[x]
            for f in range(fields):
                at = (f * 2 + n) * DEPTH
                sides[at : at + levels, :] = side[f, :, 0, :] * weight
        wide[:, :rows], wide[:, rows:] = halves(sides[...])
        value = grouped(wide[...], group[...])
        for f in range(fields):
            for n in range(2):
                at = (f * 2 + n) * DEPTH
                fill_stack(stack.at[f], chunk(n), value[at : at + DEPTH])
        part = weighted(lambda x: nudging[x : x + 1, :] * kappa[x])
        fill_fix(part + pltpu.roll(part, LANE - 2, 1) + pltpu.roll(part, LANE - 4, 1))

    @pl.when(is_child[0] == 0)
    def _():
        back = lax.rem(rows - nest_y[0], rows)
        reached = (nest_x[0] == 0, nest_x[0] + blocks == cols)
        for n, (x, side) in enumerate(ends):
            weight = kappa[x] * reached[n].astype(F32)
            for f in range(fields):
                at = (f * 2 + n) * DEPTH
                sides[at : at + levels, :] = side[f, :, 0, :] * weight
                value = pltpu.roll(sides[at : at + DEPTH, :], back, 1)[:, :LANE]
                fill_stack(stack.at[f], chunk(n), value)
        starts = (nest_y[0] == 0).astype(F32)
        finals = (nest_y[0] == rows - LANE).astype(F32)
        part = weighted(lambda x: kappa[x])
        part = part * jnp.where(lax.rem(lanes, 2) == 0, starts, finals)
        value = jnp.zeros((PAD, LANE), F32)
        for b in range(blocks):
            shift = lax.rem(LANE + 4 * b - 2 * nest_x[0], LANE)
            here = lax.rem(turned, 2 * cols) // 2 == 3 * b
            value = jnp.where(here, pltpu.roll(part, shift, 1), value)
        fill_fix(value)

    fixes = jnp.zeros((PAD, LANE), F32)
    for f in range(fields):
        mixed = mix(matrices[f], stack[f])
        for n in range(2):
            at = pl.ds(f * (2 * levels) + n, levels, stride=2)
            out[at, :] = base[f, :levels, chunk(n)] + mixed[:levels, chunk(n)]
        fixes = jnp.where(turned // (2 * cols) == f, mixed[:PAD, chunk(2)], fixes)
    out[out.shape[0] - PAD :, :] = fixes


def outer(is_child, ty, matrices, base, kappa, nudging, x_halos, firsts, nests, dims, peers):
    fields, levels, cols, chunks = dims
    rows = chunks * LANE
    height = -(-fields * 2 * levels // 8) * 8 + PAD
    return pl.pallas_call(
        functools.partial(outer_kernel, levels, peers),
        in_specs=[SMEM] * 2 + [VMEM] * 8 + [SMEM] * 2,
        out_specs=VMEM,
        out_shape=pltpu.VMEM((height, LANE), F32),
        scratch_shapes=[
            pltpu.VMEM((fields * 2 * DEPTH, rows), F32),
            pltpu.VMEM((fields * 2 * DEPTH, 2 * rows), jnp.bfloat16),
            pltpu.VMEM((fields, 2 * DEPTH, 3 * LANE), jnp.bfloat16),
            pltpu.VMEM((2 * rows, LANE), jnp.bfloat16),
        ],
        compiler_params=pltpu.CompilerParams(vmem_limit_bytes=12 * MIB),
        cost_estimate=COST,
        name="outer",
    )(is_child, ty, matrices, base, kappa, nudging, *x_halos, *firsts, *nests)


def tile_kernel(
    levels, peers, ty, places, counts, values, own, state, mask, matrices, kappa, x_low, x_high,
    first, second,
    out, masked, sides, halo, stack,
):
    cols, _, rows = masked.shape
    chunks = rows // LANE
    size = levels * cols * chunks
    fields = state.shape[0] // size

    sides[...] = jnp.zeros_like(sides)
    halo[...] = y_halos(ty, peers, first, second)
    pair = 2

    def field(f, carry):
        fill_masked(levels, state, f, mask, masked)
        sides[0, :levels, :] = x_low[f, :, 0, :]
        sides[1, :levels, :] = x_high[f, :, 0, :]
        for x0 in range(0, cols, pair):
            for x in range(x0, x0 + pair):
                above = masked[x - 1] if x > 0 else sides[0]
                below = masked[x + 1] if x < cols - 1 else sides[1]
                shift = lax.rem(LANE - 2 * (f * cols + x), LANE)
                edge = pltpu.roll(halo[...], lax.rem(LANE + shift, LANE), 1)
                value = spread_of(masked[x], above, below, kappa[x], edge)
                part = slice((x - x0) * rows, (x - x0 + 1) * rows)
                fill_stack(stack, part, deepened(value))
            mixed = mix(matrices[f], stack[...])
            for n in range(pair * chunks):
                out[aligned((f * cols + x0) * chunks + n, PAD), :] = mixed[:PAD, chunk(n)]
        return carry

    lax.fori_loop(0, fields, field, 0)
    lanes = lane_ids((1, LANE))
    sources, slots = places.shape

    def source(s, carry):
        at_values = s ^ own[0]
        count = counts[0, s]
        for k in range(0, slots, 2):
            ats, adds = [], []
            for n in range(k, k + 2):
                place = places[s, n]
                value = jnp.where(n < count, values[n, at_values], 0.0)
                ats.append(place >> 7)
                adds.append(jnp.where(lanes == (place & (LANE - 1)), value, 0.0))
            olds = [out[pl.ds(at, 1), :] for at in ats]
            also = jnp.where(ats[0] == ats[1], adds[0], 0.0)
            out[pl.ds(ats[0], 1), :] = olds[0] + adds[0]
            out[pl.ds(ats[1], 1), :] = olds[1] + adds[1] + also
        return carry

    lax.fori_loop(0, sources, source, 0)


def tile_of(ty, seen, state2, mask, matrices, kappa, x_halos, firsts, dims, peers):
    fields, levels, cols, chunks = dims
    rows = chunks * LANE
    return pl.pallas_call(
        functools.partial(tile_kernel, levels, peers),
        in_specs=[SMEM] * 5 + [VMEM] * 8,
        out_specs=VMEM,
        out_shape=pltpu.VMEM((fields * cols * chunks * PAD, LANE), F32),
        scratch_shapes=[
            pltpu.VMEM((cols, PAD, rows), F32),
            pltpu.VMEM((2, PAD, rows), F32),
            pltpu.VMEM((PAD, LANE), F32),
            pltpu.VMEM((2 * DEPTH, 2 * rows), jnp.bfloat16),
        ],
        compiler_params=pltpu.CompilerParams(vmem_limit_bytes=16 * MIB),
        cost_estimate=COST,
        name="tile",
    )(ty, *seen, state2, mask, matrices, kappa, *x_halos, *firsts)


def finish_kernel(
    levels, is_child, tile, mask, in_arrived, out_arrived, in_sent, out_sent, nest_x, nest_y,
    out, buf, group, sems,
):
    cols = mask.shape[0]
    rows = mask.shape[2]
    chunks = rows // LANE
    step = cols * chunks
    size = levels * step
    fields = out.shape[0] // size
    blocks = cols // 3
    inner = blocks - 2
    lanes = lane_ids((levels, LANE))
    ends = jnp.logical_or(lanes == 0, lanes == LANE - 1)
    height = out_arrived.shape[0]

    half = size // 16 * 8

    def copies(f):
        for n, (start, length) in enumerate(((0, half), (half, size - half))):
            at = pl.ds(f * size + start, length)
            yield pltpu.make_async_copy(buf.at[at], out.at[at], sems.at[f, n])

    def start(f):
        for n, copy in enumerate(copies(f)):
            copy.start(priority=n)

    def piece_of(f, piece):
        return tile[pl.ds(pl.multiple_of((f * step + piece) * PAD, 8), levels), :]

    def payload(f, b, inner_ref, outer_ref):
        if b in (0, blocks - 1):
            value = outer_ref[pl.ds(f * (2 * levels) + min(b, 1), levels, stride=2), :]
        else:
            value = inner_ref[pl.ds(f * (levels * inner) + b - 1, levels, stride=inner), :]
        fixes = outer_ref[height - PAD : height - PAD + levels, :]
        shift = lax.rem(LANE - 2 * (f * cols + 3 * b), LANE)
        fixes = pltpu.roll(fixes, lax.rem(LANE + shift, LANE), 1)
        return value + jnp.where(ends, fixes, 0.0)

    def fill_child(f, carry):
        for b in range(blocks):
            high, low = halves(payload(f, b, in_arrived, out_arrived))
            both = jnp.concatenate([high, low], axis=1)
            value = jnp.dot(both, group[...], preferred_element_type=F32) * (1.0 / 9.0)
            for x in range(3 * b, 3 * b + 3):
                row = row_of(mask, x)
                for c in range(chunks):
                    piece = x * chunks + c
                    at = pl.ds(f * size + piece, levels, stride=step)
                    total = piece_of(f, piece) + value[:, chunk(c)]
                    buf[at, :] = total * row[:, chunk(c)]
        start(f)
        return carry

    def fill_plain(f, carry):
        for x in range(cols):
            row = row_of(mask, x)
            for c in range(chunks):
                piece = x * chunks + c
                at = pl.ds(f * size + piece, levels, stride=step)
                buf[at, :] = piece_of(f, piece) * row[:, chunk(c)]
        return carry

    def fill_parent(f, carry):
        fill_plain(f, carry)
        for b in range(blocks):
            delta = payload(f, b, in_arrived, out_arrived) - payload(f, b, in_sent, out_sent)
            wide = jnp.concatenate([delta, jnp.zeros((levels, rows - LANE), F32)], 1)
            x = nest_x[0] + b
            value = pltpu.roll(wide, nest_y[0], 1) * row_of(mask, x)
            for c in range(chunks):
                at = pl.ds(f * size + x * chunks + c, levels, stride=step)
                buf[at, :] = buf[at, :] + value[:, chunk(c)]
        start(f)
        return carry

    @pl.when(is_child[0] == 1)
    def _():
        ids = lax.broadcasted_iota(jnp.int32, group.shape, 0)
        ids = jnp.where(ids < LANE, ids, ids - LANE)
        group[...] = jnp.where(lane_ids(group.shape) // 3 == ids, 1.0, 0.0).astype(jnp.bfloat16)
        lax.fori_loop(0, fields, fill_child, 0)

    @pl.when(is_child[0] == 0)
    def _():
        lax.fori_loop(0, fields, fill_parent, 0)

    for f in range(fields):
        for copy in copies(f):
            copy.wait()


def finish(is_child, tile, mask, arrived, sent, nests, dims):
    fields, levels, cols, chunks = dims
    rows = chunks * LANE
    size = (fields * levels * cols * chunks, LANE)
    return pl.pallas_call(
        functools.partial(finish_kernel, levels),
        in_specs=[SMEM] + [VMEM] * 6 + [SMEM] * 2,
        out_specs=HBM,
        out_shape=pltpu.HBM(size, F32),
        scratch_shapes=[
            pltpu.VMEM(size, F32),
            pltpu.VMEM((2 * LANE, rows), jnp.bfloat16),
            pltpu.SemaphoreType.DMA((fields, 2)),
        ],
        compiler_params=pltpu.CompilerParams(vmem_limit_bytes=16 * MIB),
        cost_estimate=COST,
        name="finish",
    )(is_child, in_vmem(tile), mask, *arrived, *sent, *nests)


def from_neighbours(low, high, axis):
    ends = lax.axis_size(axis) - 1
    before = lax.ppermute(high, axis, [(i, i + 1) for i in range(ends)])
    after = lax.ppermute(low, axis, [(i + 1, i) for i in range(ends)])
    return before, after


def swapped(value, axis, mask):
    return lax.ppermute(value, axis, [(i, i ^ mask) for i in range(lax.axis_size(axis))])


def stacked(blocks):
    width = blocks.shape[1]
    blocks = jnp.pad(blocks, ((0, 0), (0, -width % LANE)))
    return jnp.concatenate([blocks[:, chunk(n)] for n in range(blocks.shape[1] // LANE)])


def unstacked(rows, slots, width):
    parts = [rows[n : n + slots] for n in range(0, rows.shape[0], slots)]
    return jnp.concatenate(parts, axis=1)[:, :width]


def places_of(cells, dims):
    _, levels, cols, chunks = dims
    rows = chunks * LANE
    column, inside = cells // (cols * rows), cells % (cols * rows)
    at = (column // levels) * (cols * chunks) + inside // LANE
    return ((at * PAD + column % levels) << 7) | (inside % LANE)


def local(
    adjoint_state,
    land_mask,
    diffusivity,
    mixing,
    nudging,
    nest_x,
    nest_y,
    obs_forcing,
    obs_cell,
    obs_count,
):
    _, fields, levels, cols, rows = adjoint_state.shape
    chunks = rows // LANE
    dims = (fields, levels, cols, chunks)
    state5 = adjoint_state.reshape(fields, levels, cols, 1, rows)
    state2 = adjoint_state.reshape(fields * levels * cols * chunks, LANE)
    mask = land_mask.reshape(cols, 1, rows)
    kappa = diffusivity.reshape(cols, 1, rows)
    mixing = mixing.reshape(fields, levels, 1, levels)
    peers, across = lax.axis_size("ty"), lax.axis_size("tx")
    assert peers == 4 and across & (across - 1) == 0 and 2 * fields * cols <= LANE
    assert levels <= PAD and cols % 3 == 0 and rows == 3 * LANE
    row = lax.axis_index("ty").astype(jnp.int32)
    column = lax.axis_index("tx").astype(jnp.int32)
    ty = row.reshape(1)
    is_child = (lax.axis_index("grp") == 0).astype(jnp.int32).reshape(1)
    nests = (nest_x, nest_y)

    forcing = obs_forcing[0, 0]
    slots, dests = forcing.shape
    others = [swapped(forcing, "tx", n) for n in range(1, min(across, 4))]
    line = jnp.concatenate([forcing, *others], axis=1)
    for n in range(2, across.bit_length() - 1):
        line = jnp.concatenate([line, swapped(line, "tx", 1 << n)], axis=1)
    x_low, x_high = x_edges(state5, mask)
    x_halos = from_neighbours(x_low, x_high, "tx")
    matrices, edges, in_sent, base = front(
        is_child, state2, mask, kappa, nudging, mixing, nests, dims
    )
    parcel = jnp.concatenate([edges, stacked(line)])
    first = swapped(parcel, "ty", 1)
    second = swapped(parcel, "ty", 3)
    third = swapped(parcel[PAD:], "ty", 2)
    in_arrived = swapped(in_sent, "grp", 1)
    firsts = (first, second)
    out_sent = outer(
        is_child, ty, matrices, base, kappa, nudging, x_halos, firsts, nests, dims, peers
    )
    out_arrived = swapped(out_sent, "grp", 1)
    width = line.shape[1]
    others = [unstacked(rows, slots, width) for rows in (first[PAD:], third, second[PAD:])]
    values = jnp.concatenate([line, *others], axis=1).reshape(slots, -1, dests)
    me = row * across + column
    values = lax.dynamic_slice_in_dim(values, me, 1, axis=2)[..., 0]
    places = places_of(obs_cell[0, :, :, 0], dims)
    seen = (places, obs_count.reshape(1, -1), values, me.reshape(1))
    tile = tile_of(ty, seen, state2, mask, matrices, kappa, x_halos, firsts, dims, peers)
    out = finish(is_child, tile, mask, (in_arrived, out_arrived), (in_sent, out_sent), nests, dims)
    return out.reshape(adjoint_state.shape)


def solution(mesh):
    in_specs = (
        P("grp", None, None, "tx", "ty"),
        P("grp", "tx", "ty"),
        P("grp", "tx", "ty"),
        P("grp", None, None, None),
        P("tx", "ty"),
        P(("ty", "tx")),
        P(("ty", "tx")),
        P("grp", ("ty", "tx"), None, None),
        P("grp", None, None, ("ty", "tx")),
        P("grp", None, ("ty", "tx")),
    )
    out_specs = P("grp", None, None, "tx", "ty")
    return jax.shard_map(local, mesh=mesh, in_specs=in_specs, out_specs=out_specs, check_vma=False)
```

```python
import functools

import jax
import jax.numpy as jnp
from jax import lax
from jax.experimental import pallas as pl
from jax.experimental.pallas import tpu as pltpu
from jax.sharding import PartitionSpec as P

LANE = 128
PAD = 56
DEPTH = 64
MIB = 1 << 20
HBM = pl.BlockSpec(memory_space=pltpu.HBM)
SMEM = pl.BlockSpec(memory_space=pltpu.SMEM)
VMEM = pl.BlockSpec(memory_space=pltpu.VMEM)
F32 = jnp.float32
COST = pl.CostEstimate(flops=10**10, bytes_accessed=10**8, transcendentals=0)


def lane_ids(shape):
    return lax.broadcasted_iota(jnp.int32, shape, len(shape) - 1)


def row_of(ref, x):
    return ref[x].astype(F32)


def chunk(c):
    return slice(c * LANE, (c + 1) * LANE)


def in_hbm(value):
    return pltpu.with_memory_space_constraint(value, pltpu.HBM)


def in_vmem(value):
    return pltpu.with_memory_space_constraint(value, pltpu.VMEM)


def x_edges_kernel(state, mask, low, high, buf, mask_buf, sems):
    fields, _, cols = state.shape[:3]
    copies = [pltpu.make_async_copy(mask, mask_buf, sems.at[2 * fields])]
    for n, x in enumerate((0, cols - 1)):
        for f in range(fields):
            copies.append(
                pltpu.make_async_copy(state.at[f, :, x], buf.at[n, f], sems.at[n * fields + f])
            )
    for copy in copies:
        copy.start()
    copies[0].wait()
    for n, (x, out) in enumerate(((0, low), (cols - 1, high))):
        for f in range(fields):
            copies[1 + n * fields + f].wait()
            out[f] = buf[n, f] * row_of(mask_buf, x)[None]


def x_edges(state5, mask):
    fields, levels, cols, _, rows = state5.shape
    edge = (fields, levels, 1, rows)
    return pl.pallas_call(
        x_edges_kernel,
        in_specs=[HBM, HBM],
        out_specs=[VMEM] * 2,
        out_shape=[pltpu.VMEM(edge, F32)] * 2,
        scratch_shapes=[
            pltpu.VMEM((2,) + edge, F32),
            pltpu.VMEM(mask.shape, jnp.int32),
            pltpu.SemaphoreType.DMA((2 * fields + 1,)),
        ],
        compiler_params=pltpu.CompilerParams(vmem_limit_bytes=8 * MIB),
        cost_estimate=COST,
        name="x_edges",
    )(in_hbm(state5), in_hbm(mask))


def spread_of(here, above, below, kappa, edge=None):
    rows = here.shape[1]
    lanes = lane_ids((here.shape[0], LANE))
    edge = 0.0 if edge is None else edge
    before = pltpu.roll(here, 1, 1)
    after = pltpu.roll(here, rows - 1, 1)
    before = jnp.concatenate([jnp.where(lanes == 0, edge, before[:, :LANE]), before[:, LANE:]], 1)
    after = jnp.concatenate(
        [after[:, :-LANE], jnp.where(lanes == LANE - 1, edge, after[:, -LANE:])], 1
    )
    return here + kappa * (above + below + before + after - 4.0 * here)


def halves(value):
    high = value.astype(jnp.bfloat16)
    return high, (value - high.astype(F32)).astype(jnp.bfloat16)


def deepened(value):
    return jnp.concatenate([value, jnp.zeros((DEPTH - value.shape[0], value.shape[1]), F32)], 0)


def fill_matrix(levels, mixing, square, matrix):
    square[:levels, :levels] = mixing
    value = square[...]
    high = value.astype(jnp.bfloat16).astype(F32)
    matrix[:DEPTH, :] = (high + pltpu.roll(high, DEPTH, 1)).astype(jnp.bfloat16)
    matrix[DEPTH:, :] = (value - high).astype(jnp.bfloat16)


def fill_stack(stack, part, value):
    high, low = halves(value)
    stack[:DEPTH, part] = high
    stack[DEPTH:, part] = low


def mix(matrix, stack):
    both = jnp.dot(matrix, stack, preferred_element_type=F32)
    return both[:DEPTH] + both[DEPTH:]


def fill_group(group):
    rows = group.shape[0] // 2
    ids = lax.broadcasted_iota(jnp.int32, group.shape, 0)
    ids = jnp.where(ids < rows, ids, ids - rows) // 3
    group[...] = jnp.where(ids == lane_ids(group.shape), 1.0, 0.0).astype(jnp.bfloat16)


def grouped(wide, group):
    return jnp.dot(wide, group, preferred_element_type=F32)


def aligned(index, size):
    return pl.ds(pl.multiple_of(index * size, size), size)


def packed(rows_of, cols):
    parts = []
    for x in range(cols):
        first, last = rows_of(x)
        lanes = lane_ids(first.shape)
        parts.append(jnp.where(lanes == 0, first, jnp.where(lanes == LANE - 1, last, 0.0)))
    shift = 2
    while len(parts) > 1:
        pairs = [parts[n : n + 2] for n in range(0, len(parts), 2)]
        parts = [p[0] + pltpu.roll(p[1], shift, 1) if len(p) == 2 else p[0] for p in pairs]
        shift *= 2
    return parts[0]


def fill_masked(levels, state, f, mask, masked):
    cols, _, rows = masked.shape
    chunks = rows // LANE
    step = cols * chunks
    for x in range(cols):
        row = row_of(mask, x)
        masked[x, PAD - 8 :, :] = jnp.zeros((8, rows), F32)
        for c in range(chunks):
            at = pl.ds(f * (levels * step) + x * chunks + c, levels, stride=step)
            masked[x, :levels, chunk(c)] = state[at, :] * row[:, chunk(c)]


def front_kernel(
    levels, is_child, state, mask, kappa, nudging, mixing, nest_x, nest_y,
    masked_out, matrices, edges, inner, base,
    buf, masked, mask_buf, kappa_buf, nudging_buf, mixing_buf, square, weights,
    wide, stack, group, sems, out_sems,
):
    fields, cols, _, rows = masked.shape
    chunks = rows // LANE
    step = cols * chunks
    size = levels * step
    blocks = cols // 3
    terms = 11

    def copy(f):
        at = pl.ds(f * size, size)
        return pltpu.make_async_copy(state.at[at], buf.at[at], sems.at[f])

    def copy_out(f):
        return pltpu.make_async_copy(masked.at[f], masked_out.at[f], out_sems.at[f])

    pairs = (
        (mask, mask_buf),
        (kappa, kappa_buf),
        (nudging, nudging_buf),
        (mixing, mixing_buf),
    )
    smalls = [
        pltpu.make_async_copy(source, target, sems.at[fields + n])
        for n, (source, target) in enumerate(pairs)
    ]
    copy(0).start()
    for small in smalls:
        small.start()
    for f in range(1, fields):
        copy(f).start()
    square[...] = jnp.zeros_like(square)
    for small in smalls:
        small.wait()

    @pl.when(is_child[0] == 1)
    def _():
        fill_group(group)
        ids = lane_ids((1, rows))
        for b in range(blocks):
            own = range(3 * b, 3 * b + 3)
            both = {x: nudging_buf[x : x + 1, :] * kappa_buf[x] for x in own}
            for n, x in enumerate(range(3 * b - 1, 3 * b + 4)):
                total = None
                for near in (x - 1, x + 1):
                    if near in both:
                        total = both[near] if total is None else total + both[near]
                if x in both:
                    total = total + (nudging_buf[x : x + 1, :] - 4.0 * both[x])
                weights[b * terms + n : b * terms + n + 1, :] = total
            for n, x in enumerate(own):
                at = b * terms + 5 + n
                value = jnp.where(ids == rows - 1, 0.0, pltpu.roll(both[x], rows - 1, 1))
                weights[at : at + 1, :] = value
                value = jnp.where(ids == 0, 0.0, pltpu.roll(both[x], 1, 1))
                weights[at + 3 : at + 4, :] = value

    def weight(b, n):
        return weights[b * terms + n : b * terms + n + 1, :]

    def field(f, total_edges):
        copy(f).wait()
        fill_matrix(levels, mixing_buf[f, :, 0, :], square, matrices.at[f])
        fill_masked(levels, buf, f, mask_buf, masked.at[f])
        copy_out(f).start()
        own_edges = packed(
            lambda x: (masked[f, x, :, :LANE], masked[f, x, :, rows - LANE :]), cols
        )

        @pl.when(is_child[0] == 1)
        def _():
            for b in range(blocks):
                total = None
                for n, x in enumerate(range(3 * b - 1, 3 * b + 4)):
                    if 0 <= x < cols:
                        term = weight(b, n) * masked[f, x]
                        total = term if total is None else total + term
                for side, shift in ((0, 1), (3, rows - 1)):
                    value = None
                    for n in range(3):
                        term = weight(b, 5 + side + n) * masked[f, 3 * b + n]
                        value = term if value is None else value + term
                    total = total + pltpu.roll(value, shift, 1)
                at = aligned(f * blocks + b, DEPTH)
                wide[at, :rows], wide[at, rows:] = halves(deepened(total))

        @pl.when(is_child[0] == 0)
        def _():
            back = lax.rem(rows - nest_y[0], rows)
            for b in range(blocks):
                x = nest_x[0] + b
                above = masked[f, jnp.maximum(x - 1, 0)]
                below = masked[f, jnp.minimum(x + 1, cols - 1)]
                if b == 0:
                    above = jnp.where(x == 0, 0.0, above)
                if b == blocks - 1:
                    below = jnp.where(x == cols - 1, 0.0, below)
                value = spread_of(masked[f, x], above, below, kappa_buf[x])
                value = deepened(pltpu.roll(value, back, 1)[:, :LANE])
                fill_stack(stack.at[f], chunk(b), value)

        return total_edges + pltpu.roll(own_edges, 2 * f * cols, 1)

    edges[...] = lax.fori_loop(0, fields, field, jnp.zeros((PAD, LANE), F32))

    @pl.when(is_child[0] == 1)
    def _():
        value = grouped(wide[...], group[...])
        for f in range(fields):
            for b in range(blocks):
                at = (f * blocks + b) * DEPTH
                fill_stack(stack.at[f], chunk(b), value[at : at + DEPTH])

    for f in range(fields):
        mixed = mix(matrices[f], stack[f])
        for b in range(1, blocks - 1):
            at = pl.ds(f * levels * (blocks - 2) + b - 1, levels, stride=blocks - 2)
            inner[at, :] = mixed[:levels, chunk(b)]
        base[f, :, :LANE] = mixed[:PAD, :LANE]
        base[f, :, LANE:] = mixed[:PAD, chunk(blocks - 1)]
    for f in range(fields):
        copy_out(f).wait()


def front(is_child, state2, mask, kappa, nudging, mixing, nests, dims):
    fields, levels, cols, chunks = dims
    rows = chunks * LANE
    blocks = cols // 3
    arrays = (state2, mask, kappa, nudging, mixing)
    tile = (fields, cols, PAD, rows)
    return pl.pallas_call(
        functools.partial(front_kernel, levels),
        in_specs=[SMEM] + [HBM] * 5 + [SMEM] * 2,
        out_specs=[HBM] + [VMEM] * 4,
        out_shape=[
            pltpu.HBM(tile, F32),
            pltpu.VMEM((fields, 2 * DEPTH, 2 * DEPTH), jnp.bfloat16),
            pltpu.VMEM((PAD, LANE), F32),
            pltpu.VMEM((fields * levels * (blocks - 2), LANE), F32),
            pltpu.VMEM((fields, PAD, 2 * LANE), F32),
        ],
        scratch_shapes=[
            pltpu.VMEM(state2.shape, F32),
            pltpu.VMEM(tile, F32),
            pltpu.VMEM(mask.shape, jnp.int32),
            pltpu.VMEM(kappa.shape, F32),
            pltpu.VMEM(nudging.shape, F32),
            pltpu.VMEM(mixing.shape, F32),
            pltpu.VMEM((DEPTH, LANE), F32),
            pltpu.VMEM((-(-blocks * 11 // 8) * 8, rows), F32),
            pltpu.VMEM((fields * blocks * DEPTH, 2 * rows), jnp.bfloat16),
            pltpu.VMEM((fields, 2 * DEPTH, blocks * LANE), jnp.bfloat16),
            pltpu.VMEM((2 * rows, LANE), jnp.bfloat16),
            pltpu.SemaphoreType.DMA((fields + 4,)),
            pltpu.SemaphoreType.DMA((fields,)),
        ],
        compiler_params=pltpu.CompilerParams(vmem_limit_bytes=28 * MIB),
        cost_estimate=COST,
        name="front",
    )(is_child, *map(in_hbm, arrays), *nests)


def y_halos(ty, peers, first, second):
    one, two = first[:PAD, :], second[:PAD, :]
    even = (lax.rem(ty[0], 2) == 0).astype(F32)
    odd = 1.0 - even
    before = (two * even + one * odd) * (ty[0] > 0).astype(F32)
    after = (one * even + two * odd) * (ty[0] < peers - 1).astype(F32)
    low = lax.rem(lane_ids((PAD, LANE)), 2) == 0
    return jnp.where(low, pltpu.roll(before, 1, 1), pltpu.roll(after, LANE - 1, 1))


def outer_kernel(
    levels, peers, is_child, ty, matrices, base, kappa, nudging, x_low, x_high, first, second,
    nest_x, nest_y, out, sides, wide, stack, group,
):
    fields = matrices.shape[0]
    cols, _, rows = kappa.shape
    blocks = cols // 3
    lanes = lane_ids((PAD, LANE))
    turned = lax.rem(lanes + 1, LANE)
    ends = ((0, x_low), (cols - 1, x_high))
    sides[...] = jnp.zeros_like(sides)
    halo = y_halos(ty, peers, first, second)

    def weighted(row_of_x):
        one = packed(lambda x: (row_of_x(x)[:, :LANE], row_of_x(x)[:, rows - LANE :]), cols)
        total = one
        for f in range(1, fields):
            total = total + pltpu.roll(one, 2 * f * cols, 1)
        return halo * total

    def fill_fix(value):
        for f in range(fields):
            fill_stack(stack.at[f], chunk(2), deepened(value))

    @pl.when(is_child[0] == 1)
    def _():
        fill_group(group)
        for n, (x, side) in enumerate(ends):
            weight = nudging[x : x + 1, :] * kappa[x]
            for f in range(fields):
                at = (f * 2 + n) * DEPTH
                sides[at : at + levels, :] = side[f, :, 0, :] * weight
        wide[:, :rows], wide[:, rows:] = halves(sides[...])
        value = grouped(wide[...], group[...])
        for f in range(fields):
            for n in range(2):
                at = (f * 2 + n) * DEPTH
                fill_stack(stack.at[f], chunk(n), value[at : at + DEPTH])
        part = weighted(lambda x: nudging[x : x + 1, :] * kappa[x])
        fill_fix(part + pltpu.roll(part, LANE - 2, 1) + pltpu.roll(part, LANE - 4, 1))

    @pl.when(is_child[0] == 0)
    def _():
        back = lax.rem(rows - nest_y[0], rows)
        reached = (nest_x[0] == 0, nest_x[0] + blocks == cols)
        for n, (x, side) in enumerate(ends):
            weight = kappa[x] * reached[n].astype(F32)
            for f in range(fields):
                at = (f * 2 + n) * DEPTH
                sides[at : at + levels, :] = side[f, :, 0, :] * weight
                value = pltpu.roll(sides[at : at + DEPTH, :], back, 1)[:, :LANE]
                fill_stack(stack.at[f], chunk(n), value)
        starts = (nest_y[0] == 0).astype(F32)
        finals = (nest_y[0] == rows - LANE).astype(F32)
        part = weighted(lambda x: kappa[x])
        part = part * jnp.where(lax.rem(lanes, 2) == 0, starts, finals)
        value = jnp.zeros((PAD, LANE), F32)
        for b in range(blocks):
            shift = lax.rem(LANE + 4 * b - 2 * nest_x[0], LANE)
            here = lax.rem(turned, 2 * cols) // 2 == 3 * b
            value = jnp.where(here, pltpu.roll(part, shift, 1), value)
        fill_fix(value)

    fixes = jnp.zeros((PAD, LANE), F32)
    for f in range(fields):
        mixed = mix(matrices[f], stack[f])
        for n in range(2):
            at = pl.ds(f * (2 * levels) + n, levels, stride=2)
            out[at, :] = base[f, :levels, chunk(n)] + mixed[:levels, chunk(n)]
        fixes = jnp.where(turned // (2 * cols) == f, mixed[:PAD, chunk(2)], fixes)
    out[out.shape[0] - PAD :, :] = fixes


def outer(is_child, ty, matrices, base, kappa, nudging, x_halos, firsts, nests, dims, peers):
    fields, levels, cols, chunks = dims
    rows = chunks * LANE
    height = -(-fields * 2 * levels // 8) * 8 + PAD
    return pl.pallas_call(
        functools.partial(outer_kernel, levels, peers),
        in_specs=[SMEM] * 2 + [VMEM] * 8 + [SMEM] * 2,
        out_specs=VMEM,
        out_shape=pltpu.VMEM((height, LANE), F32),
        scratch_shapes=[
            pltpu.VMEM((fields * 2 * DEPTH, rows), F32),
            pltpu.VMEM((fields * 2 * DEPTH, 2 * rows), jnp.bfloat16),
            pltpu.VMEM((fields, 2 * DEPTH, 3 * LANE), jnp.bfloat16),
            pltpu.VMEM((2 * rows, LANE), jnp.bfloat16),
        ],
        compiler_params=pltpu.CompilerParams(vmem_limit_bytes=12 * MIB),
        cost_estimate=COST,
        name="outer",
    )(is_child, ty, matrices, base, kappa, nudging, *x_halos, *firsts, *nests)


def tile_kernel(
    levels, peers, ty, masked_in, matrices, kappa, x_low, x_high, first, second,
    out, masked, sides, halo, stack, sems,
):
    fields, cols, _, rows = masked.shape
    chunks = rows // LANE

    def copy(f):
        return pltpu.make_async_copy(masked_in.at[f], masked.at[f], sems.at[f])

    for f in range(fields):
        copy(f).start()
    sides[...] = jnp.zeros_like(sides)
    halo[...] = y_halos(ty, peers, first, second)
    pair = 2

    def field(f, carry):
        copy(f).wait()
        sides[0, :levels, :] = x_low[f, :, 0, :]
        sides[1, :levels, :] = x_high[f, :, 0, :]
        for x0 in range(0, cols, pair):
            for x in range(x0, x0 + pair):
                above = masked[f, x - 1] if x > 0 else sides[0]
                below = masked[f, x + 1] if x < cols - 1 else sides[1]
                shift = lax.rem(LANE - 2 * (f * cols + x), LANE)
                edge = pltpu.roll(halo[...], lax.rem(LANE + shift, LANE), 1)
                value = spread_of(masked[f, x], above, below, kappa[x], edge)
                part = slice((x - x0) * rows, (x - x0 + 1) * rows)
                fill_stack(stack, part, deepened(value))
            mixed = mix(matrices[f], stack[...])
            for n in range(pair * chunks):
                out[aligned((f * cols + x0) * chunks + n, PAD), :] = mixed[:PAD, chunk(n)]
        return carry

    lax.fori_loop(0, fields, field, 0)


def tile_of(ty, masked, matrices, kappa, x_halos, firsts, dims, peers):
    fields, levels, cols, chunks = dims
    rows = chunks * LANE
    return pl.pallas_call(
        functools.partial(tile_kernel, levels, peers),
        in_specs=[SMEM] + [HBM] + [VMEM] * 6,
        out_specs=VMEM,
        out_shape=pltpu.VMEM((fields * cols * chunks * PAD, LANE), F32),
        scratch_shapes=[
            pltpu.VMEM(masked.shape, F32),
            pltpu.VMEM((2, PAD, rows), F32),
            pltpu.VMEM((PAD, LANE), F32),
            pltpu.VMEM((2 * DEPTH, 2 * rows), jnp.bfloat16),
            pltpu.SemaphoreType.DMA((fields,)),
        ],
        compiler_params=pltpu.CompilerParams(vmem_limit_bytes=16 * MIB),
        cost_estimate=COST,
        name="tile",
    )(ty, in_hbm(masked), matrices, kappa, *x_halos, *firsts)


def add_observations(own, places, counts, values, tile):
    lanes = lane_ids((1, LANE))
    sources, slots = places.shape

    def source(s, carry):
        at_values = s ^ own[0]
        count = counts[0, s]
        for k in range(0, slots, 2):
            ats, adds = [], []
            for n in range(k, k + 2):
                place = places[s, n]
                value = jnp.where(n < count, values[n, at_values], 0.0)
                ats.append(place >> 7)
                adds.append(jnp.where(lanes == (place & (LANE - 1)), value, 0.0))
            olds = [tile[pl.ds(at, 1), :] for at in ats]
            also = jnp.where(ats[0] == ats[1], adds[0], 0.0)
            tile[pl.ds(ats[0], 1), :] = olds[0] + adds[0]
            tile[pl.ds(ats[1], 1), :] = olds[1] + adds[1] + also
        return carry

    lax.fori_loop(0, sources, source, 0)


def finish_kernel(
    levels, is_child, own, places, counts, values, nest_x, nest_y,
    _, mask, in_arrived, out_arrived, in_sent, out_sent,
    out, tile, buf, group, sems,
):
    cols = mask.shape[0]
    rows = mask.shape[2]
    chunks = rows // LANE
    step = cols * chunks
    size = levels * step
    fields = out.shape[0] // size
    blocks = cols // 3
    inner = blocks - 2
    lanes = lane_ids((levels, LANE))
    ends = jnp.logical_or(lanes == 0, lanes == LANE - 1)
    height = out_arrived.shape[0]
    add_observations(own, places, counts, values, tile)

    def copy(f):
        at = pl.ds(f * size, size)
        return pltpu.make_async_copy(buf.at[at], out.at[at], sems.at[f])

    def piece_of(f, piece):
        return tile[pl.ds(pl.multiple_of((f * step + piece) * PAD, 8), levels), :]

    def payload(f, b, inner_ref, outer_ref):
        if b in (0, blocks - 1):
            value = outer_ref[pl.ds(f * (2 * levels) + min(b, 1), levels, stride=2), :]
        else:
            value = inner_ref[pl.ds(f * (levels * inner) + b - 1, levels, stride=inner), :]
        fixes = outer_ref[height - PAD : height - PAD + levels, :]
        shift = lax.rem(LANE - 2 * (f * cols + 3 * b), LANE)
        fixes = pltpu.roll(fixes, lax.rem(LANE + shift, LANE), 1)
        return value + jnp.where(ends, fixes, 0.0)

    def fill_child(f, carry):
        for b in range(blocks):
            high, low = halves(payload(f, b, in_arrived, out_arrived))
            both = jnp.concatenate([high, low], axis=1)
            value = jnp.dot(both, group[...], preferred_element_type=F32) * (1.0 / 9.0)
            for x in range(3 * b, 3 * b + 3):
                row = row_of(mask, x)
                for c in range(chunks):
                    piece = x * chunks + c
                    at = pl.ds(f * size + piece, levels, stride=step)
                    total = piece_of(f, piece) + value[:, chunk(c)]
                    buf[at, :] = total * row[:, chunk(c)]
        copy(f).start()
        return carry

    def fill_plain(f, carry):
        for x in range(cols):
            row = row_of(mask, x)
            for c in range(chunks):
                piece = x * chunks + c
                at = pl.ds(f * size + piece, levels, stride=step)
                buf[at, :] = piece_of(f, piece) * row[:, chunk(c)]
        return carry

    def fill_parent(f, carry):
        fill_plain(f, carry)
        for b in range(blocks):
            delta = payload(f, b, in_arrived, out_arrived) - payload(f, b, in_sent, out_sent)
            wide = jnp.concatenate([delta, jnp.zeros((levels, rows - LANE), F32)], 1)
            x = nest_x[0] + b
            value = pltpu.roll(wide, nest_y[0], 1) * row_of(mask, x)
            for c in range(chunks):
                at = pl.ds(f * size + x * chunks + c, levels, stride=step)
                buf[at, :] = buf[at, :] + value[:, chunk(c)]
        copy(f).start()
        return carry

    @pl.when(is_child[0] == 1)
    def _():
        ids = lax.broadcasted_iota(jnp.int32, group.shape, 0)
        ids = jnp.where(ids < LANE, ids, ids - LANE)
        group[...] = jnp.where(lane_ids(group.shape) // 3 == ids, 1.0, 0.0).astype(jnp.bfloat16)
        lax.fori_loop(0, fields, fill_child, 0)

    @pl.when(is_child[0] == 0)
    def _():
        lax.fori_loop(0, fields, fill_parent, 0)

    for f in range(fields):
        copy(f).wait()


def finish(is_child, seen, nests, tile, mask, arrived, sent, dims):
    fields, levels, cols, chunks = dims
    rows = chunks * LANE
    size = (fields * levels * cols * chunks, LANE)
    return pl.pallas_call(
        functools.partial(finish_kernel, levels),
        in_specs=[SMEM] * 7 + [VMEM] * 6,
        out_specs=[HBM, VMEM],
        out_shape=[pltpu.HBM(size, F32), pltpu.VMEM(tile.shape, F32)],
        scratch_shapes=[
            pltpu.VMEM(size, F32),
            pltpu.VMEM((2 * LANE, rows), jnp.bfloat16),
            pltpu.SemaphoreType.DMA((fields,)),
        ],
        input_output_aliases={7: 1},
        compiler_params=pltpu.CompilerParams(vmem_limit_bytes=16 * MIB),
        cost_estimate=COST,
        name="finish",
    )(is_child, *seen, *nests, in_vmem(tile), mask, *arrived, *sent)[0]


def from_neighbours(low, high, axis):
    ends = lax.axis_size(axis) - 1
    before = lax.ppermute(high, axis, [(i, i + 1) for i in range(ends)])
    after = lax.ppermute(low, axis, [(i + 1, i) for i in range(ends)])
    return before, after


def swapped(value, axis, mask):
    return lax.ppermute(value, axis, [(i, i ^ mask) for i in range(lax.axis_size(axis))])


def stacked(blocks):
    width = blocks.shape[1]
    blocks = jnp.pad(blocks, ((0, 0), (0, -width % LANE)))
    return jnp.concatenate([blocks[:, chunk(n)] for n in range(blocks.shape[1] // LANE)])


def unstacked(rows, slots, width):
    parts = [rows[n : n + slots] for n in range(0, rows.shape[0], slots)]
    return jnp.concatenate(parts, axis=1)[:, :width]


def places_of(cells, dims):
    _, levels, cols, chunks = dims
    rows = chunks * LANE
    column, inside = cells // (cols * rows), cells % (cols * rows)
    at = (column // levels) * (cols * chunks) + inside // LANE
    return ((at * PAD + column % levels) << 7) | (inside % LANE)


def local(
    adjoint_state,
    land_mask,
    diffusivity,
    mixing,
    nudging,
    nest_x,
    nest_y,
    obs_forcing,
    obs_cell,
    obs_count,
):
    _, fields, levels, cols, rows = adjoint_state.shape
    chunks = rows // LANE
    dims = (fields, levels, cols, chunks)
    state5 = adjoint_state.reshape(fields, levels, cols, 1, rows)
    state2 = adjoint_state.reshape(fields * levels * cols * chunks, LANE)
    mask = land_mask.reshape(cols, 1, rows)
    kappa = diffusivity.reshape(cols, 1, rows)
    mixing = mixing.reshape(fields, levels, 1, levels)
    peers, across = lax.axis_size("ty"), lax.axis_size("tx")
    assert peers == 4 and across & (across - 1) == 0 and 2 * fields * cols <= LANE
    assert levels <= PAD and cols % 3 == 0 and rows == 3 * LANE
    row = lax.axis_index("ty").astype(jnp.int32)
    column = lax.axis_index("tx").astype(jnp.int32)
    ty = row.reshape(1)
    is_child = (lax.axis_index("grp") == 0).astype(jnp.int32).reshape(1)
    nests = (nest_x, nest_y)

    forcing = obs_forcing[0, 0]
    slots, dests = forcing.shape
    x_low, x_high = x_edges(state5, mask)
    line = jnp.concatenate([forcing, swapped(forcing, "tx", 1)], axis=1)
    line, x_low, x_high = lax.optimization_barrier((line, x_low, x_high))
    for n in range(1, across.bit_length() - 1):
        line = jnp.concatenate([line, swapped(line, "tx", 1 << n)], axis=1)
    x_halos = from_neighbours(x_low, x_high, "tx")
    line, state2 = lax.optimization_barrier((line, state2))
    masked, matrices, edges, in_sent, base = front(
        is_child, state2, mask, kappa, nudging, mixing, nests, dims
    )
    in_arrived = swapped(in_sent, "grp", 1)
    parcel = jnp.concatenate([edges, stacked(line)])
    first = swapped(parcel, "ty", 1)
    second = swapped(parcel, "ty", 3)
    firsts = (first, second)
    out_sent = outer(
        is_child, ty, matrices, base, kappa, nudging, x_halos, firsts, nests, dims, peers
    )
    out_arrived = swapped(out_sent, "grp", 1)
    line, out_sent = lax.optimization_barrier((line, out_sent))
    third = swapped(stacked(line), "ty", 2)
    width = line.shape[1]
    others = [unstacked(rows, slots, width) for rows in (first[PAD:], third, second[PAD:])]
    values = jnp.concatenate([line, *others], axis=1).reshape(slots, -1, dests)
    me = row * across + column
    values = lax.dynamic_slice_in_dim(values, me, 1, axis=2)[..., 0]
    places = places_of(obs_cell[0, :, :, 0], dims)
    seen = (me.reshape(1), places, obs_count.reshape(1, -1), values)
    tile = tile_of(ty, masked, matrices, kappa, x_halos, firsts, dims, peers)
    arrived, sent = (in_arrived, out_arrived), (in_sent, out_sent)
    out = finish(is_child, seen, nests, tile, mask, arrived, sent, dims)
    return out.reshape(adjoint_state.shape)


def solution(mesh):
    in_specs = (
        P("grp", None, None, "tx", "ty"),
        P("grp", "tx", "ty"),
        P("grp", "tx", "ty"),
        P("grp", None, None, None),
        P("tx", "ty"),
        P(("ty", "tx")),
        P(("ty", "tx")),
        P("grp", ("ty", "tx"), None, None),
        P("grp", None, None, ("ty", "tx")),
        P("grp", None, ("ty", "tx")),
    )
    out_specs = P("grp", None, None, "tx", "ty")
    return jax.shard_map(local, mesh=mesh, in_specs=in_specs, out_specs=out_specs, check_vma=False)
```

```python
import functools

import jax
import jax.numpy as jnp
from jax import lax
from jax.experimental import pallas as pl
from jax.experimental.pallas import tpu as pltpu
from jax.sharding import PartitionSpec as P

LANE = 128
PAD = 56
DEPTH = 64
MIB = 1 << 20
HBM = pl.BlockSpec(memory_space=pltpu.HBM)
SMEM = pl.BlockSpec(memory_space=pltpu.SMEM)
VMEM = pl.BlockSpec(memory_space=pltpu.VMEM)
F32 = jnp.float32
COST = pl.CostEstimate(flops=10**10, bytes_accessed=10**8, transcendentals=0)


def lane_ids(shape):
    return lax.broadcasted_iota(jnp.int32, shape, len(shape) - 1)


def row_of(ref, x):
    return ref[x].astype(F32)


def chunk(c):
    return slice(c * LANE, (c + 1) * LANE)


def in_hbm(value):
    return pltpu.with_memory_space_constraint(value, pltpu.HBM)


def in_vmem(value):
    return pltpu.with_memory_space_constraint(value, pltpu.VMEM)


def x_edges_kernel(state, mask, low, high, buf, mask_buf, sems):
    fields, _, cols = state.shape[:3]
    copies = [pltpu.make_async_copy(mask, mask_buf, sems.at[2 * fields])]
    for n, x in enumerate((0, cols - 1)):
        for f in range(fields):
            copies.append(
                pltpu.make_async_copy(state.at[f, :, x], buf.at[n, f], sems.at[n * fields + f])
            )
    for copy in copies:
        copy.start()
    copies[0].wait()
    for n, (x, out) in enumerate(((0, low), (cols - 1, high))):
        for f in range(fields):
            copies[1 + n * fields + f].wait()
            out[f] = buf[n, f] * row_of(mask_buf, x)[None]


def x_edges(state5, mask):
    fields, levels, cols, _, rows = state5.shape
    edge = (fields, levels, 1, rows)
    return pl.pallas_call(
        x_edges_kernel,
        in_specs=[HBM, HBM],
        out_specs=[VMEM] * 2,
        out_shape=[pltpu.VMEM(edge, F32)] * 2,
        scratch_shapes=[
            pltpu.VMEM((2,) + edge, F32),
            pltpu.VMEM(mask.shape, jnp.int32),
            pltpu.SemaphoreType.DMA((2 * fields + 1,)),
        ],
        compiler_params=pltpu.CompilerParams(vmem_limit_bytes=8 * MIB),
        cost_estimate=COST,
        name="x_edges",
    )(in_hbm(state5), in_hbm(mask))


def spread_of(here, above, below, kappa, edge=None):
    rows = here.shape[1]
    lanes = lane_ids((here.shape[0], LANE))
    edge = 0.0 if edge is None else edge
    before = pltpu.roll(here, 1, 1)
    after = pltpu.roll(here, rows - 1, 1)
    before = jnp.concatenate([jnp.where(lanes == 0, edge, before[:, :LANE]), before[:, LANE:]], 1)
    after = jnp.concatenate(
        [after[:, :-LANE], jnp.where(lanes == LANE - 1, edge, after[:, -LANE:])], 1
    )
    return here + kappa * (above + below + before + after - 4.0 * here)


def halves(value):
    high = value.astype(jnp.bfloat16)
    return high, (value - high.astype(F32)).astype(jnp.bfloat16)


def deepened(value):
    return jnp.concatenate([value, jnp.zeros((DEPTH - value.shape[0], value.shape[1]), F32)], 0)


def fill_matrix(levels, mixing, square, matrix):
    square[:levels, :levels] = mixing
    value = square[...]
    high = value.astype(jnp.bfloat16).astype(F32)
    matrix[:DEPTH, :] = (high + pltpu.roll(high, DEPTH, 1)).astype(jnp.bfloat16)
    matrix[DEPTH:, :] = (value - high).astype(jnp.bfloat16)


def fill_stack(stack, part, value):
    high, low = halves(value)
    stack[:DEPTH, part] = high
    stack[DEPTH:, part] = low


def mix(matrix, stack):
    both = jnp.dot(matrix, stack, preferred_element_type=F32)
    return both[:DEPTH] + both[DEPTH:]


def fill_group(group):
    rows = group.shape[0] // 2
    ids = lax.broadcasted_iota(jnp.int32, group.shape, 0)
    ids = jnp.where(ids < rows, ids, ids - rows) // 3
    group[...] = jnp.where(ids == lane_ids(group.shape), 1.0, 0.0).astype(jnp.bfloat16)


def grouped(wide, group):
    return jnp.dot(wide, group, preferred_element_type=F32)


def aligned(index, size):
    return pl.ds(pl.multiple_of(index * size, size), size)


def packed(rows_of, cols):
    parts = []
    for x in range(cols):
        first, last = rows_of(x)
        lanes = lane_ids(first.shape)
        parts.append(jnp.where(lanes == 0, first, jnp.where(lanes == LANE - 1, last, 0.0)))
    shift = 2
    while len(parts) > 1:
        pairs = [parts[n : n + 2] for n in range(0, len(parts), 2)]
        parts = [p[0] + pltpu.roll(p[1], shift, 1) if len(p) == 2 else p[0] for p in pairs]
        shift *= 2
    return parts[0]


def fill_masked(levels, state, f, mask, masked):
    cols, _, rows = masked.shape
    chunks = rows // LANE
    step = cols * chunks
    for x in range(cols):
        row = row_of(mask, x)
        masked[x, PAD - 8 :, :] = jnp.zeros((8, rows), F32)
        for c in range(chunks):
            at = pl.ds(f * (levels * step) + x * chunks + c, levels, stride=step)
            masked[x, :levels, chunk(c)] = state[at, :] * row[:, chunk(c)]


def front_kernel(
    levels, is_child, state, mask, kappa, nudging, mixing, nest_x, nest_y,
    forcing, other, masked, matrices, parcel, inner, base,
    buf, mask_buf, kappa_buf, nudging_buf, mixing_buf, square, weights,
    wide, stack, group, sems,
):
    fields, cols, _, rows = masked.shape
    chunks = rows // LANE
    step = cols * chunks
    size = levels * step
    blocks = cols // 3
    terms = 11

    def copy(f):
        at = pl.ds(f * size, size)
        return pltpu.make_async_copy(state.at[at], buf.at[at], sems.at[f])

    pairs = (
        (mask, mask_buf),
        (kappa, kappa_buf),
        (nudging, nudging_buf),
        (mixing, mixing_buf),
    )
    smalls = [
        pltpu.make_async_copy(source, target, sems.at[fields + n])
        for n, (source, target) in enumerate(pairs)
    ]
    copy(0).start()
    for small in smalls:
        small.start()
    for f in range(1, fields):
        copy(f).start()
    square[...] = jnp.zeros_like(square)
    for small in smalls:
        small.wait()

    @pl.when(is_child[0] == 1)
    def _():
        fill_group(group)
        ids = lane_ids((1, rows))
        for b in range(blocks):
            own = range(3 * b, 3 * b + 3)
            both = {x: nudging_buf[x : x + 1, :] * kappa_buf[x] for x in own}
            for n, x in enumerate(range(3 * b - 1, 3 * b + 4)):
                total = None
                for near in (x - 1, x + 1):
                    if near in both:
                        total = both[near] if total is None else total + both[near]
                if x in both:
                    total = total + (nudging_buf[x : x + 1, :] - 4.0 * both[x])
                weights[b * terms + n : b * terms + n + 1, :] = total
            for n, x in enumerate(own):
                at = b * terms + 5 + n
                value = jnp.where(ids == rows - 1, 0.0, pltpu.roll(both[x], rows - 1, 1))
                weights[at : at + 1, :] = value
                value = jnp.where(ids == 0, 0.0, pltpu.roll(both[x], 1, 1))
                weights[at + 3 : at + 4, :] = value

    def weight(b, n):
        return weights[b * terms + n : b * terms + n + 1, :]

    def field(f, total_edges):
        copy(f).wait()
        fill_matrix(levels, mixing_buf[f, :, 0, :], square, matrices.at[f])
        fill_masked(levels, buf, f, mask_buf, masked.at[f])
        own_edges = packed(
            lambda x: (masked[f, x, :, :LANE], masked[f, x, :, rows - LANE :]), cols
        )

        @pl.when(is_child[0] == 1)
        def _():
            for b in range(blocks):
                total = None
                for n, x in enumerate(range(3 * b - 1, 3 * b + 4)):
                    if 0 <= x < cols:
                        term = weight(b, n) * masked[f, x]
                        total = term if total is None else total + term
                for side, shift in ((0, 1), (3, rows - 1)):
                    value = None
                    for n in range(3):
                        term = weight(b, 5 + side + n) * masked[f, 3 * b + n]
                        value = term if value is None else value + term
                    total = total + pltpu.roll(value, shift, 1)
                at = aligned(f * blocks + b, DEPTH)
                wide[at, :rows], wide[at, rows:] = halves(deepened(total))

        @pl.when(is_child[0] == 0)
        def _():
            back = lax.rem(rows - nest_y[0], rows)
            for b in range(blocks):
                x = nest_x[0] + b
                above = masked[f, jnp.maximum(x - 1, 0)]
                below = masked[f, jnp.minimum(x + 1, cols - 1)]
                if b == 0:
                    above = jnp.where(x == 0, 0.0, above)
                if b == blocks - 1:
                    below = jnp.where(x == cols - 1, 0.0, below)
                value = spread_of(masked[f, x], above, below, kappa_buf[x])
                value = deepened(pltpu.roll(value, back, 1)[:, :LANE])
                fill_stack(stack.at[f], chunk(b), value)

        return total_edges + pltpu.roll(own_edges, 2 * f * cols, 1)

    parcel[:PAD, :] = lax.fori_loop(0, fields, field, jnp.zeros((PAD, LANE), F32))
    slots, dests = forcing.shape
    parcel[PAD:, :] = jnp.zeros((parcel.shape[0] - PAD, LANE), F32)
    parcel[PAD : PAD + slots, :dests] = forcing[...]
    if 2 * dests <= LANE:
        parcel[PAD : PAD + slots, dests : 2 * dests] = other[...]
    else:
        parcel[PAD + slots :, :dests] = other[...]

    @pl.when(is_child[0] == 1)
    def _():
        value = grouped(wide[...], group[...])
        for f in range(fields):
            for b in range(blocks):
                at = (f * blocks + b) * DEPTH
                fill_stack(stack.at[f], chunk(b), value[at : at + DEPTH])

    for f in range(fields):
        mixed = mix(matrices[f], stack[f])
        for b in range(1, blocks - 1):
            at = pl.ds(f * levels * (blocks - 2) + b - 1, levels, stride=blocks - 2)
            inner[at, :] = mixed[:levels, chunk(b)]
        base[f, :, :LANE] = mixed[:PAD, :LANE]
        base[f, :, LANE:] = mixed[:PAD, chunk(blocks - 1)]


def front(is_child, state2, mask, kappa, nudging, mixing, nests, forcing, other, dims):
    fields, levels, cols, chunks = dims
    rows = chunks * LANE
    blocks = cols // 3
    arrays = (state2, mask, kappa, nudging, mixing)
    tile = (fields, cols, PAD, rows)
    slots, dests = forcing.shape
    height = slots if 2 * dests <= LANE else 2 * slots
    return pl.pallas_call(
        functools.partial(front_kernel, levels),
        in_specs=[SMEM] + [HBM] * 5 + [SMEM] * 2 + [VMEM] * 2,
        out_specs=[VMEM] * 5,
        out_shape=[
            pltpu.VMEM(tile, F32),
            pltpu.VMEM((fields, 2 * DEPTH, 2 * DEPTH), jnp.bfloat16),
            pltpu.VMEM((PAD + height, LANE), F32),
            pltpu.VMEM((fields * levels * (blocks - 2), LANE), F32),
            pltpu.VMEM((fields, PAD, 2 * LANE), F32),
        ],
        scratch_shapes=[
            pltpu.VMEM(state2.shape, F32),
            pltpu.VMEM(mask.shape, jnp.int32),
            pltpu.VMEM(kappa.shape, F32),
            pltpu.VMEM(nudging.shape, F32),
            pltpu.VMEM(mixing.shape, F32),
            pltpu.VMEM((DEPTH, LANE), F32),
            pltpu.VMEM((-(-blocks * 11 // 8) * 8, rows), F32),
            pltpu.VMEM((fields * blocks * DEPTH, 2 * rows), jnp.bfloat16),
            pltpu.VMEM((fields, 2 * DEPTH, blocks * LANE), jnp.bfloat16),
            pltpu.VMEM((2 * rows, LANE), jnp.bfloat16),
            pltpu.SemaphoreType.DMA((fields + 4,)),
        ],
        compiler_params=pltpu.CompilerParams(vmem_limit_bytes=28 * MIB),
        cost_estimate=COST,
        name="front",
    )(is_child, *map(in_hbm, arrays), *nests, forcing, other)


def merged(own, other, width):
    if 2 * width <= LANE:
        return own + pltpu.roll(other, width, 1)
    return jnp.concatenate([own, other], axis=0)


def repack_kernel(width, parcel, arrived, out):
    out[:PAD, :] = parcel[:PAD, :]
    out[PAD:, :] = merged(parcel[PAD:, :], arrived[PAD:, :], width)


def repack(parcel, arrived, width):
    height = (parcel.shape[0] - PAD) * (1 if 2 * width <= LANE else 2)
    return pl.pallas_call(
        functools.partial(repack_kernel, width),
        in_specs=[VMEM] * 2,
        out_specs=VMEM,
        out_shape=pltpu.VMEM((PAD + height, LANE), F32),
        compiler_params=pltpu.CompilerParams(vmem_limit_bytes=4 * MIB),
        name="repack",
    )(parcel, arrived)


def y_halos(ty, peers, first, second):
    one, two = first[:PAD, :], second[:PAD, :]
    even = (lax.rem(ty[0], 2) == 0).astype(F32)
    odd = 1.0 - even
    before = (two * even + one * odd) * (ty[0] > 0).astype(F32)
    after = (one * even + two * odd) * (ty[0] < peers - 1).astype(F32)
    low = lax.rem(lane_ids((PAD, LANE)), 2) == 0
    return jnp.where(low, pltpu.roll(before, 1, 1), pltpu.roll(after, LANE - 1, 1))


def outer_kernel(
    levels, peers, width, is_child, ty, matrices, base, kappa, nudging, x_low, x_high, first, second,
    parcel, nest_x, nest_y, out, seen, sides, wide, stack, group,
):
    fields = matrices.shape[0]
    cols, _, rows = kappa.shape
    blocks = cols // 3
    lanes = lane_ids((PAD, LANE))
    turned = lax.rem(lanes + 1, LANE)
    ends = ((0, x_low), (cols - 1, x_high))
    sides[...] = jnp.zeros_like(sides)
    seen[...] = merged(parcel[PAD:, :], second[PAD:, :], width)
    halo = y_halos(ty, peers, first, second)

    def weighted(row_of_x):
        one = packed(lambda x: (row_of_x(x)[:, :LANE], row_of_x(x)[:, rows - LANE :]), cols)
        total = one
        for f in range(1, fields):
            total = total + pltpu.roll(one, 2 * f * cols, 1)
        return halo * total

    def fill_fix(value):
        for f in range(fields):
            fill_stack(stack.at[f], chunk(2), deepened(value))

    @pl.when(is_child[0] == 1)
    def _():
        fill_group(group)
        for n, (x, side) in enumerate(ends):
            weight = nudging[x : x + 1, :] * kappa[x]
            for f in range(fields):
                at = (f * 2 + n) * DEPTH
                sides[at : at + levels, :] = side[f, :, 0, :] * weight
        wide[:, :rows], wide[:, rows:] = halves(sides[...])
        value = grouped(wide[...], group[...])
        for f in range(fields):
            for n in range(2):
                at = (f * 2 + n) * DEPTH
                fill_stack(stack.at[f], chunk(n), value[at : at + DEPTH])
        part = weighted(lambda x: nudging[x : x + 1, :] * kappa[x])
        fill_fix(part + pltpu.roll(part, LANE - 2, 1) + pltpu.roll(part, LANE - 4, 1))

    @pl.when(is_child[0] == 0)
    def _():
        back = lax.rem(rows - nest_y[0], rows)
        reached = (nest_x[0] == 0, nest_x[0] + blocks == cols)
        for n, (x, side) in enumerate(ends):
            weight = kappa[x] * reached[n].astype(F32)
            for f in range(fields):
                at = (f * 2 + n) * DEPTH
                sides[at : at + levels, :] = side[f, :, 0, :] * weight
                value = pltpu.roll(sides[at : at + DEPTH, :], back, 1)[:, :LANE]
                fill_stack(stack.at[f], chunk(n), value)
        starts = (nest_y[0] == 0).astype(F32)
        finals = (nest_y[0] == rows - LANE).astype(F32)
        part = weighted(lambda x: kappa[x])
        part = part * jnp.where(lax.rem(lanes, 2) == 0, starts, finals)
        value = jnp.zeros((PAD, LANE), F32)
        for b in range(blocks):
            shift = lax.rem(LANE + 4 * b - 2 * nest_x[0], LANE)
            here = lax.rem(turned, 2 * cols) // 2 == 3 * b
            value = jnp.where(here, pltpu.roll(part, shift, 1), value)
        fill_fix(value)

    fixes = jnp.zeros((PAD, LANE), F32)
    for f in range(fields):
        mixed = mix(matrices[f], stack[f])
        for n in range(2):
            at = pl.ds(f * (2 * levels) + n, levels, stride=2)
            out[at, :] = base[f, :levels, chunk(n)] + mixed[:levels, chunk(n)]
        fixes = jnp.where(turned // (2 * cols) == f, mixed[:PAD, chunk(2)], fixes)
    out[out.shape[0] - PAD :, :] = fixes


def outer(
    is_child, ty, matrices, base, kappa, nudging, x_halos, firsts, parcel, nests, width, dims, peers
):
    fields, levels, cols, chunks = dims
    rows = chunks * LANE
    height = -(-fields * 2 * levels // 8) * 8 + PAD
    seen = (parcel.shape[0] - PAD) * (1 if 2 * width <= LANE else 2)
    return pl.pallas_call(
        functools.partial(outer_kernel, levels, peers, width),
        in_specs=[SMEM] * 2 + [VMEM] * 9 + [SMEM] * 2,
        out_specs=[VMEM] * 2,
        out_shape=[pltpu.VMEM((height, LANE), F32), pltpu.VMEM((seen, LANE), F32)],
        scratch_shapes=[
            pltpu.VMEM((fields * 2 * DEPTH, rows), F32),
            pltpu.VMEM((fields * 2 * DEPTH, 2 * rows), jnp.bfloat16),
            pltpu.VMEM((fields, 2 * DEPTH, 3 * LANE), jnp.bfloat16),
            pltpu.VMEM((2 * rows, LANE), jnp.bfloat16),
        ],
        compiler_params=pltpu.CompilerParams(vmem_limit_bytes=12 * MIB),
        name="outer",
    )(is_child, ty, matrices, base, kappa, nudging, *x_halos, *firsts, parcel, *nests)


def tile_kernel(
    levels, peers, ty, masked, matrices, kappa, x_low, x_high, first, second,
    out, sides, halo, stack,
):
    fields, cols, _, rows = masked.shape
    chunks = rows // LANE

    sides[...] = jnp.zeros_like(sides)
    halo[...] = y_halos(ty, peers, first, second)
    pair = 2

    def field(f, carry):
        sides[0, :levels, :] = x_low[f, :, 0, :]
        sides[1, :levels, :] = x_high[f, :, 0, :]
        for x0 in range(0, cols, pair):
            for x in range(x0, x0 + pair):
                above = masked[f, x - 1] if x > 0 else sides[0]
                below = masked[f, x + 1] if x < cols - 1 else sides[1]
                shift = lax.rem(LANE - 2 * (f * cols + x), LANE)
                edge = pltpu.roll(halo[...], lax.rem(LANE + shift, LANE), 1)
                value = spread_of(masked[f, x], above, below, kappa[x], edge)
                part = slice((x - x0) * rows, (x - x0 + 1) * rows)
                fill_stack(stack, part, deepened(value))
            mixed = mix(matrices[f], stack[...])
            for n in range(pair * chunks):
                out[aligned((f * cols + x0) * chunks + n, PAD), :] = mixed[:PAD, chunk(n)]
        return carry

    lax.fori_loop(0, fields, field, 0)


def tile_of(ty, masked, matrices, kappa, x_halos, firsts, dims, peers):
    fields, levels, cols, chunks = dims
    rows = chunks * LANE
    return pl.pallas_call(
        functools.partial(tile_kernel, levels, peers),
        in_specs=[SMEM] + [VMEM] * 7,
        out_specs=VMEM,
        out_shape=pltpu.VMEM((fields * cols * chunks * PAD, LANE), F32),
        scratch_shapes=[
            pltpu.VMEM((2, PAD, rows), F32),
            pltpu.VMEM((PAD, LANE), F32),
            pltpu.VMEM((2 * DEPTH, 2 * rows), jnp.bfloat16),
        ],
        compiler_params=pltpu.CompilerParams(vmem_limit_bytes=16 * MIB),
        cost_estimate=COST,
        name="tile",
    )(ty, in_vmem(masked), matrices, kappa, *x_halos, *firsts)


def observe_kernel(dests, across, row, column, places, counts, mine, theirs, _, tile):
    lanes = lane_ids((1, LANE))
    slots = places.shape[1]
    ty, tx = row[0], column[0]
    me = ty * across + tx
    half = mine.shape[0] // slots * (LANE // dests)

    def source(first, ref, n, carry):
        g = first + n
        origin = (((g >> 1) & 1) ^ (3 * ((g >> 2) & 1)) ^ ty) * across
        origin = origin + (((g & 1) | ((g >> 3) << 1)) ^ tx)
        lane_in = lax.rem(n, LANE // dests) * dests + me
        block = lax.div(n, LANE // dests) * slots
        count = counts[0, origin]
        for k in range(0, slots, 2):
            ats, adds = [], []
            for m in range(k, k + 2):
                place = places[origin, m]
                lane = place & (LANE - 1)
                value = pltpu.roll(ref[pl.ds(block + m, 1), :], (lane - lane_in) & (LANE - 1), 1)
                ats.append(place >> 7)
                adds.append(jnp.where(lanes == jnp.where(m < count, lane, LANE), value, 0.0))
            olds = [tile[pl.ds(at, 1), :] for at in ats]
            also = jnp.where(ats[0] == ats[1], adds[0], 0.0)
            tile[pl.ds(ats[0], 1), :] = olds[0] + adds[0]
            tile[pl.ds(ats[1], 1), :] = olds[1] + adds[1] + also
        return carry

    lax.fori_loop(0, half, functools.partial(source, 0, mine), 0)
    lax.fori_loop(0, half, functools.partial(source, half, theirs), 0)


def observe(row, column, places, counts, seen, tile, dests, across):
    return pl.pallas_call(
        functools.partial(observe_kernel, dests, across),
        in_specs=[SMEM] * 4 + [VMEM] * 3,
        out_specs=VMEM,
        out_shape=pltpu.VMEM(tile.shape, F32),
        input_output_aliases={6: 0},
        compiler_params=pltpu.CompilerParams(vmem_limit_bytes=4 * MIB),
        name="observe",
    )(row, column, places, counts, *seen, in_vmem(tile))


def finish_kernel(
    levels, is_child, nest_x, nest_y, tile, mask, in_arrived, out_arrived, in_sent, out_sent,
    out, buf, group, sems,
):
    cols = mask.shape[0]
    rows = mask.shape[2]
    chunks = rows // LANE
    step = cols * chunks
    size = levels * step
    fields = out.shape[0] // size
    blocks = cols // 3
    inner = blocks - 2
    lanes = lane_ids((levels, LANE))
    ends = jnp.logical_or(lanes == 0, lanes == LANE - 1)
    height = out_arrived.shape[0]

    def copy(f):
        at = pl.ds(f * size, size)
        return pltpu.make_async_copy(buf.at[at], out.at[at], sems.at[f])

    def piece_of(f, piece):
        return tile[pl.ds(pl.multiple_of((f * step + piece) * PAD, 8), levels), :]

    def payload(f, b, inner_ref, outer_ref):
        if b in (0, blocks - 1):
            value = outer_ref[pl.ds(f * (2 * levels) + min(b, 1), levels, stride=2), :]
        else:
            value = inner_ref[pl.ds(f * (levels * inner) + b - 1, levels, stride=inner), :]
        fixes = outer_ref[height - PAD : height - PAD + levels, :]
        shift = lax.rem(LANE - 2 * (f * cols + 3 * b), LANE)
        fixes = pltpu.roll(fixes, lax.rem(LANE + shift, LANE), 1)
        return value + jnp.where(ends, fixes, 0.0)

    def fill_child(f, carry):
        for b in range(blocks):
            high, low = halves(payload(f, b, in_arrived, out_arrived))
            both = jnp.concatenate([high, low], axis=1)
            value = jnp.dot(both, group[...], preferred_element_type=F32) * (1.0 / 9.0)
            for x in range(3 * b, 3 * b + 3):
                row = row_of(mask, x)
                for c in range(chunks):
                    piece = x * chunks + c
                    at = pl.ds(f * size + piece, levels, stride=step)
                    total = piece_of(f, piece) + value[:, chunk(c)]
                    buf[at, :] = total * row[:, chunk(c)]
        copy(f).start()
        return carry

    def fill_plain(f, carry):
        for x in range(cols):
            row = row_of(mask, x)
            for c in range(chunks):
                piece = x * chunks + c
                at = pl.ds(f * size + piece, levels, stride=step)
                buf[at, :] = piece_of(f, piece) * row[:, chunk(c)]
        return carry

    def fill_parent(f, carry):
        fill_plain(f, carry)
        for b in range(blocks):
            delta = payload(f, b, in_arrived, out_arrived) - payload(f, b, in_sent, out_sent)
            wide = jnp.concatenate([delta, jnp.zeros((levels, rows - LANE), F32)], 1)
            x = nest_x[0] + b
            value = pltpu.roll(wide, nest_y[0], 1) * row_of(mask, x)
            for c in range(chunks):
                at = pl.ds(f * size + x * chunks + c, levels, stride=step)
                buf[at, :] = buf[at, :] + value[:, chunk(c)]
        copy(f).start()
        return carry

    @pl.when(is_child[0] == 1)
    def _():
        ids = lax.broadcasted_iota(jnp.int32, group.shape, 0)
        ids = jnp.where(ids < LANE, ids, ids - LANE)
        group[...] = jnp.where(lane_ids(group.shape) // 3 == ids, 1.0, 0.0).astype(jnp.bfloat16)
        lax.fori_loop(0, fields, fill_child, 0)

    @pl.when(is_child[0] == 0)
    def _():
        lax.fori_loop(0, fields, fill_parent, 0)

    for f in range(fields):
        copy(f).wait()


def finish(is_child, nests, tile, mask, arrived, sent, dims):
    fields, levels, cols, chunks = dims
    rows = chunks * LANE
    size = (fields * levels * cols * chunks, LANE)
    return pl.pallas_call(
        functools.partial(finish_kernel, levels),
        in_specs=[SMEM] * 3 + [VMEM] * 6,
        out_specs=HBM,
        out_shape=pltpu.HBM(size, F32),
        scratch_shapes=[
            pltpu.VMEM(size, F32),
            pltpu.VMEM((2 * LANE, rows), jnp.bfloat16),
            pltpu.SemaphoreType.DMA((fields,)),
        ],
        compiler_params=pltpu.CompilerParams(vmem_limit_bytes=16 * MIB),
        cost_estimate=COST,
        name="finish",
    )(is_child, *nests, in_vmem(tile), mask, *arrived, *sent)


def from_neighbours(low, high, axis):
    ends = lax.axis_size(axis) - 1
    before = lax.ppermute(high, axis, [(i, i + 1) for i in range(ends)])
    after = lax.ppermute(low, axis, [(i + 1, i) for i in range(ends)])
    return before, after


def swapped(value, axis, mask):
    return lax.ppermute(value, axis, [(i, i ^ mask) for i in range(lax.axis_size(axis))])


def places_of(cells, dims):
    _, levels, cols, chunks = dims
    rows = chunks * LANE
    column, inside = cells // (cols * rows), cells % (cols * rows)
    at = (column // levels) * (cols * chunks) + inside // LANE
    return ((at * PAD + column % levels) << 7) | (inside % LANE)


def local(
    adjoint_state,
    land_mask,
    diffusivity,
    mixing,
    nudging,
    nest_x,
    nest_y,
    obs_forcing,
    obs_cell,
    obs_count,
):
    _, fields, levels, cols, rows = adjoint_state.shape
    chunks = rows // LANE
    dims = (fields, levels, cols, chunks)
    state5 = adjoint_state.reshape(fields, levels, cols, 1, rows)
    state2 = adjoint_state.reshape(fields * levels * cols * chunks, LANE)
    mask = land_mask.reshape(cols, 1, rows)
    kappa = diffusivity.reshape(cols, 1, rows)
    mixing = mixing.reshape(fields, levels, 1, levels)
    peers, across = lax.axis_size("ty"), lax.axis_size("tx")
    assert peers == 4 and across & (across - 1) == 0 and 2 * fields * cols <= LANE
    assert levels <= PAD and cols % 3 == 0 and rows == 3 * LANE
    row = lax.axis_index("ty").astype(jnp.int32)
    column = lax.axis_index("tx").astype(jnp.int32)
    ty = row.reshape(1)
    is_child = (lax.axis_index("grp") == 0).astype(jnp.int32).reshape(1)
    nests = (nest_x, nest_y)

    forcing = obs_forcing[0, 0]
    dests = forcing.shape[1]
    places = places_of(obs_cell[0, :, :, 0], dims)
    counts = obs_count.reshape(1, -1)
    other = swapped(forcing, "tx", 1)
    x_low, x_high = x_edges(state5, mask)
    x_halos = from_neighbours(x_low, x_high, "tx")
    places, state2 = lax.optimization_barrier((places, state2))
    masked, matrices, parcel, in_sent, base = front(
        is_child, state2, mask, kappa, nudging, mixing, nests, forcing, other, dims
    )
    first = swapped(parcel, "ty", 1)
    in_arrived = swapped(in_sent, "grp", 1)
    parcel = repack(parcel, first, 2 * dests)
    parcel, x_halos = lax.optimization_barrier((parcel, x_halos))
    second = swapped(parcel, "ty", 3)
    firsts = (first, second)
    out_sent, seen = outer(
        is_child, ty, matrices, base, kappa, nudging, x_halos, firsts, parcel, nests, 4 * dests, dims, peers
    )
    out_sent, in_arrived = lax.optimization_barrier((out_sent, in_arrived))
    out_arrived = swapped(out_sent, "grp", 1)
    for n in range(1, across.bit_length() - 2):
        seen = jnp.concatenate([seen, swapped(seen, "tx", 1 << n)])
    seen = (seen, swapped(seen, "tx", across // 2))
    tile = tile_of(ty, masked, matrices, kappa, x_halos, firsts, dims, peers)
    tile = observe(ty, column.reshape(1), places, counts, seen, tile, dests, across)
    arrived, sent = (in_arrived, out_arrived), (in_sent, out_sent)
    out = finish(is_child, nests, tile, mask, arrived, sent, dims)
    return out.reshape(adjoint_state.shape)


def solution(mesh):
    in_specs = (
        P("grp", None, None, "tx", "ty"),
        P("grp", "tx", "ty"),
        P("grp", "tx", "ty"),
        P("grp", None, None, None),
        P("tx", "ty"),
        P(("ty", "tx")),
        P(("ty", "tx")),
        P("grp", ("ty", "tx"), None, None),
        P("grp", None, None, ("ty", "tx")),
        P("grp", None, ("ty", "tx")),
    )
    out_specs = P("grp", None, None, "tx", "ty")
    return jax.shard_map(local, mesh=mesh, in_specs=in_specs, out_specs=out_specs, check_vma=False)
```

```python
import functools

import jax
import jax.numpy as jnp
from jax import lax
from jax.experimental import pallas as pl
from jax.experimental.pallas import tpu as pltpu
from jax.sharding import PartitionSpec as P

LANE = 128
PAD = 56
DEPTH = 64
MIB = 1 << 20
HBM = pl.BlockSpec(memory_space=pltpu.HBM)
SMEM = pl.BlockSpec(memory_space=pltpu.SMEM)
VMEM = pl.BlockSpec(memory_space=pltpu.VMEM)
F32 = jnp.float32
COST = pl.CostEstimate(flops=10**10, bytes_accessed=10**8, transcendentals=0)


def lane_ids(shape):
    return lax.broadcasted_iota(jnp.int32, shape, len(shape) - 1)


def row_of(ref, x):
    return ref[x].astype(F32)


def chunk(c):
    return slice(c * LANE, (c + 1) * LANE)


def in_hbm(value):
    return pltpu.with_memory_space_constraint(value, pltpu.HBM)


def in_vmem(value):
    return pltpu.with_memory_space_constraint(value, pltpu.VMEM)


def x_edges_kernel(tx, state, mask, first, second, buf, mask_buf, sems):
    fields, _, cols = state.shape[:3]
    even = lax.rem(tx[0], 2) == 0
    ends = (jnp.where(even, cols - 1, 0), jnp.where(even, 0, cols - 1))
    copies = [pltpu.make_async_copy(mask, mask_buf, sems.at[2 * fields])]
    for n, x in enumerate(ends):
        for f in range(fields):
            copies.append(
                pltpu.make_async_copy(state.at[f, :, x], buf.at[n, f], sems.at[n * fields + f])
            )
    for copy in copies:
        copy.start()
    copies[0].wait()
    for n, (x, out) in enumerate(zip(ends, (first, second))):
        for f in range(fields):
            copies[1 + n * fields + f].wait()
            out[f] = buf[n, f] * row_of(mask_buf, x)[None]


def x_edges(tx, state5, mask):
    fields, levels, cols, _, rows = state5.shape
    edge = (fields, levels, 1, rows)
    return pl.pallas_call(
        x_edges_kernel,
        in_specs=[SMEM, HBM, HBM],
        out_specs=[VMEM] * 2,
        out_shape=[pltpu.VMEM(edge, F32)] * 2,
        scratch_shapes=[
            pltpu.VMEM((2,) + edge, F32),
            pltpu.VMEM(mask.shape, jnp.int32),
            pltpu.SemaphoreType.DMA((2 * fields + 1,)),
        ],
        compiler_params=pltpu.CompilerParams(vmem_limit_bytes=8 * MIB),
        cost_estimate=COST,
        name="x_edges",
    )(tx, in_hbm(state5), in_hbm(mask))


def x_halos_of(tx, first, second, f):
    one, two = first[f, :, 0, :], second[f, :, 0, :]
    even = lax.rem(tx[0], 2) == 0
    return jnp.where(even, two, one), jnp.where(even, one, two)


def spread_of(here, above, below, kappa, edge=None):
    rows = here.shape[1]
    lanes = lane_ids((here.shape[0], LANE))
    edge = 0.0 if edge is None else edge
    before = pltpu.roll(here, 1, 1)
    after = pltpu.roll(here, rows - 1, 1)
    before = jnp.concatenate([jnp.where(lanes == 0, edge, before[:, :LANE]), before[:, LANE:]], 1)
    after = jnp.concatenate(
        [after[:, :-LANE], jnp.where(lanes == LANE - 1, edge, after[:, -LANE:])], 1
    )
    return here + kappa * (above + below + before + after - 4.0 * here)


def halves(value):
    high = value.astype(jnp.bfloat16)
    return high, (value - high.astype(F32)).astype(jnp.bfloat16)


def deepened(value):
    return jnp.concatenate([value, jnp.zeros((DEPTH - value.shape[0], value.shape[1]), F32)], 0)


def fill_matrix(levels, mixing, square, matrix):
    square[:levels, :levels] = mixing
    value = square[...]
    high = value.astype(jnp.bfloat16).astype(F32)
    matrix[:DEPTH, :] = (high + pltpu.roll(high, DEPTH, 1)).astype(jnp.bfloat16)
    matrix[DEPTH:, :] = (value - high).astype(jnp.bfloat16)


def fill_stack(stack, part, value):
    high, low = halves(value)
    stack[:DEPTH, part] = high
    stack[DEPTH:, part] = low


def mix(matrix, stack):
    both = jnp.dot(matrix, stack, preferred_element_type=F32)
    return both[:DEPTH] + both[DEPTH:]


def fill_group(group):
    rows = group.shape[0] // 2
    ids = lax.broadcasted_iota(jnp.int32, group.shape, 0)
    ids = jnp.where(ids < rows, ids, ids - rows) // 3
    group[...] = jnp.where(ids == lane_ids(group.shape), 1.0, 0.0).astype(jnp.bfloat16)


def grouped(wide, group):
    return jnp.dot(wide, group, preferred_element_type=F32)


def aligned(index, size):
    return pl.ds(pl.multiple_of(index * size, size), size)


def packed(rows_of, cols):
    parts = []
    for x in range(cols):
        first, last = rows_of(x)
        lanes = lane_ids(first.shape)
        parts.append(jnp.where(lanes == 0, first, jnp.where(lanes == LANE - 1, last, 0.0)))
    shift = 2
    while len(parts) > 1:
        pairs = [parts[n : n + 2] for n in range(0, len(parts), 2)]
        parts = [p[0] + pltpu.roll(p[1], shift, 1) if len(p) == 2 else p[0] for p in pairs]
        shift *= 2
    return parts[0]


def fill_masked(levels, state, f, mask, masked):
    cols, _, rows = masked.shape
    chunks = rows // LANE
    step = cols * chunks
    for x in range(cols):
        row = row_of(mask, x)
        masked[x, PAD - 8 :, :] = jnp.zeros((8, rows), F32)
        for c in range(chunks):
            at = pl.ds(f * (levels * step) + x * chunks + c, levels, stride=step)
            masked[x, :levels, chunk(c)] = state[at, :] * row[:, chunk(c)]


def front_kernel(
    levels, is_child, state, mask, kappa, nudging, mixing, nest_x, nest_y, forcing, other,
    matrices, parcel, inner, base,
    buf, masked, mask_buf, kappa_buf, nudging_buf, mixing_buf, square, weights,
    wide, stack, group, sems,
):
    fields, cols, _, rows = masked.shape
    chunks = rows // LANE
    step = cols * chunks
    size = levels * step
    blocks = cols // 3
    terms = 11

    def copy(f):
        at = pl.ds(f * size, size)
        return pltpu.make_async_copy(state.at[at], buf.at[at], sems.at[f])

    pairs = (
        (mask, mask_buf),
        (kappa, kappa_buf),
        (nudging, nudging_buf),
        (mixing, mixing_buf),
    )
    smalls = [
        pltpu.make_async_copy(source, target, sems.at[fields + n])
        for n, (source, target) in enumerate(pairs)
    ]
    copy(0).start()
    for small in smalls:
        small.start()
    for f in range(1, fields):
        copy(f).start()
    square[...] = jnp.zeros_like(square)
    for small in smalls:
        small.wait()

    @pl.when(is_child[0] == 1)
    def _():
        fill_group(group)
        ids = lane_ids((1, rows))
        for b in range(blocks):
            own = range(3 * b, 3 * b + 3)
            both = {x: nudging_buf[x : x + 1, :] * kappa_buf[x] for x in own}
            for n, x in enumerate(range(3 * b - 1, 3 * b + 4)):
                total = None
                for near in (x - 1, x + 1):
                    if near in both:
                        total = both[near] if total is None else total + both[near]
                if x in both:
                    total = total + (nudging_buf[x : x + 1, :] - 4.0 * both[x])
                weights[b * terms + n : b * terms + n + 1, :] = total
            for n, x in enumerate(own):
                at = b * terms + 5 + n
                value = jnp.where(ids == rows - 1, 0.0, pltpu.roll(both[x], rows - 1, 1))
                weights[at : at + 1, :] = value
                value = jnp.where(ids == 0, 0.0, pltpu.roll(both[x], 1, 1))
                weights[at + 3 : at + 4, :] = value

    def weight(b, n):
        return weights[b * terms + n : b * terms + n + 1, :]

    def field(f, total_edges):
        copy(f).wait()
        fill_matrix(levels, mixing_buf[f, :, 0, :], square, matrices.at[f])
        fill_masked(levels, buf, f, mask_buf, masked.at[f])
        own_edges = packed(
            lambda x: (masked[f, x, :, :LANE], masked[f, x, :, rows - LANE :]), cols
        )

        @pl.when(is_child[0] == 1)
        def _():
            for b in range(blocks):
                total = None
                for n, x in enumerate(range(3 * b - 1, 3 * b + 4)):
                    if 0 <= x < cols:
                        term = weight(b, n) * masked[f, x]
                        total = term if total is None else total + term
                for side, shift in ((0, 1), (3, rows - 1)):
                    value = None
                    for n in range(3):
                        term = weight(b, 5 + side + n) * masked[f, 3 * b + n]
                        value = term if value is None else value + term
                    total = total + pltpu.roll(value, shift, 1)
                at = aligned(f * blocks + b, DEPTH)
                wide[at, :rows], wide[at, rows:] = halves(deepened(total))

        @pl.when(is_child[0] == 0)
        def _():
            back = lax.rem(rows - nest_y[0], rows)
            for b in range(blocks):
                x = nest_x[0] + b
                above = masked[f, jnp.maximum(x - 1, 0)]
                below = masked[f, jnp.minimum(x + 1, cols - 1)]
                if b == 0:
                    above = jnp.where(x == 0, 0.0, above)
                if b == blocks - 1:
                    below = jnp.where(x == cols - 1, 0.0, below)
                value = spread_of(masked[f, x], above, below, kappa_buf[x])
                value = deepened(pltpu.roll(value, back, 1)[:, :LANE])
                fill_stack(stack.at[f], chunk(b), value)

        return total_edges + pltpu.roll(own_edges, 2 * f * cols, 1)

    parcel[:PAD, :] = lax.fori_loop(0, fields, field, jnp.zeros((PAD, LANE), F32))
    slots, dests = forcing.shape
    parcel[PAD:, :] = jnp.zeros((parcel.shape[0] - PAD, LANE), F32)
    parcel[PAD : PAD + slots, :dests] = forcing[...]
    if 2 * dests <= LANE:
        parcel[PAD : PAD + slots, dests : 2 * dests] = other[...]
    else:
        parcel[PAD + slots :, :dests] = other[...]

    @pl.when(is_child[0] == 1)
    def _():
        value = grouped(wide[...], group[...])
        for f in range(fields):
            for b in range(blocks):
                at = (f * blocks + b) * DEPTH
                fill_stack(stack.at[f], chunk(b), value[at : at + DEPTH])

    for f in range(fields):
        mixed = mix(matrices[f], stack[f])
        for b in range(1, blocks - 1):
            at = pl.ds(f * levels * (blocks - 2) + b - 1, levels, stride=blocks - 2)
            inner[at, :] = mixed[:levels, chunk(b)]
        base[f, :, :LANE] = mixed[:PAD, :LANE]
        base[f, :, LANE:] = mixed[:PAD, chunk(blocks - 1)]


def front(is_child, state2, mask, kappa, nudging, mixing, nests, forcing, other, dims):
    fields, levels, cols, chunks = dims
    rows = chunks * LANE
    blocks = cols // 3
    arrays = (state2, mask, kappa, nudging, mixing)
    tile = (fields, cols, PAD, rows)
    slots, dests = forcing.shape
    height = slots if 2 * dests <= LANE else 2 * slots
    return pl.pallas_call(
        functools.partial(front_kernel, levels),
        in_specs=[SMEM] + [HBM] * 5 + [SMEM] * 2 + [VMEM] * 2,
        out_specs=[VMEM] * 4,
        out_shape=[
            pltpu.VMEM((fields, 2 * DEPTH, 2 * DEPTH), jnp.bfloat16),
            pltpu.VMEM((PAD + height, LANE), F32),
            pltpu.VMEM((fields * levels * (blocks - 2), LANE), F32),
            pltpu.VMEM((fields, PAD, 2 * LANE), F32),
        ],
        scratch_shapes=[
            pltpu.VMEM(state2.shape, F32),
            pltpu.VMEM(tile, F32),
            pltpu.VMEM(mask.shape, jnp.int32),
            pltpu.VMEM(kappa.shape, F32),
            pltpu.VMEM(nudging.shape, F32),
            pltpu.VMEM(mixing.shape, F32),
            pltpu.VMEM((DEPTH, LANE), F32),
            pltpu.VMEM((-(-blocks * 11 // 8) * 8, rows), F32),
            pltpu.VMEM((fields * blocks * DEPTH, 2 * rows), jnp.bfloat16),
            pltpu.VMEM((fields, 2 * DEPTH, blocks * LANE), jnp.bfloat16),
            pltpu.VMEM((2 * rows, LANE), jnp.bfloat16),
            pltpu.SemaphoreType.DMA((fields + 4,)),
        ],
        compiler_params=pltpu.CompilerParams(vmem_limit_bytes=28 * MIB),
        cost_estimate=COST,
        name="front",
    )(is_child, *map(in_hbm, arrays), *nests, forcing, other)


def merged(own, other, width):
    if 2 * width <= LANE:
        return own + pltpu.roll(other, width, 1)
    return jnp.concatenate([own, other], axis=0)


def repack_kernel(width, edges, parcel, arrived, out):
    if edges:
        out[:edges, :] = parcel[:edges, :]
    out[edges:, :] = merged(parcel[PAD:, :], arrived[PAD:, :], width)


def repack(parcel, arrived, width, edges):
    height = (parcel.shape[0] - PAD) * (1 if 2 * width <= LANE else 2)
    return pl.pallas_call(
        functools.partial(repack_kernel, width, edges),
        in_specs=[VMEM] * 2,
        out_specs=VMEM,
        out_shape=pltpu.VMEM((edges + height, LANE), F32),
        compiler_params=pltpu.CompilerParams(vmem_limit_bytes=4 * MIB),
        name="repack",
    )(parcel, arrived)


def y_halos(ty, peers, first, second):
    one, two = first[:PAD, :], second[:PAD, :]
    even = (lax.rem(ty[0], 2) == 0).astype(F32)
    odd = 1.0 - even
    before = (two * even + one * odd) * (ty[0] > 0).astype(F32)
    after = (one * even + two * odd) * (ty[0] < peers - 1).astype(F32)
    low = lax.rem(lane_ids((PAD, LANE)), 2) == 0
    return jnp.where(low, pltpu.roll(before, 1, 1), pltpu.roll(after, LANE - 1, 1))


def outer_kernel(
    levels, peers, is_child, tx, ty, state, matrices, base, kappa, nudging, x_first, x_second,
    first, second, nest_x, nest_y, out, ahead, sides, wide, stack, group, sem,
):
    fields = matrices.shape[0]
    cols, _, rows = kappa.shape
    blocks = cols // 3
    lanes = lane_ids((PAD, LANE))
    turned = lax.rem(lanes + 1, LANE)
    copy = pltpu.make_async_copy(state.at[pl.ds(0, ahead.shape[0])], ahead, sem)
    copy.start()
    sides[...] = jnp.zeros_like(sides)
    halo = y_halos(ty, peers, first, second)

    def weighted(row_of_x):
        one = packed(lambda x: (row_of_x(x)[:, :LANE], row_of_x(x)[:, rows - LANE :]), cols)
        total = one
        for f in range(1, fields):
            total = total + pltpu.roll(one, 2 * f * cols, 1)
        return halo * total

    def fill_fix(value):
        for f in range(fields):
            fill_stack(stack.at[f], chunk(2), deepened(value))

    @pl.when(is_child[0] == 1)
    def _():
        fill_group(group)
        for f in range(fields):
            for n, side in enumerate(x_halos_of(tx, x_first, x_second, f)):
                x = (0, cols - 1)[n]
                at = (f * 2 + n) * DEPTH
                sides[at : at + levels, :] = side * (nudging[x : x + 1, :] * kappa[x])
        wide[:, :rows], wide[:, rows:] = halves(sides[...])
        value = grouped(wide[...], group[...])
        for f in range(fields):
            for n in range(2):
                at = (f * 2 + n) * DEPTH
                fill_stack(stack.at[f], chunk(n), value[at : at + DEPTH])
        part = weighted(lambda x: nudging[x : x + 1, :] * kappa[x])
        fill_fix(part + pltpu.roll(part, LANE - 2, 1) + pltpu.roll(part, LANE - 4, 1))

    @pl.when(is_child[0] == 0)
    def _():
        back = lax.rem(rows - nest_y[0], rows)
        reached = (nest_x[0] == 0, nest_x[0] + blocks == cols)
        for f in range(fields):
            for n, side in enumerate(x_halos_of(tx, x_first, x_second, f)):
                at = (f * 2 + n) * DEPTH
                weight = kappa[(0, cols - 1)[n]] * reached[n].astype(F32)
                sides[at : at + levels, :] = side * weight
                value = pltpu.roll(sides[at : at + DEPTH, :], back, 1)[:, :LANE]
                fill_stack(stack.at[f], chunk(n), value)
        starts = (nest_y[0] == 0).astype(F32)
        finals = (nest_y[0] == rows - LANE).astype(F32)
        part = weighted(lambda x: kappa[x])
        part = part * jnp.where(lax.rem(lanes, 2) == 0, starts, finals)
        value = jnp.zeros((PAD, LANE), F32)
        for b in range(blocks):
            shift = lax.rem(LANE + 4 * b - 2 * nest_x[0], LANE)
            here = lax.rem(turned, 2 * cols) // 2 == 3 * b
            value = jnp.where(here, pltpu.roll(part, shift, 1), value)
        fill_fix(value)

    fixes = jnp.zeros((PAD, LANE), F32)
    for f in range(fields):
        mixed = mix(matrices[f], stack[f])
        for n in range(2):
            at = pl.ds(f * (2 * levels) + n, levels, stride=2)
            out[at, :] = base[f, :levels, chunk(n)] + mixed[:levels, chunk(n)]
        fixes = jnp.where(turned // (2 * cols) == f, mixed[:PAD, chunk(2)], fixes)
    out[out.shape[0] - PAD :, :] = fixes
    copy.wait()


def outer(
    is_child, tx, ty, state2, matrices, base, kappa, nudging, x_halos, firsts, nests, dims, peers
):
    fields, levels, cols, chunks = dims
    rows = chunks * LANE
    height = -(-fields * 2 * levels // 8) * 8 + PAD
    return pl.pallas_call(
        functools.partial(outer_kernel, levels, peers),
        in_specs=[SMEM] * 3 + [HBM] + [VMEM] * 8 + [SMEM] * 2,
        out_specs=[VMEM] * 2,
        out_shape=[
            pltpu.VMEM((height, LANE), F32),
            pltpu.VMEM((state2.shape[0] // fields, LANE), F32),
        ],
        scratch_shapes=[
            pltpu.VMEM((fields * 2 * DEPTH, rows), F32),
            pltpu.VMEM((fields * 2 * DEPTH, 2 * rows), jnp.bfloat16),
            pltpu.VMEM((fields, 2 * DEPTH, 3 * LANE), jnp.bfloat16),
            pltpu.VMEM((2 * rows, LANE), jnp.bfloat16),
            pltpu.SemaphoreType.DMA,
        ],
        compiler_params=pltpu.CompilerParams(vmem_limit_bytes=12 * MIB),
        name="outer",
    )(is_child, tx, ty, in_hbm(state2), matrices, base, kappa, nudging, *x_halos, *firsts, *nests)


def tile_kernel(
    levels, peers, tx, ty, state, mask, matrices, kappa, x_first, x_second, first, second, ahead,
    out, buf, masked, sides, halo, stack, sems,
):
    cols, _, rows = masked.shape
    chunks = rows // LANE
    size = levels * cols * chunks
    fields = state.shape[0] // size

    def copy(f):
        at = pl.ds(f * size, size)
        return pltpu.make_async_copy(state.at[at], buf.at[at], sems.at[f])

    for f in range(1, fields):
        copy(f).start()
    sides[...] = jnp.zeros_like(sides)
    halo[...] = y_halos(ty, peers, first, second)
    pair = 2

    def field(f, carry, leading=False):
        if leading:
            fill_masked(levels, ahead, f, mask, masked)
        else:
            copy(f).wait()
            fill_masked(levels, buf, f, mask, masked)
        for n, side in enumerate(x_halos_of(tx, x_first, x_second, f)):
            sides[n, :levels, :] = side
        for x0 in range(0, cols, pair):
            for x in range(x0, x0 + pair):
                above = masked[x - 1] if x > 0 else sides[0]
                below = masked[x + 1] if x < cols - 1 else sides[1]
                shift = lax.rem(LANE - 2 * (f * cols + x), LANE)
                edge = pltpu.roll(halo[...], lax.rem(LANE + shift, LANE), 1)
                value = spread_of(masked[x], above, below, kappa[x], edge)
                part = slice((x - x0) * rows, (x - x0 + 1) * rows)
                fill_stack(stack, part, deepened(value))
            mixed = mix(matrices[f], stack[...])
            for n in range(pair * chunks):
                out[aligned((f * cols + x0) * chunks + n, PAD), :] = mixed[:PAD, chunk(n)]
        return carry

    field(0, 0, leading=True)
    lax.fori_loop(1, fields, field, 0)


def tile_of(tx, ty, state2, mask, matrices, kappa, x_halos, firsts, ahead, dims, peers):
    fields, levels, cols, chunks = dims
    rows = chunks * LANE
    return pl.pallas_call(
        functools.partial(tile_kernel, levels, peers),
        in_specs=[SMEM] * 2 + [HBM] + [VMEM] * 8,
        out_specs=VMEM,
        out_shape=pltpu.VMEM((fields * cols * chunks * PAD, LANE), F32),
        scratch_shapes=[
            pltpu.VMEM(state2.shape, F32),
            pltpu.VMEM((cols, PAD, rows), F32),
            pltpu.VMEM((2, PAD, rows), F32),
            pltpu.VMEM((PAD, LANE), F32),
            pltpu.VMEM((2 * DEPTH, 2 * rows), jnp.bfloat16),
            pltpu.SemaphoreType.DMA((fields,)),
        ],
        compiler_params=pltpu.CompilerParams(vmem_limit_bytes=16 * MIB),
        cost_estimate=COST,
        name="tile",
    )(tx, ty, in_hbm(state2), mask, matrices, kappa, *x_halos, *firsts, in_vmem(ahead))


def observe_kernel(dests, across, row, column, places, counts, mine, theirs, _, tile):
    lanes = lane_ids((1, LANE))
    slots = places.shape[1]
    ty, tx = row[0], column[0]
    me = ty * across + tx
    half = mine.shape[0] // slots * (LANE // dests)

    def source(first, ref, n, carry):
        g = first + n
        origin = (((g >> 1) & 1) ^ (3 * ((g >> 2) & 1)) ^ ty) * across
        origin = origin + (((g & 1) | ((g >> 3) << 1)) ^ tx)
        lane_in = lax.rem(n, LANE // dests) * dests + me
        block = lax.div(n, LANE // dests) * slots
        count = counts[0, origin]
        for k in range(0, slots, 2):
            ats, adds = [], []
            for m in range(k, k + 2):
                place = places[origin, m]
                lane = place & (LANE - 1)
                value = pltpu.roll(ref[pl.ds(block + m, 1), :], (lane - lane_in) & (LANE - 1), 1)
                ats.append(place >> 7)
                adds.append(jnp.where(lanes == jnp.where(m < count, lane, LANE), value, 0.0))
            olds = [tile[pl.ds(at, 1), :] for at in ats]
            also = jnp.where(ats[0] == ats[1], adds[0], 0.0)
            tile[pl.ds(ats[0], 1), :] = olds[0] + adds[0]
            tile[pl.ds(ats[1], 1), :] = olds[1] + adds[1] + also
        return carry

    lax.fori_loop(0, half, functools.partial(source, 0, mine), 0)
    lax.fori_loop(0, half, functools.partial(source, half, theirs), 0)


def observe(row, column, places, counts, seen, tile, dests, across):
    return pl.pallas_call(
        functools.partial(observe_kernel, dests, across),
        in_specs=[SMEM] * 4 + [VMEM] * 3,
        out_specs=VMEM,
        out_shape=pltpu.VMEM(tile.shape, F32),
        input_output_aliases={6: 0},
        compiler_params=pltpu.CompilerParams(vmem_limit_bytes=4 * MIB),
        name="observe",
    )(row, column, places, counts, *seen, in_vmem(tile))


def finish_kernel(
    levels, is_child, nest_x, nest_y, tile, mask, in_arrived, out_arrived, in_sent, out_sent,
    out, buf, group, sems,
):
    cols = mask.shape[0]
    rows = mask.shape[2]
    chunks = rows // LANE
    step = cols * chunks
    size = levels * step
    fields = out.shape[0] // size
    blocks = cols // 3
    inner = blocks - 2
    lanes = lane_ids((levels, LANE))
    ends = jnp.logical_or(lanes == 0, lanes == LANE - 1)
    height = out_arrived.shape[0]

    def copy(f):
        at = pl.ds(f * size, size)
        return pltpu.make_async_copy(buf.at[at], out.at[at], sems.at[f])

    def piece_of(f, piece):
        return tile[pl.ds(pl.multiple_of((f * step + piece) * PAD, 8), levels), :]

    def payload(f, b, inner_ref, outer_ref):
        if b in (0, blocks - 1):
            value = outer_ref[pl.ds(f * (2 * levels) + min(b, 1), levels, stride=2), :]
        else:
            value = inner_ref[pl.ds(f * (levels * inner) + b - 1, levels, stride=inner), :]
        fixes = outer_ref[height - PAD : height - PAD + levels, :]
        shift = lax.rem(LANE - 2 * (f * cols + 3 * b), LANE)
        fixes = pltpu.roll(fixes, lax.rem(LANE + shift, LANE), 1)
        return value + jnp.where(ends, fixes, 0.0)

    def fill_child(f, carry):
        for b in range(blocks):
            high, low = halves(payload(f, b, in_arrived, out_arrived))
            both = jnp.concatenate([high, low], axis=1)
            value = jnp.dot(both, group[...], preferred_element_type=F32) * (1.0 / 9.0)
            for x in range(3 * b, 3 * b + 3):
                row = row_of(mask, x)
                for c in range(chunks):
                    piece = x * chunks + c
                    at = pl.ds(f * size + piece, levels, stride=step)
                    total = piece_of(f, piece) + value[:, chunk(c)]
                    buf[at, :] = total * row[:, chunk(c)]
        copy(f).start()
        return carry

    def fill_plain(f, carry):
        for x in range(cols):
            row = row_of(mask, x)
            for c in range(chunks):
                piece = x * chunks + c
                at = pl.ds(f * size + piece, levels, stride=step)
                buf[at, :] = piece_of(f, piece) * row[:, chunk(c)]
        return carry

    def fill_parent(f, carry):
        fill_plain(f, carry)
        for b in range(blocks):
            delta = payload(f, b, in_arrived, out_arrived) - payload(f, b, in_sent, out_sent)
            wide = jnp.concatenate([delta, jnp.zeros((levels, rows - LANE), F32)], 1)
            x = nest_x[0] + b
            value = pltpu.roll(wide, nest_y[0], 1) * row_of(mask, x)
            for c in range(chunks):
                at = pl.ds(f * size + x * chunks + c, levels, stride=step)
                buf[at, :] = buf[at, :] + value[:, chunk(c)]
        copy(f).start()
        return carry

    @pl.when(is_child[0] == 1)
    def _():
        ids = lax.broadcasted_iota(jnp.int32, group.shape, 0)
        ids = jnp.where(ids < LANE, ids, ids - LANE)
        group[...] = jnp.where(lane_ids(group.shape) // 3 == ids, 1.0, 0.0).astype(jnp.bfloat16)
        lax.fori_loop(0, fields, fill_child, 0)

    @pl.when(is_child[0] == 0)
    def _():
        lax.fori_loop(0, fields, fill_parent, 0)

    for f in range(fields):
        copy(f).wait()


def finish(is_child, nests, tile, mask, arrived, sent, dims):
    fields, levels, cols, chunks = dims
    rows = chunks * LANE
    size = (fields * levels * cols * chunks, LANE)
    return pl.pallas_call(
        functools.partial(finish_kernel, levels),
        in_specs=[SMEM] * 3 + [VMEM] * 6,
        out_specs=HBM,
        out_shape=pltpu.HBM(size, F32),
        scratch_shapes=[
            pltpu.VMEM(size, F32),
            pltpu.VMEM((2 * LANE, rows), jnp.bfloat16),
            pltpu.SemaphoreType.DMA((fields,)),
        ],
        compiler_params=pltpu.CompilerParams(vmem_limit_bytes=16 * MIB),
        cost_estimate=COST,
        name="finish",
    )(is_child, *nests, in_vmem(tile), mask, *arrived, *sent)


def from_neighbours(first, second, axis):
    size = lax.axis_size(axis)
    inner = [(i, i + 1) for i in range(1, size - 1, 2)]
    one = swapped(first, axis, 1)
    return one, lax.ppermute(second, axis, inner + [(j, i) for i, j in inner])


def swapped(value, axis, mask):
    return lax.ppermute(value, axis, [(i, i ^ mask) for i in range(lax.axis_size(axis))])


def places_of(cells, dims):
    _, levels, cols, chunks = dims
    rows = chunks * LANE
    column, inside = cells // (cols * rows), cells % (cols * rows)
    at = (column // levels) * (cols * chunks) + inside // LANE
    return ((at * PAD + column % levels) << 7) | (inside % LANE)


def local(
    adjoint_state,
    land_mask,
    diffusivity,
    mixing,
    nudging,
    nest_x,
    nest_y,
    obs_forcing,
    obs_cell,
    obs_count,
):
    _, fields, levels, cols, rows = adjoint_state.shape
    chunks = rows // LANE
    dims = (fields, levels, cols, chunks)
    state5 = adjoint_state.reshape(fields, levels, cols, 1, rows)
    state2 = adjoint_state.reshape(fields * levels * cols * chunks, LANE)
    mask = land_mask.reshape(cols, 1, rows)
    kappa = diffusivity.reshape(cols, 1, rows)
    mixing = mixing.reshape(fields, levels, 1, levels)
    peers, across = lax.axis_size("ty"), lax.axis_size("tx")
    assert peers == 4 and across & (across - 1) == 0 and 2 * fields * cols <= LANE
    assert levels <= PAD and cols % 3 == 0 and rows == 3 * LANE
    row = lax.axis_index("ty").astype(jnp.int32)
    column = lax.axis_index("tx").astype(jnp.int32)
    ty = row.reshape(1)
    is_child = (lax.axis_index("grp") == 0).astype(jnp.int32).reshape(1)
    nests = (nest_x, nest_y)

    forcing = obs_forcing[0, 0]
    dests = forcing.shape[1]
    places = places_of(obs_cell[0, :, :, 0], dims)
    counts = obs_count.reshape(1, -1)
    other = swapped(forcing, "tx", 1)
    tx = column.reshape(1)
    x_sent = x_edges(tx, state5, mask)
    x_halos = from_neighbours(*x_sent, "tx")
    places, state2 = lax.optimization_barrier((places, state2))
    matrices, parcel, in_sent, base = front(
        is_child, state2, mask, kappa, nudging, mixing, nests, forcing, other, dims
    )
    first = swapped(parcel, "ty", 1)
    in_arrived = swapped(in_sent, "grp", 1)
    parcel = repack(parcel, first, 2 * dests, PAD)
    parcel, x_halos = lax.optimization_barrier((parcel, x_halos))
    second = swapped(parcel, "ty", 3)
    firsts = (first, second)
    seen = repack(parcel, second, 4 * dests, 0)
    for n in range(1, across.bit_length() - 2):
        seen = jnp.concatenate([seen, swapped(seen, "tx", 1 << n)])
    seen = (seen, swapped(seen, "tx", across // 2))
    out_sent, ahead = outer(
        is_child, tx, ty, state2, matrices, base, kappa, nudging, x_halos, firsts, nests, dims, peers
    )
    out_sent, in_arrived = lax.optimization_barrier((out_sent, in_arrived))
    out_arrived = swapped(out_sent, "grp", 1)
    tile = tile_of(tx, ty, state2, mask, matrices, kappa, x_halos, firsts, ahead, dims, peers)
    tile = observe(ty, tx, places, counts, seen, tile, dests, across)
    arrived, sent = (in_arrived, out_arrived), (in_sent, out_sent)
    out = finish(is_child, nests, tile, mask, arrived, sent, dims)
    return out.reshape(adjoint_state.shape)


def solution(mesh):
    in_specs = (
        P("grp", None, None, "tx", "ty"),
        P("grp", "tx", "ty"),
        P("grp", "tx", "ty"),
        P("grp", None, None, None),
        P("tx", "ty"),
        P(("ty", "tx")),
        P(("ty", "tx")),
        P("grp", ("ty", "tx"), None, None),
        P("grp", None, None, ("ty", "tx")),
        P("grp", None, ("ty", "tx")),
    )
    out_specs = P("grp", None, None, "tx", "ty")
    return jax.shard_map(local, mesh=mesh, in_specs=in_specs, out_specs=out_specs, check_vma=False)
```

```python
import functools

import jax
import jax.numpy as jnp
from jax import lax
from jax.experimental import pallas as pl
from jax.experimental.pallas import tpu as pltpu
from jax.sharding import PartitionSpec as P

LANE = 128
PAD = 56
DEPTH = 64
MIB = 1 << 20
HBM = pl.BlockSpec(memory_space=pltpu.HBM)
SMEM = pl.BlockSpec(memory_space=pltpu.SMEM)
VMEM = pl.BlockSpec(memory_space=pltpu.VMEM)
F32 = jnp.float32
COST = pl.CostEstimate(flops=10**10, bytes_accessed=10**8, transcendentals=0)


def lane_ids(shape):
    return lax.broadcasted_iota(jnp.int32, shape, len(shape) - 1)


def row_of(ref, x):
    return ref[x].astype(F32)


def chunk(c):
    return slice(c * LANE, (c + 1) * LANE)


def in_hbm(value):
    return pltpu.with_memory_space_constraint(value, pltpu.HBM)


def in_vmem(value):
    return pltpu.with_memory_space_constraint(value, pltpu.VMEM)


def x_edges_kernel(tx, state, mask, first, second, ahead, buf, mask_buf, sems):
    fields, _, cols = state.shape[:3]
    even = lax.rem(tx[0], 2) == 0
    ends = (jnp.where(even, cols - 1, 0), jnp.where(even, 0, cols - 1))
    copies = [pltpu.make_async_copy(mask, mask_buf, sems.at[2 * fields])]
    for n, x in enumerate(ends):
        for f in range(fields):
            copies.append(
                pltpu.make_async_copy(state.at[f, :, x], buf.at[n, f], sems.at[n * fields + f])
            )
    copies.append(pltpu.make_async_copy(state.at[0], ahead, sems.at[2 * fields + 1]))
    for copy in copies:
        copy.start()
    copies[0].wait()
    for n, (x, out) in enumerate(zip(ends, (first, second))):
        for f in range(fields):
            copies[1 + n * fields + f].wait()
            out[f] = buf[n, f] * row_of(mask_buf, x)[None]
    copies[-1].wait()


def x_edges(tx, state5, mask):
    fields, levels, cols, _, rows = state5.shape
    edge = (fields, levels, 1, rows)
    return pl.pallas_call(
        x_edges_kernel,
        in_specs=[SMEM, HBM, HBM],
        out_specs=[VMEM] * 3,
        out_shape=[pltpu.VMEM(edge, F32)] * 2 + [pltpu.VMEM(state5.shape[1:], F32)],
        scratch_shapes=[
            pltpu.VMEM((2,) + edge, F32),
            pltpu.VMEM(mask.shape, jnp.int32),
            pltpu.SemaphoreType.DMA((2 * fields + 2,)),
        ],
        compiler_params=pltpu.CompilerParams(vmem_limit_bytes=8 * MIB),
        cost_estimate=COST,
        name="x_edges",
    )(tx, in_hbm(state5), in_hbm(mask))


def x_halos_of(tx, first, second, f):
    one, two = first[f, :, 0, :], second[f, :, 0, :]
    even = lax.rem(tx[0], 2) == 0
    return jnp.where(even, two, one), jnp.where(even, one, two)


def spread_of(here, above, below, kappa, edge=None):
    rows = here.shape[1]
    lanes = lane_ids((here.shape[0], LANE))
    edge = 0.0 if edge is None else edge
    before = pltpu.roll(here, 1, 1)
    after = pltpu.roll(here, rows - 1, 1)
    before = jnp.concatenate([jnp.where(lanes == 0, edge, before[:, :LANE]), before[:, LANE:]], 1)
    after = jnp.concatenate(
        [after[:, :-LANE], jnp.where(lanes == LANE - 1, edge, after[:, -LANE:])], 1
    )
    return here + kappa * (above + below + before + after - 4.0 * here)


def halves(value):
    high = value.astype(jnp.bfloat16)
    return high, (value - high.astype(F32)).astype(jnp.bfloat16)


def deepened(value):
    return jnp.concatenate([value, jnp.zeros((DEPTH - value.shape[0], value.shape[1]), F32)], 0)


def fill_matrix(levels, mixing, square, matrix):
    square[:levels, :levels] = mixing
    value = square[...]
    high = value.astype(jnp.bfloat16).astype(F32)
    matrix[:DEPTH, :] = (high + pltpu.roll(high, DEPTH, 1)).astype(jnp.bfloat16)
    matrix[DEPTH:, :] = (value - high).astype(jnp.bfloat16)


def fill_stack(stack, part, value):
    high, low = halves(value)
    stack[:DEPTH, part] = high
    stack[DEPTH:, part] = low


def mix(matrix, stack):
    both = jnp.dot(matrix, stack, preferred_element_type=F32)
    return both[:DEPTH] + both[DEPTH:]


def fill_group(group):
    rows = group.shape[0] // 2
    ids = lax.broadcasted_iota(jnp.int32, group.shape, 0)
    ids = jnp.where(ids < rows, ids, ids - rows) // 3
    group[...] = jnp.where(ids == lane_ids(group.shape), 1.0, 0.0).astype(jnp.bfloat16)


def grouped(wide, group):
    return jnp.dot(wide, group, preferred_element_type=F32)


def aligned(index, size):
    return pl.ds(pl.multiple_of(index * size, size), size)


def packed(rows_of, cols):
    parts = []
    for x in range(cols):
        first, last = rows_of(x)
        lanes = lane_ids(first.shape)
        parts.append(jnp.where(lanes == 0, first, jnp.where(lanes == LANE - 1, last, 0.0)))
    shift = 2
    while len(parts) > 1:
        pairs = [parts[n : n + 2] for n in range(0, len(parts), 2)]
        parts = [p[0] + pltpu.roll(p[1], shift, 1) if len(p) == 2 else p[0] for p in pairs]
        shift *= 2
    return parts[0]


def fill_masked(levels, state, f, mask, masked):
    cols, _, rows = masked.shape
    chunks = rows // LANE
    step = cols * chunks
    for x in range(cols):
        row = row_of(mask, x)
        masked[x, PAD - 8 :, :] = jnp.zeros((8, rows), F32)
        for c in range(chunks):
            at = pl.ds(f * (levels * step) + x * chunks + c, levels, stride=step)
            masked[x, :levels, chunk(c)] = state[at, :] * row[:, chunk(c)]


TERMS = 11


def join_weights(bs, cols, kappa, nudging, weights):
    rows = weights.shape[1]
    ids = lane_ids((1, rows))
    for i, b in enumerate(bs):
        own = range(3 * b, 3 * b + 3)
        both = {x: nudging[x : x + 1, :] * kappa[x] for x in own}
        for n, x in enumerate(range(3 * b - 1, 3 * b + 4)):
            total = None
            for near in (x - 1, x + 1):
                if near in both:
                    total = both[near] if total is None else total + both[near]
            if x in both:
                total = total + (nudging[x : x + 1, :] - 4.0 * both[x])
            weights[i * TERMS + n : i * TERMS + n + 1, :] = total
        for n, x in enumerate(own):
            at = i * TERMS + 5 + n
            value = jnp.where(ids == rows - 1, 0.0, pltpu.roll(both[x], rows - 1, 1))
            weights[at : at + 1, :] = value
            value = jnp.where(ids == 0, 0.0, pltpu.roll(both[x], 1, 1))
            weights[at + 3 : at + 4, :] = value


def child_rows(f, bs, masked, weights, wide):
    cols, _, rows = masked.shape[1:]
    for i, b in enumerate(bs):

        def term(n, x):
            at = i * TERMS + n
            return weights[at : at + 1, :] * masked[f, x]

        total = None
        for n, x in enumerate(range(3 * b - 1, 3 * b + 4)):
            if 0 <= x < cols:
                total = term(n, x) if total is None else total + term(n, x)
        for side, shift in ((5, 1), (8, rows - 1)):
            value = term(side, 3 * b) + term(side + 1, 3 * b + 1) + term(side + 2, 3 * b + 2)
            total = total + pltpu.roll(value, shift, 1)
        at = aligned(f * len(bs) + i, DEPTH)
        wide[at, :rows], wide[at, rows:] = halves(deepened(total))


def parent_rows(f, bs, nest_x, nest_y, masked, kappa, stack):
    cols, _, rows = masked.shape[1:]
    back = lax.rem(rows - nest_y[0], rows)
    for i, b in enumerate(bs):
        x = nest_x[0] + b
        above = masked[f, jnp.maximum(x - 1, 0)]
        below = masked[f, jnp.minimum(x + 1, cols - 1)]
        if b == 0:
            above = jnp.where(x == 0, 0.0, above)
        if b == cols // 3 - 1:
            below = jnp.where(x == cols - 1, 0.0, below)
        value = spread_of(masked[f, x], above, below, kappa[x])
        value = deepened(pltpu.roll(value, back, 1)[:, :LANE])
        fill_stack(stack.at[f], chunk(i), value)


def mix_rows(bs, is_child, wide, group, stack, matrices, emit):
    fields = stack.shape[0]

    @pl.when(is_child[0] == 1)
    def _():
        value = grouped(wide[...], group[...])
        for f in range(fields):
            for i in range(len(bs)):
                at = (f * len(bs) + i) * DEPTH
                fill_stack(stack.at[f], chunk(i), value[at : at + DEPTH])

    for f in range(fields):
        emit(f, mix(matrices[f], stack[f]))


def row_scratch(bs, fields, rows):
    return [
        pltpu.VMEM((-(-len(bs) * TERMS // 8) * 8, rows), F32),
        pltpu.VMEM((fields * len(bs) * DEPTH, 2 * rows), jnp.bfloat16),
        pltpu.VMEM((fields, 2 * DEPTH, len(bs) * LANE), jnp.bfloat16),
        pltpu.VMEM((2 * rows, LANE), jnp.bfloat16),
    ]


def front_kernel(
    levels, bs, is_child, state, mask, kappa, nudging, mixing, nest_x, nest_y, forcing, other, ahead,
    cells, masked, matrices, parcel, inner, places,
    buf, mask_buf, kappa_buf, nudging_buf, mixing_buf, square, weights, wide, stack, group, sems,
):
    fields, cols, _, rows = masked.shape
    chunks = rows // LANE
    step = cols * chunks
    size = levels * step

    def copy(f):
        at = pl.ds(f * size, size)
        return pltpu.make_async_copy(state.at[at], buf.at[at], sems.at[f])

    pairs = (
        (mask, mask_buf),
        (kappa, kappa_buf),
        (nudging, nudging_buf),
        (mixing, mixing_buf),
    )
    smalls = [
        pltpu.make_async_copy(source, target, sems.at[fields + n])
        for n, (source, target) in enumerate(pairs)
    ]
    for small in smalls:
        small.start()
    for f in range(1, fields):
        copy(f).start()
    square[...] = jnp.zeros_like(square)
    cell = cells[...]
    column, inside = cell // (cols * rows), lax.rem(cell, cols * rows)
    piece = (column // levels) * step + inside // LANE
    place = (piece * PAD + lax.rem(column, levels)) * LANE + lax.rem(inside, LANE)
    places[...] = place
    for small in smalls:
        small.wait()

    @pl.when(is_child[0] == 1)
    def _():
        fill_group(group)
        join_weights(bs, cols, kappa_buf, nudging_buf, weights)

    def field(f, total_edges, first=False):
        fill_matrix(levels, mixing_buf[f, :, 0, :], square, matrices.at[f])
        if first:
            fill_masked(levels, ahead, f, mask_buf, masked.at[f])
        else:
            copy(f).wait()
            fill_masked(levels, buf, f, mask_buf, masked.at[f])
        own_edges = packed(
            lambda x: (masked[f, x, :, :LANE], masked[f, x, :, rows - LANE :]), cols
        )

        @pl.when(is_child[0] == 1)
        def _():
            child_rows(f, bs, masked, weights, wide)

        @pl.when(is_child[0] == 0)
        def _():
            parent_rows(f, bs, nest_x, nest_y, masked, kappa_buf, stack)

        return total_edges + pltpu.roll(own_edges, 2 * f * cols, 1)

    own_edges = field(0, jnp.zeros((PAD, LANE), F32), first=True)
    parcel[:PAD, :] = lax.fori_loop(1, fields, field, own_edges)
    slots, dests = forcing.shape
    parcel[PAD:, :] = jnp.zeros((parcel.shape[0] - PAD, LANE), F32)
    parcel[PAD : PAD + slots, :dests] = forcing[...]
    if 2 * dests <= LANE:
        parcel[PAD : PAD + slots, dests : 2 * dests] = other[...]
    else:
        parcel[PAD + slots :, :dests] = other[...]

    def emit(f, mixed):
        for i in range(len(bs)):
            at = pl.ds(f * levels * len(bs) + i, levels, stride=len(bs))
            inner[at, :] = mixed[:levels, chunk(i)]

    mix_rows(bs, is_child, wide, group, stack, matrices, emit)


def front(is_child, state2, mask, kappa, nudging, mixing, nests, forcing, other, ahead, cells, dims):
    fields, levels, cols, chunks = dims
    rows = chunks * LANE
    bs = tuple(range(1, cols // 3 - 1))
    arrays = (state2, mask, kappa, nudging, mixing)
    slots, dests = forcing.shape
    height = slots if 2 * dests <= LANE else 2 * slots
    return pl.pallas_call(
        functools.partial(front_kernel, levels, bs),
        in_specs=[SMEM] + [HBM] * 5 + [SMEM] * 2 + [VMEM] * 4,
        out_specs=[VMEM] * 5,
        out_shape=[
            pltpu.VMEM((fields, cols, PAD, rows), F32),
            pltpu.VMEM((fields, 2 * DEPTH, 2 * DEPTH), jnp.bfloat16),
            pltpu.VMEM((PAD + height, LANE), F32),
            pltpu.VMEM((fields * levels * len(bs), LANE), F32),
            pltpu.VMEM(cells.shape, jnp.int32),
        ],
        scratch_shapes=[
            pltpu.VMEM(state2.shape, F32),
            pltpu.VMEM(mask.shape, jnp.int32),
            pltpu.VMEM(kappa.shape, F32),
            pltpu.VMEM(nudging.shape, F32),
            pltpu.VMEM(mixing.shape, F32),
            pltpu.VMEM((DEPTH, LANE), F32),
        ]
        + row_scratch(bs, fields, rows)
        + [pltpu.SemaphoreType.DMA((fields + 4,))],
        compiler_params=pltpu.CompilerParams(vmem_limit_bytes=16 * MIB),
        cost_estimate=COST,
        name="front",
    )(is_child, *map(in_hbm, arrays), *nests, forcing, other, in_vmem(ahead), cells)


def base_kernel(
    levels, bs, is_child, nest_x, nest_y, masked, matrices, kappa, nudging, base,
    weights, wide, stack, group,
):
    fields, cols = masked.shape[:2]

    @pl.when(is_child[0] == 1)
    def _():
        fill_group(group)
        join_weights(bs, cols, kappa, nudging, weights)

        def field(f, carry):
            child_rows(f, bs, masked, weights, wide)
            return carry

        lax.fori_loop(0, fields, field, 0)

    @pl.when(is_child[0] == 0)
    def _():
        def field(f, carry):
            parent_rows(f, bs, nest_x, nest_y, masked, kappa, stack)
            return carry

        lax.fori_loop(0, fields, field, 0)

    def emit(f, mixed):
        base[f, :, :] = mixed[:PAD, :]

    mix_rows(bs, is_child, wide, group, stack, matrices, emit)


def base_of(is_child, nests, masked, matrices, kappa, nudging, dims):
    fields, levels, cols, chunks = dims
    rows = chunks * LANE
    bs = (0, cols // 3 - 1)
    return pl.pallas_call(
        functools.partial(base_kernel, levels, bs),
        in_specs=[SMEM] * 3 + [VMEM] * 4,
        out_specs=VMEM,
        out_shape=pltpu.VMEM((fields, PAD, 2 * LANE), F32),
        scratch_shapes=row_scratch(bs, fields, rows),
        compiler_params=pltpu.CompilerParams(vmem_limit_bytes=12 * MIB),
        cost_estimate=COST,
        name="base",
    )(is_child, *nests, in_vmem(masked), matrices, kappa, nudging)


def merged(own, other, width):
    if 2 * width <= LANE:
        return own + pltpu.roll(other, width, 1)
    return jnp.concatenate([own, other], axis=0)


def repack_kernel(width, edges, parcel, arrived, out):
    if edges:
        out[:edges, :] = parcel[:edges, :]
    out[edges:, :] = merged(parcel[PAD:, :], arrived[PAD:, :], width)


def repack(parcel, arrived, width, edges):
    height = (parcel.shape[0] - PAD) * (1 if 2 * width <= LANE else 2)
    return pl.pallas_call(
        functools.partial(repack_kernel, width, edges),
        in_specs=[VMEM] * 2,
        out_specs=VMEM,
        out_shape=pltpu.VMEM((edges + height, LANE), F32),
        compiler_params=pltpu.CompilerParams(vmem_limit_bytes=4 * MIB),
        name="repack",
    )(parcel, arrived)


def y_halos(ty, peers, first, second):
    one, two = first[:PAD, :], second[:PAD, :]
    even = (lax.rem(ty[0], 2) == 0).astype(F32)
    odd = 1.0 - even
    before = (two * even + one * odd) * (ty[0] > 0).astype(F32)
    after = (one * even + two * odd) * (ty[0] < peers - 1).astype(F32)
    low = lax.rem(lane_ids((PAD, LANE)), 2) == 0
    return jnp.where(low, pltpu.roll(before, 1, 1), pltpu.roll(after, LANE - 1, 1))


def outer_kernel(
    levels, peers, is_child, tx, ty, state, matrices, base, kappa, nudging, x_first, x_second,
    first, second, nest_x, nest_y, out, ahead, sides, wide, stack, group, sem,
):
    fields = matrices.shape[0]
    cols, _, rows = kappa.shape
    blocks = cols // 3
    lanes = lane_ids((PAD, LANE))
    turned = lax.rem(lanes + 1, LANE)
    copy = pltpu.make_async_copy(state.at[pl.ds(0, ahead.shape[0])], ahead, sem)
    copy.start()
    sides[...] = jnp.zeros_like(sides)
    halo = y_halos(ty, peers, first, second)

    def weighted(row_of_x):
        one = packed(lambda x: (row_of_x(x)[:, :LANE], row_of_x(x)[:, rows - LANE :]), cols)
        total = one
        for f in range(1, fields):
            total = total + pltpu.roll(one, 2 * f * cols, 1)
        return halo * total

    def fill_fix(value):
        for f in range(fields):
            fill_stack(stack.at[f], chunk(2), deepened(value))

    @pl.when(is_child[0] == 1)
    def _():
        fill_group(group)
        for f in range(fields):
            for n, side in enumerate(x_halos_of(tx, x_first, x_second, f)):
                x = (0, cols - 1)[n]
                at = (f * 2 + n) * DEPTH
                sides[at : at + levels, :] = side * (nudging[x : x + 1, :] * kappa[x])
        wide[:, :rows], wide[:, rows:] = halves(sides[...])
        value = grouped(wide[...], group[...])
        for f in range(fields):
            for n in range(2):
                at = (f * 2 + n) * DEPTH
                fill_stack(stack.at[f], chunk(n), value[at : at + DEPTH])
        part = weighted(lambda x: nudging[x : x + 1, :] * kappa[x])
        fill_fix(part + pltpu.roll(part, LANE - 2, 1) + pltpu.roll(part, LANE - 4, 1))

    @pl.when(is_child[0] == 0)
    def _():
        back = lax.rem(rows - nest_y[0], rows)
        reached = (nest_x[0] == 0, nest_x[0] + blocks == cols)
        for f in range(fields):
            for n, side in enumerate(x_halos_of(tx, x_first, x_second, f)):
                at = (f * 2 + n) * DEPTH
                weight = kappa[(0, cols - 1)[n]] * reached[n].astype(F32)
                sides[at : at + levels, :] = side * weight
                value = pltpu.roll(sides[at : at + DEPTH, :], back, 1)[:, :LANE]
                fill_stack(stack.at[f], chunk(n), value)
        starts = (nest_y[0] == 0).astype(F32)
        finals = (nest_y[0] == rows - LANE).astype(F32)
        part = weighted(lambda x: kappa[x])
        part = part * jnp.where(lax.rem(lanes, 2) == 0, starts, finals)
        value = jnp.zeros((PAD, LANE), F32)
        for b in range(blocks):
            shift = lax.rem(LANE + 4 * b - 2 * nest_x[0], LANE)
            here = lax.rem(turned, 2 * cols) // 2 == 3 * b
            value = jnp.where(here, pltpu.roll(part, shift, 1), value)
        fill_fix(value)

    fixes = jnp.zeros((PAD, LANE), F32)
    for f in range(fields):
        mixed = mix(matrices[f], stack[f])
        for n in range(2):
            at = pl.ds(f * (2 * levels) + n, levels, stride=2)
            out[at, :] = base[f, :levels, chunk(n)] + mixed[:levels, chunk(n)]
        fixes = jnp.where(turned // (2 * cols) == f, mixed[:PAD, chunk(2)], fixes)
    out[out.shape[0] - PAD :, :] = fixes
    copy.wait()


def outer(
    is_child, tx, ty, state2, matrices, base, kappa, nudging, x_halos, firsts, nests, dims, peers
):
    fields, levels, cols, chunks = dims
    rows = chunks * LANE
    height = -(-fields * 2 * levels // 8) * 8 + PAD
    return pl.pallas_call(
        functools.partial(outer_kernel, levels, peers),
        in_specs=[SMEM] * 3 + [HBM] + [VMEM] * 8 + [SMEM] * 2,
        out_specs=[VMEM] * 2,
        out_shape=[
            pltpu.VMEM((height, LANE), F32),
            pltpu.VMEM((state2.shape[0] // fields, LANE), F32),
        ],
        scratch_shapes=[
            pltpu.VMEM((fields * 2 * DEPTH, rows), F32),
            pltpu.VMEM((fields * 2 * DEPTH, 2 * rows), jnp.bfloat16),
            pltpu.VMEM((fields, 2 * DEPTH, 3 * LANE), jnp.bfloat16),
            pltpu.VMEM((2 * rows, LANE), jnp.bfloat16),
            pltpu.SemaphoreType.DMA,
        ],
        compiler_params=pltpu.CompilerParams(vmem_limit_bytes=12 * MIB),
        name="outer",
    )(is_child, tx, ty, in_hbm(state2), matrices, base, kappa, nudging, *x_halos, *firsts, *nests)


def tile_kernel(
    levels, peers, tx, ty, state, mask, matrices, kappa, x_first, x_second, first, second, ahead,
    out, buf, masked, sides, halo, stack_a, stack_b, sems,
):
    cols, _, rows = masked.shape
    chunks = rows // LANE
    size = levels * cols * chunks
    fields = state.shape[0] // size

    def copy(f):
        at = pl.ds(f * size, size)
        return pltpu.make_async_copy(state.at[at], buf.at[at], sems.at[f])

    for f in range(1, fields):
        copy(f).start()
    sides[...] = jnp.zeros_like(sides)
    halo[...] = y_halos(ty, peers, first, second)
    pair = 2

    def field(f, carry, leading=False):
        if leading:
            fill_masked(levels, ahead, f, mask, masked)
        else:
            copy(f).wait()
            fill_masked(levels, buf, f, mask, masked)
        for n, side in enumerate(x_halos_of(tx, x_first, x_second, f)):
            sides[n, :levels, :] = side
        for x0 in range(0, cols, pair):
            stack = (stack_a, stack_b)[x0 // pair % 2]
            for x in range(x0, x0 + pair):
                above = masked[x - 1] if x > 0 else sides[0]
                below = masked[x + 1] if x < cols - 1 else sides[1]
                shift = lax.rem(LANE - 2 * (f * cols + x), LANE)
                edge = pltpu.roll(halo[...], lax.rem(LANE + shift, LANE), 1)
                value = spread_of(masked[x], above, below, kappa[x], edge)
                part = slice((x - x0) * rows, (x - x0 + 1) * rows)
                fill_stack(stack, part, deepened(value))
            mixed = mix(matrices[f], stack[...])
            for n in range(pair * chunks):
                out[aligned((f * cols + x0) * chunks + n, PAD), :] = mixed[:PAD, chunk(n)]
        return carry

    field(0, 0, leading=True)
    lax.fori_loop(1, fields, field, 0)


def tile_of(tx, ty, state2, mask, matrices, kappa, x_halos, firsts, ahead, dims, peers):
    fields, levels, cols, chunks = dims
    rows = chunks * LANE
    return pl.pallas_call(
        functools.partial(tile_kernel, levels, peers),
        in_specs=[SMEM] * 2 + [HBM] + [VMEM] * 8,
        out_specs=VMEM,
        out_shape=pltpu.VMEM((fields * cols * chunks * PAD, LANE), F32),
        scratch_shapes=[
            pltpu.VMEM(state2.shape, F32),
            pltpu.VMEM((cols, PAD, rows), F32),
            pltpu.VMEM((2, PAD, rows), F32),
            pltpu.VMEM((PAD, LANE), F32),
            pltpu.VMEM((2 * DEPTH, 2 * rows), jnp.bfloat16),
            pltpu.VMEM((2 * DEPTH, 2 * rows), jnp.bfloat16),
            pltpu.SemaphoreType.DMA((fields,)),
        ],
        compiler_params=pltpu.CompilerParams(vmem_limit_bytes=16 * MIB),
        cost_estimate=COST,
        name="tile",
    )(tx, ty, in_hbm(state2), mask, matrices, kappa, *x_halos, *firsts, in_vmem(ahead))


def observe_kernel(dests, across, row, column, counts, placed, mine, theirs, _, tile, places, sem):
    copy = pltpu.make_async_copy(placed, places, sem)
    copy.start()
    copy.wait()
    lanes = lane_ids((1, LANE))
    slots = places.shape[1]
    ty, tx = row[0], column[0]
    me = ty * across + tx
    half = mine.shape[0] // slots * (LANE // dests)

    def source(first, ref, n, carry):
        g = first + n
        origin = (((g >> 1) & 1) ^ (3 * ((g >> 2) & 1)) ^ ty) * across
        origin = origin + (((g & 1) | ((g >> 3) << 1)) ^ tx)
        lane_in = lax.rem(n, LANE // dests) * dests + me
        block = lax.div(n, LANE // dests) * slots
        count = counts[0, origin]
        for k in range(0, slots, 2):
            ats, adds = [], []
            for m in range(k, k + 2):
                place = places[origin, m]
                lane = place & (LANE - 1)
                value = pltpu.roll(ref[pl.ds(block + m, 1), :], (lane - lane_in) & (LANE - 1), 1)
                ats.append(place >> 7)
                adds.append(jnp.where(lanes == jnp.where(m < count, lane, LANE), value, 0.0))
            olds = [tile[pl.ds(at, 1), :] for at in ats]
            also = jnp.where(ats[0] == ats[1], adds[0], 0.0)
            tile[pl.ds(ats[0], 1), :] = olds[0] + adds[0]
            tile[pl.ds(ats[1], 1), :] = olds[1] + adds[1] + also
        return carry

    lax.fori_loop(0, half, functools.partial(source, 0, mine), 0)
    lax.fori_loop(0, half, functools.partial(source, half, theirs), 0)


def observe(row, column, places, counts, seen, tile, dests, across):
    return pl.pallas_call(
        functools.partial(observe_kernel, dests, across),
        in_specs=[SMEM] * 3 + [VMEM] * 4,
        out_specs=VMEM,
        out_shape=pltpu.VMEM(tile.shape, F32),
        scratch_shapes=[pltpu.SMEM(places.shape, jnp.int32), pltpu.SemaphoreType.DMA],
        input_output_aliases={6: 0},
        compiler_params=pltpu.CompilerParams(vmem_limit_bytes=4 * MIB),
        name="observe",
    )(row, column, counts, places, *seen, in_vmem(tile))


def finish_kernel(
    levels, is_child, nest_x, nest_y, tile, mask, in_arrived, out_arrived, in_sent, out_sent,
    out, buf, group, sems,
):
    cols = mask.shape[0]
    rows = mask.shape[2]
    chunks = rows // LANE
    step = cols * chunks
    size = levels * step
    fields = out.shape[0] // size
    blocks = cols // 3
    inner = blocks - 2
    lanes = lane_ids((levels, LANE))
    ends = jnp.logical_or(lanes == 0, lanes == LANE - 1)
    height = out_arrived.shape[0]

    def copy(f):
        at = pl.ds(f * size, size)
        return pltpu.make_async_copy(buf.at[at], out.at[at], sems.at[f])

    def piece_of(f, piece):
        return tile[pl.ds(pl.multiple_of((f * step + piece) * PAD, 8), levels), :]

    def payload(f, b, inner_ref, outer_ref):
        if b in (0, blocks - 1):
            value = outer_ref[pl.ds(f * (2 * levels) + min(b, 1), levels, stride=2), :]
        else:
            value = inner_ref[pl.ds(f * (levels * inner) + b - 1, levels, stride=inner), :]
        fixes = outer_ref[height - PAD : height - PAD + levels, :]
        shift = lax.rem(LANE - 2 * (f * cols + 3 * b), LANE)
        fixes = pltpu.roll(fixes, lax.rem(LANE + shift, LANE), 1)
        return value + jnp.where(ends, fixes, 0.0)

    def fill_child(f, carry):
        for b in range(blocks):
            high, low = halves(payload(f, b, in_arrived, out_arrived))
            both = jnp.concatenate([high, low], axis=1)
            value = jnp.dot(both, group[...], preferred_element_type=F32) * (1.0 / 9.0)
            for x in range(3 * b, 3 * b + 3):
                row = row_of(mask, x)
                for c in range(chunks):
                    piece = x * chunks + c
                    at = pl.ds(f * size + piece, levels, stride=step)
                    total = piece_of(f, piece) + value[:, chunk(c)]
                    buf[at, :] = total * row[:, chunk(c)]
        copy(f).start()
        return carry

    def fill_plain(f, carry):
        for x in range(cols):
            row = row_of(mask, x)
            for c in range(chunks):
                piece = x * chunks + c
                at = pl.ds(f * size + piece, levels, stride=step)
                buf[at, :] = piece_of(f, piece) * row[:, chunk(c)]
        return carry

    def fill_parent(f, carry):
        fill_plain(f, carry)
        for b in range(blocks):
            delta = payload(f, b, in_arrived, out_arrived) - payload(f, b, in_sent, out_sent)
            wide = jnp.concatenate([delta, jnp.zeros((levels, rows - LANE), F32)], 1)
            x = nest_x[0] + b
            value = pltpu.roll(wide, nest_y[0], 1) * row_of(mask, x)
            for c in range(chunks):
                at = pl.ds(f * size + x * chunks + c, levels, stride=step)
                buf[at, :] = buf[at, :] + value[:, chunk(c)]
        copy(f).start()
        return carry

    @pl.when(is_child[0] == 1)
    def _():
        ids = lax.broadcasted_iota(jnp.int32, group.shape, 0)
        ids = jnp.where(ids < LANE, ids, ids - LANE)
        group[...] = jnp.where(lane_ids(group.shape) // 3 == ids, 1.0, 0.0).astype(jnp.bfloat16)
        lax.fori_loop(0, fields, fill_child, 0)

    @pl.when(is_child[0] == 0)
    def _():
        lax.fori_loop(0, fields, fill_parent, 0)

    for f in range(fields):
        copy(f).wait()


def finish(is_child, nests, tile, mask, arrived, sent, dims):
    fields, levels, cols, chunks = dims
    rows = chunks * LANE
    size = (fields * levels * cols * chunks, LANE)
    return pl.pallas_call(
        functools.partial(finish_kernel, levels),
        in_specs=[SMEM] * 3 + [VMEM] * 6,
        out_specs=HBM,
        out_shape=pltpu.HBM(size, F32),
        scratch_shapes=[
            pltpu.VMEM(size, F32),
            pltpu.VMEM((2 * LANE, rows), jnp.bfloat16),
            pltpu.SemaphoreType.DMA((fields,)),
        ],
        compiler_params=pltpu.CompilerParams(vmem_limit_bytes=16 * MIB),
        cost_estimate=COST,
        name="finish",
    )(is_child, *nests, in_vmem(tile), mask, *arrived, *sent)


def from_neighbours(first, second, axis):
    size = lax.axis_size(axis)
    inner = [(i, i + 1) for i in range(1, size - 1, 2)]
    one = swapped(first, axis, 1)
    return one, lax.ppermute(second, axis, inner + [(j, i) for i, j in inner])


def swapped(value, axis, mask):
    return lax.ppermute(value, axis, [(i, i ^ mask) for i in range(lax.axis_size(axis))])


def local(
    adjoint_state,
    land_mask,
    diffusivity,
    mixing,
    nudging,
    nest_x,
    nest_y,
    obs_forcing,
    obs_cell,
    obs_count,
):
    _, fields, levels, cols, rows = adjoint_state.shape
    chunks = rows // LANE
    dims = (fields, levels, cols, chunks)
    state5 = adjoint_state.reshape(fields, levels, cols, 1, rows)
    state2 = adjoint_state.reshape(fields * levels * cols * chunks, LANE)
    mask = land_mask.reshape(cols, 1, rows)
    kappa = diffusivity.reshape(cols, 1, rows)
    mixing = mixing.reshape(fields, levels, 1, levels)
    peers, across = lax.axis_size("ty"), lax.axis_size("tx")
    assert peers == 4 and across & (across - 1) == 0 and 2 * fields * cols <= LANE
    assert levels <= PAD and cols % 3 == 0 and rows == 3 * LANE
    row = lax.axis_index("ty").astype(jnp.int32)
    column = lax.axis_index("tx").astype(jnp.int32)
    ty = row.reshape(1)
    is_child = (lax.axis_index("grp") == 0).astype(jnp.int32).reshape(1)
    nests = (nest_x, nest_y)

    forcing = obs_forcing[0, 0]
    dests = forcing.shape[1]
    counts = obs_count.reshape(1, -1)
    other = swapped(forcing, "tx", 1)
    tx = column.reshape(1)
    *x_sent, ahead = x_edges(tx, state5, mask)
    ahead = ahead.reshape(-1, LANE)
    x_halos = from_neighbours(*x_sent, "tx")
    masked, matrices, parcel, in_sent, places = front(
        is_child, state2, mask, kappa, nudging, mixing, nests, forcing, other, ahead,
        obs_cell[0, :, :, 0], dims,
    )
    base = base_of(is_child, nests, masked, matrices, kappa, nudging, dims)
    first = swapped(parcel, "ty", 1)
    in_arrived = swapped(in_sent, "grp", 1)
    parcel = repack(parcel, first, 2 * dests, PAD)
    parcel, x_halos = lax.optimization_barrier((parcel, x_halos))
    second = swapped(parcel, "ty", 3)
    firsts = (first, second)
    seen = repack(parcel, second, 4 * dests, 0)
    for n in range(1, across.bit_length() - 2):
        seen = jnp.concatenate([seen, swapped(seen, "tx", 1 << n)])
    seen = (seen, swapped(seen, "tx", across // 2))
    out_sent, ahead = outer(
        is_child, tx, ty, state2, matrices, base, kappa, nudging, x_halos, firsts, nests, dims, peers
    )
    out_sent, in_arrived = lax.optimization_barrier((out_sent, in_arrived))
    out_arrived = swapped(out_sent, "grp", 1)
    tile = tile_of(tx, ty, state2, mask, matrices, kappa, x_halos, firsts, ahead, dims, peers)
    tile = observe(ty, tx, places, counts, seen, tile, dests, across)
    arrived, sent = (in_arrived, out_arrived), (in_sent, out_sent)
    out = finish(is_child, nests, tile, mask, arrived, sent, dims)
    return out.reshape(adjoint_state.shape)


def solution(mesh):
    in_specs = (
        P("grp", None, None, "tx", "ty"),
        P("grp", "tx", "ty"),
        P("grp", "tx", "ty"),
        P("grp", None, None, None),
        P("tx", "ty"),
        P(("ty", "tx")),
        P(("ty", "tx")),
        P("grp", ("ty", "tx"), None, None),
        P("grp", None, None, ("ty", "tx")),
        P("grp", None, ("ty", "tx")),
    )
    out_specs = P("grp", None, None, "tx", "ty")
    return jax.shard_map(local, mesh=mesh, in_specs=in_specs, out_specs=out_specs, check_vma=False)
```

```python
import functools

import jax
import jax.numpy as jnp
from jax import lax
from jax.experimental import pallas as pl
from jax.experimental.pallas import tpu as pltpu
from jax.sharding import PartitionSpec as P

LANE = 128
PAD = 56
DEPTH = 64
MIB = 1 << 20
HBM = pl.BlockSpec(memory_space=pltpu.HBM)
SMEM = pl.BlockSpec(memory_space=pltpu.SMEM)
VMEM = pl.BlockSpec(memory_space=pltpu.VMEM)
F32 = jnp.float32
COST = pl.CostEstimate(flops=10**10, bytes_accessed=10**8, transcendentals=0)


def lane_ids(shape):
    return lax.broadcasted_iota(jnp.int32, shape, len(shape) - 1)


def row_of(ref, x):
    return ref[x].astype(F32)


def chunk(c):
    return slice(c * LANE, (c + 1) * LANE)


def in_hbm(value):
    return pltpu.with_memory_space_constraint(value, pltpu.HBM)


def in_vmem(value):
    return pltpu.with_memory_space_constraint(value, pltpu.VMEM)


def x_edges_kernel(tx, state, mask, first, second, ahead, buf, mask_buf, sems):
    fields, _, cols = state.shape[:3]
    even = lax.rem(tx[0], 2) == 0
    ends = (jnp.where(even, cols - 1, 0), jnp.where(even, 0, cols - 1))
    copies = [pltpu.make_async_copy(mask, mask_buf, sems.at[2 * fields])]
    for n, x in enumerate(ends):
        for f in range(fields):
            copies.append(
                pltpu.make_async_copy(state.at[f, :, x], buf.at[n, f], sems.at[n * fields + f])
            )
    copies.append(pltpu.make_async_copy(state.at[0], ahead, sems.at[2 * fields + 1]))
    for copy in copies:
        copy.start()
    copies[0].wait()
    for n, (x, out) in enumerate(zip(ends, (first, second))):
        for f in range(fields):
            copies[1 + n * fields + f].wait()
            out[f] = buf[n, f] * row_of(mask_buf, x)[None]
    copies[-1].wait()


def x_edges(tx, state5, mask):
    fields, levels, cols, _, rows = state5.shape
    edge = (fields, levels, 1, rows)
    return pl.pallas_call(
        x_edges_kernel,
        in_specs=[SMEM, HBM, HBM],
        out_specs=[VMEM] * 3,
        out_shape=[pltpu.VMEM(edge, F32)] * 2 + [pltpu.VMEM(state5.shape[1:], F32)],
        scratch_shapes=[
            pltpu.VMEM((2,) + edge, F32),
            pltpu.VMEM(mask.shape, jnp.int32),
            pltpu.SemaphoreType.DMA((2 * fields + 2,)),
        ],
        compiler_params=pltpu.CompilerParams(vmem_limit_bytes=8 * MIB),
        cost_estimate=COST,
        name="x_edges",
    )(tx, in_hbm(state5), in_hbm(mask))


def x_halos_of(tx, first, second, f):
    one, two = first[f, :, 0, :], second[f, :, 0, :]
    even = lax.rem(tx[0], 2) == 0
    return jnp.where(even, two, one), jnp.where(even, one, two)


def spread_of(here, above, below, kappa, edge=None):
    rows = here.shape[1]
    lanes = lane_ids((here.shape[0], LANE))
    edge = 0.0 if edge is None else edge
    before = pltpu.roll(here, 1, 1)
    after = pltpu.roll(here, rows - 1, 1)
    before = jnp.concatenate([jnp.where(lanes == 0, edge, before[:, :LANE]), before[:, LANE:]], 1)
    after = jnp.concatenate(
        [after[:, :-LANE], jnp.where(lanes == LANE - 1, edge, after[:, -LANE:])], 1
    )
    return here + kappa * (above + below + before + after - 4.0 * here)


def halves(value):
    high = value.astype(jnp.bfloat16)
    return high, (value - high.astype(F32)).astype(jnp.bfloat16)


def deepened(value):
    return jnp.concatenate([value, jnp.zeros((DEPTH - value.shape[0], value.shape[1]), F32)], 0)


def fill_matrix(levels, mixing, square, matrix):
    square[:levels, :levels] = mixing
    value = square[...]
    high = value.astype(jnp.bfloat16).astype(F32)
    matrix[:DEPTH, :] = (high + pltpu.roll(high, DEPTH, 1)).astype(jnp.bfloat16)
    matrix[DEPTH:, :] = (value - high).astype(jnp.bfloat16)


def fill_stack(stack, part, value):
    high, low = halves(value)
    stack[:DEPTH, part] = high
    stack[DEPTH:, part] = low


def mix(matrix, stack):
    both = jnp.dot(matrix, stack, preferred_element_type=F32)
    return both[:DEPTH] + both[DEPTH:]


def fill_group(group):
    rows = group.shape[0] // 2
    ids = lax.broadcasted_iota(jnp.int32, group.shape, 0)
    ids = jnp.where(ids < rows, ids, ids - rows) // 3
    group[...] = jnp.where(ids == lane_ids(group.shape), 1.0, 0.0).astype(jnp.bfloat16)


def grouped(wide, group):
    return jnp.dot(wide, group, preferred_element_type=F32)


def aligned(index, size):
    return pl.ds(pl.multiple_of(index * size, size), size)


def packed(rows_of, cols):
    parts = []
    for x in range(cols):
        first, last = rows_of(x)
        lanes = lane_ids(first.shape)
        parts.append(jnp.where(lanes == 0, first, jnp.where(lanes == LANE - 1, last, 0.0)))
    shift = 2
    while len(parts) > 1:
        pairs = [parts[n : n + 2] for n in range(0, len(parts), 2)]
        parts = [p[0] + pltpu.roll(p[1], shift, 1) if len(p) == 2 else p[0] for p in pairs]
        shift *= 2
    return parts[0]


def fill_masked(levels, state, f, mask, masked):
    cols, _, rows = masked.shape
    chunks = rows // LANE
    step = cols * chunks
    for x in range(cols):
        row = row_of(mask, x)
        masked[x, PAD - 8 :, :] = jnp.zeros((8, rows), F32)
        for c in range(chunks):
            at = pl.ds(f * (levels * step) + x * chunks + c, levels, stride=step)
            masked[x, :levels, chunk(c)] = state[at, :] * row[:, chunk(c)]


TERMS = 11


def join_weights(bs, cols, kappa, nudging, weights):
    rows = weights.shape[1]
    ids = lane_ids((1, rows))
    for i, b in enumerate(bs):
        own = range(3 * b, 3 * b + 3)
        both = {x: nudging[x : x + 1, :] * kappa[x] for x in own}
        for n, x in enumerate(range(3 * b - 1, 3 * b + 4)):
            total = None
            for near in (x - 1, x + 1):
                if near in both:
                    total = both[near] if total is None else total + both[near]
            if x in both:
                total = total + (nudging[x : x + 1, :] - 4.0 * both[x])
            weights[i * TERMS + n : i * TERMS + n + 1, :] = total
        for n, x in enumerate(own):
            at = i * TERMS + 5 + n
            value = jnp.where(ids == rows - 1, 0.0, pltpu.roll(both[x], rows - 1, 1))
            weights[at : at + 1, :] = value
            value = jnp.where(ids == 0, 0.0, pltpu.roll(both[x], 1, 1))
            weights[at + 3 : at + 4, :] = value


def child_rows(f, bs, masked, weights, wide):
    cols, _, rows = masked.shape[1:]
    for i, b in enumerate(bs):

        def term(n, x):
            at = i * TERMS + n
            return weights[at : at + 1, :] * masked[f, x]

        total = None
        for n, x in enumerate(range(3 * b - 1, 3 * b + 4)):
            if 0 <= x < cols:
                total = term(n, x) if total is None else total + term(n, x)
        for side, shift in ((5, 1), (8, rows - 1)):
            value = term(side, 3 * b) + term(side + 1, 3 * b + 1) + term(side + 2, 3 * b + 2)
            total = total + pltpu.roll(value, shift, 1)
        at = aligned(f * len(bs) + i, DEPTH)
        wide[at, :rows], wide[at, rows:] = halves(deepened(total))


def parent_rows(f, bs, nest_x, nest_y, masked, kappa, stack):
    cols, _, rows = masked.shape[1:]
    back = lax.rem(rows - nest_y[0], rows)
    for i, b in enumerate(bs):
        x = nest_x[0] + b
        above = masked[f, jnp.maximum(x - 1, 0)]
        below = masked[f, jnp.minimum(x + 1, cols - 1)]
        if b == 0:
            above = jnp.where(x == 0, 0.0, above)
        if b == cols // 3 - 1:
            below = jnp.where(x == cols - 1, 0.0, below)
        value = spread_of(masked[f, x], above, below, kappa[x])
        value = deepened(pltpu.roll(value, back, 1)[:, :LANE])
        fill_stack(stack.at[f], chunk(i), value)


def mix_rows(bs, is_child, wide, group, stack, matrices, emit):
    fields = stack.shape[0]

    @pl.when(is_child[0] == 1)
    def _():
        value = grouped(wide[...], group[...])
        for f in range(fields):
            for i in range(len(bs)):
                at = (f * len(bs) + i) * DEPTH
                fill_stack(stack.at[f], chunk(i), value[at : at + DEPTH])

    for f in range(fields):
        emit(f, mix(matrices[f], stack[f]))


def row_scratch(bs, fields, rows):
    return [
        pltpu.VMEM((-(-len(bs) * TERMS // 8) * 8, rows), F32),
        pltpu.VMEM((fields * len(bs) * DEPTH, 2 * rows), jnp.bfloat16),
        pltpu.VMEM((fields, 2 * DEPTH, len(bs) * LANE), jnp.bfloat16),
        pltpu.VMEM((2 * rows, LANE), jnp.bfloat16),
    ]


def front_kernel(
    levels, bs, is_child, state, mask, kappa, nudging, mixing, nest_x, nest_y, forcing, other, ahead,
    cells, masked_out, matrices, parcel, inner, places,
    buf, masked, mask_buf, kappa_buf, nudging_buf, mixing_buf, square, weights, wide, stack, group, sems, out_sems,
):
    fields, cols, _, rows = masked.shape
    chunks = rows // LANE
    step = cols * chunks
    size = levels * step

    def copy(f):
        at = pl.ds(f * size, size)
        return pltpu.make_async_copy(state.at[at], buf.at[at], sems.at[f])

    def copy_out(f):
        return pltpu.make_async_copy(masked.at[f], masked_out.at[f], out_sems.at[f])

    pairs = (
        (mask, mask_buf),
        (kappa, kappa_buf),
        (nudging, nudging_buf),
        (mixing, mixing_buf),
    )
    smalls = [
        pltpu.make_async_copy(source, target, sems.at[fields + n])
        for n, (source, target) in enumerate(pairs)
    ]
    for small in smalls:
        small.start()
    for f in range(1, fields):
        copy(f).start()
    square[...] = jnp.zeros_like(square)
    cell = cells[...]
    column, inside = cell // (cols * rows), lax.rem(cell, cols * rows)
    piece = (column // levels) * step + inside // LANE
    place = (piece * PAD + lax.rem(column, levels)) * LANE + lax.rem(inside, LANE)
    places[...] = place
    for small in smalls:
        small.wait()

    @pl.when(is_child[0] == 1)
    def _():
        fill_group(group)
        join_weights(bs, cols, kappa_buf, nudging_buf, weights)

    def field(f, total_edges, first=False):
        fill_matrix(levels, mixing_buf[f, :, 0, :], square, matrices.at[f])
        if first:
            fill_masked(levels, ahead, f, mask_buf, masked.at[f])
        else:
            copy(f).wait()
            fill_masked(levels, buf, f, mask_buf, masked.at[f])
        copy_out(f).start()
        own_edges = packed(
            lambda x: (masked[f, x, :, :LANE], masked[f, x, :, rows - LANE :]), cols
        )

        @pl.when(is_child[0] == 1)
        def _():
            child_rows(f, bs, masked, weights, wide)

        @pl.when(is_child[0] == 0)
        def _():
            parent_rows(f, bs, nest_x, nest_y, masked, kappa_buf, stack)

        return total_edges + pltpu.roll(own_edges, 2 * f * cols, 1)

    own_edges = field(0, jnp.zeros((PAD, LANE), F32), first=True)
    parcel[:PAD, :] = lax.fori_loop(1, fields, field, own_edges)
    slots, dests = forcing.shape
    parcel[PAD:, :] = jnp.zeros((parcel.shape[0] - PAD, LANE), F32)
    parcel[PAD : PAD + slots, :dests] = forcing[...]
    if 2 * dests <= LANE:
        parcel[PAD : PAD + slots, dests : 2 * dests] = other[...]
    else:
        parcel[PAD + slots :, :dests] = other[...]

    def emit(f, mixed):
        for i in range(len(bs)):
            at = pl.ds(f * levels * len(bs) + i, levels, stride=len(bs))
            inner[at, :] = mixed[:levels, chunk(i)]

    mix_rows(bs, is_child, wide, group, stack, matrices, emit)
    for f in range(fields):
        copy_out(f).wait()


def front(is_child, state2, mask, kappa, nudging, mixing, nests, forcing, other, ahead, cells, dims):
    fields, levels, cols, chunks = dims
    rows = chunks * LANE
    bs = tuple(range(1, cols // 3 - 1))
    arrays = (state2, mask, kappa, nudging, mixing)
    slots, dests = forcing.shape
    height = slots if 2 * dests <= LANE else 2 * slots
    return pl.pallas_call(
        functools.partial(front_kernel, levels, bs),
        in_specs=[SMEM] + [HBM] * 5 + [SMEM] * 2 + [VMEM] * 4,
        out_specs=[HBM] + [VMEM] * 4,
        out_shape=[
            pltpu.HBM((fields, cols, PAD, rows), F32),
            pltpu.VMEM((fields, 2 * DEPTH, 2 * DEPTH), jnp.bfloat16),
            pltpu.VMEM((PAD + height, LANE), F32),
            pltpu.VMEM((fields * levels * len(bs), LANE), F32),
            pltpu.VMEM(cells.shape, jnp.int32),
        ],
        scratch_shapes=[
            pltpu.VMEM(state2.shape, F32),
            pltpu.VMEM((fields, cols, PAD, rows), F32),
            pltpu.VMEM(mask.shape, jnp.int32),
            pltpu.VMEM(kappa.shape, F32),
            pltpu.VMEM(nudging.shape, F32),
            pltpu.VMEM(mixing.shape, F32),
            pltpu.VMEM((DEPTH, LANE), F32),
        ]
        + row_scratch(bs, fields, rows)
        + [pltpu.SemaphoreType.DMA((fields + 4,)), pltpu.SemaphoreType.DMA((fields,))],
        compiler_params=pltpu.CompilerParams(vmem_limit_bytes=24 * MIB),
        cost_estimate=COST,
        name="front",
    )(is_child, *map(in_hbm, arrays), *nests, forcing, other, in_vmem(ahead), cells)


def base_kernel(
    levels, bs, is_child, nest_x, nest_y, masked_in, matrices, kappa, nudging, base,
    masked, weights, wide, stack, group, sems,
):
    fields, cols = masked.shape[:2]
    near = cols // 3
    reach = near + 2

    def child_copies(f):
        for n, x in enumerate((0, cols - near)):
            at = pl.ds(x, near)
            yield pltpu.make_async_copy(masked_in.at[f, at], masked.at[f, at], sems.at[f, n])

    def parent_copy(f):
        at = pl.ds(jnp.clip(nest_x[0] - 1, 0, cols - reach), reach)
        return pltpu.make_async_copy(masked_in.at[f, at], masked.at[f, at], sems.at[f, 0])

    @pl.when(is_child[0] == 1)
    def _():
        for f in range(fields):
            for copy in child_copies(f):
                copy.start()
        fill_group(group)
        join_weights(bs, cols, kappa, nudging, weights)

        def field(f, carry):
            for copy in child_copies(f):
                copy.wait()
            child_rows(f, bs, masked, weights, wide)
            return carry

        lax.fori_loop(0, fields, field, 0)

    @pl.when(is_child[0] == 0)
    def _():
        for f in range(fields):
            parent_copy(f).start()

        def field(f, carry):
            parent_copy(f).wait()
            parent_rows(f, bs, nest_x, nest_y, masked, kappa, stack)
            return carry

        lax.fori_loop(0, fields, field, 0)

    def emit(f, mixed):
        base[f, :, :] = mixed[:PAD, :]

    mix_rows(bs, is_child, wide, group, stack, matrices, emit)


def base_of(is_child, nests, masked, matrices, kappa, nudging, dims):
    fields, levels, cols, chunks = dims
    rows = chunks * LANE
    bs = (0, cols // 3 - 1)
    return pl.pallas_call(
        functools.partial(base_kernel, levels, bs),
        in_specs=[SMEM] * 3 + [HBM] + [VMEM] * 3,
        out_specs=VMEM,
        out_shape=pltpu.VMEM((fields, PAD, 2 * LANE), F32),
        scratch_shapes=[pltpu.VMEM(masked.shape, F32)]
        + row_scratch(bs, fields, rows)
        + [pltpu.SemaphoreType.DMA((fields, 2))],
        compiler_params=pltpu.CompilerParams(vmem_limit_bytes=16 * MIB),
        cost_estimate=COST,
        name="base",
    )(is_child, *nests, in_hbm(masked), matrices, kappa, nudging)


def merged(own, other, width):
    if 2 * width <= LANE:
        return own + pltpu.roll(other, width, 1)
    return jnp.concatenate([own, other], axis=0)


def repack_kernel(width, edges, parcel, arrived, out):
    if edges:
        out[:edges, :] = parcel[:edges, :]
    out[edges:, :] = merged(parcel[PAD:, :], arrived[PAD:, :], width)


def repack(parcel, arrived, width, edges):
    height = (parcel.shape[0] - PAD) * (1 if 2 * width <= LANE else 2)
    return pl.pallas_call(
        functools.partial(repack_kernel, width, edges),
        in_specs=[VMEM] * 2,
        out_specs=VMEM,
        out_shape=pltpu.VMEM((edges + height, LANE), F32),
        compiler_params=pltpu.CompilerParams(vmem_limit_bytes=4 * MIB),
        name="repack",
    )(parcel, arrived)


def y_halos(ty, peers, first, second):
    one, two = first[:PAD, :], second[:PAD, :]
    even = (lax.rem(ty[0], 2) == 0).astype(F32)
    odd = 1.0 - even
    before = (two * even + one * odd) * (ty[0] > 0).astype(F32)
    after = (one * even + two * odd) * (ty[0] < peers - 1).astype(F32)
    low = lax.rem(lane_ids((PAD, LANE)), 2) == 0
    return jnp.where(low, pltpu.roll(before, 1, 1), pltpu.roll(after, LANE - 1, 1))


def outer_kernel(
    levels, peers, is_child, tx, ty, state, matrices, base, kappa, nudging, x_first, x_second,
    first, second, nest_x, nest_y, out, ahead, sides, wide, stack, group, sem,
):
    fields = matrices.shape[0]
    cols, _, rows = kappa.shape
    blocks = cols // 3
    lanes = lane_ids((PAD, LANE))
    turned = lax.rem(lanes + 1, LANE)
    copy = pltpu.make_async_copy(state.at[pl.ds(0, ahead.shape[0])], ahead, sem)
    copy.start()
    sides[...] = jnp.zeros_like(sides)
    halo = y_halos(ty, peers, first, second)

    def weighted(row_of_x):
        one = packed(lambda x: (row_of_x(x)[:, :LANE], row_of_x(x)[:, rows - LANE :]), cols)
        total = one
        for f in range(1, fields):
            total = total + pltpu.roll(one, 2 * f * cols, 1)
        return halo * total

    def fill_fix(value):
        for f in range(fields):
            fill_stack(stack.at[f], chunk(2), deepened(value))

    @pl.when(is_child[0] == 1)
    def _():
        fill_group(group)
        for f in range(fields):
            for n, side in enumerate(x_halos_of(tx, x_first, x_second, f)):
                x = (0, cols - 1)[n]
                at = (f * 2 + n) * DEPTH
                sides[at : at + levels, :] = side * (nudging[x : x + 1, :] * kappa[x])
        wide[:, :rows], wide[:, rows:] = halves(sides[...])
        value = grouped(wide[...], group[...])
        for f in range(fields):
            for n in range(2):
                at = (f * 2 + n) * DEPTH
                fill_stack(stack.at[f], chunk(n), value[at : at + DEPTH])
        part = weighted(lambda x: nudging[x : x + 1, :] * kappa[x])
        fill_fix(part + pltpu.roll(part, LANE - 2, 1) + pltpu.roll(part, LANE - 4, 1))

    @pl.when(is_child[0] == 0)
    def _():
        back = lax.rem(rows - nest_y[0], rows)
        reached = (nest_x[0] == 0, nest_x[0] + blocks == cols)
        for f in range(fields):
            for n, side in enumerate(x_halos_of(tx, x_first, x_second, f)):
                at = (f * 2 + n) * DEPTH
                weight = kappa[(0, cols - 1)[n]] * reached[n].astype(F32)
                sides[at : at + levels, :] = side * weight
                value = pltpu.roll(sides[at : at + DEPTH, :], back, 1)[:, :LANE]
                fill_stack(stack.at[f], chunk(n), value)
        starts = (nest_y[0] == 0).astype(F32)
        finals = (nest_y[0] == rows - LANE).astype(F32)
        part = weighted(lambda x: kappa[x])
        part = part * jnp.where(lax.rem(lanes, 2) == 0, starts, finals)
        value = jnp.zeros((PAD, LANE), F32)
        for b in range(blocks):
            shift = lax.rem(LANE + 4 * b - 2 * nest_x[0], LANE)
            here = lax.rem(turned, 2 * cols) // 2 == 3 * b
            value = jnp.where(here, pltpu.roll(part, shift, 1), value)
        fill_fix(value)

    fixes = jnp.zeros((PAD, LANE), F32)
    for f in range(fields):
        mixed = mix(matrices[f], stack[f])
        for n in range(2):
            at = pl.ds(f * (2 * levels) + n, levels, stride=2)
            out[at, :] = base[f, :levels, chunk(n)] + mixed[:levels, chunk(n)]
        fixes = jnp.where(turned // (2 * cols) == f, mixed[:PAD, chunk(2)], fixes)
    out[out.shape[0] - PAD :, :] = fixes
    copy.wait()


def outer(
    is_child, tx, ty, state2, matrices, base, kappa, nudging, x_halos, firsts, nests, dims, peers
):
    fields, levels, cols, chunks = dims
    rows = chunks * LANE
    height = -(-fields * 2 * levels // 8) * 8 + PAD
    return pl.pallas_call(
        functools.partial(outer_kernel, levels, peers),
        in_specs=[SMEM] * 3 + [HBM] + [VMEM] * 8 + [SMEM] * 2,
        out_specs=[VMEM] * 2,
        out_shape=[
            pltpu.VMEM((height, LANE), F32),
            pltpu.VMEM((state2.shape[0] // fields, LANE), F32),
        ],
        scratch_shapes=[
            pltpu.VMEM((fields * 2 * DEPTH, rows), F32),
            pltpu.VMEM((fields * 2 * DEPTH, 2 * rows), jnp.bfloat16),
            pltpu.VMEM((fields, 2 * DEPTH, 3 * LANE), jnp.bfloat16),
            pltpu.VMEM((2 * rows, LANE), jnp.bfloat16),
            pltpu.SemaphoreType.DMA,
        ],
        compiler_params=pltpu.CompilerParams(vmem_limit_bytes=12 * MIB),
        name="outer",
    )(is_child, tx, ty, in_hbm(state2), matrices, base, kappa, nudging, *x_halos, *firsts, *nests)


def tile_kernel(
    levels, peers, tx, ty, state, mask, matrices, kappa, x_first, x_second, first, second, ahead,
    out, buf, masked, sides, halo, stack, sems,
):
    cols, _, rows = masked.shape
    chunks = rows // LANE
    size = levels * cols * chunks
    fields = state.shape[0] // size

    def copy(f):
        at = pl.ds(f * size, size)
        return pltpu.make_async_copy(state.at[at], buf.at[at], sems.at[f])

    for f in range(1, fields):
        copy(f).start()
    sides[...] = jnp.zeros_like(sides)
    halo[...] = y_halos(ty, peers, first, second)
    pair = 2

    def field(f, carry, leading=False):
        if leading:
            fill_masked(levels, ahead, f, mask, masked)
        else:
            copy(f).wait()
            fill_masked(levels, buf, f, mask, masked)
        for n, side in enumerate(x_halos_of(tx, x_first, x_second, f)):
            sides[n, :levels, :] = side
        for x0 in range(0, cols, pair):
            for x in range(x0, x0 + pair):
                above = masked[x - 1] if x > 0 else sides[0]
                below = masked[x + 1] if x < cols - 1 else sides[1]
                shift = lax.rem(LANE - 2 * (f * cols + x), LANE)
                edge = pltpu.roll(halo[...], lax.rem(LANE + shift, LANE), 1)
                value = spread_of(masked[x], above, below, kappa[x], edge)
                part = slice((x - x0) * rows, (x - x0 + 1) * rows)
                fill_stack(stack, part, deepened(value))
            mixed = mix(matrices[f], stack[...])
            for n in range(pair * chunks):
                out[aligned((f * cols + x0) * chunks + n, PAD), :] = mixed[:PAD, chunk(n)]
        return carry

    field(0, 0, leading=True)
    lax.fori_loop(1, fields, field, 0)


def tile_of(tx, ty, state2, mask, matrices, kappa, x_halos, firsts, ahead, dims, peers):
    fields, levels, cols, chunks = dims
    rows = chunks * LANE
    return pl.pallas_call(
        functools.partial(tile_kernel, levels, peers),
        in_specs=[SMEM] * 2 + [HBM] + [VMEM] * 8,
        out_specs=VMEM,
        out_shape=pltpu.VMEM((fields * cols * chunks * PAD, LANE), F32),
        scratch_shapes=[
            pltpu.VMEM(state2.shape, F32),
            pltpu.VMEM((cols, PAD, rows), F32),
            pltpu.VMEM((2, PAD, rows), F32),
            pltpu.VMEM((PAD, LANE), F32),
            pltpu.VMEM((2 * DEPTH, 2 * rows), jnp.bfloat16),
            pltpu.SemaphoreType.DMA((fields,)),
        ],
        compiler_params=pltpu.CompilerParams(vmem_limit_bytes=16 * MIB),
        cost_estimate=COST,
        name="tile",
    )(tx, ty, in_hbm(state2), mask, matrices, kappa, *x_halos, *firsts, in_vmem(ahead))


def observe_kernel(dests, across, row, column, counts, places, mine, theirs, _, tile):
    lanes = lane_ids((1, LANE))
    slots = places.shape[1]
    ty, tx = row[0], column[0]
    me = ty * across + tx
    half = mine.shape[0] // slots * (LANE // dests)

    def source(first, ref, n, carry):
        g = first + n
        origin = (((g >> 1) & 1) ^ (3 * ((g >> 2) & 1)) ^ ty) * across
        origin = origin + (((g & 1) | ((g >> 3) << 1)) ^ tx)
        lane_in = lax.rem(n, LANE // dests) * dests + me
        block = lax.div(n, LANE // dests) * slots
        count = counts[0, origin]
        for k in range(0, slots, 2):
            ats, adds = [], []
            for m in range(k, k + 2):
                place = places[origin, m]
                lane = place & (LANE - 1)
                value = pltpu.roll(ref[pl.ds(block + m, 1), :], (lane - lane_in) & (LANE - 1), 1)
                ats.append(place >> 7)
                adds.append(jnp.where(lanes == jnp.where(m < count, lane, LANE), value, 0.0))
            olds = [tile[pl.ds(at, 1), :] for at in ats]
            also = jnp.where(ats[0] == ats[1], adds[0], 0.0)
            tile[pl.ds(ats[0], 1), :] = olds[0] + adds[0]
            tile[pl.ds(ats[1], 1), :] = olds[1] + adds[1] + also
        return carry

    lax.fori_loop(0, half, functools.partial(source, 0, mine), 0)
    lax.fori_loop(0, half, functools.partial(source, half, theirs), 0)


def observe(row, column, places, counts, seen, tile, dests, across):
    return pl.pallas_call(
        functools.partial(observe_kernel, dests, across),
        in_specs=[SMEM] * 4 + [VMEM] * 3,
        out_specs=VMEM,
        out_shape=pltpu.VMEM(tile.shape, F32),
        input_output_aliases={6: 0},
        compiler_params=pltpu.CompilerParams(vmem_limit_bytes=4 * MIB),
        name="observe",
    )(row, column, counts, places, *seen, in_vmem(tile))


def finish_kernel(
    levels, is_child, nest_x, nest_y, tile, mask, in_arrived, out_arrived, in_sent, out_sent,
    out, buf, group, sems,
):
    cols = mask.shape[0]
    rows = mask.shape[2]
    chunks = rows // LANE
    step = cols * chunks
    size = levels * step
    fields = out.shape[0] // size
    blocks = cols // 3
    inner = blocks - 2
    lanes = lane_ids((levels, LANE))
    ends = jnp.logical_or(lanes == 0, lanes == LANE - 1)
    height = out_arrived.shape[0]

    def copy(f):
        at = pl.ds(f * size, size)
        return pltpu.make_async_copy(buf.at[at], out.at[at], sems.at[f])

    def piece_of(f, piece):
        return tile[pl.ds(pl.multiple_of((f * step + piece) * PAD, 8), levels), :]

    def payload(f, b, inner_ref, outer_ref):
        if b in (0, blocks - 1):
            value = outer_ref[pl.ds(f * (2 * levels) + min(b, 1), levels, stride=2), :]
        else:
            value = inner_ref[pl.ds(f * (levels * inner) + b - 1, levels, stride=inner), :]
        fixes = outer_ref[height - PAD : height - PAD + levels, :]
        shift = lax.rem(LANE - 2 * (f * cols + 3 * b), LANE)
        fixes = pltpu.roll(fixes, lax.rem(LANE + shift, LANE), 1)
        return value + jnp.where(ends, fixes, 0.0)

    def fill_child(f, carry):
        for b in range(blocks):
            high, low = halves(payload(f, b, in_arrived, out_arrived))
            both = jnp.concatenate([high, low], axis=1)
            value = jnp.dot(both, group[...], preferred_element_type=F32) * (1.0 / 9.0)
            for x in range(3 * b, 3 * b + 3):
                row = row_of(mask, x)
                for c in range(chunks):
                    piece = x * chunks + c
                    at = pl.ds(f * size + piece, levels, stride=step)
                    total = piece_of(f, piece) + value[:, chunk(c)]
                    buf[at, :] = total * row[:, chunk(c)]
        copy(f).start()
        return carry

    def fill_plain(f, carry):
        for x in range(cols):
            row = row_of(mask, x)
            for c in range(chunks):
                piece = x * chunks + c
                at = pl.ds(f * size + piece, levels, stride=step)
                buf[at, :] = piece_of(f, piece) * row[:, chunk(c)]
        return carry

    def fill_parent(f, carry):
        fill_plain(f, carry)
        for b in range(blocks):
            delta = payload(f, b, in_arrived, out_arrived) - payload(f, b, in_sent, out_sent)
            wide = jnp.concatenate([delta, jnp.zeros((levels, rows - LANE), F32)], 1)
            x = nest_x[0] + b
            value = pltpu.roll(wide, nest_y[0], 1) * row_of(mask, x)
            for c in range(chunks):
                at = pl.ds(f * size + x * chunks + c, levels, stride=step)
                buf[at, :] = buf[at, :] + value[:, chunk(c)]
        copy(f).start()
        return carry

    @pl.when(is_child[0] == 1)
    def _():
        ids = lax.broadcasted_iota(jnp.int32, group.shape, 0)
        ids = jnp.where(ids < LANE, ids, ids - LANE)
        group[...] = jnp.where(lane_ids(group.shape) // 3 == ids, 1.0, 0.0).astype(jnp.bfloat16)
        lax.fori_loop(0, fields, fill_child, 0)

    @pl.when(is_child[0] == 0)
    def _():
        lax.fori_loop(0, fields, fill_parent, 0)

    for f in range(fields):
        copy(f).wait()


def finish(is_child, nests, tile, mask, arrived, sent, dims):
    fields, levels, cols, chunks = dims
    rows = chunks * LANE
    size = (fields * levels * cols * chunks, LANE)
    return pl.pallas_call(
        functools.partial(finish_kernel, levels),
        in_specs=[SMEM] * 3 + [VMEM] * 6,
        out_specs=HBM,
        out_shape=pltpu.HBM(size, F32),
        scratch_shapes=[
            pltpu.VMEM(size, F32),
            pltpu.VMEM((2 * LANE, rows), jnp.bfloat16),
            pltpu.SemaphoreType.DMA((fields,)),
        ],
        compiler_params=pltpu.CompilerParams(vmem_limit_bytes=16 * MIB),
        cost_estimate=COST,
        name="finish",
    )(is_child, *nests, in_vmem(tile), mask, *arrived, *sent)


def from_neighbours(first, second, axis):
    size = lax.axis_size(axis)
    inner = [(i, i + 1) for i in range(1, size - 1, 2)]
    one = swapped(first, axis, 1)
    return one, lax.ppermute(second, axis, inner + [(j, i) for i, j in inner])


def swapped(value, axis, mask):
    return lax.ppermute(value, axis, [(i, i ^ mask) for i in range(lax.axis_size(axis))])


def local(
    adjoint_state,
    land_mask,
    diffusivity,
    mixing,
    nudging,
    nest_x,
    nest_y,
    obs_forcing,
    obs_cell,
    obs_count,
):
    _, fields, levels, cols, rows = adjoint_state.shape
    chunks = rows // LANE
    dims = (fields, levels, cols, chunks)
    state5 = adjoint_state.reshape(fields, levels, cols, 1, rows)
    state2 = adjoint_state.reshape(fields * levels * cols * chunks, LANE)
    mask = land_mask.reshape(cols, 1, rows)
    kappa = diffusivity.reshape(cols, 1, rows)
    mixing = mixing.reshape(fields, levels, 1, levels)
    peers, across = lax.axis_size("ty"), lax.axis_size("tx")
    assert peers == 4 and across & (across - 1) == 0 and 2 * fields * cols <= LANE
    assert levels <= PAD and cols % 3 == 0 and rows == 3 * LANE
    row = lax.axis_index("ty").astype(jnp.int32)
    column = lax.axis_index("tx").astype(jnp.int32)
    ty = row.reshape(1)
    is_child = (lax.axis_index("grp") == 0).astype(jnp.int32).reshape(1)
    nests = (nest_x, nest_y)

    forcing = obs_forcing[0, 0]
    dests = forcing.shape[1]
    counts = obs_count.reshape(1, -1)
    other = swapped(forcing, "tx", 1)
    tx = column.reshape(1)
    *x_sent, ahead = x_edges(tx, state5, mask)
    ahead = ahead.reshape(-1, LANE)
    x_halos = from_neighbours(*x_sent, "tx")
    masked, matrices, parcel, in_sent, places = front(
        is_child, state2, mask, kappa, nudging, mixing, nests, forcing, other, ahead,
        obs_cell[0, :, :, 0], dims,
    )
    base = base_of(is_child, nests, masked, matrices, kappa, nudging, dims)
    first = swapped(parcel, "ty", 1)
    in_arrived = swapped(in_sent, "grp", 1)
    parcel = repack(parcel, first, 2 * dests, PAD)
    parcel, x_halos = lax.optimization_barrier((parcel, x_halos))
    second = swapped(parcel, "ty", 3)
    firsts = (first, second)
    seen = repack(parcel, second, 4 * dests, 0)
    for n in range(1, across.bit_length() - 2):
        seen = jnp.concatenate([seen, swapped(seen, "tx", 1 << n)])
    seen = (seen, swapped(seen, "tx", across // 2))
    out_sent, ahead = outer(
        is_child, tx, ty, state2, matrices, base, kappa, nudging, x_halos, firsts, nests, dims, peers
    )
    out_sent, in_arrived = lax.optimization_barrier((out_sent, in_arrived))
    out_arrived = swapped(out_sent, "grp", 1)
    tile = tile_of(tx, ty, state2, mask, matrices, kappa, x_halos, firsts, ahead, dims, peers)
    tile = observe(ty, tx, places, counts, seen, tile, dests, across)
    arrived, sent = (in_arrived, out_arrived), (in_sent, out_sent)
    out = finish(is_child, nests, tile, mask, arrived, sent, dims)
    return out.reshape(adjoint_state.shape)


def solution(mesh):
    in_specs = (
        P("grp", None, None, "tx", "ty"),
        P("grp", "tx", "ty"),
        P("grp", "tx", "ty"),
        P("grp", None, None, None),
        P("tx", "ty"),
        P(("ty", "tx")),
        P(("ty", "tx")),
        P("grp", ("ty", "tx"), None, None),
        P("grp", None, None, ("ty", "tx")),
        P("grp", None, ("ty", "tx")),
    )
    out_specs = P("grp", None, None, "tx", "ty")
    return jax.shard_map(local, mesh=mesh, in_specs=in_specs, out_specs=out_specs, check_vma=False)
```

```python
import functools

import jax
import jax.numpy as jnp
from jax import lax
from jax.experimental import pallas as pl
from jax.experimental.pallas import tpu as pltpu
from jax.sharding import PartitionSpec as P

LANE = 128
PAD = 56
DEPTH = 64
MIB = 1 << 20
HBM = pl.BlockSpec(memory_space=pltpu.HBM)
SMEM = pl.BlockSpec(memory_space=pltpu.SMEM)
VMEM = pl.BlockSpec(memory_space=pltpu.VMEM)
F32 = jnp.float32
COST = pl.CostEstimate(flops=10**10, bytes_accessed=10**8, transcendentals=0)


def lane_ids(shape):
    return lax.broadcasted_iota(jnp.int32, shape, len(shape) - 1)


def row_of(ref, x):
    return ref[x].astype(F32)


def chunk(c):
    return slice(c * LANE, (c + 1) * LANE)


def in_hbm(value):
    return pltpu.with_memory_space_constraint(value, pltpu.HBM)


def in_vmem(value):
    return pltpu.with_memory_space_constraint(value, pltpu.VMEM)


def x_edges_kernel(tx, state, mask, first, second, ahead, buf, mask_buf, sems):
    fields, _, cols = state.shape[:3]
    even = lax.rem(tx[0], 2) == 0
    ends = (jnp.where(even, cols - 1, 0), jnp.where(even, 0, cols - 1))
    copies = [pltpu.make_async_copy(mask, mask_buf, sems.at[2 * fields])]
    for n, x in enumerate(ends):
        for f in range(fields):
            copies.append(
                pltpu.make_async_copy(state.at[f, :, x], buf.at[n, f], sems.at[n * fields + f])
            )
    copies.append(pltpu.make_async_copy(state.at[0], ahead, sems.at[2 * fields + 1]))
    for copy in copies:
        copy.start()
    copies[0].wait()
    for n, (x, out) in enumerate(zip(ends, (first, second))):
        for f in range(fields):
            copies[1 + n * fields + f].wait()
            out[f] = buf[n, f] * row_of(mask_buf, x)[None]
    copies[-1].wait()


def x_edges(tx, state5, mask):
    fields, levels, cols, _, rows = state5.shape
    edge = (fields, levels, 1, rows)
    return pl.pallas_call(
        x_edges_kernel,
        in_specs=[SMEM, HBM, HBM],
        out_specs=[VMEM] * 3,
        out_shape=[pltpu.VMEM(edge, F32)] * 2 + [pltpu.VMEM(state5.shape[1:], F32)],
        scratch_shapes=[
            pltpu.VMEM((2,) + edge, F32),
            pltpu.VMEM(mask.shape, jnp.int32),
            pltpu.SemaphoreType.DMA((2 * fields + 2,)),
        ],
        compiler_params=pltpu.CompilerParams(vmem_limit_bytes=8 * MIB),
        cost_estimate=COST,
        name="x_edges",
    )(tx, in_hbm(state5), in_hbm(mask))


def x_halos_of(tx, first, second, f):
    one, two = first[f, :, 0, :], second[f, :, 0, :]
    even = lax.rem(tx[0], 2) == 0
    return jnp.where(even, two, one), jnp.where(even, one, two)


def spread_of(here, above, below, kappa, edge=None):
    rows = here.shape[1]
    lanes = lane_ids((here.shape[0], LANE))
    edge = 0.0 if edge is None else edge
    before = pltpu.roll(here, 1, 1)
    after = pltpu.roll(here, rows - 1, 1)
    before = jnp.concatenate([jnp.where(lanes == 0, edge, before[:, :LANE]), before[:, LANE:]], 1)
    after = jnp.concatenate(
        [after[:, :-LANE], jnp.where(lanes == LANE - 1, edge, after[:, -LANE:])], 1
    )
    return here + kappa * (above + below + before + after - 4.0 * here)


def halves(value):
    high = value.astype(jnp.bfloat16)
    return high, (value - high.astype(F32)).astype(jnp.bfloat16)


def deepened(value):
    return jnp.concatenate([value, jnp.zeros((DEPTH - value.shape[0], value.shape[1]), F32)], 0)


def fill_matrix(levels, mixing, square, matrix):
    square[:levels, :levels] = mixing
    value = square[...]
    high = value.astype(jnp.bfloat16).astype(F32)
    matrix[:DEPTH, :] = (high + pltpu.roll(high, DEPTH, 1)).astype(jnp.bfloat16)
    matrix[DEPTH:, :] = (value - high).astype(jnp.bfloat16)


def fill_stack(stack, part, value):
    high, low = halves(value)
    stack[:DEPTH, part] = high
    stack[DEPTH:, part] = low


def mix(matrix, stack):
    both = jnp.dot(matrix, stack, preferred_element_type=F32)
    return both[:DEPTH] + both[DEPTH:]


def fill_group(group):
    rows = group.shape[0] // 2
    ids = lax.broadcasted_iota(jnp.int32, group.shape, 0)
    ids = jnp.where(ids < rows, ids, ids - rows) // 3
    group[...] = jnp.where(ids == lane_ids(group.shape), 1.0, 0.0).astype(jnp.bfloat16)


def grouped(wide, group):
    return jnp.dot(wide, group, preferred_element_type=F32)


def aligned(index, size):
    return pl.ds(pl.multiple_of(index * size, size), size)


def packed(rows_of, cols):
    parts = []
    for x in range(cols):
        first, last = rows_of(x)
        lanes = lane_ids(first.shape)
        parts.append(jnp.where(lanes == 0, first, jnp.where(lanes == LANE - 1, last, 0.0)))
    shift = 2
    while len(parts) > 1:
        pairs = [parts[n : n + 2] for n in range(0, len(parts), 2)]
        parts = [p[0] + pltpu.roll(p[1], shift, 1) if len(p) == 2 else p[0] for p in pairs]
        shift *= 2
    return parts[0]


def fill_masked(levels, state, f, mask, masked):
    cols, _, rows = masked.shape
    chunks = rows // LANE
    step = cols * chunks
    for x in range(cols):
        row = row_of(mask, x)
        masked[x, PAD - 8 :, :] = jnp.zeros((8, rows), F32)
        for c in range(chunks):
            at = pl.ds(f * (levels * step) + x * chunks + c, levels, stride=step)
            masked[x, :levels, chunk(c)] = state[at, :] * row[:, chunk(c)]


TERMS = 11


def join_weights(bs, cols, kappa, nudging, weights):
    rows = weights.shape[1]
    ids = lane_ids((1, rows))
    for i, b in enumerate(bs):
        own = range(3 * b, 3 * b + 3)
        both = {x: nudging[x : x + 1, :] * kappa[x] for x in own}
        for n, x in enumerate(range(3 * b - 1, 3 * b + 4)):
            total = None
            for near in (x - 1, x + 1):
                if near in both:
                    total = both[near] if total is None else total + both[near]
            if x in both:
                total = total + (nudging[x : x + 1, :] - 4.0 * both[x])
            weights[i * TERMS + n : i * TERMS + n + 1, :] = total
        for n, x in enumerate(own):
            at = i * TERMS + 5 + n
            value = jnp.where(ids == rows - 1, 0.0, pltpu.roll(both[x], rows - 1, 1))
            weights[at : at + 1, :] = value
            value = jnp.where(ids == 0, 0.0, pltpu.roll(both[x], 1, 1))
            weights[at + 3 : at + 4, :] = value


def child_rows(f, bs, masked, weights, wide):
    cols, _, rows = masked.shape[1:]
    for i, b in enumerate(bs):

        def term(n, x):
            at = i * TERMS + n
            return weights[at : at + 1, :] * masked[f, x]

        total = None
        for n, x in enumerate(range(3 * b - 1, 3 * b + 4)):
            if 0 <= x < cols:
                total = term(n, x) if total is None else total + term(n, x)
        for side, shift in ((5, 1), (8, rows - 1)):
            value = term(side, 3 * b) + term(side + 1, 3 * b + 1) + term(side + 2, 3 * b + 2)
            total = total + pltpu.roll(value, shift, 1)
        at = aligned(f * len(bs) + i, DEPTH)
        wide[at, :rows], wide[at, rows:] = halves(deepened(total))


def parent_rows(f, bs, nest_x, nest_y, masked, kappa, stack):
    cols, _, rows = masked.shape[1:]
    back = lax.rem(rows - nest_y[0], rows)
    for i, b in enumerate(bs):
        x = nest_x[0] + b
        above = masked[f, jnp.maximum(x - 1, 0)]
        below = masked[f, jnp.minimum(x + 1, cols - 1)]
        if b == 0:
            above = jnp.where(x == 0, 0.0, above)
        if b == cols // 3 - 1:
            below = jnp.where(x == cols - 1, 0.0, below)
        value = spread_of(masked[f, x], above, below, kappa[x])
        value = deepened(pltpu.roll(value, back, 1)[:, :LANE])
        fill_stack(stack.at[f], chunk(i), value)


def mix_rows(bs, is_child, wide, group, stack, matrices, emit):
    fields = stack.shape[0]

    @pl.when(is_child[0] == 1)
    def _():
        value = grouped(wide[...], group[...])
        for f in range(fields):
            for i in range(len(bs)):
                at = (f * len(bs) + i) * DEPTH
                fill_stack(stack.at[f], chunk(i), value[at : at + DEPTH])

    for f in range(fields):
        emit(f, mix(matrices[f], stack[f]))


def row_scratch(bs, fields, rows):
    return [
        pltpu.VMEM((-(-len(bs) * TERMS // 8) * 8, rows), F32),
        pltpu.VMEM((fields * len(bs) * DEPTH, 2 * rows), jnp.bfloat16),
        pltpu.VMEM((fields, 2 * DEPTH, len(bs) * LANE), jnp.bfloat16),
        pltpu.VMEM((2 * rows, LANE), jnp.bfloat16),
    ]


def front_kernel(
    levels, bs, is_child, state, mask, kappa, nudging, mixing, nest_x, nest_y, forcing, other, ahead,
    cells, masked_out, matrices, parcel, inner, places,
    buf, masked, mask_buf, kappa_buf, nudging_buf, mixing_buf, square, weights, wide, stack, group, sems, out_sems,
):
    fields, cols, _, rows = masked.shape
    chunks = rows // LANE
    step = cols * chunks
    size = levels * step

    def copy(f):
        at = pl.ds(f * size, size)
        return pltpu.make_async_copy(state.at[at], buf.at[at], sems.at[f])

    def copy_out(f):
        return pltpu.make_async_copy(masked.at[f], masked_out.at[f], out_sems.at[f])

    pairs = (
        (mask, mask_buf),
        (kappa, kappa_buf),
        (nudging, nudging_buf),
        (mixing, mixing_buf),
    )
    smalls = [
        pltpu.make_async_copy(source, target, sems.at[fields + n])
        for n, (source, target) in enumerate(pairs)
    ]
    for small in smalls:
        small.start()
    for f in range(1, fields):
        copy(f).start()
    square[...] = jnp.zeros_like(square)
    cell = cells[...]
    column, inside = cell // (cols * rows), lax.rem(cell, cols * rows)
    piece = (column // levels) * step + inside // LANE
    place = (piece * PAD + lax.rem(column, levels)) * LANE + lax.rem(inside, LANE)
    places[...] = place
    for small in smalls:
        small.wait()

    @pl.when(is_child[0] == 1)
    def _():
        fill_group(group)
        join_weights(bs, cols, kappa_buf, nudging_buf, weights)

    def field(f, total_edges, first=False):
        fill_matrix(levels, mixing_buf[f, :, 0, :], square, matrices.at[f])
        if first:
            fill_masked(levels, ahead, f, mask_buf, masked.at[f])
        else:
            copy(f).wait()
            fill_masked(levels, buf, f, mask_buf, masked.at[f])
        copy_out(f).start()
        own_edges = packed(
            lambda x: (masked[f, x, :, :LANE], masked[f, x, :, rows - LANE :]), cols
        )

        @pl.when(is_child[0] == 1)
        def _():
            child_rows(f, bs, masked, weights, wide)

        @pl.when(is_child[0] == 0)
        def _():
            parent_rows(f, bs, nest_x, nest_y, masked, kappa_buf, stack)

        return total_edges + pltpu.roll(own_edges, 2 * f * cols, 1)

    own_edges = field(0, jnp.zeros((PAD, LANE), F32), first=True)
    parcel[:PAD, :] = lax.fori_loop(1, fields, field, own_edges)
    slots, dests = forcing.shape
    parcel[PAD:, :] = jnp.zeros((parcel.shape[0] - PAD, LANE), F32)
    parcel[PAD : PAD + slots, :dests] = forcing[...]
    if 2 * dests <= LANE:
        parcel[PAD : PAD + slots, dests : 2 * dests] = other[...]
    else:
        parcel[PAD + slots :, :dests] = other[...]

    def emit(f, mixed):
        for i in range(len(bs)):
            at = pl.ds(f * levels * len(bs) + i, levels, stride=len(bs))
            inner[at, :] = mixed[:levels, chunk(i)]

    mix_rows(bs, is_child, wide, group, stack, matrices, emit)
    for f in range(fields):
        copy_out(f).wait()


def front(is_child, state2, mask, kappa, nudging, mixing, nests, forcing, other, ahead, cells, dims):
    fields, levels, cols, chunks = dims
    rows = chunks * LANE
    bs = tuple(range(1, cols // 3 - 1))
    arrays = (state2, mask, kappa, nudging, mixing)
    slots, dests = forcing.shape
    height = slots if 2 * dests <= LANE else 2 * slots
    return pl.pallas_call(
        functools.partial(front_kernel, levels, bs),
        in_specs=[SMEM] + [HBM] * 5 + [SMEM] * 2 + [VMEM] * 4,
        out_specs=[HBM] + [VMEM] * 4,
        out_shape=[
            pltpu.HBM((fields, cols, PAD, rows), F32),
            pltpu.VMEM((fields, 2 * DEPTH, 2 * DEPTH), jnp.bfloat16),
            pltpu.VMEM((PAD + height, LANE), F32),
            pltpu.VMEM((fields * levels * len(bs), LANE), F32),
            pltpu.VMEM(cells.shape, jnp.int32),
        ],
        scratch_shapes=[
            pltpu.VMEM(state2.shape, F32),
            pltpu.VMEM((fields, cols, PAD, rows), F32),
            pltpu.VMEM(mask.shape, jnp.int32),
            pltpu.VMEM(kappa.shape, F32),
            pltpu.VMEM(nudging.shape, F32),
            pltpu.VMEM(mixing.shape, F32),
            pltpu.VMEM((DEPTH, LANE), F32),
        ]
        + row_scratch(bs, fields, rows)
        + [pltpu.SemaphoreType.DMA((fields + 4,)), pltpu.SemaphoreType.DMA((fields,))],
        compiler_params=pltpu.CompilerParams(vmem_limit_bytes=24 * MIB),
        cost_estimate=COST,
        name="front",
    )(is_child, *map(in_hbm, arrays), *nests, forcing, other, in_vmem(ahead), cells)


def base_kernel(
    levels, bs, is_child, nest_x, nest_y, masked_in, matrices, kappa, nudging, base,
    masked, weights, wide, stack, group, sems,
):
    fields, cols = masked.shape[:2]
    near = cols // 3
    reach = near + 2

    def child_copies(f):
        for n, x in enumerate((0, cols - near)):
            at = pl.ds(x, near)
            yield pltpu.make_async_copy(masked_in.at[f, at], masked.at[f, at], sems.at[f, n])

    def parent_copy(f):
        at = pl.ds(jnp.clip(nest_x[0] - 1, 0, cols - reach), reach)
        return pltpu.make_async_copy(masked_in.at[f, at], masked.at[f, at], sems.at[f, 0])

    @pl.when(is_child[0] == 1)
    def _():
        for f in range(fields):
            for copy in child_copies(f):
                copy.start()
        fill_group(group)
        join_weights(bs, cols, kappa, nudging, weights)

        def field(f, carry):
            for copy in child_copies(f):
                copy.wait()
            child_rows(f, bs, masked, weights, wide)
            return carry

        lax.fori_loop(0, fields, field, 0)

    @pl.when(is_child[0] == 0)
    def _():
        for f in range(fields):
            parent_copy(f).start()

        def field(f, carry):
            parent_copy(f).wait()
            parent_rows(f, bs, nest_x, nest_y, masked, kappa, stack)
            return carry

        lax.fori_loop(0, fields, field, 0)

    def emit(f, mixed):
        base[f, :, :] = mixed[:PAD, :]

    mix_rows(bs, is_child, wide, group, stack, matrices, emit)


def base_of(is_child, nests, masked, matrices, kappa, nudging, dims):
    fields, levels, cols, chunks = dims
    rows = chunks * LANE
    bs = (0, cols // 3 - 1)
    return pl.pallas_call(
        functools.partial(base_kernel, levels, bs),
        in_specs=[SMEM] * 3 + [HBM] + [VMEM] * 3,
        out_specs=VMEM,
        out_shape=pltpu.VMEM((fields, PAD, 2 * LANE), F32),
        scratch_shapes=[pltpu.VMEM(masked.shape, F32)]
        + row_scratch(bs, fields, rows)
        + [pltpu.SemaphoreType.DMA((fields, 2))],
        compiler_params=pltpu.CompilerParams(vmem_limit_bytes=16 * MIB),
        cost_estimate=COST,
        name="base",
    )(is_child, *nests, in_hbm(masked), matrices, kappa, nudging)


def merged(own, other, width):
    if 2 * width <= LANE:
        return own + pltpu.roll(other, width, 1)
    return jnp.concatenate([own, other], axis=0)


def repack_kernel(width, edges, parcel, arrived, out):
    if edges:
        out[:edges, :] = parcel[:edges, :]
    out[edges:, :] = merged(parcel[PAD:, :], arrived[PAD:, :], width)


def repack(parcel, arrived, width, edges):
    height = (parcel.shape[0] - PAD) * (1 if 2 * width <= LANE else 2)
    return pl.pallas_call(
        functools.partial(repack_kernel, width, edges),
        in_specs=[VMEM] * 2,
        out_specs=VMEM,
        out_shape=pltpu.VMEM((edges + height, LANE), F32),
        compiler_params=pltpu.CompilerParams(vmem_limit_bytes=4 * MIB),
        name="repack",
    )(parcel, arrived)


def y_halos(ty, peers, first, second):
    one, two = first[:PAD, :], second[:PAD, :]
    even = (lax.rem(ty[0], 2) == 0).astype(F32)
    odd = 1.0 - even
    before = (two * even + one * odd) * (ty[0] > 0).astype(F32)
    after = (one * even + two * odd) * (ty[0] < peers - 1).astype(F32)
    low = lax.rem(lane_ids((PAD, LANE)), 2) == 0
    return jnp.where(low, pltpu.roll(before, 1, 1), pltpu.roll(after, LANE - 1, 1))


def outer_kernel(
    levels, peers, is_child, tx, ty, state, matrices, base, kappa, nudging, x_first, x_second,
    first, second, nest_x, nest_y, out, ahead, sides, wide, stack, group, sem,
):
    fields = matrices.shape[0]
    cols, _, rows = kappa.shape
    blocks = cols // 3
    lanes = lane_ids((PAD, LANE))
    turned = lax.rem(lanes + 1, LANE)
    copy = pltpu.make_async_copy(state.at[pl.ds(0, ahead.shape[0])], ahead, sem)
    copy.start()
    sides[...] = jnp.zeros_like(sides)
    halo = y_halos(ty, peers, first, second)

    def weighted(row_of_x):
        one = packed(lambda x: (row_of_x(x)[:, :LANE], row_of_x(x)[:, rows - LANE :]), cols)
        total = one
        for f in range(1, fields):
            total = total + pltpu.roll(one, 2 * f * cols, 1)
        return halo * total

    def fill_fix(value):
        for f in range(fields):
            fill_stack(stack.at[f], chunk(2), deepened(value))

    @pl.when(is_child[0] == 1)
    def _():
        fill_group(group)
        for f in range(fields):
            for n, side in enumerate(x_halos_of(tx, x_first, x_second, f)):
                x = (0, cols - 1)[n]
                at = (f * 2 + n) * DEPTH
                sides[at : at + levels, :] = side * (nudging[x : x + 1, :] * kappa[x])
        wide[:, :rows], wide[:, rows:] = halves(sides[...])
        value = grouped(wide[...], group[...])
        for f in range(fields):
            for n in range(2):
                at = (f * 2 + n) * DEPTH
                fill_stack(stack.at[f], chunk(n), value[at : at + DEPTH])
        part = weighted(lambda x: nudging[x : x + 1, :] * kappa[x])
        fill_fix(part + pltpu.roll(part, LANE - 2, 1) + pltpu.roll(part, LANE - 4, 1))

    @pl.when(is_child[0] == 0)
    def _():
        back = lax.rem(rows - nest_y[0], rows)
        reached = (nest_x[0] == 0, nest_x[0] + blocks == cols)
        for f in range(fields):
            for n, side in enumerate(x_halos_of(tx, x_first, x_second, f)):
                at = (f * 2 + n) * DEPTH
                weight = kappa[(0, cols - 1)[n]] * reached[n].astype(F32)
                sides[at : at + levels, :] = side * weight
                value = pltpu.roll(sides[at : at + DEPTH, :], back, 1)[:, :LANE]
                fill_stack(stack.at[f], chunk(n), value)
        starts = (nest_y[0] == 0).astype(F32)
        finals = (nest_y[0] == rows - LANE).astype(F32)
        part = weighted(lambda x: kappa[x])
        part = part * jnp.where(lax.rem(lanes, 2) == 0, starts, finals)
        value = jnp.zeros((PAD, LANE), F32)
        for b in range(blocks):
            shift = lax.rem(LANE + 4 * b - 2 * nest_x[0], LANE)
            here = lax.rem(turned, 2 * cols) // 2 == 3 * b
            value = jnp.where(here, pltpu.roll(part, shift, 1), value)
        fill_fix(value)

    fixes = jnp.zeros((PAD, LANE), F32)
    for f in range(fields):
        mixed = mix(matrices[f], stack[f])
        for n in range(2):
            at = pl.ds(f * (2 * levels) + n, levels, stride=2)
            out[at, :] = base[f, :levels, chunk(n)] + mixed[:levels, chunk(n)]
        fixes = jnp.where(turned // (2 * cols) == f, mixed[:PAD, chunk(2)], fixes)
    out[out.shape[0] - PAD :, :] = fixes
    copy.wait()


def outer(
    is_child, tx, ty, state2, matrices, base, kappa, nudging, x_halos, firsts, nests, dims, peers
):
    fields, levels, cols, chunks = dims
    rows = chunks * LANE
    height = -(-fields * 2 * levels // 8) * 8 + PAD
    return pl.pallas_call(
        functools.partial(outer_kernel, levels, peers),
        in_specs=[SMEM] * 3 + [HBM] + [VMEM] * 8 + [SMEM] * 2,
        out_specs=[VMEM] * 2,
        out_shape=[
            pltpu.VMEM((height, LANE), F32),
            pltpu.VMEM((state2.shape[0] // fields, LANE), F32),
        ],
        scratch_shapes=[
            pltpu.VMEM((fields * 2 * DEPTH, rows), F32),
            pltpu.VMEM((fields * 2 * DEPTH, 2 * rows), jnp.bfloat16),
            pltpu.VMEM((fields, 2 * DEPTH, 3 * LANE), jnp.bfloat16),
            pltpu.VMEM((2 * rows, LANE), jnp.bfloat16),
            pltpu.SemaphoreType.DMA,
        ],
        compiler_params=pltpu.CompilerParams(vmem_limit_bytes=12 * MIB),
        name="outer",
    )(is_child, tx, ty, in_hbm(state2), matrices, base, kappa, nudging, *x_halos, *firsts, *nests)


def tile_kernel(
    levels, peers, tx, ty, state, mask, matrices, kappa, x_first, x_second, first, second, ahead,
    out, buf, masked, sides, halo, stack, sems,
):
    cols, _, rows = masked.shape
    chunks = rows // LANE
    size = levels * cols * chunks
    fields = state.shape[0] // size

    def copy(f):
        at = pl.ds(f * size, size)
        return pltpu.make_async_copy(state.at[at], buf.at[at], sems.at[f])

    for f in range(1, fields):
        copy(f).start()
    sides[...] = jnp.zeros_like(sides)
    halo[...] = y_halos(ty, peers, first, second)
    pair = 2

    def field(f, carry, leading=False):
        if leading:
            fill_masked(levels, ahead, f, mask, masked)
        else:
            copy(f).wait()
            fill_masked(levels, buf, f, mask, masked)
        for n, side in enumerate(x_halos_of(tx, x_first, x_second, f)):
            sides[n, :levels, :] = side
        for x0 in range(0, cols, pair):
            for x in range(x0, x0 + pair):
                above = masked[x - 1] if x > 0 else sides[0]
                below = masked[x + 1] if x < cols - 1 else sides[1]
                shift = lax.rem(LANE - 2 * (f * cols + x), LANE)
                edge = pltpu.roll(halo[...], lax.rem(LANE + shift, LANE), 1)
                value = spread_of(masked[x], above, below, kappa[x], edge)
                part = slice((x - x0) * rows, (x - x0 + 1) * rows)
                fill_stack(stack, part, deepened(value))
            mixed = mix(matrices[f], stack[...])
            for n in range(pair * chunks):
                out[aligned((f * cols + x0) * chunks + n, PAD), :] = mixed[:PAD, chunk(n)]
        return carry

    field(0, 0, leading=True)
    lax.fori_loop(1, fields, field, 0)


def tile_of(tx, ty, state2, mask, matrices, kappa, x_halos, firsts, ahead, dims, peers):
    fields, levels, cols, chunks = dims
    rows = chunks * LANE
    return pl.pallas_call(
        functools.partial(tile_kernel, levels, peers),
        in_specs=[SMEM] * 2 + [HBM] + [VMEM] * 8,
        out_specs=VMEM,
        out_shape=pltpu.VMEM((fields * cols * chunks * PAD, LANE), F32),
        scratch_shapes=[
            pltpu.VMEM(state2.shape, F32),
            pltpu.VMEM((cols, PAD, rows), F32),
            pltpu.VMEM((2, PAD, rows), F32),
            pltpu.VMEM((PAD, LANE), F32),
            pltpu.VMEM((2 * DEPTH, 2 * rows), jnp.bfloat16),
            pltpu.SemaphoreType.DMA((fields,)),
        ],
        compiler_params=pltpu.CompilerParams(vmem_limit_bytes=16 * MIB),
        cost_estimate=COST,
        name="tile",
    )(tx, ty, in_hbm(state2), mask, matrices, kappa, *x_halos, *firsts, in_vmem(ahead))


def observe_kernel(dests, across, row, column, counts, places, mine, theirs, _, tile):
    lanes = lane_ids((1, LANE))
    slots = places.shape[1]
    ty, tx = row[0], column[0]
    me = ty * across + tx
    half = mine.shape[0] // slots * (LANE // dests)

    def source(first, ref, n, carry):
        g = first + n
        origin = (((g >> 1) & 1) ^ (3 * ((g >> 2) & 1)) ^ ty) * across
        origin = origin + (((g & 1) | ((g >> 3) << 1)) ^ tx)
        lane_in = lax.rem(n, LANE // dests) * dests + me
        block = lax.div(n, LANE // dests) * slots
        count = counts[0, origin]
        for k in range(0, slots, 2):
            ats, adds = [], []
            for m in range(k, k + 2):
                place = places[origin, m]
                lane = place & (LANE - 1)
                value = pltpu.roll(ref[pl.ds(block + m, 1), :], (lane - lane_in) & (LANE - 1), 1)
                ats.append(place >> 7)
                adds.append(jnp.where(lanes == jnp.where(m < count, lane, LANE), value, 0.0))
            olds = [tile[pl.ds(at, 1), :] for at in ats]
            also = jnp.where(ats[0] == ats[1], adds[0], 0.0)
            tile[pl.ds(ats[0], 1), :] = olds[0] + adds[0]
            tile[pl.ds(ats[1], 1), :] = olds[1] + adds[1] + also
        return carry

    lax.fori_loop(0, half, functools.partial(source, 0, mine), 0)
    lax.fori_loop(0, half, functools.partial(source, half, theirs), 0)


def observe(row, column, places, counts, seen, tile, dests, across):
    return pl.pallas_call(
        functools.partial(observe_kernel, dests, across),
        in_specs=[SMEM] * 4 + [VMEM] * 3,
        out_specs=VMEM,
        out_shape=pltpu.VMEM(tile.shape, F32),
        input_output_aliases={6: 0},
        compiler_params=pltpu.CompilerParams(vmem_limit_bytes=4 * MIB),
        name="observe",
    )(row, column, counts, places, *seen, in_vmem(tile))


def finish_kernel(
    levels, is_child, nest_x, nest_y, tile, mask, in_arrived, out_arrived, in_sent, out_sent,
    out, buf, group, sems,
):
    cols = mask.shape[0]
    rows = mask.shape[2]
    chunks = rows // LANE
    step = cols * chunks
    size = levels * step
    fields = out.shape[0] // size
    blocks = cols // 3
    inner = blocks - 2
    lanes = lane_ids((levels, LANE))
    ends = jnp.logical_or(lanes == 0, lanes == LANE - 1)
    height = out_arrived.shape[0]

    def copy(f):
        at = pl.ds(f * size, size)
        return pltpu.make_async_copy(buf.at[at], out.at[at], sems.at[f])

    def piece_of(f, piece):
        return tile[pl.ds(pl.multiple_of((f * step + piece) * PAD, 8), levels), :]

    def payload(f, b, inner_ref, outer_ref):
        if b in (0, blocks - 1):
            value = outer_ref[pl.ds(f * (2 * levels) + min(b, 1), levels, stride=2), :]
        else:
            value = inner_ref[pl.ds(f * (levels * inner) + b - 1, levels, stride=inner), :]
        fixes = outer_ref[height - PAD : height - PAD + levels, :]
        shift = lax.rem(LANE - 2 * (f * cols + 3 * b), LANE)
        fixes = pltpu.roll(fixes, lax.rem(LANE + shift, LANE), 1)
        return value + jnp.where(ends, fixes, 0.0)

    def fill_child(f, carry):
        for b in range(blocks):
            high, low = halves(payload(f, b, in_arrived, out_arrived))
            both = jnp.concatenate([high, low], axis=1)
            value = jnp.dot(both, group[...], preferred_element_type=F32) * (1.0 / 9.0)
            for x in range(3 * b, 3 * b + 3):
                row = row_of(mask, x)
                for c in range(chunks):
                    piece = x * chunks + c
                    at = pl.ds(f * size + piece, levels, stride=step)
                    total = piece_of(f, piece) + value[:, chunk(c)]
                    buf[at, :] = total * row[:, chunk(c)]
        copy(f).start()
        return carry

    def fill_plain(f, carry):
        for x in range(cols):
            row = row_of(mask, x)
            for c in range(chunks):
                piece = x * chunks + c
                at = pl.ds(f * size + piece, levels, stride=step)
                buf[at, :] = piece_of(f, piece) * row[:, chunk(c)]
        return carry

    def fill_parent(f, carry):
        fill_plain(f, carry)
        for b in range(blocks):
            delta = payload(f, b, in_arrived, out_arrived) - payload(f, b, in_sent, out_sent)
            wide = jnp.concatenate([delta, jnp.zeros((levels, rows - LANE), F32)], 1)
            x = nest_x[0] + b
            value = pltpu.roll(wide, nest_y[0], 1) * row_of(mask, x)
            for c in range(chunks):
                at = pl.ds(f * size + x * chunks + c, levels, stride=step)
                buf[at, :] = buf[at, :] + value[:, chunk(c)]
        copy(f).start()
        return carry

    @pl.when(is_child[0] == 1)
    def _():
        ids = lax.broadcasted_iota(jnp.int32, group.shape, 0)
        ids = jnp.where(ids < LANE, ids, ids - LANE)
        group[...] = jnp.where(lane_ids(group.shape) // 3 == ids, 1.0, 0.0).astype(jnp.bfloat16)
        lax.fori_loop(0, fields, fill_child, 0)

    @pl.when(is_child[0] == 0)
    def _():
        lax.fori_loop(0, fields, fill_parent, 0)

    for f in range(fields):
        copy(f).wait()


def finish(is_child, nests, tile, mask, arrived, sent, dims):
    fields, levels, cols, chunks = dims
    rows = chunks * LANE
    size = (fields * levels * cols * chunks, LANE)
    return pl.pallas_call(
        functools.partial(finish_kernel, levels),
        in_specs=[SMEM] * 3 + [VMEM] * 6,
        out_specs=HBM,
        out_shape=pltpu.HBM(size, F32),
        scratch_shapes=[
            pltpu.VMEM(size, F32),
            pltpu.VMEM((2 * LANE, rows), jnp.bfloat16),
            pltpu.SemaphoreType.DMA((fields,)),
        ],
        compiler_params=pltpu.CompilerParams(vmem_limit_bytes=16 * MIB),
        cost_estimate=COST,
        name="finish",
    )(is_child, *nests, in_vmem(tile), mask, *arrived, *sent)


def from_neighbours(first, second, axis):
    size = lax.axis_size(axis)
    inner = [(i, i + 1) for i in range(1, size - 1, 2)]
    one = swapped(first, axis, 1)
    return one, lax.ppermute(second, axis, inner + [(j, i) for i, j in inner])


def swapped(value, axis, mask):
    return lax.ppermute(value, axis, [(i, i ^ mask) for i in range(lax.axis_size(axis))])


def local(
    adjoint_state,
    land_mask,
    diffusivity,
    mixing,
    nudging,
    nest_x,
    nest_y,
    obs_forcing,
    obs_cell,
    obs_count,
):
    _, fields, levels, cols, rows = adjoint_state.shape
    chunks = rows // LANE
    dims = (fields, levels, cols, chunks)
    state5 = adjoint_state.reshape(fields, levels, cols, 1, rows)
    state2 = adjoint_state.reshape(fields * levels * cols * chunks, LANE)
    mask = land_mask.reshape(cols, 1, rows)
    kappa = diffusivity.reshape(cols, 1, rows)
    mixing = mixing.reshape(fields, levels, 1, levels)
    peers, across = lax.axis_size("ty"), lax.axis_size("tx")
    assert peers == 4 and across & (across - 1) == 0 and 2 * fields * cols <= LANE
    assert levels <= PAD and cols % 3 == 0 and rows == 3 * LANE
    row = lax.axis_index("ty").astype(jnp.int32)
    column = lax.axis_index("tx").astype(jnp.int32)
    ty = row.reshape(1)
    is_child = (lax.axis_index("grp") == 0).astype(jnp.int32).reshape(1)
    nests = (nest_x, nest_y)

    forcing = obs_forcing[0, 0]
    dests = forcing.shape[1]
    counts = obs_count.reshape(1, -1)
    other = swapped(forcing, "tx", 1)
    tx = column.reshape(1)
    *x_sent, ahead = x_edges(tx, state5, mask)
    ahead = ahead.reshape(-1, LANE)
    x_halos = from_neighbours(*x_sent, "tx")
    masked, matrices, parcel, in_sent, places = front(
        is_child, state2, mask, kappa, nudging, mixing, nests, forcing, other, ahead,
        obs_cell[0, :, :, 0], dims,
    )
    first = swapped(parcel, "ty", 1)
    in_arrived = swapped(in_sent, "grp", 1)
    parcel = repack(parcel, first, 2 * dests, PAD)
    second = swapped(parcel, "ty", 3)
    firsts = (first, second)
    masked, x_halos, parcel = lax.optimization_barrier((masked, x_halos, parcel))
    base = base_of(is_child, nests, masked, matrices, kappa, nudging, dims)
    out_sent, ahead = outer(
        is_child, tx, ty, state2, matrices, base, kappa, nudging, x_halos, firsts, nests, dims, peers
    )
    out_sent, in_arrived = lax.optimization_barrier((out_sent, in_arrived))
    out_arrived = swapped(out_sent, "grp", 1)
    seen = repack(parcel, second, 4 * dests, 0)
    seen, out_sent = lax.optimization_barrier((seen, out_sent))
    for n in range(1, across.bit_length() - 2):
        seen = jnp.concatenate([seen, swapped(seen, "tx", 1 << n)])
    seen = (seen, swapped(seen, "tx", across // 2))
    tile = tile_of(tx, ty, state2, mask, matrices, kappa, x_halos, firsts, ahead, dims, peers)
    tile = observe(ty, tx, places, counts, seen, tile, dests, across)
    arrived, sent = (in_arrived, out_arrived), (in_sent, out_sent)
    out = finish(is_child, nests, tile, mask, arrived, sent, dims)
    return out.reshape(adjoint_state.shape)


def solution(mesh):
    in_specs = (
        P("grp", None, None, "tx", "ty"),
        P("grp", "tx", "ty"),
        P("grp", "tx", "ty"),
        P("grp", None, None, None),
        P("tx", "ty"),
        P(("ty", "tx")),
        P(("ty", "tx")),
        P("grp", ("ty", "tx"), None, None),
        P("grp", None, None, ("ty", "tx")),
        P("grp", None, ("ty", "tx")),
    )
    out_specs = P("grp", None, None, "tx", "ty")
    return jax.shard_map(local, mesh=mesh, in_specs=in_specs, out_specs=out_specs, check_vma=False)
```

```python
import functools

import jax
import jax.numpy as jnp
from jax import lax
from jax.experimental import pallas as pl
from jax.experimental.pallas import tpu as pltpu
from jax.sharding import PartitionSpec as P

LANE = 128
PAD = 56
DEPTH = 64
MIB = 1 << 20
HBM = pl.BlockSpec(memory_space=pltpu.HBM)
SMEM = pl.BlockSpec(memory_space=pltpu.SMEM)
VMEM = pl.BlockSpec(memory_space=pltpu.VMEM)
F32 = jnp.float32
COST = pl.CostEstimate(flops=10**10, bytes_accessed=10**8, transcendentals=0)


def lane_ids(shape):
    return lax.broadcasted_iota(jnp.int32, shape, len(shape) - 1)


def row_of(ref, x):
    return ref[x].astype(F32)


def chunk(c):
    return slice(c * LANE, (c + 1) * LANE)


def in_hbm(value):
    return pltpu.with_memory_space_constraint(value, pltpu.HBM)


def in_vmem(value):
    return pltpu.with_memory_space_constraint(value, pltpu.VMEM)


def x_edges_kernel(tx, state, mask, first, second, ahead, buf, mask_buf, sems):
    fields, _, cols = state.shape[:3]
    even = lax.rem(tx[0], 2) == 0
    ends = (jnp.where(even, cols - 1, 0), jnp.where(even, 0, cols - 1))
    copies = [pltpu.make_async_copy(mask, mask_buf, sems.at[2 * fields])]
    for n, x in enumerate(ends):
        for f in range(fields):
            copies.append(
                pltpu.make_async_copy(state.at[f, :, x], buf.at[n, f], sems.at[n * fields + f])
            )
    copies.append(pltpu.make_async_copy(state.at[0], ahead, sems.at[2 * fields + 1]))
    for copy in copies:
        copy.start()
    copies[0].wait()
    for n, (x, out) in enumerate(zip(ends, (first, second))):
        for f in range(fields):
            copies[1 + n * fields + f].wait()
            out[f] = buf[n, f] * row_of(mask_buf, x)[None]
    copies[-1].wait()


def x_edges(tx, state5, mask):
    fields, levels, cols, _, rows = state5.shape
    edge = (fields, levels, 1, rows)
    return pl.pallas_call(
        x_edges_kernel,
        in_specs=[SMEM, HBM, HBM],
        out_specs=[VMEM] * 3,
        out_shape=[pltpu.VMEM(edge, F32)] * 2 + [pltpu.VMEM(state5.shape[1:], F32)],
        scratch_shapes=[
            pltpu.VMEM((2,) + edge, F32),
            pltpu.VMEM(mask.shape, jnp.int32),
            pltpu.SemaphoreType.DMA((2 * fields + 2,)),
        ],
        compiler_params=pltpu.CompilerParams(vmem_limit_bytes=8 * MIB),
        cost_estimate=COST,
        name="x_edges",
    )(tx, in_hbm(state5), in_hbm(mask))


def x_halos_of(tx, first, second, f):
    one, two = first[f, :, 0, :], second[f, :, 0, :]
    even = lax.rem(tx[0], 2) == 0
    return jnp.where(even, two, one), jnp.where(even, one, two)


def spread_of(here, above, below, kappa, edge=None):
    rows = here.shape[1]
    lanes = lane_ids((here.shape[0], LANE))
    edge = 0.0 if edge is None else edge
    before = pltpu.roll(here, 1, 1)
    after = pltpu.roll(here, rows - 1, 1)
    before = jnp.concatenate([jnp.where(lanes == 0, edge, before[:, :LANE]), before[:, LANE:]], 1)
    after = jnp.concatenate(
        [after[:, :-LANE], jnp.where(lanes == LANE - 1, edge, after[:, -LANE:])], 1
    )
    return here + kappa * (above + below + before + after - 4.0 * here)


def halves(value):
    high = value.astype(jnp.bfloat16)
    return high, (value - high.astype(F32)).astype(jnp.bfloat16)


def deepened(value):
    return jnp.concatenate([value, jnp.zeros((DEPTH - value.shape[0], value.shape[1]), F32)], 0)


def fill_matrix(levels, mixing, square, matrix):
    square[:levels, :levels] = mixing
    value = square[...]
    high = value.astype(jnp.bfloat16).astype(F32)
    matrix[:DEPTH, :] = (high + pltpu.roll(high, DEPTH, 1)).astype(jnp.bfloat16)
    matrix[DEPTH:, :] = (value - high).astype(jnp.bfloat16)


def fill_stack(stack, part, value):
    high, low = halves(value)
    stack[:DEPTH, part] = high
    stack[DEPTH:, part] = low


def mix(matrix, stack):
    both = jnp.dot(matrix, stack, preferred_element_type=F32)
    return both[:DEPTH] + both[DEPTH:]


def fill_group(group):
    rows = group.shape[0] // 2
    ids = lax.broadcasted_iota(jnp.int32, group.shape, 0)
    ids = jnp.where(ids < rows, ids, ids - rows) // 3
    group[...] = jnp.where(ids == lane_ids(group.shape), 1.0, 0.0).astype(jnp.bfloat16)


def grouped(wide, group):
    return jnp.dot(wide, group, preferred_element_type=F32)


def aligned(index, size):
    return pl.ds(pl.multiple_of(index * size, size), size)


def packed(rows_of, cols):
    parts = []
    for x in range(cols):
        first, last = rows_of(x)
        lanes = lane_ids(first.shape)
        parts.append(jnp.where(lanes == 0, first, jnp.where(lanes == LANE - 1, last, 0.0)))
    shift = 2
    while len(parts) > 1:
        pairs = [parts[n : n + 2] for n in range(0, len(parts), 2)]
        parts = [p[0] + pltpu.roll(p[1], shift, 1) if len(p) == 2 else p[0] for p in pairs]
        shift *= 2
    return parts[0]


def fill_masked(levels, state, f, mask, masked):
    cols, _, rows = masked.shape
    chunks = rows // LANE
    step = cols * chunks
    for x in range(cols):
        row = row_of(mask, x)
        masked[x, PAD - 8 :, :] = jnp.zeros((8, rows), F32)
        for c in range(chunks):
            at = pl.ds(f * (levels * step) + x * chunks + c, levels, stride=step)
            masked[x, :levels, chunk(c)] = state[at, :] * row[:, chunk(c)]


TERMS = 11


def join_weights(bs, cols, kappa, nudging, weights):
    rows = weights.shape[1]
    ids = lane_ids((1, rows))
    for i, b in enumerate(bs):
        own = range(3 * b, 3 * b + 3)
        both = {x: nudging[x : x + 1, :] * kappa[x] for x in own}
        for n, x in enumerate(range(3 * b - 1, 3 * b + 4)):
            total = None
            for near in (x - 1, x + 1):
                if near in both:
                    total = both[near] if total is None else total + both[near]
            if x in both:
                total = total + (nudging[x : x + 1, :] - 4.0 * both[x])
            weights[i * TERMS + n : i * TERMS + n + 1, :] = total
        for n, x in enumerate(own):
            at = i * TERMS + 5 + n
            value = jnp.where(ids == rows - 1, 0.0, pltpu.roll(both[x], rows - 1, 1))
            weights[at : at + 1, :] = value
            value = jnp.where(ids == 0, 0.0, pltpu.roll(both[x], 1, 1))
            weights[at + 3 : at + 4, :] = value


def child_rows(f, bs, masked, weights, wide):
    cols, _, rows = masked.shape[1:]
    for i, b in enumerate(bs):

        def term(n, x):
            at = i * TERMS + n
            return weights[at : at + 1, :] * masked[f, x]

        total = None
        for n, x in enumerate(range(3 * b - 1, 3 * b + 4)):
            if 0 <= x < cols:
                total = term(n, x) if total is None else total + term(n, x)
        for side, shift in ((5, 1), (8, rows - 1)):
            value = term(side, 3 * b) + term(side + 1, 3 * b + 1) + term(side + 2, 3 * b + 2)
            total = total + pltpu.roll(value, shift, 1)
        at = aligned(f * len(bs) + i, DEPTH)
        wide[at, :rows], wide[at, rows:] = halves(deepened(total))


def parent_rows(f, bs, nest_x, nest_y, masked, kappa, stack):
    cols, _, rows = masked.shape[1:]
    back = lax.rem(rows - nest_y[0], rows)
    for i, b in enumerate(bs):
        x = nest_x[0] + b
        above = masked[f, jnp.maximum(x - 1, 0)]
        below = masked[f, jnp.minimum(x + 1, cols - 1)]
        if b == 0:
            above = jnp.where(x == 0, 0.0, above)
        if b == cols // 3 - 1:
            below = jnp.where(x == cols - 1, 0.0, below)
        value = spread_of(masked[f, x], above, below, kappa[x])
        value = deepened(pltpu.roll(value, back, 1)[:, :LANE])
        fill_stack(stack.at[f], chunk(i), value)


def mix_rows(bs, is_child, wide, group, stack, matrices, emit):
    fields = stack.shape[0]

    @pl.when(is_child[0] == 1)
    def _():
        value = grouped(wide[...], group[...])
        for f in range(fields):
            for i in range(len(bs)):
                at = (f * len(bs) + i) * DEPTH
                fill_stack(stack.at[f], chunk(i), value[at : at + DEPTH])

    for f in range(fields):
        emit(f, mix(matrices[f], stack[f]))


def row_scratch(bs, fields, rows):
    return [
        pltpu.VMEM((-(-len(bs) * TERMS // 8) * 8, rows), F32),
        pltpu.VMEM((fields * len(bs) * DEPTH, 2 * rows), jnp.bfloat16),
        pltpu.VMEM((fields, 2 * DEPTH, len(bs) * LANE), jnp.bfloat16),
        pltpu.VMEM((2 * rows, LANE), jnp.bfloat16),
    ]


ROOM = 18


def front_kernel(
    levels, bs, slots, is_child, state, mask, kappa, nudging, mixing, nest_x, nest_y, ahead, cells, *refs
):
    refs = list(refs)
    line = [refs.pop(0) for _ in range(len(refs) - ROOM)]
    front_steps(
        levels, bs, slots, line, is_child, state, mask, kappa, nudging, mixing, nest_x, nest_y, ahead,
        cells, *refs
    )


def front_steps(
    levels, bs, slots, line, is_child, state, mask, kappa, nudging, mixing, nest_x, nest_y, ahead,
    cells, masked_out, matrices, parcel, inner, places,
    buf, masked, mask_buf, kappa_buf, nudging_buf, mixing_buf, square, weights, wide, stack, group, sems, out_sems,
):
    fields, cols, _, rows = masked.shape
    chunks = rows // LANE
    step = cols * chunks
    size = levels * step

    def copy(f):
        at = pl.ds(f * size, size)
        return pltpu.make_async_copy(state.at[at], buf.at[at], sems.at[f])

    def copy_out(f):
        return pltpu.make_async_copy(masked.at[f], masked_out.at[f], out_sems.at[f])

    pairs = (
        (mask, mask_buf),
        (kappa, kappa_buf),
        (nudging, nudging_buf),
        (mixing, mixing_buf),
    )
    smalls = [
        pltpu.make_async_copy(source, target, sems.at[fields + n])
        for n, (source, target) in enumerate(pairs)
    ]
    for small in smalls:
        small.start()
    for f in range(1, fields):
        copy(f).start()
    square[...] = jnp.zeros_like(square)
    cell = cells[...]
    column, inside = cell // (cols * rows), lax.rem(cell, cols * rows)
    piece = (column // levels) * step + inside // LANE
    place = (piece * PAD + lax.rem(column, levels)) * LANE + lax.rem(inside, LANE)
    places[...] = place
    for small in smalls:
        small.wait()

    @pl.when(is_child[0] == 1)
    def _():
        fill_group(group)
        join_weights(bs, cols, kappa_buf, nudging_buf, weights)

    def field(f, total_edges, first=False):
        fill_matrix(levels, mixing_buf[f, :, 0, :], square, matrices.at[f])
        if first:
            fill_masked(levels, ahead, f, mask_buf, masked.at[f])
        else:
            copy(f).wait()
            fill_masked(levels, buf, f, mask_buf, masked.at[f])
        copy_out(f).start()
        own_edges = packed(
            lambda x: (masked[f, x, :, :LANE], masked[f, x, :, rows - LANE :]), cols
        )

        @pl.when(is_child[0] == 1)
        def _():
            child_rows(f, bs, masked, weights, wide)

        @pl.when(is_child[0] == 0)
        def _():
            parent_rows(f, bs, nest_x, nest_y, masked, kappa_buf, stack)

        return total_edges + pltpu.roll(own_edges, 2 * f * cols, 1)

    own_edges = field(0, jnp.zeros((PAD, LANE), F32), first=True)
    parcel[:PAD, :] = lax.fori_loop(1, fields, field, own_edges)
    parcel[PAD:, :] = jnp.zeros((parcel.shape[0] - PAD, LANE), F32)
    lane = 0
    for blocks in line:
        dests = blocks.shape[1]
        for start in range(0, blocks.shape[0], slots):
            at = PAD + lane // LANE * slots
            part = slice(lane % LANE, lane % LANE + dests)
            parcel[at : at + slots, part] = blocks[start : start + slots, :]
            lane += dests

    def emit(f, mixed):
        for i in range(len(bs)):
            at = pl.ds(f * levels * len(bs) + i, levels, stride=len(bs))
            inner[at, :] = mixed[:levels, chunk(i)]

    mix_rows(bs, is_child, wide, group, stack, matrices, emit)
    for f in range(fields):
        copy_out(f).wait()


def front(is_child, state2, mask, kappa, nudging, mixing, nests, line, ahead, cells, dims):
    fields, levels, cols, chunks = dims
    rows = chunks * LANE
    bs = tuple(range(1, cols // 3 - 1))
    arrays = (state2, mask, kappa, nudging, mixing)
    slots = cells.shape[1]
    height = -(-sum(blocks.size for blocks in line) // (LANE * slots)) * slots
    return pl.pallas_call(
        functools.partial(front_kernel, levels, bs, slots),
        in_specs=[SMEM] + [HBM] * 5 + [SMEM] * 2 + [VMEM] * (2 + len(line)),
        out_specs=[HBM] + [VMEM] * 4,
        out_shape=[
            pltpu.HBM((fields, cols, PAD, rows), F32),
            pltpu.VMEM((fields, 2 * DEPTH, 2 * DEPTH), jnp.bfloat16),
            pltpu.VMEM((PAD + height, LANE), F32),
            pltpu.VMEM((fields * levels * len(bs), LANE), F32),
            pltpu.VMEM(cells.shape, jnp.int32),
        ],
        scratch_shapes=[
            pltpu.VMEM(state2.shape, F32),
            pltpu.VMEM((fields, cols, PAD, rows), F32),
            pltpu.VMEM(mask.shape, jnp.int32),
            pltpu.VMEM(kappa.shape, F32),
            pltpu.VMEM(nudging.shape, F32),
            pltpu.VMEM(mixing.shape, F32),
            pltpu.VMEM((DEPTH, LANE), F32),
        ]
        + row_scratch(bs, fields, rows)
        + [pltpu.SemaphoreType.DMA((fields + 4,)), pltpu.SemaphoreType.DMA((fields,))],
        compiler_params=pltpu.CompilerParams(vmem_limit_bytes=24 * MIB),
        cost_estimate=COST,
        name="front",
    )(is_child, *map(in_hbm, arrays), *nests, in_vmem(ahead), cells, *line)


def base_kernel(
    levels, bs, is_child, nest_x, nest_y, masked_in, matrices, kappa, nudging, base,
    masked, weights, wide, stack, group, sems,
):
    fields, cols = masked.shape[:2]
    near = cols // 3
    reach = near + 2

    def child_copies(f):
        for n, x in enumerate((0, cols - near)):
            at = pl.ds(x, near)
            yield pltpu.make_async_copy(masked_in.at[f, at], masked.at[f, at], sems.at[f, n])

    def parent_copy(f):
        at = pl.ds(jnp.clip(nest_x[0] - 1, 0, cols - reach), reach)
        return pltpu.make_async_copy(masked_in.at[f, at], masked.at[f, at], sems.at[f, 0])

    @pl.when(is_child[0] == 1)
    def _():
        for f in range(fields):
            for copy in child_copies(f):
                copy.start()
        fill_group(group)
        join_weights(bs, cols, kappa, nudging, weights)

        def field(f, carry):
            for copy in child_copies(f):
                copy.wait()
            child_rows(f, bs, masked, weights, wide)
            return carry

        lax.fori_loop(0, fields, field, 0)

    @pl.when(is_child[0] == 0)
    def _():
        for f in range(fields):
            parent_copy(f).start()

        def field(f, carry):
            parent_copy(f).wait()
            parent_rows(f, bs, nest_x, nest_y, masked, kappa, stack)
            return carry

        lax.fori_loop(0, fields, field, 0)

    def emit(f, mixed):
        base[f, :, :] = mixed[:PAD, :]

    mix_rows(bs, is_child, wide, group, stack, matrices, emit)


def base_of(is_child, nests, masked, matrices, kappa, nudging, dims):
    fields, levels, cols, chunks = dims
    rows = chunks * LANE
    bs = (0, cols // 3 - 1)
    return pl.pallas_call(
        functools.partial(base_kernel, levels, bs),
        in_specs=[SMEM] * 3 + [HBM] + [VMEM] * 3,
        out_specs=VMEM,
        out_shape=pltpu.VMEM((fields, PAD, 2 * LANE), F32),
        scratch_shapes=[pltpu.VMEM(masked.shape, F32)]
        + row_scratch(bs, fields, rows)
        + [pltpu.SemaphoreType.DMA((fields, 2))],
        compiler_params=pltpu.CompilerParams(vmem_limit_bytes=16 * MIB),
        cost_estimate=COST,
        name="base",
    )(is_child, *nests, in_hbm(masked), matrices, kappa, nudging)


def merged(own, other, width):
    if 2 * width <= LANE:
        return own + pltpu.roll(other, width, 1)
    return jnp.concatenate([own, other], axis=0)


def repack_kernel(width, edges, parcel, arrived, out):
    if edges:
        out[:edges, :] = parcel[:edges, :]
    out[edges:, :] = merged(parcel[PAD:, :], arrived[PAD:, :], width)


def repack(parcel, arrived, width, edges):
    height = (parcel.shape[0] - PAD) * (1 if 2 * width <= LANE else 2)
    return pl.pallas_call(
        functools.partial(repack_kernel, width, edges),
        in_specs=[VMEM] * 2,
        out_specs=VMEM,
        out_shape=pltpu.VMEM((edges + height, LANE), F32),
        compiler_params=pltpu.CompilerParams(vmem_limit_bytes=4 * MIB),
        name="repack",
    )(parcel, arrived)


def y_halos(ty, peers, first, second):
    one, two = first[:PAD, :], second[:PAD, :]
    even = (lax.rem(ty[0], 2) == 0).astype(F32)
    odd = 1.0 - even
    before = (two * even + one * odd) * (ty[0] > 0).astype(F32)
    after = (one * even + two * odd) * (ty[0] < peers - 1).astype(F32)
    low = lax.rem(lane_ids((PAD, LANE)), 2) == 0
    return jnp.where(low, pltpu.roll(before, 1, 1), pltpu.roll(after, LANE - 1, 1))


def outer_kernel(
    levels, peers, is_child, tx, ty, state, matrices, base, kappa, nudging, x_first, x_second,
    first, second, nest_x, nest_y, out, ahead, sides, wide, stack, group, sem,
):
    fields = matrices.shape[0]
    cols, _, rows = kappa.shape
    blocks = cols // 3
    lanes = lane_ids((PAD, LANE))
    turned = lax.rem(lanes + 1, LANE)
    copy = pltpu.make_async_copy(state.at[pl.ds(0, ahead.shape[0])], ahead, sem)
    copy.start()
    sides[...] = jnp.zeros_like(sides)
    halo = y_halos(ty, peers, first, second)

    def weighted(row_of_x):
        one = packed(lambda x: (row_of_x(x)[:, :LANE], row_of_x(x)[:, rows - LANE :]), cols)
        total = one
        for f in range(1, fields):
            total = total + pltpu.roll(one, 2 * f * cols, 1)
        return halo * total

    def fill_fix(value):
        for f in range(fields):
            fill_stack(stack.at[f], chunk(2), deepened(value))

    @pl.when(is_child[0] == 1)
    def _():
        fill_group(group)
        for f in range(fields):
            for n, side in enumerate(x_halos_of(tx, x_first, x_second, f)):
                x = (0, cols - 1)[n]
                at = (f * 2 + n) * DEPTH
                sides[at : at + levels, :] = side * (nudging[x : x + 1, :] * kappa[x])
        wide[:, :rows], wide[:, rows:] = halves(sides[...])
        value = grouped(wide[...], group[...])
        for f in range(fields):
            for n in range(2):
                at = (f * 2 + n) * DEPTH
                fill_stack(stack.at[f], chunk(n), value[at : at + DEPTH])
        part = weighted(lambda x: nudging[x : x + 1, :] * kappa[x])
        fill_fix(part + pltpu.roll(part, LANE - 2, 1) + pltpu.roll(part, LANE - 4, 1))

    @pl.when(is_child[0] == 0)
    def _():
        back = lax.rem(rows - nest_y[0], rows)
        reached = (nest_x[0] == 0, nest_x[0] + blocks == cols)
        for f in range(fields):
            for n, side in enumerate(x_halos_of(tx, x_first, x_second, f)):
                at = (f * 2 + n) * DEPTH
                weight = kappa[(0, cols - 1)[n]] * reached[n].astype(F32)
                sides[at : at + levels, :] = side * weight
                value = pltpu.roll(sides[at : at + DEPTH, :], back, 1)[:, :LANE]
                fill_stack(stack.at[f], chunk(n), value)
        starts = (nest_y[0] == 0).astype(F32)
        finals = (nest_y[0] == rows - LANE).astype(F32)
        part = weighted(lambda x: kappa[x])
        part = part * jnp.where(lax.rem(lanes, 2) == 0, starts, finals)
        value = jnp.zeros((PAD, LANE), F32)
        for b in range(blocks):
            shift = lax.rem(LANE + 4 * b - 2 * nest_x[0], LANE)
            here = lax.rem(turned, 2 * cols) // 2 == 3 * b
            value = jnp.where(here, pltpu.roll(part, shift, 1), value)
        fill_fix(value)

    fixes = jnp.zeros((PAD, LANE), F32)
    for f in range(fields):
        mixed = mix(matrices[f], stack[f])
        for n in range(2):
            at = pl.ds(f * (2 * levels) + n, levels, stride=2)
            out[at, :] = base[f, :levels, chunk(n)] + mixed[:levels, chunk(n)]
        fixes = jnp.where(turned // (2 * cols) == f, mixed[:PAD, chunk(2)], fixes)
    out[out.shape[0] - PAD :, :] = fixes
    copy.wait()


def outer(
    is_child, tx, ty, state2, matrices, base, kappa, nudging, x_halos, firsts, nests, dims, peers
):
    fields, levels, cols, chunks = dims
    rows = chunks * LANE
    height = -(-fields * 2 * levels // 8) * 8 + PAD
    return pl.pallas_call(
        functools.partial(outer_kernel, levels, peers),
        in_specs=[SMEM] * 3 + [HBM] + [VMEM] * 8 + [SMEM] * 2,
        out_specs=[VMEM] * 2,
        out_shape=[
            pltpu.VMEM((height, LANE), F32),
            pltpu.VMEM((state2.shape[0] // fields, LANE), F32),
        ],
        scratch_shapes=[
            pltpu.VMEM((fields * 2 * DEPTH, rows), F32),
            pltpu.VMEM((fields * 2 * DEPTH, 2 * rows), jnp.bfloat16),
            pltpu.VMEM((fields, 2 * DEPTH, 3 * LANE), jnp.bfloat16),
            pltpu.VMEM((2 * rows, LANE), jnp.bfloat16),
            pltpu.SemaphoreType.DMA,
        ],
        compiler_params=pltpu.CompilerParams(vmem_limit_bytes=12 * MIB),
        name="outer",
    )(is_child, tx, ty, in_hbm(state2), matrices, base, kappa, nudging, *x_halos, *firsts, *nests)


def tile_kernel(
    levels, peers, tx, ty, state, mask, matrices, kappa, x_first, x_second, first, second, ahead,
    out, buf, masked, sides, halo, stack, sems,
):
    cols, _, rows = masked.shape
    chunks = rows // LANE
    size = levels * cols * chunks
    fields = state.shape[0] // size

    def copy(f):
        at = pl.ds(f * size, size)
        return pltpu.make_async_copy(state.at[at], buf.at[at], sems.at[f])

    for f in range(1, fields):
        copy(f).start()
    sides[...] = jnp.zeros_like(sides)
    halo[...] = y_halos(ty, peers, first, second)
    pair = 2

    def field(f, carry, leading=False):
        if leading:
            fill_masked(levels, ahead, f, mask, masked)
        else:
            copy(f).wait()
            fill_masked(levels, buf, f, mask, masked)
        for n, side in enumerate(x_halos_of(tx, x_first, x_second, f)):
            sides[n, :levels, :] = side
        for x0 in range(0, cols, pair):
            for x in range(x0, x0 + pair):
                above = masked[x - 1] if x > 0 else sides[0]
                below = masked[x + 1] if x < cols - 1 else sides[1]
                shift = lax.rem(LANE - 2 * (f * cols + x), LANE)
                edge = pltpu.roll(halo[...], lax.rem(LANE + shift, LANE), 1)
                value = spread_of(masked[x], above, below, kappa[x], edge)
                part = slice((x - x0) * rows, (x - x0 + 1) * rows)
                fill_stack(stack, part, deepened(value))
            mixed = mix(matrices[f], stack[...])
            for n in range(pair * chunks):
                out[aligned((f * cols + x0) * chunks + n, PAD), :] = mixed[:PAD, chunk(n)]
        return carry

    field(0, 0, leading=True)
    lax.fori_loop(1, fields, field, 0)


def tile_of(tx, ty, state2, mask, matrices, kappa, x_halos, firsts, ahead, dims, peers):
    fields, levels, cols, chunks = dims
    rows = chunks * LANE
    return pl.pallas_call(
        functools.partial(tile_kernel, levels, peers),
        in_specs=[SMEM] * 2 + [HBM] + [VMEM] * 8,
        out_specs=VMEM,
        out_shape=pltpu.VMEM((fields * cols * chunks * PAD, LANE), F32),
        scratch_shapes=[
            pltpu.VMEM(state2.shape, F32),
            pltpu.VMEM((cols, PAD, rows), F32),
            pltpu.VMEM((2, PAD, rows), F32),
            pltpu.VMEM((PAD, LANE), F32),
            pltpu.VMEM((2 * DEPTH, 2 * rows), jnp.bfloat16),
            pltpu.SemaphoreType.DMA((fields,)),
        ],
        compiler_params=pltpu.CompilerParams(vmem_limit_bytes=16 * MIB),
        cost_estimate=COST,
        name="tile",
    )(tx, ty, in_hbm(state2), mask, matrices, kappa, *x_halos, *firsts, in_vmem(ahead))


def observe_kernel(dests, across, row, column, counts, places, mine, theirs, _, tile):
    lanes = lane_ids((1, LANE))
    slots = places.shape[1]
    ty, tx = row[0], column[0]
    me = ty * across + tx
    half = (mine.shape[0] - PAD) // slots * (LANE // dests)

    def source(turn, ref, g, carry):
        origin = (lax.div(g, across) ^ turn ^ ty) * across + (lax.rem(g, across) ^ tx)
        lane_in = lax.rem(g, LANE // dests) * dests + me
        block = PAD + lax.div(g, LANE // dests) * slots
        count = counts[0, origin]
        for k in range(0, slots, 2):
            ats, adds = [], []
            for m in range(k, k + 2):
                place = places[origin, m]
                lane = place & (LANE - 1)
                value = pltpu.roll(ref[pl.ds(block + m, 1), :], (lane - lane_in) & (LANE - 1), 1)
                ats.append(place >> 7)
                adds.append(jnp.where(lanes == jnp.where(m < count, lane, LANE), value, 0.0))
            olds = [tile[pl.ds(at, 1), :] for at in ats]
            also = jnp.where(ats[0] == ats[1], adds[0], 0.0)
            tile[pl.ds(ats[0], 1), :] = olds[0] + adds[0]
            tile[pl.ds(ats[1], 1), :] = olds[1] + adds[1] + also
        return carry

    lax.fori_loop(0, half, functools.partial(source, 0, mine), 0)
    lax.fori_loop(0, half, functools.partial(source, 3, theirs), 0)


def observe(row, column, places, counts, seen, tile, dests, across):
    return pl.pallas_call(
        functools.partial(observe_kernel, dests, across),
        in_specs=[SMEM] * 4 + [VMEM] * 3,
        out_specs=VMEM,
        out_shape=pltpu.VMEM(tile.shape, F32),
        input_output_aliases={6: 0},
        compiler_params=pltpu.CompilerParams(vmem_limit_bytes=4 * MIB),
        name="observe",
    )(row, column, counts, places, *seen, in_vmem(tile))


def finish_kernel(
    levels, is_child, nest_x, nest_y, tile, mask, in_arrived, out_arrived, in_sent, out_sent,
    out, buf, group, sems,
):
    cols = mask.shape[0]
    rows = mask.shape[2]
    chunks = rows // LANE
    step = cols * chunks
    size = levels * step
    fields = out.shape[0] // size
    blocks = cols // 3
    inner = blocks - 2
    lanes = lane_ids((levels, LANE))
    ends = jnp.logical_or(lanes == 0, lanes == LANE - 1)
    height = out_arrived.shape[0]

    def copy(f):
        at = pl.ds(f * size, size)
        return pltpu.make_async_copy(buf.at[at], out.at[at], sems.at[f])

    def piece_of(f, piece):
        return tile[pl.ds(pl.multiple_of((f * step + piece) * PAD, 8), levels), :]

    def payload(f, b, inner_ref, outer_ref):
        if b in (0, blocks - 1):
            value = outer_ref[pl.ds(f * (2 * levels) + min(b, 1), levels, stride=2), :]
        else:
            value = inner_ref[pl.ds(f * (levels * inner) + b - 1, levels, stride=inner), :]
        fixes = outer_ref[height - PAD : height - PAD + levels, :]
        shift = lax.rem(LANE - 2 * (f * cols + 3 * b), LANE)
        fixes = pltpu.roll(fixes, lax.rem(LANE + shift, LANE), 1)
        return value + jnp.where(ends, fixes, 0.0)

    def fill_child(f, carry):
        for b in range(blocks):
            high, low = halves(payload(f, b, in_arrived, out_arrived))
            both = jnp.concatenate([high, low], axis=1)
            value = jnp.dot(both, group[...], preferred_element_type=F32) * (1.0 / 9.0)
            for x in range(3 * b, 3 * b + 3):
                row = row_of(mask, x)
                for c in range(chunks):
                    piece = x * chunks + c
                    at = pl.ds(f * size + piece, levels, stride=step)
                    total = piece_of(f, piece) + value[:, chunk(c)]
                    buf[at, :] = total * row[:, chunk(c)]
        copy(f).start()
        return carry

    def fill_plain(f, carry):
        for x in range(cols):
            row = row_of(mask, x)
            for c in range(chunks):
                piece = x * chunks + c
                at = pl.ds(f * size + piece, levels, stride=step)
                buf[at, :] = piece_of(f, piece) * row[:, chunk(c)]
        return carry

    def fill_parent(f, carry):
        fill_plain(f, carry)
        for b in range(blocks):
            delta = payload(f, b, in_arrived, out_arrived) - payload(f, b, in_sent, out_sent)
            wide = jnp.concatenate([delta, jnp.zeros((levels, rows - LANE), F32)], 1)
            x = nest_x[0] + b
            value = pltpu.roll(wide, nest_y[0], 1) * row_of(mask, x)
            for c in range(chunks):
                at = pl.ds(f * size + x * chunks + c, levels, stride=step)
                buf[at, :] = buf[at, :] + value[:, chunk(c)]
        copy(f).start()
        return carry

    @pl.when(is_child[0] == 1)
    def _():
        ids = lax.broadcasted_iota(jnp.int32, group.shape, 0)
        ids = jnp.where(ids < LANE, ids, ids - LANE)
        group[...] = jnp.where(lane_ids(group.shape) // 3 == ids, 1.0, 0.0).astype(jnp.bfloat16)
        lax.fori_loop(0, fields, fill_child, 0)

    @pl.when(is_child[0] == 0)
    def _():
        lax.fori_loop(0, fields, fill_parent, 0)

    for f in range(fields):
        copy(f).wait()


def finish(is_child, nests, tile, mask, arrived, sent, dims):
    fields, levels, cols, chunks = dims
    rows = chunks * LANE
    size = (fields * levels * cols * chunks, LANE)
    return pl.pallas_call(
        functools.partial(finish_kernel, levels),
        in_specs=[SMEM] * 3 + [VMEM] * 6,
        out_specs=HBM,
        out_shape=pltpu.HBM(size, F32),
        scratch_shapes=[
            pltpu.VMEM(size, F32),
            pltpu.VMEM((2 * LANE, rows), jnp.bfloat16),
            pltpu.SemaphoreType.DMA((fields,)),
        ],
        compiler_params=pltpu.CompilerParams(vmem_limit_bytes=16 * MIB),
        cost_estimate=COST,
        name="finish",
    )(is_child, *nests, in_vmem(tile), mask, *arrived, *sent)


def from_neighbours(first, second, axis):
    size = lax.axis_size(axis)
    inner = [(i, i + 1) for i in range(1, size - 1, 2)]
    one = swapped(first, axis, 1)
    return one, lax.ppermute(second, axis, inner + [(j, i) for i, j in inner])


def swapped(value, axis, mask):
    return lax.ppermute(value, axis, [(i, i ^ mask) for i in range(lax.axis_size(axis))])


def local(
    adjoint_state,
    land_mask,
    diffusivity,
    mixing,
    nudging,
    nest_x,
    nest_y,
    obs_forcing,
    obs_cell,
    obs_count,
):
    _, fields, levels, cols, rows = adjoint_state.shape
    chunks = rows // LANE
    dims = (fields, levels, cols, chunks)
    state5 = adjoint_state.reshape(fields, levels, cols, 1, rows)
    state2 = adjoint_state.reshape(fields * levels * cols * chunks, LANE)
    mask = land_mask.reshape(cols, 1, rows)
    kappa = diffusivity.reshape(cols, 1, rows)
    mixing = mixing.reshape(fields, levels, 1, levels)
    peers, across = lax.axis_size("ty"), lax.axis_size("tx")
    assert peers == 4 and across & (across - 1) == 0 and 2 * fields * cols <= LANE
    assert levels <= PAD and cols % 3 == 0 and rows == 3 * LANE
    row = lax.axis_index("ty").astype(jnp.int32)
    column = lax.axis_index("tx").astype(jnp.int32)
    ty = row.reshape(1)
    is_child = (lax.axis_index("grp") == 0).astype(jnp.int32).reshape(1)
    nests = (nest_x, nest_y)

    forcing = obs_forcing[0, 0]
    dests = forcing.shape[1]
    counts = obs_count.reshape(1, -1)
    line = [forcing, *(swapped(forcing, "tx", n) for n in range(1, min(across, 4)))]
    for n in range(2, across.bit_length() - 1):
        blocks = jnp.concatenate(line)
        line = [blocks, swapped(blocks, "tx", 1 << n)]
    tx = column.reshape(1)
    *x_sent, ahead = x_edges(tx, state5, mask)
    ahead = ahead.reshape(-1, LANE)
    x_halos = from_neighbours(*x_sent, "tx")
    masked, matrices, parcel, in_sent, places = front(
        is_child, state2, mask, kappa, nudging, mixing, nests, line, ahead,
        obs_cell[0, :, :, 0], dims,
    )
    first = swapped(parcel, "ty", 1)
    in_arrived = swapped(in_sent, "grp", 1)
    parcel = repack(parcel, first, across * dests, PAD)
    second = swapped(parcel, "ty", 3)
    firsts = (first, second)
    masked, x_halos, parcel = lax.optimization_barrier((masked, x_halos, parcel))
    base = base_of(is_child, nests, masked, matrices, kappa, nudging, dims)
    out_sent, ahead = outer(
        is_child, tx, ty, state2, matrices, base, kappa, nudging, x_halos, firsts, nests, dims, peers
    )
    out_arrived = swapped(out_sent, "grp", 1)
    tile = tile_of(tx, ty, state2, mask, matrices, kappa, x_halos, firsts, ahead, dims, peers)
    tile = observe(ty, tx, places, counts, (parcel, second), tile, dests, across)
    arrived, sent = (in_arrived, out_arrived), (in_sent, out_sent)
    out = finish(is_child, nests, tile, mask, arrived, sent, dims)
    return out.reshape(adjoint_state.shape)


def solution(mesh):
    in_specs = (
        P("grp", None, None, "tx", "ty"),
        P("grp", "tx", "ty"),
        P("grp", "tx", "ty"),
        P("grp", None, None, None),
        P("tx", "ty"),
        P(("ty", "tx")),
        P(("ty", "tx")),
        P("grp", ("ty", "tx"), None, None),
        P("grp", None, None, ("ty", "tx")),
        P("grp", None, ("ty", "tx")),
    )
    out_specs = P("grp", None, None, "tx", "ty")
    return jax.shard_map(local, mesh=mesh, in_specs=in_specs, out_specs=out_specs, check_vma=False)
```

```python
import functools

import jax
import jax.numpy as jnp
from jax import lax
from jax.experimental import pallas as pl
from jax.experimental.pallas import tpu as pltpu
from jax.sharding import PartitionSpec as P

LANE = 128
PAD = 56
DEPTH = 64
MIB = 1 << 20
HBM = pl.BlockSpec(memory_space=pltpu.HBM)
SMEM = pl.BlockSpec(memory_space=pltpu.SMEM)
VMEM = pl.BlockSpec(memory_space=pltpu.VMEM)
F32 = jnp.float32
COST = pl.CostEstimate(flops=10**10, bytes_accessed=10**8, transcendentals=0)


def lane_ids(shape):
    return lax.broadcasted_iota(jnp.int32, shape, len(shape) - 1)


def row_of(ref, x):
    return ref[x].astype(F32)


def chunk(c):
    return slice(c * LANE, (c + 1) * LANE)


def in_hbm(value):
    return pltpu.with_memory_space_constraint(value, pltpu.HBM)


def in_vmem(value):
    return pltpu.with_memory_space_constraint(value, pltpu.VMEM)


def x_edges_kernel(tx, state, mask, first, second, ahead, buf, mask_buf, sems):
    fields, _, cols = state.shape[:3]
    even = lax.rem(tx[0], 2) == 0
    ends = (jnp.where(even, cols - 1, 0), jnp.where(even, 0, cols - 1))
    copies = [pltpu.make_async_copy(mask, mask_buf, sems.at[2 * fields])]
    for n, x in enumerate(ends):
        for f in range(fields):
            copies.append(
                pltpu.make_async_copy(state.at[f, :, x], buf.at[n, f], sems.at[n * fields + f])
            )
    copies.append(pltpu.make_async_copy(state.at[0], ahead, sems.at[2 * fields + 1]))
    for copy in copies:
        copy.start()
    copies[0].wait()
    for n, (x, out) in enumerate(zip(ends, (first, second))):
        for f in range(fields):
            copies[1 + n * fields + f].wait()
            out[f] = buf[n, f] * row_of(mask_buf, x)[None]
    copies[-1].wait()


def x_edges(tx, state5, mask):
    fields, levels, cols, _, rows = state5.shape
    edge = (fields, levels, 1, rows)
    return pl.pallas_call(
        x_edges_kernel,
        in_specs=[SMEM, HBM, HBM],
        out_specs=[VMEM] * 3,
        out_shape=[pltpu.VMEM(edge, F32)] * 2 + [pltpu.VMEM(state5.shape[1:], F32)],
        scratch_shapes=[
            pltpu.VMEM((2,) + edge, F32),
            pltpu.VMEM(mask.shape, jnp.int32),
            pltpu.SemaphoreType.DMA((2 * fields + 2,)),
        ],
        compiler_params=pltpu.CompilerParams(vmem_limit_bytes=8 * MIB),
        cost_estimate=COST,
        name="x_edges",
    )(tx, in_hbm(state5), in_hbm(mask))


def x_halos_of(tx, first, second, f):
    one, two = first[f, :, 0, :], second[f, :, 0, :]
    even = lax.rem(tx[0], 2) == 0
    return jnp.where(even, two, one), jnp.where(even, one, two)


def spread_of(here, above, below, kappa, edge=None):
    rows = here.shape[1]
    lanes = lane_ids((here.shape[0], LANE))
    edge = 0.0 if edge is None else edge
    before = pltpu.roll(here, 1, 1)
    after = pltpu.roll(here, rows - 1, 1)
    before = jnp.concatenate([jnp.where(lanes == 0, edge, before[:, :LANE]), before[:, LANE:]], 1)
    after = jnp.concatenate(
        [after[:, :-LANE], jnp.where(lanes == LANE - 1, edge, after[:, -LANE:])], 1
    )
    return here + kappa * (above + below + before + after - 4.0 * here)


def halves(value):
    high = value.astype(jnp.bfloat16)
    return high, (value - high.astype(F32)).astype(jnp.bfloat16)


def deepened(value):
    return jnp.concatenate([value, jnp.zeros((DEPTH - value.shape[0], value.shape[1]), F32)], 0)


def fill_matrix(levels, mixing, square, matrix):
    square[:levels, :levels] = mixing
    value = square[...]
    high = value.astype(jnp.bfloat16).astype(F32)
    matrix[:DEPTH, :] = (high + pltpu.roll(high, DEPTH, 1)).astype(jnp.bfloat16)
    matrix[DEPTH:, :] = (value - high).astype(jnp.bfloat16)


def fill_stack(stack, part, value):
    high, low = halves(value)
    stack[:DEPTH, part] = high
    stack[DEPTH:, part] = low


def mix(matrix, stack):
    both = jnp.dot(matrix, stack, preferred_element_type=F32)
    return both[:DEPTH] + both[DEPTH:]


def fill_group(group):
    rows = group.shape[0] // 2
    ids = lax.broadcasted_iota(jnp.int32, group.shape, 0)
    ids = jnp.where(ids < rows, ids, ids - rows) // 3
    group[...] = jnp.where(ids == lane_ids(group.shape), 1.0, 0.0).astype(jnp.bfloat16)


def grouped(wide, group):
    return jnp.dot(wide, group, preferred_element_type=F32)


def aligned(index, size):
    return pl.ds(pl.multiple_of(index * size, size), size)


def packed(rows_of, cols):
    parts = []
    for x in range(cols):
        first, last = rows_of(x)
        lanes = lane_ids(first.shape)
        parts.append(jnp.where(lanes == 0, first, jnp.where(lanes == LANE - 1, last, 0.0)))
    shift = 2
    while len(parts) > 1:
        pairs = [parts[n : n + 2] for n in range(0, len(parts), 2)]
        parts = [p[0] + pltpu.roll(p[1], shift, 1) if len(p) == 2 else p[0] for p in pairs]
        shift *= 2
    return parts[0]


def fill_masked(levels, state, f, mask, masked):
    cols, _, rows = masked.shape
    chunks = rows // LANE
    step = cols * chunks
    for x in range(cols):
        row = row_of(mask, x)
        masked[x, PAD - 8 :, :] = jnp.zeros((8, rows), F32)
        for c in range(chunks):
            at = pl.ds(f * (levels * step) + x * chunks + c, levels, stride=step)
            masked[x, :levels, chunk(c)] = state[at, :] * row[:, chunk(c)]


TERMS = 11


def join_weights(bs, cols, kappa, nudging, weights):
    rows = weights.shape[1]
    ids = lane_ids((1, rows))
    for i, b in enumerate(bs):
        own = range(3 * b, 3 * b + 3)
        both = {x: nudging[x : x + 1, :] * kappa[x] for x in own}
        for n, x in enumerate(range(3 * b - 1, 3 * b + 4)):
            total = None
            for near in (x - 1, x + 1):
                if near in both:
                    total = both[near] if total is None else total + both[near]
            if x in both:
                total = total + (nudging[x : x + 1, :] - 4.0 * both[x])
            weights[i * TERMS + n : i * TERMS + n + 1, :] = total
        for n, x in enumerate(own):
            at = i * TERMS + 5 + n
            value = jnp.where(ids == rows - 1, 0.0, pltpu.roll(both[x], rows - 1, 1))
            weights[at : at + 1, :] = value
            value = jnp.where(ids == 0, 0.0, pltpu.roll(both[x], 1, 1))
            weights[at + 3 : at + 4, :] = value


def child_rows(f, g, bs, masked, weights, wide):
    cols, _, rows = masked.shape[1:]
    for i, b in enumerate(bs):

        def term(n, x):
            at = i * TERMS + n
            return weights[at : at + 1, :] * masked[g, x]

        total = None
        for n, x in enumerate(range(3 * b - 1, 3 * b + 4)):
            if 0 <= x < cols:
                total = term(n, x) if total is None else total + term(n, x)
        for side, shift in ((5, 1), (8, rows - 1)):
            value = term(side, 3 * b) + term(side + 1, 3 * b + 1) + term(side + 2, 3 * b + 2)
            total = total + pltpu.roll(value, shift, 1)
        at = aligned(f * len(bs) + i, DEPTH)
        wide[at, :rows], wide[at, rows:] = halves(deepened(total))


def parent_rows(f, g, bs, nest_x, nest_y, masked, kappa, stack):
    cols, _, rows = masked.shape[1:]
    back = lax.rem(rows - nest_y[0], rows)
    for i, b in enumerate(bs):
        x = nest_x[0] + b
        above = masked[g, jnp.maximum(x - 1, 0)]
        below = masked[g, jnp.minimum(x + 1, cols - 1)]
        if b == 0:
            above = jnp.where(x == 0, 0.0, above)
        if b == cols // 3 - 1:
            below = jnp.where(x == cols - 1, 0.0, below)
        value = spread_of(masked[g, x], above, below, kappa[x])
        value = deepened(pltpu.roll(value, back, 1)[:, :LANE])
        fill_stack(stack.at[f], chunk(i), value)


def mix_rows(bs, is_child, wide, group, stack, matrices, emit):
    fields = stack.shape[0]

    @pl.when(is_child[0] == 1)
    def _():
        value = grouped(wide[...], group[...])
        for f in range(fields):
            for i in range(len(bs)):
                at = (f * len(bs) + i) * DEPTH
                fill_stack(stack.at[f], chunk(i), value[at : at + DEPTH])

    for f in range(fields):
        emit(f, mix(matrices[f], stack[f]))


def row_scratch(bs, fields, rows):
    return [
        pltpu.VMEM((-(-len(bs) * TERMS // 8) * 8, rows), F32),
        pltpu.VMEM((fields * len(bs) * DEPTH, 2 * rows), jnp.bfloat16),
        pltpu.VMEM((fields, 2 * DEPTH, len(bs) * LANE), jnp.bfloat16),
        pltpu.VMEM((2 * rows, LANE), jnp.bfloat16),
    ]


ROOM = 19


def front_kernel(
    levels, bs, slots, is_child, state, mask, kappa, nudging, mixing, nest_x, nest_y, ahead, cells, *refs
):
    refs = list(refs)
    line = [refs.pop(0) for _ in range(len(refs) - ROOM)]
    front_steps(
        levels, bs, slots, line, is_child, state, mask, kappa, nudging, mixing, nest_x, nest_y, ahead,
        cells, *refs
    )


def front_steps(
    levels, bs, slots, line, is_child, state, mask, kappa, nudging, mixing, nest_x, nest_y, ahead,
    cells, masked_out, lead, matrices, parcel, inner, places,
    buf, masked, mask_buf, kappa_buf, nudging_buf, mixing_buf, square, weights, wide, stack, group, sems, out_sems,
):
    fields, cols, _, rows = masked.shape
    chunks = rows // LANE
    step = cols * chunks
    size = levels * step

    def copy(f):
        at = pl.ds(f * size, size)
        return pltpu.make_async_copy(state.at[at], buf.at[at], sems.at[f])

    def copy_out(f):
        return pltpu.make_async_copy(masked.at[f], masked_out.at[f], out_sems.at[f])

    pairs = (
        (mask, mask_buf),
        (kappa, kappa_buf),
        (nudging, nudging_buf),
        (mixing, mixing_buf),
    )
    smalls = [
        pltpu.make_async_copy(source, target, sems.at[fields + n])
        for n, (source, target) in enumerate(pairs)
    ]
    for small in smalls:
        small.start()
    for f in range(1, fields):
        copy(f).start()
    square[...] = jnp.zeros_like(square)
    cell = cells[...]
    column, inside = cell // (cols * rows), lax.rem(cell, cols * rows)
    piece = (column // levels) * step + inside // LANE
    place = (piece * PAD + lax.rem(column, levels)) * LANE + lax.rem(inside, LANE)
    places[...] = place
    for small in smalls:
        small.wait()

    @pl.when(is_child[0] == 1)
    def _():
        fill_group(group)
        join_weights(bs, cols, kappa_buf, nudging_buf, weights)

    def field(f, total_edges, first=False):
        fill_matrix(levels, mixing_buf[f, :, 0, :], square, matrices.at[f])
        here, g = (lead, 0) if first else (masked, f)
        if first:
            fill_masked(levels, ahead, f, mask_buf, lead.at[0])
        else:
            copy(f).wait()
            fill_masked(levels, buf, f, mask_buf, masked.at[f])
            copy_out(f).start()
        own_edges = packed(
            lambda x: (here[g, x, :, :LANE], here[g, x, :, rows - LANE :]), cols
        )

        @pl.when(is_child[0] == 1)
        def _():
            child_rows(f, g, bs, here, weights, wide)

        @pl.when(is_child[0] == 0)
        def _():
            parent_rows(f, g, bs, nest_x, nest_y, here, kappa_buf, stack)

        return total_edges + pltpu.roll(own_edges, 2 * f * cols, 1)

    own_edges = field(0, jnp.zeros((PAD, LANE), F32), first=True)
    parcel[:PAD, :] = lax.fori_loop(1, fields, field, own_edges)
    parcel[PAD:, :] = jnp.zeros((parcel.shape[0] - PAD, LANE), F32)
    lane = 0
    for blocks in line:
        dests = blocks.shape[1]
        for start in range(0, blocks.shape[0], slots):
            at = PAD + lane // LANE * slots
            part = slice(lane % LANE, lane % LANE + dests)
            parcel[at : at + slots, part] = blocks[start : start + slots, :]
            lane += dests

    def emit(f, mixed):
        for i in range(len(bs)):
            at = pl.ds(f * levels * len(bs) + i, levels, stride=len(bs))
            inner[at, :] = mixed[:levels, chunk(i)]

    mix_rows(bs, is_child, wide, group, stack, matrices, emit)
    for f in range(1, fields):
        copy_out(f).wait()


def front(is_child, state2, mask, kappa, nudging, mixing, nests, line, ahead, cells, dims):
    fields, levels, cols, chunks = dims
    rows = chunks * LANE
    bs = tuple(range(1, cols // 3 - 1))
    arrays = (state2, mask, kappa, nudging, mixing)
    slots = cells.shape[1]
    height = -(-sum(blocks.size for blocks in line) // (LANE * slots)) * slots
    return pl.pallas_call(
        functools.partial(front_kernel, levels, bs, slots),
        in_specs=[SMEM] + [HBM] * 5 + [SMEM] * 2 + [VMEM] * (2 + len(line)),
        out_specs=[HBM] + [VMEM] * 5,
        out_shape=[
            pltpu.HBM((fields, cols, PAD, rows), F32),
            pltpu.VMEM((1, cols, PAD, rows), F32),
            pltpu.VMEM((fields, 2 * DEPTH, 2 * DEPTH), jnp.bfloat16),
            pltpu.VMEM((PAD + height, LANE), F32),
            pltpu.VMEM((fields * levels * len(bs), LANE), F32),
            pltpu.VMEM(cells.shape, jnp.int32),
        ],
        scratch_shapes=[
            pltpu.VMEM(state2.shape, F32),
            pltpu.VMEM((fields, cols, PAD, rows), F32),
            pltpu.VMEM(mask.shape, jnp.int32),
            pltpu.VMEM(kappa.shape, F32),
            pltpu.VMEM(nudging.shape, F32),
            pltpu.VMEM(mixing.shape, F32),
            pltpu.VMEM((DEPTH, LANE), F32),
        ]
        + row_scratch(bs, fields, rows)
        + [pltpu.SemaphoreType.DMA((fields + 4,)), pltpu.SemaphoreType.DMA((fields,))],
        compiler_params=pltpu.CompilerParams(vmem_limit_bytes=24 * MIB),
        cost_estimate=COST,
        name="front",
    )(is_child, *map(in_hbm, arrays), *nests, in_vmem(ahead), cells, *line)


def base_kernel(
    levels, bs, is_child, nest_x, nest_y, masked_in, lead, matrices, kappa, nudging, base,
    masked, weights, wide, stack, group, sems,
):
    fields, cols = masked.shape[:2]
    near = cols // 3
    reach = near + 2

    def child_copies(f):
        for n, x in enumerate((0, cols - near)):
            at = pl.ds(x, near)
            yield pltpu.make_async_copy(masked_in.at[f, at], masked.at[f, at], sems.at[f, n])

    def parent_copy(f):
        at = pl.ds(jnp.clip(nest_x[0] - 1, 0, cols - reach), reach)
        return pltpu.make_async_copy(masked_in.at[f, at], masked.at[f, at], sems.at[f, 0])

    @pl.when(is_child[0] == 1)
    def _():
        for f in range(1, fields):
            for copy in child_copies(f):
                copy.start()
        fill_group(group)
        join_weights(bs, cols, kappa, nudging, weights)

        def field(f, carry):
            for copy in child_copies(f):
                copy.wait()
            child_rows(f, f, bs, masked, weights, wide)
            return carry

        child_rows(0, 0, bs, lead, weights, wide)
        lax.fori_loop(1, fields, field, 0)

    @pl.when(is_child[0] == 0)
    def _():
        for f in range(1, fields):
            parent_copy(f).start()

        def field(f, carry):
            parent_copy(f).wait()
            parent_rows(f, f, bs, nest_x, nest_y, masked, kappa, stack)
            return carry

        parent_rows(0, 0, bs, nest_x, nest_y, lead, kappa, stack)
        lax.fori_loop(1, fields, field, 0)

    def emit(f, mixed):
        base[f, :, :] = mixed[:PAD, :]

    mix_rows(bs, is_child, wide, group, stack, matrices, emit)


def base_of(is_child, nests, masked, lead, matrices, kappa, nudging, dims):
    fields, levels, cols, chunks = dims
    rows = chunks * LANE
    bs = (0, cols // 3 - 1)
    return pl.pallas_call(
        functools.partial(base_kernel, levels, bs),
        in_specs=[SMEM] * 3 + [HBM] + [VMEM] * 4,
        out_specs=VMEM,
        out_shape=pltpu.VMEM((fields, PAD, 2 * LANE), F32),
        scratch_shapes=[pltpu.VMEM(masked.shape, F32)]
        + row_scratch(bs, fields, rows)
        + [pltpu.SemaphoreType.DMA((fields, 2))],
        compiler_params=pltpu.CompilerParams(vmem_limit_bytes=16 * MIB),
        cost_estimate=COST,
        name="base",
    )(is_child, *nests, in_hbm(masked), in_vmem(lead), matrices, kappa, nudging)


def merged(own, other, width):
    if 2 * width <= LANE:
        return own + pltpu.roll(other, width, 1)
    return jnp.concatenate([own, other], axis=0)


def repack_kernel(width, edges, parcel, arrived, out):
    if edges:
        out[:edges, :] = parcel[:edges, :]
    out[edges:, :] = merged(parcel[PAD:, :], arrived[PAD:, :], width)


def repack(parcel, arrived, width, edges):
    height = (parcel.shape[0] - PAD) * (1 if 2 * width <= LANE else 2)
    return pl.pallas_call(
        functools.partial(repack_kernel, width, edges),
        in_specs=[VMEM] * 2,
        out_specs=VMEM,
        out_shape=pltpu.VMEM((edges + height, LANE), F32),
        compiler_params=pltpu.CompilerParams(vmem_limit_bytes=4 * MIB),
        name="repack",
    )(parcel, arrived)


def y_halos(ty, peers, first, second):
    one, two = first[:PAD, :], second[:PAD, :]
    even = (lax.rem(ty[0], 2) == 0).astype(F32)
    odd = 1.0 - even
    before = (two * even + one * odd) * (ty[0] > 0).astype(F32)
    after = (one * even + two * odd) * (ty[0] < peers - 1).astype(F32)
    low = lax.rem(lane_ids((PAD, LANE)), 2) == 0
    return jnp.where(low, pltpu.roll(before, 1, 1), pltpu.roll(after, LANE - 1, 1))


def outer_kernel(
    levels, peers, is_child, tx, ty, state, matrices, base, kappa, nudging, x_first, x_second,
    first, second, nest_x, nest_y, out, ahead, sides, wide, stack, group, sem,
):
    fields = matrices.shape[0]
    cols, _, rows = kappa.shape
    blocks = cols // 3
    lanes = lane_ids((PAD, LANE))
    turned = lax.rem(lanes + 1, LANE)
    copy = pltpu.make_async_copy(state.at[pl.ds(0, ahead.shape[0])], ahead, sem)
    copy.start()
    sides[...] = jnp.zeros_like(sides)
    halo = y_halos(ty, peers, first, second)

    def weighted(row_of_x):
        one = packed(lambda x: (row_of_x(x)[:, :LANE], row_of_x(x)[:, rows - LANE :]), cols)
        total = one
        for f in range(1, fields):
            total = total + pltpu.roll(one, 2 * f * cols, 1)
        return halo * total

    def fill_fix(value):
        for f in range(fields):
            fill_stack(stack.at[f], chunk(2), deepened(value))

    @pl.when(is_child[0] == 1)
    def _():
        fill_group(group)
        for f in range(fields):
            for n, side in enumerate(x_halos_of(tx, x_first, x_second, f)):
                x = (0, cols - 1)[n]
                at = (f * 2 + n) * DEPTH
                sides[at : at + levels, :] = side * (nudging[x : x + 1, :] * kappa[x])
        wide[:, :rows], wide[:, rows:] = halves(sides[...])
        value = grouped(wide[...], group[...])
        for f in range(fields):
            for n in range(2):
                at = (f * 2 + n) * DEPTH
                fill_stack(stack.at[f], chunk(n), value[at : at + DEPTH])
        part = weighted(lambda x: nudging[x : x + 1, :] * kappa[x])
        fill_fix(part + pltpu.roll(part, LANE - 2, 1) + pltpu.roll(part, LANE - 4, 1))

    @pl.when(is_child[0] == 0)
    def _():
        back = lax.rem(rows - nest_y[0], rows)
        reached = (nest_x[0] == 0, nest_x[0] + blocks == cols)
        for f in range(fields):
            for n, side in enumerate(x_halos_of(tx, x_first, x_second, f)):
                at = (f * 2 + n) * DEPTH
                weight = kappa[(0, cols - 1)[n]] * reached[n].astype(F32)
                sides[at : at + levels, :] = side * weight
                value = pltpu.roll(sides[at : at + DEPTH, :], back, 1)[:, :LANE]
                fill_stack(stack.at[f], chunk(n), value)
        starts = (nest_y[0] == 0).astype(F32)
        finals = (nest_y[0] == rows - LANE).astype(F32)
        part = weighted(lambda x: kappa[x])
        part = part * jnp.where(lax.rem(lanes, 2) == 0, starts, finals)
        value = jnp.zeros((PAD, LANE), F32)
        for b in range(blocks):
            shift = lax.rem(LANE + 4 * b - 2 * nest_x[0], LANE)
            here = lax.rem(turned, 2 * cols) // 2 == 3 * b
            value = jnp.where(here, pltpu.roll(part, shift, 1), value)
        fill_fix(value)

    fixes = jnp.zeros((PAD, LANE), F32)
    for f in range(fields):
        mixed = mix(matrices[f], stack[f])
        for n in range(2):
            at = pl.ds(f * (2 * levels) + n, levels, stride=2)
            out[at, :] = base[f, :levels, chunk(n)] + mixed[:levels, chunk(n)]
        fixes = jnp.where(turned // (2 * cols) == f, mixed[:PAD, chunk(2)], fixes)
    out[out.shape[0] - PAD :, :] = fixes
    copy.wait()


def outer(
    is_child, tx, ty, state2, matrices, base, kappa, nudging, x_halos, firsts, nests, dims, peers
):
    fields, levels, cols, chunks = dims
    rows = chunks * LANE
    height = -(-fields * 2 * levels // 8) * 8 + PAD
    return pl.pallas_call(
        functools.partial(outer_kernel, levels, peers),
        in_specs=[SMEM] * 3 + [HBM] + [VMEM] * 8 + [SMEM] * 2,
        out_specs=[VMEM] * 2,
        out_shape=[
            pltpu.VMEM((height, LANE), F32),
            pltpu.VMEM((state2.shape[0] // fields, LANE), F32),
        ],
        scratch_shapes=[
            pltpu.VMEM((fields * 2 * DEPTH, rows), F32),
            pltpu.VMEM((fields * 2 * DEPTH, 2 * rows), jnp.bfloat16),
            pltpu.VMEM((fields, 2 * DEPTH, 3 * LANE), jnp.bfloat16),
            pltpu.VMEM((2 * rows, LANE), jnp.bfloat16),
            pltpu.SemaphoreType.DMA,
        ],
        compiler_params=pltpu.CompilerParams(vmem_limit_bytes=12 * MIB),
        name="outer",
    )(is_child, tx, ty, in_hbm(state2), matrices, base, kappa, nudging, *x_halos, *firsts, *nests)


def tile_kernel(
    levels, peers, tx, ty, state, mask, matrices, kappa, x_first, x_second, first, second, ahead,
    out, buf, masked, sides, halo, stack, sems,
):
    cols, _, rows = masked.shape
    chunks = rows // LANE
    size = levels * cols * chunks
    fields = state.shape[0] // size

    def copy(f):
        at = pl.ds(f * size, size)
        return pltpu.make_async_copy(state.at[at], buf.at[at], sems.at[f])

    for f in range(1, fields):
        copy(f).start()
    sides[...] = jnp.zeros_like(sides)
    halo[...] = y_halos(ty, peers, first, second)
    pair = 2

    def field(f, carry, leading=False):
        if leading:
            fill_masked(levels, ahead, f, mask, masked)
        else:
            copy(f).wait()
            fill_masked(levels, buf, f, mask, masked)
        for n, side in enumerate(x_halos_of(tx, x_first, x_second, f)):
            sides[n, :levels, :] = side
        for x0 in range(0, cols, pair):
            for x in range(x0, x0 + pair):
                above = masked[x - 1] if x > 0 else sides[0]
                below = masked[x + 1] if x < cols - 1 else sides[1]
                shift = lax.rem(LANE - 2 * (f * cols + x), LANE)
                edge = pltpu.roll(halo[...], lax.rem(LANE + shift, LANE), 1)
                value = spread_of(masked[x], above, below, kappa[x], edge)
                part = slice((x - x0) * rows, (x - x0 + 1) * rows)
                fill_stack(stack, part, deepened(value))
            mixed = mix(matrices[f], stack[...])
            for n in range(pair * chunks):
                out[aligned((f * cols + x0) * chunks + n, PAD), :] = mixed[:PAD, chunk(n)]
        return carry

    field(0, 0, leading=True)
    lax.fori_loop(1, fields, field, 0)


def tile_of(tx, ty, state2, mask, matrices, kappa, x_halos, firsts, ahead, dims, peers):
    fields, levels, cols, chunks = dims
    rows = chunks * LANE
    return pl.pallas_call(
        functools.partial(tile_kernel, levels, peers),
        in_specs=[SMEM] * 2 + [HBM] + [VMEM] * 8,
        out_specs=VMEM,
        out_shape=pltpu.VMEM((fields * cols * chunks * PAD, LANE), F32),
        scratch_shapes=[
            pltpu.VMEM(state2.shape, F32),
            pltpu.VMEM((cols, PAD, rows), F32),
            pltpu.VMEM((2, PAD, rows), F32),
            pltpu.VMEM((PAD, LANE), F32),
            pltpu.VMEM((2 * DEPTH, 2 * rows), jnp.bfloat16),
            pltpu.SemaphoreType.DMA((fields,)),
        ],
        compiler_params=pltpu.CompilerParams(vmem_limit_bytes=16 * MIB),
        cost_estimate=COST,
        name="tile",
    )(tx, ty, in_hbm(state2), mask, matrices, kappa, *x_halos, *firsts, in_vmem(ahead))


def observe_kernel(dests, across, row, column, counts, places, mine, theirs, _, tile):
    lanes = lane_ids((1, LANE))
    slots = places.shape[1]
    ty, tx = row[0], column[0]
    me = ty * across + tx
    half = (mine.shape[0] - PAD) // slots * (LANE // dests)

    def source(turn, ref, g, carry):
        origin = (lax.div(g, across) ^ turn ^ ty) * across + (lax.rem(g, across) ^ tx)
        lane_in = lax.rem(g, LANE // dests) * dests + me
        block = PAD + lax.div(g, LANE // dests) * slots
        count = counts[0, origin]
        for k0 in range(0, slots, 4):
            ats, adds = [], []
            for m in range(k0, k0 + 4):
                place = places[origin, m]
                lane = place & (LANE - 1)
                value = pltpu.roll(ref[pl.ds(block + m, 1), :], (lane - lane_in) & (LANE - 1), 1)
                ats.append(place >> 7)
                adds.append(jnp.where(lanes == jnp.where(m < count, lane, LANE), value, 0.0))
            olds = [tile[pl.ds(at, 1), :] for at in ats]
            for k, (at, total) in enumerate(zip(ats, olds)):
                total = total + adds[k]
                for j in range(k):
                    total = total + jnp.where(ats[j] == at, adds[j], 0.0)
                tile[pl.ds(at, 1), :] = total
        return carry

    def both(n, carry):
        source(0, mine, n, carry)
        return source(3, theirs, n, carry)

    lax.fori_loop(0, half, both, 0)


def observe(row, column, places, counts, seen, tile, dests, across):
    return pl.pallas_call(
        functools.partial(observe_kernel, dests, across),
        in_specs=[SMEM] * 4 + [VMEM] * 3,
        out_specs=VMEM,
        out_shape=pltpu.VMEM(tile.shape, F32),
        input_output_aliases={6: 0},
        compiler_params=pltpu.CompilerParams(vmem_limit_bytes=4 * MIB),
        name="observe",
    )(row, column, counts, places, *seen, in_vmem(tile))


def finish_kernel(
    levels, is_child, nest_x, nest_y, tile, mask, in_arrived, out_arrived, in_sent, out_sent,
    out, buf, group, sems,
):
    cols = mask.shape[0]
    rows = mask.shape[2]
    chunks = rows // LANE
    step = cols * chunks
    size = levels * step
    fields = out.shape[0] // size
    blocks = cols // 3
    inner = blocks - 2
    lanes = lane_ids((levels, LANE))
    ends = jnp.logical_or(lanes == 0, lanes == LANE - 1)
    height = out_arrived.shape[0]

    def copy(f):
        at = pl.ds(f * size, size)
        return pltpu.make_async_copy(buf.at[at], out.at[at], sems.at[f])

    def piece_of(f, piece):
        return tile[pl.ds(pl.multiple_of((f * step + piece) * PAD, 8), levels), :]

    def payload(f, b, inner_ref, outer_ref):
        if b in (0, blocks - 1):
            value = outer_ref[pl.ds(f * (2 * levels) + min(b, 1), levels, stride=2), :]
        else:
            value = inner_ref[pl.ds(f * (levels * inner) + b - 1, levels, stride=inner), :]
        fixes = outer_ref[height - PAD : height - PAD + levels, :]
        shift = lax.rem(LANE - 2 * (f * cols + 3 * b), LANE)
        fixes = pltpu.roll(fixes, lax.rem(LANE + shift, LANE), 1)
        return value + jnp.where(ends, fixes, 0.0)

    def fill_child(f, carry):
        for b in range(blocks):
            high, low = halves(payload(f, b, in_arrived, out_arrived))
            both = jnp.concatenate([high, low], axis=1)
            value = jnp.dot(both, group[...], preferred_element_type=F32) * (1.0 / 9.0)
            for x in range(3 * b, 3 * b + 3):
                row = row_of(mask, x)
                for c in range(chunks):
                    piece = x * chunks + c
                    at = pl.ds(f * size + piece, levels, stride=step)
                    total = piece_of(f, piece) + value[:, chunk(c)]
                    buf[at, :] = total * row[:, chunk(c)]
        copy(f).start()
        return carry

    def fill_plain(f, carry):
        for x in range(cols):
            row = row_of(mask, x)
            for c in range(chunks):
                piece = x * chunks + c
                at = pl.ds(f * size + piece, levels, stride=step)
                buf[at, :] = piece_of(f, piece) * row[:, chunk(c)]
        return carry

    def fill_parent(f, carry):
        fill_plain(f, carry)
        for b in range(blocks):
            delta = payload(f, b, in_arrived, out_arrived) - payload(f, b, in_sent, out_sent)
            wide = jnp.concatenate([delta, jnp.zeros((levels, rows - LANE), F32)], 1)
            x = nest_x[0] + b
            value = pltpu.roll(wide, nest_y[0], 1) * row_of(mask, x)
            for c in range(chunks):
                at = pl.ds(f * size + x * chunks + c, levels, stride=step)
                buf[at, :] = buf[at, :] + value[:, chunk(c)]
        copy(f).start()
        return carry

    @pl.when(is_child[0] == 1)
    def _():
        ids = lax.broadcasted_iota(jnp.int32, group.shape, 0)
        ids = jnp.where(ids < LANE, ids, ids - LANE)
        group[...] = jnp.where(lane_ids(group.shape) // 3 == ids, 1.0, 0.0).astype(jnp.bfloat16)
        lax.fori_loop(0, fields, fill_child, 0)

    @pl.when(is_child[0] == 0)
    def _():
        lax.fori_loop(0, fields, fill_parent, 0)

    for f in range(fields):
        copy(f).wait()


def finish(is_child, nests, tile, mask, arrived, sent, dims):
    fields, levels, cols, chunks = dims
    rows = chunks * LANE
    size = (fields * levels * cols * chunks, LANE)
    return pl.pallas_call(
        functools.partial(finish_kernel, levels),
        in_specs=[SMEM] * 3 + [VMEM] * 6,
        out_specs=HBM,
        out_shape=pltpu.HBM(size, F32),
        scratch_shapes=[
            pltpu.VMEM(size, F32),
            pltpu.VMEM((2 * LANE, rows), jnp.bfloat16),
            pltpu.SemaphoreType.DMA((fields,)),
        ],
        compiler_params=pltpu.CompilerParams(vmem_limit_bytes=16 * MIB),
        cost_estimate=COST,
        name="finish",
    )(is_child, *nests, in_vmem(tile), mask, *arrived, *sent)


def from_neighbours(first, second, axis):
    size = lax.axis_size(axis)
    inner = [(i, i + 1) for i in range(1, size - 1, 2)]
    one = swapped(first, axis, 1)
    return one, lax.ppermute(second, axis, inner + [(j, i) for i, j in inner])


def swapped(value, axis, mask):
    return lax.ppermute(value, axis, [(i, i ^ mask) for i in range(lax.axis_size(axis))])


def local(
    adjoint_state,
    land_mask,
    diffusivity,
    mixing,
    nudging,
    nest_x,
    nest_y,
    obs_forcing,
    obs_cell,
    obs_count,
):
    _, fields, levels, cols, rows = adjoint_state.shape
    chunks = rows // LANE
    dims = (fields, levels, cols, chunks)
    state5 = adjoint_state.reshape(fields, levels, cols, 1, rows)
    state2 = adjoint_state.reshape(fields * levels * cols * chunks, LANE)
    mask = land_mask.reshape(cols, 1, rows)
    kappa = diffusivity.reshape(cols, 1, rows)
    mixing = mixing.reshape(fields, levels, 1, levels)
    peers, across = lax.axis_size("ty"), lax.axis_size("tx")
    assert peers == 4 and across & (across - 1) == 0 and 2 * fields * cols <= LANE
    assert levels <= PAD and cols % 3 == 0 and rows == 3 * LANE
    row = lax.axis_index("ty").astype(jnp.int32)
    column = lax.axis_index("tx").astype(jnp.int32)
    ty = row.reshape(1)
    is_child = (lax.axis_index("grp") == 0).astype(jnp.int32).reshape(1)
    nests = (nest_x, nest_y)

    forcing = obs_forcing[0, 0]
    dests = forcing.shape[1]
    counts = obs_count.reshape(1, -1)
    line = [forcing, *(swapped(forcing, "tx", n) for n in range(1, min(across, 4)))]
    for n in range(2, across.bit_length() - 1):
        blocks = jnp.concatenate(line)
        line = [blocks, swapped(blocks, "tx", 1 << n)]
    tx = column.reshape(1)
    *x_sent, ahead = x_edges(tx, state5, mask)
    ahead = ahead.reshape(-1, LANE)
    x_halos = from_neighbours(*x_sent, "tx")
    masked, lead, matrices, parcel, in_sent, places = front(
        is_child, state2, mask, kappa, nudging, mixing, nests, line, ahead,
        obs_cell[0, :, :, 0], dims,
    )
    first = swapped(parcel, "ty", 1)
    in_arrived = swapped(in_sent, "grp", 1)
    parcel = repack(parcel, first, across * dests, PAD)
    second = swapped(parcel, "ty", 3)
    firsts = (first, second)
    masked, x_halos, parcel = lax.optimization_barrier((masked, x_halos, parcel))
    base = base_of(is_child, nests, masked, lead, matrices, kappa, nudging, dims)
    out_sent, ahead = outer(
        is_child, tx, ty, state2, matrices, base, kappa, nudging, x_halos, firsts, nests, dims, peers
    )
    out_arrived = swapped(out_sent, "grp", 1)
    tile = tile_of(tx, ty, state2, mask, matrices, kappa, x_halos, firsts, ahead, dims, peers)
    tile = observe(ty, tx, places, counts, (parcel, second), tile, dests, across)
    arrived, sent = (in_arrived, out_arrived), (in_sent, out_sent)
    out = finish(is_child, nests, tile, mask, arrived, sent, dims)
    return out.reshape(adjoint_state.shape)


def solution(mesh):
    in_specs = (
        P("grp", None, None, "tx", "ty"),
        P("grp", "tx", "ty"),
        P("grp", "tx", "ty"),
        P("grp", None, None, None),
        P("tx", "ty"),
        P(("ty", "tx")),
        P(("ty", "tx")),
        P("grp", ("ty", "tx"), None, None),
        P("grp", None, None, ("ty", "tx")),
        P("grp", None, ("ty", "tx")),
    )
    out_specs = P("grp", None, None, "tx", "ty")
    return jax.shard_map(local, mesh=mesh, in_specs=in_specs, out_specs=out_specs, check_vma=False)
```

```python
import functools

import jax
import jax.numpy as jnp
from jax import lax
from jax.experimental import pallas as pl
from jax.experimental.pallas import tpu as pltpu
from jax.sharding import PartitionSpec as P

LANE = 128
PAD = 56
DEPTH = 64
MIB = 1 << 20
HBM = pl.BlockSpec(memory_space=pltpu.HBM)
SMEM = pl.BlockSpec(memory_space=pltpu.SMEM)
VMEM = pl.BlockSpec(memory_space=pltpu.VMEM)
F32 = jnp.float32
COST = pl.CostEstimate(flops=10**10, bytes_accessed=10**8, transcendentals=0)


def lane_ids(shape):
    return lax.broadcasted_iota(jnp.int32, shape, len(shape) - 1)


def row_of(ref, x):
    return ref[x].astype(F32)


def chunk(c):
    return slice(c * LANE, (c + 1) * LANE)


def in_hbm(value):
    return pltpu.with_memory_space_constraint(value, pltpu.HBM)


def in_vmem(value):
    return pltpu.with_memory_space_constraint(value, pltpu.VMEM)


def x_edges_kernel(tx, state, mask, first, second, ahead, buf, mask_buf, sems):
    fields, _, cols = state.shape[:3]
    even = lax.rem(tx[0], 2) == 0
    ends = (jnp.where(even, cols - 1, 0), jnp.where(even, 0, cols - 1))
    copies = [pltpu.make_async_copy(mask, mask_buf, sems.at[2 * fields])]
    for n, x in enumerate(ends):
        for f in range(fields):
            copies.append(
                pltpu.make_async_copy(state.at[f, :, x], buf.at[n, f], sems.at[n * fields + f])
            )
    copies.append(pltpu.make_async_copy(state.at[0], ahead, sems.at[2 * fields + 1]))
    for copy in copies:
        copy.start()
    copies[0].wait()
    for n, (x, out) in enumerate(zip(ends, (first, second))):
        for f in range(fields):
            copies[1 + n * fields + f].wait()
            out[f] = buf[n, f] * row_of(mask_buf, x)[None]
    copies[-1].wait()


def x_edges(tx, state5, mask):
    fields, levels, cols, _, rows = state5.shape
    edge = (fields, levels, 1, rows)
    return pl.pallas_call(
        x_edges_kernel,
        in_specs=[SMEM, HBM, HBM],
        out_specs=[VMEM] * 3,
        out_shape=[pltpu.VMEM(edge, F32)] * 2 + [pltpu.VMEM(state5.shape[1:], F32)],
        scratch_shapes=[
            pltpu.VMEM((2,) + edge, F32),
            pltpu.VMEM(mask.shape, jnp.int32),
            pltpu.SemaphoreType.DMA((2 * fields + 2,)),
        ],
        compiler_params=pltpu.CompilerParams(vmem_limit_bytes=8 * MIB),
        cost_estimate=COST,
        name="x_edges",
    )(tx, in_hbm(state5), in_hbm(mask))


def x_halos_of(tx, first, second, f):
    one, two = first[f, :, 0, :], second[f, :, 0, :]
    even = lax.rem(tx[0], 2) == 0
    return jnp.where(even, two, one), jnp.where(even, one, two)


def spread_of(here, above, below, kappa, edge=None):
    rows = here.shape[1]
    lanes = lane_ids((here.shape[0], LANE))
    edge = 0.0 if edge is None else edge
    before = pltpu.roll(here, 1, 1)
    after = pltpu.roll(here, rows - 1, 1)
    before = jnp.concatenate([jnp.where(lanes == 0, edge, before[:, :LANE]), before[:, LANE:]], 1)
    after = jnp.concatenate(
        [after[:, :-LANE], jnp.where(lanes == LANE - 1, edge, after[:, -LANE:])], 1
    )
    return here + kappa * (above + below + before + after - 4.0 * here)


def halves(value):
    high = value.astype(jnp.bfloat16)
    return high, (value - high.astype(F32)).astype(jnp.bfloat16)


def deepened(value):
    return jnp.concatenate([value, jnp.zeros((DEPTH - value.shape[0], value.shape[1]), F32)], 0)


def fill_matrix(levels, mixing, square, matrix):
    square[:levels, :levels] = mixing
    value = square[...]
    high = value.astype(jnp.bfloat16).astype(F32)
    matrix[:DEPTH, :] = (high + pltpu.roll(high, DEPTH, 1)).astype(jnp.bfloat16)
    matrix[DEPTH:, :] = (value - high).astype(jnp.bfloat16)


def fill_stack(stack, part, value):
    high, low = halves(value)
    stack[:DEPTH, part] = high
    stack[DEPTH:, part] = low


def mix(matrix, stack):
    both = jnp.dot(matrix, stack, preferred_element_type=F32)
    return both[:DEPTH] + both[DEPTH:]


def fill_group(group):
    rows = group.shape[0] // 2
    ids = lax.broadcasted_iota(jnp.int32, group.shape, 0)
    ids = jnp.where(ids < rows, ids, ids - rows) // 3
    group[...] = jnp.where(ids == lane_ids(group.shape), 1.0, 0.0).astype(jnp.bfloat16)


def grouped(wide, group):
    return jnp.dot(wide, group, preferred_element_type=F32)


def aligned(index, size):
    return pl.ds(pl.multiple_of(index * size, size), size)


def packed(rows_of, cols):
    parts = []
    for x in range(cols):
        first, last = rows_of(x)
        lanes = lane_ids(first.shape)
        parts.append(jnp.where(lanes == 0, first, jnp.where(lanes == LANE - 1, last, 0.0)))
    shift = 2
    while len(parts) > 1:
        pairs = [parts[n : n + 2] for n in range(0, len(parts), 2)]
        parts = [p[0] + pltpu.roll(p[1], shift, 1) if len(p) == 2 else p[0] for p in pairs]
        shift *= 2
    return parts[0]


def fill_masked(levels, state, f, mask, masked):
    cols, _, rows = masked.shape
    chunks = rows // LANE
    step = cols * chunks
    for x in range(cols):
        row = row_of(mask, x)
        masked[x, PAD - 8 :, :] = jnp.zeros((8, rows), F32)
        for c in range(chunks):
            at = pl.ds(f * (levels * step) + x * chunks + c, levels, stride=step)
            masked[x, :levels, chunk(c)] = state[at, :] * row[:, chunk(c)]


TERMS = 11


def join_weights(bs, cols, kappa, nudging, weights):
    rows = weights.shape[1]
    ids = lane_ids((1, rows))
    for i, b in enumerate(bs):
        own = range(3 * b, 3 * b + 3)
        both = {x: nudging[x : x + 1, :] * kappa[x] for x in own}
        for n, x in enumerate(range(3 * b - 1, 3 * b + 4)):
            total = None
            for near in (x - 1, x + 1):
                if near in both:
                    total = both[near] if total is None else total + both[near]
            if x in both:
                total = total + (nudging[x : x + 1, :] - 4.0 * both[x])
            weights[i * TERMS + n : i * TERMS + n + 1, :] = total
        for n, x in enumerate(own):
            at = i * TERMS + 5 + n
            value = jnp.where(ids == rows - 1, 0.0, pltpu.roll(both[x], rows - 1, 1))
            weights[at : at + 1, :] = value
            value = jnp.where(ids == 0, 0.0, pltpu.roll(both[x], 1, 1))
            weights[at + 3 : at + 4, :] = value


def child_rows(f, bs, masked, weights, wide):
    cols, _, rows = masked.shape[1:]
    for i, b in enumerate(bs):

        def term(n, x):
            at = i * TERMS + n
            return weights[at : at + 1, :] * masked[f, x]

        total = None
        for n, x in enumerate(range(3 * b - 1, 3 * b + 4)):
            if 0 <= x < cols:
                total = term(n, x) if total is None else total + term(n, x)
        for side, shift in ((5, 1), (8, rows - 1)):
            value = term(side, 3 * b) + term(side + 1, 3 * b + 1) + term(side + 2, 3 * b + 2)
            total = total + pltpu.roll(value, shift, 1)
        at = aligned(f * len(bs) + i, DEPTH)
        wide[at, :rows], wide[at, rows:] = halves(deepened(total))


def parent_rows(f, bs, nest_x, nest_y, masked, kappa, stack):
    cols, _, rows = masked.shape[1:]
    back = lax.rem(rows - nest_y[0], rows)
    for i, b in enumerate(bs):
        x = nest_x[0] + b
        above = masked[f, jnp.maximum(x - 1, 0)]
        below = masked[f, jnp.minimum(x + 1, cols - 1)]
        if b == 0:
            above = jnp.where(x == 0, 0.0, above)
        if b == cols // 3 - 1:
            below = jnp.where(x == cols - 1, 0.0, below)
        value = spread_of(masked[f, x], above, below, kappa[x])
        value = deepened(pltpu.roll(value, back, 1)[:, :LANE])
        fill_stack(stack.at[f], chunk(i), value)


def mix_rows(bs, is_child, wide, group, stack, matrices, emit):
    fields = stack.shape[0]

    @pl.when(is_child[0] == 1)
    def _():
        value = grouped(wide[...], group[...])
        for f in range(fields):
            for i in range(len(bs)):
                at = (f * len(bs) + i) * DEPTH
                fill_stack(stack.at[f], chunk(i), value[at : at + DEPTH])

    for f in range(fields):
        emit(f, mix(matrices[f], stack[f]))


def row_scratch(bs, fields, rows):
    return [
        pltpu.VMEM((-(-len(bs) * TERMS // 8) * 8, rows), F32),
        pltpu.VMEM((fields * len(bs) * DEPTH, 2 * rows), jnp.bfloat16),
        pltpu.VMEM((fields, 2 * DEPTH, len(bs) * LANE), jnp.bfloat16),
        pltpu.VMEM((2 * rows, LANE), jnp.bfloat16),
    ]


ROOM = 18


def front_kernel(
    levels, bs, slots, is_child, state, mask, kappa, nudging, mixing, nest_x, nest_y, ahead, cells, *refs
):
    refs = list(refs)
    line = [refs.pop(0) for _ in range(len(refs) - ROOM)]
    front_steps(
        levels, bs, slots, line, is_child, state, mask, kappa, nudging, mixing, nest_x, nest_y, ahead,
        cells, *refs
    )


def front_steps(
    levels, bs, slots, line, is_child, state, mask, kappa, nudging, mixing, nest_x, nest_y, ahead,
    cells, masked_out, matrices, parcel, inner, places,
    buf, masked, mask_buf, kappa_buf, nudging_buf, mixing_buf, square, weights, wide, stack, group, sems, out_sems,
):
    fields, cols, _, rows = masked.shape
    chunks = rows // LANE
    step = cols * chunks
    size = levels * step

    def copy(f):
        at = pl.ds(f * size, size)
        return pltpu.make_async_copy(state.at[at], buf.at[at], sems.at[f])

    def copy_out(f):
        return pltpu.make_async_copy(masked.at[f], masked_out.at[f], out_sems.at[f])

    pairs = (
        (mask, mask_buf),
        (kappa, kappa_buf),
        (nudging, nudging_buf),
        (mixing, mixing_buf),
    )
    smalls = [
        pltpu.make_async_copy(source, target, sems.at[fields + n])
        for n, (source, target) in enumerate(pairs)
    ]
    for small in smalls:
        small.start()
    for f in range(1, fields):
        copy(f).start()
    square[...] = jnp.zeros_like(square)
    cell = cells[...]
    column, inside = cell // (cols * rows), lax.rem(cell, cols * rows)
    piece = (column // levels) * step + inside // LANE
    place = (piece * PAD + lax.rem(column, levels)) * LANE + lax.rem(inside, LANE)
    places[...] = place
    for small in smalls:
        small.wait()

    @pl.when(is_child[0] == 1)
    def _():
        fill_group(group)
        join_weights(bs, cols, kappa_buf, nudging_buf, weights)

    def field(f, total_edges, first=False):
        fill_matrix(levels, mixing_buf[f, :, 0, :], square, matrices.at[f])
        if first:
            fill_masked(levels, ahead, f, mask_buf, masked.at[f])
        else:
            copy(f).wait()
            fill_masked(levels, buf, f, mask_buf, masked.at[f])
        copy_out(f).start()
        own_edges = packed(
            lambda x: (masked[f, x, :, :LANE], masked[f, x, :, rows - LANE :]), cols
        )

        @pl.when(is_child[0] == 1)
        def _():
            child_rows(f, bs, masked, weights, wide)

        @pl.when(is_child[0] == 0)
        def _():
            parent_rows(f, bs, nest_x, nest_y, masked, kappa_buf, stack)

        return total_edges + pltpu.roll(own_edges, 2 * f * cols, 1)

    own_edges = field(0, jnp.zeros((PAD, LANE), F32), first=True)
    parcel[:PAD, :] = lax.fori_loop(1, fields, field, own_edges)
    parcel[PAD:, :] = jnp.zeros((parcel.shape[0] - PAD, LANE), F32)
    lane = 0
    for blocks in line:
        dests = blocks.shape[1]
        for start in range(0, blocks.shape[0], slots):
            at = PAD + lane // LANE * slots
            part = slice(lane % LANE, lane % LANE + dests)
            parcel[at : at + slots, part] = blocks[start : start + slots, :]
            lane += dests

    def emit(f, mixed):
        for i in range(len(bs)):
            at = pl.ds(f * levels * len(bs) + i, levels, stride=len(bs))
            inner[at, :] = mixed[:levels, chunk(i)]

    mix_rows(bs, is_child, wide, group, stack, matrices, emit)
    for f in range(fields):
        copy_out(f).wait()


def front(is_child, state2, mask, kappa, nudging, mixing, nests, line, ahead, cells, dims):
    fields, levels, cols, chunks = dims
    rows = chunks * LANE
    bs = tuple(range(1, cols // 3 - 1))
    arrays = (state2, mask, kappa, nudging, mixing)
    slots = cells.shape[1]
    height = -(-sum(blocks.size for blocks in line) // (LANE * slots)) * slots
    return pl.pallas_call(
        functools.partial(front_kernel, levels, bs, slots),
        in_specs=[SMEM] + [HBM] * 5 + [SMEM] * 2 + [VMEM] * (2 + len(line)),
        out_specs=[HBM] + [VMEM] * 4,
        out_shape=[
            pltpu.HBM((fields, cols, PAD, rows), F32),
            pltpu.VMEM((fields, 2 * DEPTH, 2 * DEPTH), jnp.bfloat16),
            pltpu.VMEM((PAD + height, LANE), F32),
            pltpu.VMEM((fields * levels * len(bs), LANE), F32),
            pltpu.VMEM(cells.shape, jnp.int32),
        ],
        scratch_shapes=[
            pltpu.VMEM(state2.shape, F32),
            pltpu.VMEM((fields, cols, PAD, rows), F32),
            pltpu.VMEM(mask.shape, jnp.int32),
            pltpu.VMEM(kappa.shape, F32),
            pltpu.VMEM(nudging.shape, F32),
            pltpu.VMEM(mixing.shape, F32),
            pltpu.VMEM((DEPTH, LANE), F32),
        ]
        + row_scratch(bs, fields, rows)
        + [pltpu.SemaphoreType.DMA((fields + 4,)), pltpu.SemaphoreType.DMA((fields,))],
        compiler_params=pltpu.CompilerParams(vmem_limit_bytes=24 * MIB),
        cost_estimate=COST,
        name="front",
    )(is_child, *map(in_hbm, arrays), *nests, in_vmem(ahead), cells, *line)


def base_kernel(
    levels, bs, is_child, nest_x, nest_y, masked_in, matrices, kappa, nudging, base,
    masked, weights, wide, stack, group, sems,
):
    fields, cols = masked.shape[:2]
    near = cols // 3
    reach = near + 2

    def child_copies(f):
        for n, x in enumerate((0, cols - near)):
            at = pl.ds(x, near)
            yield pltpu.make_async_copy(masked_in.at[f, at], masked.at[f, at], sems.at[f, n])

    def parent_copy(f):
        at = pl.ds(jnp.clip(nest_x[0] - 1, 0, cols - reach), reach)
        return pltpu.make_async_copy(masked_in.at[f, at], masked.at[f, at], sems.at[f, 0])

    @pl.when(is_child[0] == 1)
    def _():
        for f in range(fields):
            for copy in child_copies(f):
                copy.start()
        fill_group(group)
        join_weights(bs, cols, kappa, nudging, weights)

        def field(f, carry):
            for copy in child_copies(f):
                copy.wait()
            child_rows(f, bs, masked, weights, wide)
            return carry

        lax.fori_loop(0, fields, field, 0)

    @pl.when(is_child[0] == 0)
    def _():
        for f in range(fields):
            parent_copy(f).start()

        def field(f, carry):
            parent_copy(f).wait()
            parent_rows(f, bs, nest_x, nest_y, masked, kappa, stack)
            return carry

        lax.fori_loop(0, fields, field, 0)

    def emit(f, mixed):
        base[f, :, :] = mixed[:PAD, :]

    mix_rows(bs, is_child, wide, group, stack, matrices, emit)


def base_of(is_child, nests, masked, matrices, kappa, nudging, dims):
    fields, levels, cols, chunks = dims
    rows = chunks * LANE
    bs = (0, cols // 3 - 1)
    return pl.pallas_call(
        functools.partial(base_kernel, levels, bs),
        in_specs=[SMEM] * 3 + [HBM] + [VMEM] * 3,
        out_specs=VMEM,
        out_shape=pltpu.VMEM((fields, PAD, 2 * LANE), F32),
        scratch_shapes=[pltpu.VMEM(masked.shape, F32)]
        + row_scratch(bs, fields, rows)
        + [pltpu.SemaphoreType.DMA((fields, 2))],
        compiler_params=pltpu.CompilerParams(vmem_limit_bytes=16 * MIB),
        cost_estimate=COST,
        name="base",
    )(is_child, *nests, in_hbm(masked), matrices, kappa, nudging)


def stacked_kernel(one, two, out):
    out[: one.shape[0], :] = one[...]
    out[one.shape[0] :, :] = two[...]


def stacked(one, two):
    return pl.pallas_call(
        stacked_kernel,
        in_specs=[VMEM] * 2,
        out_specs=VMEM,
        out_shape=pltpu.VMEM((2 * one.shape[0], one.shape[1]), F32),
        compiler_params=pltpu.CompilerParams(vmem_limit_bytes=4 * MIB),
        name="stacked",
    )(one, two)


def merged(own, other, width):
    if 2 * width <= LANE:
        return own + pltpu.roll(other, width, 1)
    return jnp.concatenate([own, other], axis=0)


def repack_kernel(width, edges, parcel, arrived, out):
    if edges:
        out[:edges, :] = parcel[:edges, :]
    out[edges:, :] = merged(parcel[PAD:, :], arrived[PAD:, :], width)


def repack(parcel, arrived, width, edges):
    height = (parcel.shape[0] - PAD) * (1 if 2 * width <= LANE else 2)
    return pl.pallas_call(
        functools.partial(repack_kernel, width, edges),
        in_specs=[VMEM] * 2,
        out_specs=VMEM,
        out_shape=pltpu.VMEM((edges + height, LANE), F32),
        compiler_params=pltpu.CompilerParams(vmem_limit_bytes=4 * MIB),
        name="repack",
    )(parcel, arrived)


def y_halos(ty, peers, first, second):
    one, two = first[:PAD, :], second[:PAD, :]
    even = (lax.rem(ty[0], 2) == 0).astype(F32)
    odd = 1.0 - even
    before = (two * even + one * odd) * (ty[0] > 0).astype(F32)
    after = (one * even + two * odd) * (ty[0] < peers - 1).astype(F32)
    low = lax.rem(lane_ids((PAD, LANE)), 2) == 0
    return jnp.where(low, pltpu.roll(before, 1, 1), pltpu.roll(after, LANE - 1, 1))


def outer_kernel(
    levels, peers, is_child, tx, ty, state, matrices, base, kappa, nudging, x_first, x_second,
    first, second, nest_x, nest_y, out, ahead, sides, wide, stack, group, sem,
):
    fields = matrices.shape[0]
    cols, _, rows = kappa.shape
    blocks = cols // 3
    lanes = lane_ids((PAD, LANE))
    turned = lax.rem(lanes + 1, LANE)
    copy = pltpu.make_async_copy(state.at[pl.ds(0, ahead.shape[0])], ahead, sem)
    copy.start()
    sides[...] = jnp.zeros_like(sides)
    halo = y_halos(ty, peers, first, second)

    def weighted(row_of_x):
        one = packed(lambda x: (row_of_x(x)[:, :LANE], row_of_x(x)[:, rows - LANE :]), cols)
        total = one
        for f in range(1, fields):
            total = total + pltpu.roll(one, 2 * f * cols, 1)
        return halo * total

    def fill_fix(value):
        for f in range(fields):
            fill_stack(stack.at[f], chunk(2), deepened(value))

    @pl.when(is_child[0] == 1)
    def _():
        fill_group(group)
        for f in range(fields):
            for n, side in enumerate(x_halos_of(tx, x_first, x_second, f)):
                x = (0, cols - 1)[n]
                at = (f * 2 + n) * DEPTH
                sides[at : at + levels, :] = side * (nudging[x : x + 1, :] * kappa[x])
        wide[:, :rows], wide[:, rows:] = halves(sides[...])
        value = grouped(wide[...], group[...])
        for f in range(fields):
            for n in range(2):
                at = (f * 2 + n) * DEPTH
                fill_stack(stack.at[f], chunk(n), value[at : at + DEPTH])
        part = weighted(lambda x: nudging[x : x + 1, :] * kappa[x])
        fill_fix(part + pltpu.roll(part, LANE - 2, 1) + pltpu.roll(part, LANE - 4, 1))

    @pl.when(is_child[0] == 0)
    def _():
        back = lax.rem(rows - nest_y[0], rows)
        reached = (nest_x[0] == 0, nest_x[0] + blocks == cols)
        for f in range(fields):
            for n, side in enumerate(x_halos_of(tx, x_first, x_second, f)):
                at = (f * 2 + n) * DEPTH
                weight = kappa[(0, cols - 1)[n]] * reached[n].astype(F32)
                sides[at : at + levels, :] = side * weight
                value = pltpu.roll(sides[at : at + DEPTH, :], back, 1)[:, :LANE]
                fill_stack(stack.at[f], chunk(n), value)
        starts = (nest_y[0] == 0).astype(F32)
        finals = (nest_y[0] == rows - LANE).astype(F32)
        part = weighted(lambda x: kappa[x])
        part = part * jnp.where(lax.rem(lanes, 2) == 0, starts, finals)
        value = jnp.zeros((PAD, LANE), F32)
        for b in range(blocks):
            shift = lax.rem(LANE + 4 * b - 2 * nest_x[0], LANE)
            here = lax.rem(turned, 2 * cols) // 2 == 3 * b
            value = jnp.where(here, pltpu.roll(part, shift, 1), value)
        fill_fix(value)

    fixes = jnp.zeros((PAD, LANE), F32)
    for f in range(fields):
        mixed = mix(matrices[f], stack[f])
        for n in range(2):
            at = pl.ds(f * (2 * levels) + n, levels, stride=2)
            out[at, :] = base[f, :levels, chunk(n)] + mixed[:levels, chunk(n)]
        fixes = jnp.where(turned // (2 * cols) == f, mixed[:PAD, chunk(2)], fixes)
    out[out.shape[0] - PAD :, :] = fixes
    copy.wait()


def outer(
    is_child, tx, ty, state2, matrices, base, kappa, nudging, x_halos, firsts, nests, dims, peers
):
    fields, levels, cols, chunks = dims
    rows = chunks * LANE
    height = -(-fields * 2 * levels // 8) * 8 + PAD
    return pl.pallas_call(
        functools.partial(outer_kernel, levels, peers),
        in_specs=[SMEM] * 3 + [HBM] + [VMEM] * 8 + [SMEM] * 2,
        out_specs=[VMEM] * 2,
        out_shape=[
            pltpu.VMEM((height, LANE), F32),
            pltpu.VMEM((state2.shape[0] // fields, LANE), F32),
        ],
        scratch_shapes=[
            pltpu.VMEM((fields * 2 * DEPTH, rows), F32),
            pltpu.VMEM((fields * 2 * DEPTH, 2 * rows), jnp.bfloat16),
            pltpu.VMEM((fields, 2 * DEPTH, 3 * LANE), jnp.bfloat16),
            pltpu.VMEM((2 * rows, LANE), jnp.bfloat16),
            pltpu.SemaphoreType.DMA,
        ],
        compiler_params=pltpu.CompilerParams(vmem_limit_bytes=12 * MIB),
        name="outer",
    )(is_child, tx, ty, in_hbm(state2), matrices, base, kappa, nudging, *x_halos, *firsts, *nests)


def tile_kernel(
    levels, peers, tx, ty, state, mask, matrices, kappa, x_first, x_second, first, second, ahead,
    out, buf, masked, sides, halo, stack, sems,
):
    cols, _, rows = masked.shape
    chunks = rows // LANE
    size = levels * cols * chunks
    fields = state.shape[0] // size

    def copy(f):
        at = pl.ds(f * size, size)
        return pltpu.make_async_copy(state.at[at], buf.at[at], sems.at[f])

    for f in range(1, fields):
        copy(f).start()
    sides[...] = jnp.zeros_like(sides)
    halo[...] = y_halos(ty, peers, first, second)
    pair = 2

    def field(f, carry, leading=False):
        if leading:
            fill_masked(levels, ahead, f, mask, masked)
        else:
            copy(f).wait()
            fill_masked(levels, buf, f, mask, masked)
        for n, side in enumerate(x_halos_of(tx, x_first, x_second, f)):
            sides[n, :levels, :] = side
        for x0 in range(0, cols, pair):
            for x in range(x0, x0 + pair):
                above = masked[x - 1] if x > 0 else sides[0]
                below = masked[x + 1] if x < cols - 1 else sides[1]
                shift = lax.rem(LANE - 2 * (f * cols + x), LANE)
                edge = pltpu.roll(halo[...], lax.rem(LANE + shift, LANE), 1)
                value = spread_of(masked[x], above, below, kappa[x], edge)
                part = slice((x - x0) * rows, (x - x0 + 1) * rows)
                fill_stack(stack, part, deepened(value))
            mixed = mix(matrices[f], stack[...])
            for n in range(pair * chunks):
                out[aligned((f * cols + x0) * chunks + n, PAD), :] = mixed[:PAD, chunk(n)]
        return carry

    field(0, 0, leading=True)
    lax.fori_loop(1, fields, field, 0)


def tile_of(tx, ty, state2, mask, matrices, kappa, x_halos, firsts, ahead, dims, peers):
    fields, levels, cols, chunks = dims
    rows = chunks * LANE
    return pl.pallas_call(
        functools.partial(tile_kernel, levels, peers),
        in_specs=[SMEM] * 2 + [HBM] + [VMEM] * 8,
        out_specs=VMEM,
        out_shape=pltpu.VMEM((fields * cols * chunks * PAD, LANE), F32),
        scratch_shapes=[
            pltpu.VMEM(state2.shape, F32),
            pltpu.VMEM((cols, PAD, rows), F32),
            pltpu.VMEM((2, PAD, rows), F32),
            pltpu.VMEM((PAD, LANE), F32),
            pltpu.VMEM((2 * DEPTH, 2 * rows), jnp.bfloat16),
            pltpu.SemaphoreType.DMA((fields,)),
        ],
        compiler_params=pltpu.CompilerParams(vmem_limit_bytes=16 * MIB),
        cost_estimate=COST,
        name="tile",
    )(tx, ty, in_hbm(state2), mask, matrices, kappa, *x_halos, *firsts, in_vmem(ahead))


def observe_kernel(dests, across, row, column, counts, places, mine, theirs, _, tile):
    lanes = lane_ids((1, LANE))
    slots = places.shape[1]
    ty, tx = row[0], column[0]
    me = ty * across + tx
    half = (mine.shape[0] - PAD) // slots * (LANE // dests)

    def source(turn, ref, g, carry):
        origin = (lax.div(g, across) ^ turn ^ ty) * across + (lax.rem(g, across) ^ tx)
        lane_in = lax.rem(g, LANE // dests) * dests + me
        block = PAD + lax.div(g, LANE // dests) * slots
        count = counts[0, origin]
        for k0 in range(0, slots, 4):
            ats, adds = [], []
            for m in range(k0, k0 + 4):
                place = places[origin, m]
                lane = place & (LANE - 1)
                value = pltpu.roll(ref[pl.ds(block + m, 1), :], (lane - lane_in) & (LANE - 1), 1)
                ats.append(place >> 7)
                adds.append(jnp.where(lanes == jnp.where(m < count, lane, LANE), value, 0.0))
            olds = [tile[pl.ds(at, 1), :] for at in ats]
            for k, (at, total) in enumerate(zip(ats, olds)):
                total = total + adds[k]
                for j in range(k):
                    total = total + jnp.where(ats[j] == at, adds[j], 0.0)
                tile[pl.ds(at, 1), :] = total
        return carry

    def both(n, carry):
        source(0, mine, n, carry)
        return source(3, theirs, n, carry)

    lax.fori_loop(0, half, both, 0)


def observe(row, column, places, counts, seen, tile, dests, across):
    return pl.pallas_call(
        functools.partial(observe_kernel, dests, across),
        in_specs=[SMEM] * 4 + [VMEM] * 3,
        out_specs=VMEM,
        out_shape=pltpu.VMEM(tile.shape, F32),
        input_output_aliases={6: 0},
        compiler_params=pltpu.CompilerParams(vmem_limit_bytes=4 * MIB),
        name="observe",
    )(row, column, counts, places, *seen, in_vmem(tile))


def finish_kernel(
    levels, is_child, nest_x, nest_y, tile, mask, in_arrived, out_arrived, in_sent, out_sent,
    out, buf, group, sems,
):
    cols = mask.shape[0]
    rows = mask.shape[2]
    chunks = rows // LANE
    step = cols * chunks
    size = levels * step
    fields = out.shape[0] // size
    blocks = cols // 3
    inner = blocks - 2
    lanes = lane_ids((levels, LANE))
    ends = jnp.logical_or(lanes == 0, lanes == LANE - 1)
    height = out_arrived.shape[0]

    def copy(f):
        at = pl.ds(f * size, size)
        return pltpu.make_async_copy(buf.at[at], out.at[at], sems.at[f])

    def piece_of(f, piece):
        return tile[pl.ds(pl.multiple_of((f * step + piece) * PAD, 8), levels), :]

    def payload(f, b, inner_ref, outer_ref):
        if b in (0, blocks - 1):
            value = outer_ref[pl.ds(f * (2 * levels) + min(b, 1), levels, stride=2), :]
        else:
            value = inner_ref[pl.ds(f * (levels * inner) + b - 1, levels, stride=inner), :]
        fixes = outer_ref[height - PAD : height - PAD + levels, :]
        shift = lax.rem(LANE - 2 * (f * cols + 3 * b), LANE)
        fixes = pltpu.roll(fixes, lax.rem(LANE + shift, LANE), 1)
        return value + jnp.where(ends, fixes, 0.0)

    def fill_child(f, carry):
        for b in range(blocks):
            high, low = halves(payload(f, b, in_arrived, out_arrived))
            both = jnp.concatenate([high, low], axis=1)
            value = jnp.dot(both, group[...], preferred_element_type=F32) * (1.0 / 9.0)
            for x in range(3 * b, 3 * b + 3):
                row = row_of(mask, x)
                for c in range(chunks):
                    piece = x * chunks + c
                    at = pl.ds(f * size + piece, levels, stride=step)
                    total = piece_of(f, piece) + value[:, chunk(c)]
                    buf[at, :] = total * row[:, chunk(c)]
        copy(f).start()
        return carry

    def fill_plain(f, carry):
        for x in range(cols):
            row = row_of(mask, x)
            for c in range(chunks):
                piece = x * chunks + c
                at = pl.ds(f * size + piece, levels, stride=step)
                buf[at, :] = piece_of(f, piece) * row[:, chunk(c)]
        return carry

    def fill_parent(f, carry):
        fill_plain(f, carry)
        for b in range(blocks):
            delta = payload(f, b, in_arrived, out_arrived) - payload(f, b, in_sent, out_sent)
            wide = jnp.concatenate([delta, jnp.zeros((levels, rows - LANE), F32)], 1)
            x = nest_x[0] + b
            value = pltpu.roll(wide, nest_y[0], 1) * row_of(mask, x)
            for c in range(chunks):
                at = pl.ds(f * size + x * chunks + c, levels, stride=step)
                buf[at, :] = buf[at, :] + value[:, chunk(c)]
        copy(f).start()
        return carry

    @pl.when(is_child[0] == 1)
    def _():
        ids = lax.broadcasted_iota(jnp.int32, group.shape, 0)
        ids = jnp.where(ids < LANE, ids, ids - LANE)
        group[...] = jnp.where(lane_ids(group.shape) // 3 == ids, 1.0, 0.0).astype(jnp.bfloat16)
        lax.fori_loop(0, fields, fill_child, 0)

    @pl.when(is_child[0] == 0)
    def _():
        lax.fori_loop(0, fields, fill_parent, 0)

    for f in range(fields):
        copy(f).wait()


def finish(is_child, nests, tile, mask, arrived, sent, dims):
    fields, levels, cols, chunks = dims
    rows = chunks * LANE
    size = (fields * levels * cols * chunks, LANE)
    return pl.pallas_call(
        functools.partial(finish_kernel, levels),
        in_specs=[SMEM] * 3 + [VMEM] * 6,
        out_specs=HBM,
        out_shape=pltpu.HBM(size, F32),
        scratch_shapes=[
            pltpu.VMEM(size, F32),
            pltpu.VMEM((2 * LANE, rows), jnp.bfloat16),
            pltpu.SemaphoreType.DMA((fields,)),
        ],
        compiler_params=pltpu.CompilerParams(vmem_limit_bytes=16 * MIB),
        cost_estimate=COST,
        name="finish",
    )(is_child, *nests, in_vmem(tile), mask, *arrived, *sent)


def from_neighbours(first, second, axis):
    size = lax.axis_size(axis)
    inner = [(i, i + 1) for i in range(1, size - 1, 2)]
    one = swapped(first, axis, 1)
    return one, lax.ppermute(second, axis, inner + [(j, i) for i, j in inner])


def swapped(value, axis, mask):
    return lax.ppermute(value, axis, [(i, i ^ mask) for i in range(lax.axis_size(axis))])


def local(
    adjoint_state,
    land_mask,
    diffusivity,
    mixing,
    nudging,
    nest_x,
    nest_y,
    obs_forcing,
    obs_cell,
    obs_count,
):
    _, fields, levels, cols, rows = adjoint_state.shape
    chunks = rows // LANE
    dims = (fields, levels, cols, chunks)
    state5 = adjoint_state.reshape(fields, levels, cols, 1, rows)
    state2 = adjoint_state.reshape(fields * levels * cols * chunks, LANE)
    mask = land_mask.reshape(cols, 1, rows)
    kappa = diffusivity.reshape(cols, 1, rows)
    mixing = mixing.reshape(fields, levels, 1, levels)
    peers, across = lax.axis_size("ty"), lax.axis_size("tx")
    assert peers == 4 and across & (across - 1) == 0 and 2 * fields * cols <= LANE
    assert levels <= PAD and cols % 3 == 0 and rows == 3 * LANE
    row = lax.axis_index("ty").astype(jnp.int32)
    column = lax.axis_index("tx").astype(jnp.int32)
    ty = row.reshape(1)
    is_child = (lax.axis_index("grp") == 0).astype(jnp.int32).reshape(1)
    nests = (nest_x, nest_y)

    forcing = obs_forcing[0, 0]
    dests = forcing.shape[1]
    counts = obs_count.reshape(1, -1)
    other = swapped(forcing, "tx", 1)
    pair = stacked(forcing, other)
    tx = column.reshape(1)
    *x_sent, ahead = x_edges(tx, state5, mask)
    ahead = ahead.reshape(-1, LANE)
    pair, *x_sent = lax.optimization_barrier((pair, *x_sent))
    x_halos = from_neighbours(*x_sent, "tx")
    line = [forcing, other, swapped(pair, "tx", 2)]
    for n in range(2, across.bit_length() - 1):
        blocks = jnp.concatenate(line)
        line = [blocks, swapped(blocks, "tx", 1 << n)]
    masked, matrices, parcel, in_sent, places = front(
        is_child, state2, mask, kappa, nudging, mixing, nests, line, ahead,
        obs_cell[0, :, :, 0], dims,
    )
    first = swapped(parcel, "ty", 1)
    in_arrived = swapped(in_sent, "grp", 1)
    parcel = repack(parcel, first, across * dests, PAD)
    second = swapped(parcel, "ty", 3)
    firsts = (first, second)
    masked, x_halos, parcel = lax.optimization_barrier((masked, x_halos, parcel))
    base = base_of(is_child, nests, masked, matrices, kappa, nudging, dims)
    out_sent, ahead = outer(
        is_child, tx, ty, state2, matrices, base, kappa, nudging, x_halos, firsts, nests, dims, peers
    )
    out_arrived = swapped(out_sent, "grp", 1)
    tile = tile_of(tx, ty, state2, mask, matrices, kappa, x_halos, firsts, ahead, dims, peers)
    tile = observe(ty, tx, places, counts, (parcel, second), tile, dests, across)
    arrived, sent = (in_arrived, out_arrived), (in_sent, out_sent)
    out = finish(is_child, nests, tile, mask, arrived, sent, dims)
    return out.reshape(adjoint_state.shape)


def solution(mesh):
    in_specs = (
        P("grp", None, None, "tx", "ty"),
        P("grp", "tx", "ty"),
        P("grp", "tx", "ty"),
        P("grp", None, None, None),
        P("tx", "ty"),
        P(("ty", "tx")),
        P(("ty", "tx")),
        P("grp", ("ty", "tx"), None, None),
        P("grp", None, None, ("ty", "tx")),
        P("grp", None, ("ty", "tx")),
    )
    out_specs = P("grp", None, None, "tx", "ty")
    return jax.shard_map(local, mesh=mesh, in_specs=in_specs, out_specs=out_specs, check_vma=False)
```

```python
import functools

import jax
import jax.numpy as jnp
from jax import lax
from jax.experimental import pallas as pl
from jax.experimental.pallas import tpu as pltpu
from jax.sharding import PartitionSpec as P

LANE = 128
PAD = 56
DEPTH = 64
MIB = 1 << 20
HBM = pl.BlockSpec(memory_space=pltpu.HBM)
SMEM = pl.BlockSpec(memory_space=pltpu.SMEM)
VMEM = pl.BlockSpec(memory_space=pltpu.VMEM)
F32 = jnp.float32
COST = pl.CostEstimate(flops=10**10, bytes_accessed=10**8, transcendentals=0)


def lane_ids(shape):
    return lax.broadcasted_iota(jnp.int32, shape, len(shape) - 1)


def row_of(ref, x):
    return ref[x].astype(F32)


def chunk(c):
    return slice(c * LANE, (c + 1) * LANE)


def in_hbm(value):
    return pltpu.with_memory_space_constraint(value, pltpu.HBM)


def in_vmem(value):
    return pltpu.with_memory_space_constraint(value, pltpu.VMEM)


def x_edges_kernel(tx, _, __, state, mask, first, second, ahead, buf, mask_buf, sems):
    fields, _, cols = state.shape[:3]
    even = lax.rem(tx[0], 2) == 0
    ends = (jnp.where(even, cols - 1, 0), jnp.where(even, 0, cols - 1))
    copies = [pltpu.make_async_copy(mask, mask_buf, sems.at[2 * fields])]
    for n, x in enumerate(ends):
        for f in range(fields):
            copies.append(
                pltpu.make_async_copy(state.at[f, :, x], buf.at[n, f], sems.at[n * fields + f])
            )
    copies.append(pltpu.make_async_copy(state.at[0], ahead, sems.at[2 * fields + 1]))
    for copy in copies:
        copy.start()
    copies[0].wait()
    for n, (x, out) in enumerate(zip(ends, (first, second))):
        for f in range(fields):
            copies[1 + n * fields + f].wait()
            out[f] = buf[n, f] * row_of(mask_buf, x)[None]
    copies[-1].wait()


def x_edges(tx, nests, state5, mask):
    fields, levels, cols, _, rows = state5.shape
    edge = (fields, levels, 1, rows)
    return pl.pallas_call(
        x_edges_kernel,
        in_specs=[SMEM] * 3 + [HBM] * 2,
        out_specs=[VMEM] * 3,
        out_shape=[pltpu.VMEM(edge, F32)] * 2 + [pltpu.VMEM(state5.shape[1:], F32)],
        scratch_shapes=[
            pltpu.VMEM((2,) + edge, F32),
            pltpu.VMEM(mask.shape, jnp.int32),
            pltpu.SemaphoreType.DMA((2 * fields + 2,)),
        ],
        compiler_params=pltpu.CompilerParams(vmem_limit_bytes=8 * MIB),
        cost_estimate=COST,
        name="x_edges",
    )(tx, *nests, in_hbm(state5), in_hbm(mask))


def x_halos_of(tx, first, second, f):
    one, two = first[f, :, 0, :], second[f, :, 0, :]
    even = lax.rem(tx[0], 2) == 0
    return jnp.where(even, two, one), jnp.where(even, one, two)


def spread_of(here, above, below, kappa, edge=None):
    rows = here.shape[1]
    lanes = lane_ids((here.shape[0], LANE))
    edge = 0.0 if edge is None else edge
    before = pltpu.roll(here, 1, 1)
    after = pltpu.roll(here, rows - 1, 1)
    before = jnp.concatenate([jnp.where(lanes == 0, edge, before[:, :LANE]), before[:, LANE:]], 1)
    after = jnp.concatenate(
        [after[:, :-LANE], jnp.where(lanes == LANE - 1, edge, after[:, -LANE:])], 1
    )
    return here + kappa * (above + below + before + after - 4.0 * here)


def halves(value):
    high = value.astype(jnp.bfloat16)
    return high, (value - high.astype(F32)).astype(jnp.bfloat16)


def deepened(value):
    return jnp.concatenate([value, jnp.zeros((DEPTH - value.shape[0], value.shape[1]), F32)], 0)


def fill_matrix(levels, mixing, square, matrix):
    square[:levels, :levels] = mixing
    value = square[...]
    high = value.astype(jnp.bfloat16).astype(F32)
    matrix[:DEPTH, :] = (high + pltpu.roll(high, DEPTH, 1)).astype(jnp.bfloat16)
    matrix[DEPTH:, :] = (value - high).astype(jnp.bfloat16)


def fill_stack(stack, part, value):
    high, low = halves(value)
    stack[:DEPTH, part] = high
    stack[DEPTH:, part] = low


def mix(matrix, stack):
    both = jnp.dot(matrix, stack, preferred_element_type=F32)
    return both[:DEPTH] + both[DEPTH:]


def fill_group(group):
    rows = group.shape[0] // 2
    ids = lax.broadcasted_iota(jnp.int32, group.shape, 0)
    ids = jnp.where(ids < rows, ids, ids - rows) // 3
    group[...] = jnp.where(ids == lane_ids(group.shape), 1.0, 0.0).astype(jnp.bfloat16)


def grouped(wide, group):
    return jnp.dot(wide, group, preferred_element_type=F32)


def aligned(index, size):
    return pl.ds(pl.multiple_of(index * size, size), size)


def packed(rows_of, cols):
    parts = []
    for x in range(cols):
        first, last = rows_of(x)
        lanes = lane_ids(first.shape)
        parts.append(jnp.where(lanes == 0, first, jnp.where(lanes == LANE - 1, last, 0.0)))
    shift = 2
    while len(parts) > 1:
        pairs = [parts[n : n + 2] for n in range(0, len(parts), 2)]
        parts = [p[0] + pltpu.roll(p[1], shift, 1) if len(p) == 2 else p[0] for p in pairs]
        shift *= 2
    return parts[0]


def fill_masked(levels, state, f, mask, masked):
    cols, _, rows = masked.shape
    chunks = rows // LANE
    step = cols * chunks
    for x in range(cols):
        row = row_of(mask, x)
        masked[x, PAD - 8 :, :] = jnp.zeros((8, rows), F32)
        for c in range(chunks):
            at = pl.ds(f * (levels * step) + x * chunks + c, levels, stride=step)
            masked[x, :levels, chunk(c)] = state[at, :] * row[:, chunk(c)]


TERMS = 11


def join_weights(bs, cols, kappa, nudging, weights):
    rows = weights.shape[1]
    ids = lane_ids((1, rows))
    for i, b in enumerate(bs):
        own = range(3 * b, 3 * b + 3)
        both = {x: nudging[x : x + 1, :] * kappa[x] for x in own}
        for n, x in enumerate(range(3 * b - 1, 3 * b + 4)):
            total = None
            for near in (x - 1, x + 1):
                if near in both:
                    total = both[near] if total is None else total + both[near]
            if x in both:
                total = total + (nudging[x : x + 1, :] - 4.0 * both[x])
            weights[i * TERMS + n : i * TERMS + n + 1, :] = total
        for n, x in enumerate(own):
            at = i * TERMS + 5 + n
            value = jnp.where(ids == rows - 1, 0.0, pltpu.roll(both[x], rows - 1, 1))
            weights[at : at + 1, :] = value
            value = jnp.where(ids == 0, 0.0, pltpu.roll(both[x], 1, 1))
            weights[at + 3 : at + 4, :] = value


def child_rows(f, bs, masked, weights, wide):
    cols, _, rows = masked.shape[1:]
    for i, b in enumerate(bs):

        def term(n, x):
            at = i * TERMS + n
            return weights[at : at + 1, :] * masked[f, x]

        total = None
        for n, x in enumerate(range(3 * b - 1, 3 * b + 4)):
            if 0 <= x < cols:
                total = term(n, x) if total is None else total + term(n, x)
        for side, shift in ((5, 1), (8, rows - 1)):
            value = term(side, 3 * b) + term(side + 1, 3 * b + 1) + term(side + 2, 3 * b + 2)
            total = total + pltpu.roll(value, shift, 1)
        at = aligned(f * len(bs) + i, DEPTH)
        wide[at, :rows], wide[at, rows:] = halves(deepened(total))


def parent_rows(f, bs, nest_x, nest_y, masked, kappa, stack):
    cols, _, rows = masked.shape[1:]
    back = lax.rem(rows - nest_y[0], rows)
    for i, b in enumerate(bs):
        x = nest_x[0] + b
        above = masked[f, jnp.maximum(x - 1, 0)]
        below = masked[f, jnp.minimum(x + 1, cols - 1)]
        if b == 0:
            above = jnp.where(x == 0, 0.0, above)
        if b == cols // 3 - 1:
            below = jnp.where(x == cols - 1, 0.0, below)
        value = spread_of(masked[f, x], above, below, kappa[x])
        value = deepened(pltpu.roll(value, back, 1)[:, :LANE])
        fill_stack(stack.at[f], chunk(i), value)


def mix_rows(bs, is_child, wide, group, stack, matrices, emit):
    fields = stack.shape[0]

    @pl.when(is_child[0] == 1)
    def _():
        value = grouped(wide[...], group[...])
        for f in range(fields):
            for i in range(len(bs)):
                at = (f * len(bs) + i) * DEPTH
                fill_stack(stack.at[f], chunk(i), value[at : at + DEPTH])

    for f in range(fields):
        emit(f, mix(matrices[f], stack[f]))


def row_scratch(bs, fields, rows):
    return [
        pltpu.VMEM((-(-len(bs) * TERMS // 8) * 8, rows), F32),
        pltpu.VMEM((fields * len(bs) * DEPTH, 2 * rows), jnp.bfloat16),
        pltpu.VMEM((fields, 2 * DEPTH, len(bs) * LANE), jnp.bfloat16),
        pltpu.VMEM((2 * rows, LANE), jnp.bfloat16),
    ]


ROOM = 18


def front_kernel(
    levels, bs, slots, is_child, state, mask, kappa, nudging, mixing, nest_x, nest_y, ahead, cells, *refs
):
    refs = list(refs)
    line = [refs.pop(0) for _ in range(len(refs) - ROOM)]
    front_steps(
        levels, bs, slots, line, is_child, state, mask, kappa, nudging, mixing, nest_x, nest_y, ahead,
        cells, *refs
    )


def front_steps(
    levels, bs, slots, line, is_child, state, mask, kappa, nudging, mixing, nest_x, nest_y, ahead,
    cells, masked_out, matrices, parcel, inner, places,
    buf, masked, mask_buf, kappa_buf, nudging_buf, mixing_buf, square, weights, wide, stack, group, sems, out_sems,
):
    fields, cols, _, rows = masked.shape
    chunks = rows // LANE
    step = cols * chunks
    size = levels * step

    def copy(f):
        at = pl.ds(f * size, size)
        return pltpu.make_async_copy(state.at[at], buf.at[at], sems.at[f])

    def copy_out(f):
        return pltpu.make_async_copy(masked.at[f], masked_out.at[f], out_sems.at[f])

    pairs = (
        (mask, mask_buf),
        (kappa, kappa_buf),
        (nudging, nudging_buf),
        (mixing, mixing_buf),
    )
    smalls = [
        pltpu.make_async_copy(source, target, sems.at[fields + n])
        for n, (source, target) in enumerate(pairs)
    ]
    for small in smalls:
        small.start()
    for f in range(1, fields):
        copy(f).start()
    square[...] = jnp.zeros_like(square)
    cell = cells[...]
    column, inside = cell // (cols * rows), lax.rem(cell, cols * rows)
    piece = (column // levels) * step + inside // LANE
    place = (piece * PAD + lax.rem(column, levels)) * LANE + lax.rem(inside, LANE)
    places[...] = place
    for small in smalls:
        small.wait()

    @pl.when(is_child[0] == 1)
    def _():
        fill_group(group)
        join_weights(bs, cols, kappa_buf, nudging_buf, weights)

    def field(f, total_edges, first=False):
        fill_matrix(levels, mixing_buf[f, :, 0, :], square, matrices.at[f])
        if first:
            fill_masked(levels, ahead, f, mask_buf, masked.at[f])
        else:
            copy(f).wait()
            fill_masked(levels, buf, f, mask_buf, masked.at[f])
        copy_out(f).start()
        own_edges = packed(
            lambda x: (masked[f, x, :, :LANE], masked[f, x, :, rows - LANE :]), cols
        )

        @pl.when(is_child[0] == 1)
        def _():
            child_rows(f, bs, masked, weights, wide)

        @pl.when(is_child[0] == 0)
        def _():
            parent_rows(f, bs, nest_x, nest_y, masked, kappa_buf, stack)

        return total_edges + pltpu.roll(own_edges, 2 * f * cols, 1)

    own_edges = field(0, jnp.zeros((PAD, LANE), F32), first=True)
    parcel[:PAD, :] = lax.fori_loop(1, fields, field, own_edges)
    parcel[PAD:, :] = jnp.zeros((parcel.shape[0] - PAD, LANE), F32)
    lane = 0
    for blocks in line:
        dests = blocks.shape[1]
        for start in range(0, blocks.shape[0], slots):
            at = PAD + lane // LANE * slots
            part = slice(lane % LANE, lane % LANE + dests)
            parcel[at : at + slots, part] = blocks[start : start + slots, :]
            lane += dests

    def emit(f, mixed):
        for i in range(len(bs)):
            at = pl.ds(f * levels * len(bs) + i, levels, stride=len(bs))
            inner[at, :] = mixed[:levels, chunk(i)]

    mix_rows(bs, is_child, wide, group, stack, matrices, emit)
    for f in range(fields):
        copy_out(f).wait()


def front(is_child, state2, mask, kappa, nudging, mixing, nests, line, ahead, cells, dims):
    fields, levels, cols, chunks = dims
    rows = chunks * LANE
    bs = tuple(range(1, cols // 3 - 1))
    arrays = (state2, mask, kappa, nudging, mixing)
    slots = cells.shape[1]
    height = -(-sum(blocks.size for blocks in line) // (LANE * slots)) * slots
    return pl.pallas_call(
        functools.partial(front_kernel, levels, bs, slots),
        in_specs=[SMEM] + [HBM] * 5 + [SMEM] * 2 + [VMEM] * (2 + len(line)),
        out_specs=[HBM] + [VMEM] * 4,
        out_shape=[
            pltpu.HBM((fields, cols, PAD, rows), F32),
            pltpu.VMEM((fields, 2 * DEPTH, 2 * DEPTH), jnp.bfloat16),
            pltpu.VMEM((PAD + height, LANE), F32),
            pltpu.VMEM((fields * levels * len(bs), LANE), F32),
            pltpu.VMEM(cells.shape, jnp.int32),
        ],
        scratch_shapes=[
            pltpu.VMEM(state2.shape, F32),
            pltpu.VMEM((fields, cols, PAD, rows), F32),
            pltpu.VMEM(mask.shape, jnp.int32),
            pltpu.VMEM(kappa.shape, F32),
            pltpu.VMEM(nudging.shape, F32),
            pltpu.VMEM(mixing.shape, F32),
            pltpu.VMEM((DEPTH, LANE), F32),
        ]
        + row_scratch(bs, fields, rows)
        + [pltpu.SemaphoreType.DMA((fields + 4,)), pltpu.SemaphoreType.DMA((fields,))],
        compiler_params=pltpu.CompilerParams(vmem_limit_bytes=24 * MIB),
        cost_estimate=COST,
        name="front",
    )(is_child, *map(in_hbm, arrays), *nests, in_vmem(ahead), cells, *line)


def base_kernel(
    levels, bs, is_child, nest_x, nest_y, masked_in, matrices, kappa, nudging, base,
    masked, weights, wide, stack, group, sems,
):
    fields, cols = masked.shape[:2]
    near = cols // 3
    reach = near + 2

    def child_copies(f):
        for n, x in enumerate((0, cols - near)):
            at = pl.ds(x, near)
            yield pltpu.make_async_copy(masked_in.at[f, at], masked.at[f, at], sems.at[f, n])

    def parent_copy(f):
        at = pl.ds(jnp.clip(nest_x[0] - 1, 0, cols - reach), reach)
        return pltpu.make_async_copy(masked_in.at[f, at], masked.at[f, at], sems.at[f, 0])

    @pl.when(is_child[0] == 1)
    def _():
        for f in range(fields):
            for copy in child_copies(f):
                copy.start()
        fill_group(group)
        join_weights(bs, cols, kappa, nudging, weights)

        def field(f, carry):
            for copy in child_copies(f):
                copy.wait()
            child_rows(f, bs, masked, weights, wide)
            return carry

        lax.fori_loop(0, fields, field, 0)

    @pl.when(is_child[0] == 0)
    def _():
        for f in range(fields):
            parent_copy(f).start()

        def field(f, carry):
            parent_copy(f).wait()
            parent_rows(f, bs, nest_x, nest_y, masked, kappa, stack)
            return carry

        lax.fori_loop(0, fields, field, 0)

    def emit(f, mixed):
        base[f, :, :] = mixed[:PAD, :]

    mix_rows(bs, is_child, wide, group, stack, matrices, emit)


def base_of(is_child, nests, masked, matrices, kappa, nudging, dims):
    fields, levels, cols, chunks = dims
    rows = chunks * LANE
    bs = (0, cols // 3 - 1)
    return pl.pallas_call(
        functools.partial(base_kernel, levels, bs),
        in_specs=[SMEM] * 3 + [HBM] + [VMEM] * 3,
        out_specs=VMEM,
        out_shape=pltpu.VMEM((fields, PAD, 2 * LANE), F32),
        scratch_shapes=[pltpu.VMEM(masked.shape, F32)]
        + row_scratch(bs, fields, rows)
        + [pltpu.SemaphoreType.DMA((fields, 2))],
        compiler_params=pltpu.CompilerParams(vmem_limit_bytes=16 * MIB),
        cost_estimate=COST,
        name="base",
    )(is_child, *nests, in_hbm(masked), matrices, kappa, nudging)


def stacked_kernel(one, two, out):
    out[: one.shape[0], :] = one[...]
    out[one.shape[0] :, :] = two[...]


def stacked(one, two):
    return pl.pallas_call(
        stacked_kernel,
        in_specs=[VMEM] * 2,
        out_specs=VMEM,
        out_shape=pltpu.VMEM((2 * one.shape[0], one.shape[1]), F32),
        compiler_params=pltpu.CompilerParams(vmem_limit_bytes=4 * MIB),
        name="stacked",
    )(one, two)


def merged(own, other, width):
    if 2 * width <= LANE:
        return own + pltpu.roll(other, width, 1)
    return jnp.concatenate([own, other], axis=0)


def repack_kernel(width, edges, parcel, arrived, out):
    if edges:
        out[:edges, :] = parcel[:edges, :]
    out[edges:, :] = merged(parcel[PAD:, :], arrived[PAD:, :], width)


def repack(parcel, arrived, width, edges):
    height = (parcel.shape[0] - PAD) * (1 if 2 * width <= LANE else 2)
    return pl.pallas_call(
        functools.partial(repack_kernel, width, edges),
        in_specs=[VMEM] * 2,
        out_specs=VMEM,
        out_shape=pltpu.VMEM((edges + height, LANE), F32),
        compiler_params=pltpu.CompilerParams(vmem_limit_bytes=4 * MIB),
        name="repack",
    )(parcel, arrived)


def y_halos(ty, peers, first, second):
    one, two = first[:PAD, :], second[:PAD, :]
    even = (lax.rem(ty[0], 2) == 0).astype(F32)
    odd = 1.0 - even
    before = (two * even + one * odd) * (ty[0] > 0).astype(F32)
    after = (one * even + two * odd) * (ty[0] < peers - 1).astype(F32)
    low = lax.rem(lane_ids((PAD, LANE)), 2) == 0
    return jnp.where(low, pltpu.roll(before, 1, 1), pltpu.roll(after, LANE - 1, 1))


def outer_kernel(
    levels, peers, is_child, tx, ty, state, matrices, base, kappa, nudging, x_first, x_second,
    first, second, nest_x, nest_y, out, ahead, sides, wide, stack, group, sem,
):
    fields = matrices.shape[0]
    cols, _, rows = kappa.shape
    blocks = cols // 3
    lanes = lane_ids((PAD, LANE))
    turned = lax.rem(lanes + 1, LANE)
    copy = pltpu.make_async_copy(state.at[pl.ds(0, ahead.shape[0])], ahead, sem)
    copy.start()
    sides[...] = jnp.zeros_like(sides)
    halo = y_halos(ty, peers, first, second)

    def weighted(row_of_x):
        one = packed(lambda x: (row_of_x(x)[:, :LANE], row_of_x(x)[:, rows - LANE :]), cols)
        total = one
        for f in range(1, fields):
            total = total + pltpu.roll(one, 2 * f * cols, 1)
        return halo * total

    def fill_fix(value):
        for f in range(fields):
            fill_stack(stack.at[f], chunk(2), deepened(value))

    @pl.when(is_child[0] == 1)
    def _():
        fill_group(group)
        for f in range(fields):
            for n, side in enumerate(x_halos_of(tx, x_first, x_second, f)):
                x = (0, cols - 1)[n]
                at = (f * 2 + n) * DEPTH
                sides[at : at + levels, :] = side * (nudging[x : x + 1, :] * kappa[x])
        wide[:, :rows], wide[:, rows:] = halves(sides[...])
        value = grouped(wide[...], group[...])
        for f in range(fields):
            for n in range(2):
                at = (f * 2 + n) * DEPTH
                fill_stack(stack.at[f], chunk(n), value[at : at + DEPTH])
        part = weighted(lambda x: nudging[x : x + 1, :] * kappa[x])
        fill_fix(part + pltpu.roll(part, LANE - 2, 1) + pltpu.roll(part, LANE - 4, 1))

    @pl.when(is_child[0] == 0)
    def _():
        back = lax.rem(rows - nest_y[0], rows)
        reached = (nest_x[0] == 0, nest_x[0] + blocks == cols)
        for f in range(fields):
            for n, side in enumerate(x_halos_of(tx, x_first, x_second, f)):
                at = (f * 2 + n) * DEPTH
                weight = kappa[(0, cols - 1)[n]] * reached[n].astype(F32)
                sides[at : at + levels, :] = side * weight
                value = pltpu.roll(sides[at : at + DEPTH, :], back, 1)[:, :LANE]
                fill_stack(stack.at[f], chunk(n), value)
        starts = (nest_y[0] == 0).astype(F32)
        finals = (nest_y[0] == rows - LANE).astype(F32)
        part = weighted(lambda x: kappa[x])
        part = part * jnp.where(lax.rem(lanes, 2) == 0, starts, finals)
        value = jnp.zeros((PAD, LANE), F32)
        for b in range(blocks):
            shift = lax.rem(LANE + 4 * b - 2 * nest_x[0], LANE)
            here = lax.rem(turned, 2 * cols) // 2 == 3 * b
            value = jnp.where(here, pltpu.roll(part, shift, 1), value)
        fill_fix(value)

    fixes = jnp.zeros((PAD, LANE), F32)
    for f in range(fields):
        mixed = mix(matrices[f], stack[f])
        for n in range(2):
            at = pl.ds(f * (2 * levels) + n, levels, stride=2)
            out[at, :] = base[f, :levels, chunk(n)] + mixed[:levels, chunk(n)]
        fixes = jnp.where(turned // (2 * cols) == f, mixed[:PAD, chunk(2)], fixes)
    out[out.shape[0] - PAD :, :] = fixes
    copy.wait()


def outer(
    is_child, tx, ty, state2, matrices, base, kappa, nudging, x_halos, firsts, nests, dims, peers
):
    fields, levels, cols, chunks = dims
    rows = chunks * LANE
    height = -(-fields * 2 * levels // 8) * 8 + PAD
    return pl.pallas_call(
        functools.partial(outer_kernel, levels, peers),
        in_specs=[SMEM] * 3 + [HBM] + [VMEM] * 8 + [SMEM] * 2,
        out_specs=[VMEM] * 2,
        out_shape=[
            pltpu.VMEM((height, LANE), F32),
            pltpu.VMEM((state2.shape[0] // fields, LANE), F32),
        ],
        scratch_shapes=[
            pltpu.VMEM((fields * 2 * DEPTH, rows), F32),
            pltpu.VMEM((fields * 2 * DEPTH, 2 * rows), jnp.bfloat16),
            pltpu.VMEM((fields, 2 * DEPTH, 3 * LANE), jnp.bfloat16),
            pltpu.VMEM((2 * rows, LANE), jnp.bfloat16),
            pltpu.SemaphoreType.DMA,
        ],
        compiler_params=pltpu.CompilerParams(vmem_limit_bytes=12 * MIB),
        name="outer",
    )(is_child, tx, ty, in_hbm(state2), matrices, base, kappa, nudging, *x_halos, *firsts, *nests)


def tile_kernel(
    levels, peers, tx, ty, state, mask, matrices, kappa, x_first, x_second, first, second, ahead,
    out, buf, masked, sides, halo, stack, sems,
):
    cols, _, rows = masked.shape
    chunks = rows // LANE
    size = levels * cols * chunks
    fields = state.shape[0] // size

    def copy(f):
        at = pl.ds(f * size, size)
        return pltpu.make_async_copy(state.at[at], buf.at[at], sems.at[f])

    for f in range(1, fields):
        copy(f).start()
    sides[...] = jnp.zeros_like(sides)
    halo[...] = y_halos(ty, peers, first, second)
    pair = 2

    def field(f, carry, leading=False):
        if leading:
            fill_masked(levels, ahead, f, mask, masked)
        else:
            copy(f).wait()
            fill_masked(levels, buf, f, mask, masked)
        for n, side in enumerate(x_halos_of(tx, x_first, x_second, f)):
            sides[n, :levels, :] = side
        for x0 in range(0, cols, pair):
            for x in range(x0, x0 + pair):
                above = masked[x - 1] if x > 0 else sides[0]
                below = masked[x + 1] if x < cols - 1 else sides[1]
                shift = lax.rem(LANE - 2 * (f * cols + x), LANE)
                edge = pltpu.roll(halo[...], lax.rem(LANE + shift, LANE), 1)
                value = spread_of(masked[x], above, below, kappa[x], edge)
                part = slice((x - x0) * rows, (x - x0 + 1) * rows)
                fill_stack(stack, part, deepened(value))
            mixed = mix(matrices[f], stack[...])
            for n in range(pair * chunks):
                out[aligned((f * cols + x0) * chunks + n, PAD), :] = mixed[:PAD, chunk(n)]
        return carry

    field(0, 0, leading=True)
    lax.fori_loop(1, fields, field, 0)


def tile_of(tx, ty, state2, mask, matrices, kappa, x_halos, firsts, ahead, dims, peers):
    fields, levels, cols, chunks = dims
    rows = chunks * LANE
    return pl.pallas_call(
        functools.partial(tile_kernel, levels, peers),
        in_specs=[SMEM] * 2 + [HBM] + [VMEM] * 8,
        out_specs=VMEM,
        out_shape=pltpu.VMEM((fields * cols * chunks * PAD, LANE), F32),
        scratch_shapes=[
            pltpu.VMEM(state2.shape, F32),
            pltpu.VMEM((cols, PAD, rows), F32),
            pltpu.VMEM((2, PAD, rows), F32),
            pltpu.VMEM((PAD, LANE), F32),
            pltpu.VMEM((2 * DEPTH, 2 * rows), jnp.bfloat16),
            pltpu.SemaphoreType.DMA((fields,)),
        ],
        compiler_params=pltpu.CompilerParams(vmem_limit_bytes=16 * MIB),
        cost_estimate=COST,
        name="tile",
    )(tx, ty, in_hbm(state2), mask, matrices, kappa, *x_halos, *firsts, in_vmem(ahead))


def observe_kernel(dests, across, row, column, counts, places, mine, theirs, _, tile):
    lanes = lane_ids((1, LANE))
    slots = places.shape[1]
    ty, tx = row[0], column[0]
    me = ty * across + tx
    half = (mine.shape[0] - PAD) // slots * (LANE // dests)

    def source(turn, ref, g, carry):
        origin = (lax.div(g, across) ^ turn ^ ty) * across + (lax.rem(g, across) ^ tx)
        lane_in = lax.rem(g, LANE // dests) * dests + me
        block = PAD + lax.div(g, LANE // dests) * slots
        count = counts[0, origin]
        for k0 in range(0, slots, 4):
            ats, adds = [], []
            for m in range(k0, k0 + 4):
                place = places[origin, m]
                lane = place & (LANE - 1)
                value = pltpu.roll(ref[pl.ds(block + m, 1), :], (lane - lane_in) & (LANE - 1), 1)
                ats.append(place >> 7)
                adds.append(jnp.where(lanes == jnp.where(m < count, lane, LANE), value, 0.0))
            olds = [tile[pl.ds(at, 1), :] for at in ats]
            for k, (at, total) in enumerate(zip(ats, olds)):
                total = total + adds[k]
                for j in range(k):
                    total = total + jnp.where(ats[j] == at, adds[j], 0.0)
                tile[pl.ds(at, 1), :] = total
        return carry

    def both(n, carry):
        source(0, mine, n, carry)
        return source(3, theirs, n, carry)

    lax.fori_loop(0, half, both, 0)


def observe(row, column, places, counts, seen, tile, dests, across):
    return pl.pallas_call(
        functools.partial(observe_kernel, dests, across),
        in_specs=[SMEM] * 4 + [VMEM] * 3,
        out_specs=VMEM,
        out_shape=pltpu.VMEM(tile.shape, F32),
        input_output_aliases={6: 0},
        compiler_params=pltpu.CompilerParams(vmem_limit_bytes=4 * MIB),
        name="observe",
    )(row, column, counts, places, *seen, in_vmem(tile))


def finish_kernel(
    levels, is_child, nest_x, nest_y, tile, mask, in_arrived, out_arrived, in_sent, out_sent,
    out, buf, group, sems,
):
    cols = mask.shape[0]
    rows = mask.shape[2]
    chunks = rows // LANE
    step = cols * chunks
    size = levels * step
    fields = out.shape[0] // size
    blocks = cols // 3
    inner = blocks - 2
    lanes = lane_ids((levels, LANE))
    ends = jnp.logical_or(lanes == 0, lanes == LANE - 1)
    height = out_arrived.shape[0]

    def copy(f):
        at = pl.ds(f * size, size)
        return pltpu.make_async_copy(buf.at[at], out.at[at], sems.at[f])

    def piece_of(f, piece):
        return tile[pl.ds(pl.multiple_of((f * step + piece) * PAD, 8), levels), :]

    def payload(f, b, inner_ref, outer_ref):
        if b in (0, blocks - 1):
            value = outer_ref[pl.ds(f * (2 * levels) + min(b, 1), levels, stride=2), :]
        else:
            value = inner_ref[pl.ds(f * (levels * inner) + b - 1, levels, stride=inner), :]
        fixes = outer_ref[height - PAD : height - PAD + levels, :]
        shift = lax.rem(LANE - 2 * (f * cols + 3 * b), LANE)
        fixes = pltpu.roll(fixes, lax.rem(LANE + shift, LANE), 1)
        return value + jnp.where(ends, fixes, 0.0)

    def fill_child(f, carry):
        for b in range(blocks):
            high, low = halves(payload(f, b, in_arrived, out_arrived))
            both = jnp.concatenate([high, low], axis=1)
            value = jnp.dot(both, group[...], preferred_element_type=F32) * (1.0 / 9.0)
            for x in range(3 * b, 3 * b + 3):
                row = row_of(mask, x)
                for c in range(chunks):
                    piece = x * chunks + c
                    at = pl.ds(f * size + piece, levels, stride=step)
                    total = piece_of(f, piece) + value[:, chunk(c)]
                    buf[at, :] = total * row[:, chunk(c)]
        copy(f).start()
        return carry

    def fill_plain(f, carry):
        for x in range(cols):
            row = row_of(mask, x)
            for c in range(chunks):
                piece = x * chunks + c
                at = pl.ds(f * size + piece, levels, stride=step)
                buf[at, :] = piece_of(f, piece) * row[:, chunk(c)]
        return carry

    def fill_parent(f, carry):
        fill_plain(f, carry)
        for b in range(blocks):
            delta = payload(f, b, in_arrived, out_arrived) - payload(f, b, in_sent, out_sent)
            wide = jnp.concatenate([delta, jnp.zeros((levels, rows - LANE), F32)], 1)
            x = nest_x[0] + b
            value = pltpu.roll(wide, nest_y[0], 1) * row_of(mask, x)
            for c in range(chunks):
                at = pl.ds(f * size + x * chunks + c, levels, stride=step)
                buf[at, :] = buf[at, :] + value[:, chunk(c)]
        copy(f).start()
        return carry

    @pl.when(is_child[0] == 1)
    def _():
        ids = lax.broadcasted_iota(jnp.int32, group.shape, 0)
        ids = jnp.where(ids < LANE, ids, ids - LANE)
        group[...] = jnp.where(lane_ids(group.shape) // 3 == ids, 1.0, 0.0).astype(jnp.bfloat16)
        lax.fori_loop(0, fields, fill_child, 0)

    @pl.when(is_child[0] == 0)
    def _():
        lax.fori_loop(0, fields, fill_parent, 0)

    for f in range(fields):
        copy(f).wait()


def finish(is_child, nests, tile, mask, arrived, sent, dims):
    fields, levels, cols, chunks = dims
    rows = chunks * LANE
    size = (fields * levels * cols * chunks, LANE)
    return pl.pallas_call(
        functools.partial(finish_kernel, levels),
        in_specs=[SMEM] * 3 + [VMEM] * 6,
        out_specs=HBM,
        out_shape=pltpu.HBM(size, F32),
        scratch_shapes=[
            pltpu.VMEM(size, F32),
            pltpu.VMEM((2 * LANE, rows), jnp.bfloat16),
            pltpu.SemaphoreType.DMA((fields,)),
        ],
        compiler_params=pltpu.CompilerParams(vmem_limit_bytes=16 * MIB),
        cost_estimate=COST,
        name="finish",
    )(is_child, *nests, in_vmem(tile), mask, *arrived, *sent)


def from_neighbours(first, second, axis):
    size = lax.axis_size(axis)
    inner = [(i, i + 1) for i in range(1, size - 1, 2)]
    one = swapped(first, axis, 1)
    return one, lax.ppermute(second, axis, inner + [(j, i) for i, j in inner])


def swapped(value, axis, mask):
    return lax.ppermute(value, axis, [(i, i ^ mask) for i in range(lax.axis_size(axis))])


def local(
    adjoint_state,
    land_mask,
    diffusivity,
    mixing,
    nudging,
    nest_x,
    nest_y,
    obs_forcing,
    obs_cell,
    obs_count,
):
    _, fields, levels, cols, rows = adjoint_state.shape
    chunks = rows // LANE
    dims = (fields, levels, cols, chunks)
    state5 = adjoint_state.reshape(fields, levels, cols, 1, rows)
    state2 = adjoint_state.reshape(fields * levels * cols * chunks, LANE)
    mask = land_mask.reshape(cols, 1, rows)
    kappa = diffusivity.reshape(cols, 1, rows)
    mixing = mixing.reshape(fields, levels, 1, levels)
    peers, across = lax.axis_size("ty"), lax.axis_size("tx")
    assert peers == 4 and across & (across - 1) == 0 and 2 * fields * cols <= LANE
    assert levels <= PAD and cols % 3 == 0 and rows == 3 * LANE
    row = lax.axis_index("ty").astype(jnp.int32)
    column = lax.axis_index("tx").astype(jnp.int32)
    ty = row.reshape(1)
    is_child = (lax.axis_index("grp") == 0).astype(jnp.int32).reshape(1)
    nests = (nest_x, nest_y)

    forcing = obs_forcing[0, 0]
    dests = forcing.shape[1]
    counts = obs_count.reshape(1, -1)
    other = swapped(forcing, "tx", 1)
    pair = stacked(forcing, other)
    tx = column.reshape(1)
    *x_sent, ahead = x_edges(tx, nests, state5, mask)
    ahead = ahead.reshape(-1, LANE)
    pair, *x_sent = lax.optimization_barrier((pair, *x_sent))
    x_halos = from_neighbours(*x_sent, "tx")
    line = [forcing, other, swapped(pair, "tx", 2)]
    for n in range(2, across.bit_length() - 1):
        blocks = jnp.concatenate(line)
        line = [blocks, swapped(blocks, "tx", 1 << n)]
    masked, matrices, parcel, in_sent, places = front(
        is_child, state2, mask, kappa, nudging, mixing, nests, line, ahead,
        obs_cell[0, :, :, 0], dims,
    )
    first = swapped(parcel, "ty", 1)
    in_arrived = swapped(in_sent, "grp", 1)
    parcel = repack(parcel, first, across * dests, PAD)
    second = swapped(parcel, "ty", 3)
    firsts = (first, second)
    masked, x_halos, parcel = lax.optimization_barrier((masked, x_halos, parcel))
    base = base_of(is_child, nests, masked, matrices, kappa, nudging, dims)
    out_sent, ahead = outer(
        is_child, tx, ty, state2, matrices, base, kappa, nudging, x_halos, firsts, nests, dims, peers
    )
    out_arrived = swapped(out_sent, "grp", 1)
    tile = tile_of(tx, ty, state2, mask, matrices, kappa, x_halos, firsts, ahead, dims, peers)
    tile = observe(ty, tx, places, counts, (parcel, second), tile, dests, across)
    arrived, sent = (in_arrived, out_arrived), (in_sent, out_sent)
    out = finish(is_child, nests, tile, mask, arrived, sent, dims)
    return out.reshape(adjoint_state.shape)


def solution(mesh):
    in_specs = (
        P("grp", None, None, "tx", "ty"),
        P("grp", "tx", "ty"),
        P("grp", "tx", "ty"),
        P("grp", None, None, None),
        P("tx", "ty"),
        P(("ty", "tx")),
        P(("ty", "tx")),
        P("grp", ("ty", "tx"), None, None),
        P("grp", None, None, ("ty", "tx")),
        P("grp", None, ("ty", "tx")),
    )
    out_specs = P("grp", None, None, "tx", "ty")
    return jax.shard_map(local, mesh=mesh, in_specs=in_specs, out_specs=out_specs, check_vma=False)
```

```python
import functools

import jax
import jax.numpy as jnp
from jax import lax
from jax.experimental import pallas as pl
from jax.experimental.pallas import tpu as pltpu
from jax.sharding import PartitionSpec as P

LANE = 128
PAD = 56
DEPTH = 64
MIB = 1 << 20
HBM = pl.BlockSpec(memory_space=pltpu.HBM)
SMEM = pl.BlockSpec(memory_space=pltpu.SMEM)
VMEM = pl.BlockSpec(memory_space=pltpu.VMEM)
F32 = jnp.float32
COST = pl.CostEstimate(flops=10**10, bytes_accessed=10**8, transcendentals=0)


def lane_ids(shape):
    return lax.broadcasted_iota(jnp.int32, shape, len(shape) - 1)


def row_of(ref, x):
    return ref[x].astype(F32)


def chunk(c):
    return slice(c * LANE, (c + 1) * LANE)


def in_hbm(value):
    return pltpu.with_memory_space_constraint(value, pltpu.HBM)


def in_vmem(value):
    return pltpu.with_memory_space_constraint(value, pltpu.VMEM)


def x_edges_kernel(tx, _, __, state, mask, first, second, ahead, buf, mask_buf, sems):
    fields, _, cols = state.shape[:3]
    even = lax.rem(tx[0], 2) == 0
    ends = (jnp.where(even, cols - 1, 0), jnp.where(even, 0, cols - 1))
    copies = [pltpu.make_async_copy(mask, mask_buf, sems.at[2 * fields])]
    for n, x in enumerate(ends):
        for f in range(fields):
            copies.append(
                pltpu.make_async_copy(state.at[f, :, x], buf.at[n, f], sems.at[n * fields + f])
            )
    copies.append(pltpu.make_async_copy(state.at[0], ahead, sems.at[2 * fields + 1]))
    for copy in copies:
        copy.start()
    copies[0].wait()
    for n, (x, out) in enumerate(zip(ends, (first, second))):
        for f in range(fields):
            copies[1 + n * fields + f].wait()
            out[f] = buf[n, f] * row_of(mask_buf, x)[None]
    copies[-1].wait()


def x_edges(tx, nests, state5, mask):
    fields, levels, cols, _, rows = state5.shape
    edge = (fields, levels, 1, rows)
    return pl.pallas_call(
        x_edges_kernel,
        in_specs=[SMEM] * 3 + [HBM] * 2,
        out_specs=[VMEM] * 3,
        out_shape=[pltpu.VMEM(edge, F32)] * 2 + [pltpu.VMEM(state5.shape[1:], F32)],
        scratch_shapes=[
            pltpu.VMEM((2,) + edge, F32),
            pltpu.VMEM(mask.shape, jnp.int32),
            pltpu.SemaphoreType.DMA((2 * fields + 2,)),
        ],
        compiler_params=pltpu.CompilerParams(vmem_limit_bytes=8 * MIB),
        cost_estimate=COST,
        name="x_edges",
    )(tx, *nests, in_hbm(state5), in_hbm(mask))


def x_halos_of(tx, first, second, f):
    one, two = first[f, :, 0, :], second[f, :, 0, :]
    even = lax.rem(tx[0], 2) == 0
    return jnp.where(even, two, one), jnp.where(even, one, two)


def spread_of(here, above, below, kappa, edge=None):
    rows = here.shape[1]
    lanes = lane_ids((here.shape[0], LANE))
    edge = 0.0 if edge is None else edge
    before = pltpu.roll(here, 1, 1)
    after = pltpu.roll(here, rows - 1, 1)
    before = jnp.concatenate([jnp.where(lanes == 0, edge, before[:, :LANE]), before[:, LANE:]], 1)
    after = jnp.concatenate(
        [after[:, :-LANE], jnp.where(lanes == LANE - 1, edge, after[:, -LANE:])], 1
    )
    return here + kappa * (above + below + before + after - 4.0 * here)


def halves(value):
    high = value.astype(jnp.bfloat16)
    return high, (value - high.astype(F32)).astype(jnp.bfloat16)


def deepened(value):
    return jnp.concatenate([value, jnp.zeros((DEPTH - value.shape[0], value.shape[1]), F32)], 0)


def fill_matrix(levels, mixing, square, matrix):
    square[:levels, :levels] = mixing
    value = square[...]
    high = value.astype(jnp.bfloat16).astype(F32)
    matrix[:DEPTH, :] = (high + pltpu.roll(high, DEPTH, 1)).astype(jnp.bfloat16)
    matrix[DEPTH:, :] = (value - high).astype(jnp.bfloat16)


def fill_stack(stack, part, value):
    high, low = halves(value)
    stack[:DEPTH, part] = high
    stack[DEPTH:, part] = low


def mix(matrix, stack):
    both = jnp.dot(matrix, stack, preferred_element_type=F32)
    return both[:DEPTH] + both[DEPTH:]


def fill_group(group):
    rows = group.shape[0] // 2
    ids = lax.broadcasted_iota(jnp.int32, group.shape, 0)
    ids = jnp.where(ids < rows, ids, ids - rows) // 3
    group[...] = jnp.where(ids == lane_ids(group.shape), 1.0, 0.0).astype(jnp.bfloat16)


def grouped(wide, group):
    return jnp.dot(wide, group, preferred_element_type=F32)


def aligned(index, size):
    return pl.ds(pl.multiple_of(index * size, size), size)


def packed(rows_of, cols):
    parts = []
    for x in range(cols):
        first, last = rows_of(x)
        lanes = lane_ids(first.shape)
        parts.append(jnp.where(lanes == 0, first, jnp.where(lanes == LANE - 1, last, 0.0)))
    shift = 2
    while len(parts) > 1:
        pairs = [parts[n : n + 2] for n in range(0, len(parts), 2)]
        parts = [p[0] + pltpu.roll(p[1], shift, 1) if len(p) == 2 else p[0] for p in pairs]
        shift *= 2
    return parts[0]


def fill_masked(levels, state, f, mask, masked):
    cols, _, rows = masked.shape
    chunks = rows // LANE
    step = cols * chunks
    for x in range(cols):
        row = row_of(mask, x)
        masked[x, PAD - 8 :, :] = jnp.zeros((8, rows), F32)
        for c in range(chunks):
            at = pl.ds(f * (levels * step) + x * chunks + c, levels, stride=step)
            masked[x, :levels, chunk(c)] = state[at, :] * row[:, chunk(c)]


TERMS = 11


def join_weights(bs, cols, kappa, nudging, weights):
    rows = weights.shape[1]
    ids = lane_ids((1, rows))
    for i, b in enumerate(bs):
        own = range(3 * b, 3 * b + 3)
        both = {x: nudging[x : x + 1, :] * kappa[x] for x in own}
        for n, x in enumerate(range(3 * b - 1, 3 * b + 4)):
            total = None
            for near in (x - 1, x + 1):
                if near in both:
                    total = both[near] if total is None else total + both[near]
            if x in both:
                total = total + (nudging[x : x + 1, :] - 4.0 * both[x])
            weights[i * TERMS + n : i * TERMS + n + 1, :] = total
        for n, x in enumerate(own):
            at = i * TERMS + 5 + n
            value = jnp.where(ids == rows - 1, 0.0, pltpu.roll(both[x], rows - 1, 1))
            weights[at : at + 1, :] = value
            value = jnp.where(ids == 0, 0.0, pltpu.roll(both[x], 1, 1))
            weights[at + 3 : at + 4, :] = value


def child_rows(f, bs, masked, weights, wide):
    cols, _, rows = masked.shape[1:]
    for i, b in enumerate(bs):

        def term(n, x):
            at = i * TERMS + n
            return weights[at : at + 1, :] * masked[f, x]

        total = None
        for n, x in enumerate(range(3 * b - 1, 3 * b + 4)):
            if 0 <= x < cols:
                total = term(n, x) if total is None else total + term(n, x)
        for side, shift in ((5, 1), (8, rows - 1)):
            value = term(side, 3 * b) + term(side + 1, 3 * b + 1) + term(side + 2, 3 * b + 2)
            total = total + pltpu.roll(value, shift, 1)
        at = aligned(f * len(bs) + i, DEPTH)
        wide[at, :rows], wide[at, rows:] = halves(deepened(total))


def parent_rows(f, bs, nest_x, nest_y, masked, kappa, stack):
    cols, _, rows = masked.shape[1:]
    back = lax.rem(rows - nest_y[0], rows)
    for i, b in enumerate(bs):
        x = nest_x[0] + b
        above = masked[f, jnp.maximum(x - 1, 0)]
        below = masked[f, jnp.minimum(x + 1, cols - 1)]
        if b == 0:
            above = jnp.where(x == 0, 0.0, above)
        if b == cols // 3 - 1:
            below = jnp.where(x == cols - 1, 0.0, below)
        value = spread_of(masked[f, x], above, below, kappa[x])
        value = deepened(pltpu.roll(value, back, 1)[:, :LANE])
        fill_stack(stack.at[f], chunk(i), value)


def mix_rows(bs, is_child, wide, group, stack, matrices, emit):
    fields = stack.shape[0]

    @pl.when(is_child[0] == 1)
    def _():
        value = grouped(wide[...], group[...])
        for f in range(fields):
            for i in range(len(bs)):
                at = (f * len(bs) + i) * DEPTH
                fill_stack(stack.at[f], chunk(i), value[at : at + DEPTH])

    for f in range(fields):
        emit(f, mix(matrices[f], stack[f]))


def row_scratch(bs, fields, rows):
    return [
        pltpu.VMEM((-(-len(bs) * TERMS // 8) * 8, rows), F32),
        pltpu.VMEM((fields * len(bs) * DEPTH, 2 * rows), jnp.bfloat16),
        pltpu.VMEM((fields, 2 * DEPTH, len(bs) * LANE), jnp.bfloat16),
        pltpu.VMEM((2 * rows, LANE), jnp.bfloat16),
    ]


ROOM = 18


def front_kernel(
    levels, bs, slots, is_child, state, mask, kappa, nudging, mixing, nest_x, nest_y, ahead, cells, *refs
):
    refs = list(refs)
    line = [refs.pop(0) for _ in range(len(refs) - ROOM)]
    front_steps(
        levels, bs, slots, line, is_child, state, mask, kappa, nudging, mixing, nest_x, nest_y, ahead,
        cells, *refs
    )


def front_steps(
    levels, bs, slots, line, is_child, state, mask, kappa, nudging, mixing, nest_x, nest_y, ahead,
    cells, masked_out, matrices, parcel, inner, places,
    buf, masked, mask_buf, kappa_buf, nudging_buf, mixing_buf, square, weights, wide, stack, group, sems, out_sems,
):
    fields, cols, _, rows = masked.shape
    chunks = rows // LANE
    step = cols * chunks
    size = levels * step

    def copy(f):
        at = pl.ds(f * size, size)
        return pltpu.make_async_copy(state.at[at], buf.at[at], sems.at[f])

    def copy_out(f):
        return pltpu.make_async_copy(masked.at[f], masked_out.at[f], out_sems.at[f])

    pairs = (
        (mask, mask_buf),
        (kappa, kappa_buf),
        (nudging, nudging_buf),
        (mixing, mixing_buf),
    )
    smalls = [
        pltpu.make_async_copy(source, target, sems.at[fields + n])
        for n, (source, target) in enumerate(pairs)
    ]
    for small in smalls:
        small.start()
    for f in range(1, fields):
        copy(f).start()
    square[...] = jnp.zeros_like(square)
    cell = cells[...]
    column, inside = cell // (cols * rows), lax.rem(cell, cols * rows)
    piece = (column // levels) * step + inside // LANE
    place = (piece * PAD + lax.rem(column, levels)) * LANE + lax.rem(inside, LANE)
    places[...] = place
    for small in smalls:
        small.wait()

    @pl.when(is_child[0] == 1)
    def _():
        fill_group(group)
        join_weights(bs, cols, kappa_buf, nudging_buf, weights)

    def field(f, total_edges, first=False):
        fill_matrix(levels, mixing_buf[f, :, 0, :], square, matrices.at[f])
        if first:
            fill_masked(levels, ahead, f, mask_buf, masked.at[f])
        else:
            copy(f).wait()
            fill_masked(levels, buf, f, mask_buf, masked.at[f])
        copy_out(f).start()
        own_edges = packed(
            lambda x: (masked[f, x, :, :LANE], masked[f, x, :, rows - LANE :]), cols
        )

        @pl.when(is_child[0] == 1)
        def _():
            child_rows(f, bs, masked, weights, wide)

        @pl.when(is_child[0] == 0)
        def _():
            parent_rows(f, bs, nest_x, nest_y, masked, kappa_buf, stack)

        return total_edges + pltpu.roll(own_edges, 2 * f * cols, 1)

    own_edges = field(0, jnp.zeros((PAD, LANE), F32), first=True)
    parcel[:PAD, :] = lax.fori_loop(1, fields, field, own_edges, unroll=True)
    parcel[PAD:, :] = jnp.zeros((parcel.shape[0] - PAD, LANE), F32)
    lane = 0
    for blocks in line:
        dests = blocks.shape[1]
        for start in range(0, blocks.shape[0], slots):
            at = PAD + lane // LANE * slots
            part = slice(lane % LANE, lane % LANE + dests)
            parcel[at : at + slots, part] = blocks[start : start + slots, :]
            lane += dests

    def emit(f, mixed):
        for i in range(len(bs)):
            at = pl.ds(f * levels * len(bs) + i, levels, stride=len(bs))
            inner[at, :] = mixed[:levels, chunk(i)]

    mix_rows(bs, is_child, wide, group, stack, matrices, emit)
    for f in range(fields):
        copy_out(f).wait()


def front(is_child, state2, mask, kappa, nudging, mixing, nests, line, ahead, cells, dims):
    fields, levels, cols, chunks = dims
    rows = chunks * LANE
    bs = tuple(range(1, cols // 3 - 1))
    arrays = (state2, mask, kappa, nudging, mixing)
    slots = cells.shape[1]
    height = -(-sum(blocks.size for blocks in line) // (LANE * slots)) * slots
    return pl.pallas_call(
        functools.partial(front_kernel, levels, bs, slots),
        in_specs=[SMEM] + [HBM] * 5 + [SMEM] * 2 + [VMEM] * (2 + len(line)),
        out_specs=[HBM] + [VMEM] * 4,
        out_shape=[
            pltpu.HBM((fields, cols, PAD, rows), F32),
            pltpu.VMEM((fields, 2 * DEPTH, 2 * DEPTH), jnp.bfloat16),
            pltpu.VMEM((PAD + height, LANE), F32),
            pltpu.VMEM((fields * levels * len(bs), LANE), F32),
            pltpu.VMEM(cells.shape, jnp.int32),
        ],
        scratch_shapes=[
            pltpu.VMEM(state2.shape, F32),
            pltpu.VMEM((fields, cols, PAD, rows), F32),
            pltpu.VMEM(mask.shape, jnp.int32),
            pltpu.VMEM(kappa.shape, F32),
            pltpu.VMEM(nudging.shape, F32),
            pltpu.VMEM(mixing.shape, F32),
            pltpu.VMEM((DEPTH, LANE), F32),
        ]
        + row_scratch(bs, fields, rows)
        + [pltpu.SemaphoreType.DMA((fields + 4,)), pltpu.SemaphoreType.DMA((fields,))],
        compiler_params=pltpu.CompilerParams(vmem_limit_bytes=24 * MIB),
        cost_estimate=COST,
        name="front",
    )(is_child, *map(in_hbm, arrays), *nests, in_vmem(ahead), cells, *line)


def base_kernel(
    levels, bs, is_child, nest_x, nest_y, masked_in, matrices, kappa, nudging, base,
    masked, weights, wide, stack, group, sems,
):
    fields, cols = masked.shape[:2]
    near = cols // 3
    reach = near + 2

    def child_copies(f):
        for n, x in enumerate((0, cols - near)):
            at = pl.ds(x, near)
            yield pltpu.make_async_copy(masked_in.at[f, at], masked.at[f, at], sems.at[f, n])

    def parent_copy(f):
        at = pl.ds(jnp.clip(nest_x[0] - 1, 0, cols - reach), reach)
        return pltpu.make_async_copy(masked_in.at[f, at], masked.at[f, at], sems.at[f, 0])

    @pl.when(is_child[0] == 1)
    def _():
        for f in range(fields):
            for copy in child_copies(f):
                copy.start()
        fill_group(group)
        join_weights(bs, cols, kappa, nudging, weights)

        def field(f, carry):
            for copy in child_copies(f):
                copy.wait()
            child_rows(f, bs, masked, weights, wide)
            return carry

        lax.fori_loop(0, fields, field, 0, unroll=True)

    @pl.when(is_child[0] == 0)
    def _():
        for f in range(fields):
            parent_copy(f).start()

        def field(f, carry):
            parent_copy(f).wait()
            parent_rows(f, bs, nest_x, nest_y, masked, kappa, stack)
            return carry

        lax.fori_loop(0, fields, field, 0, unroll=True)

    def emit(f, mixed):
        base[f, :, :] = mixed[:PAD, :]

    mix_rows(bs, is_child, wide, group, stack, matrices, emit)


def base_of(is_child, nests, masked, matrices, kappa, nudging, dims):
    fields, levels, cols, chunks = dims
    rows = chunks * LANE
    bs = (0, cols // 3 - 1)
    return pl.pallas_call(
        functools.partial(base_kernel, levels, bs),
        in_specs=[SMEM] * 3 + [HBM] + [VMEM] * 3,
        out_specs=VMEM,
        out_shape=pltpu.VMEM((fields, PAD, 2 * LANE), F32),
        scratch_shapes=[pltpu.VMEM(masked.shape, F32)]
        + row_scratch(bs, fields, rows)
        + [pltpu.SemaphoreType.DMA((fields, 2))],
        compiler_params=pltpu.CompilerParams(vmem_limit_bytes=16 * MIB),
        cost_estimate=COST,
        name="base",
    )(is_child, *nests, in_hbm(masked), matrices, kappa, nudging)


def stacked_kernel(one, two, out):
    out[: one.shape[0], :] = one[...]
    out[one.shape[0] :, :] = two[...]


def stacked(one, two):
    return pl.pallas_call(
        stacked_kernel,
        in_specs=[VMEM] * 2,
        out_specs=VMEM,
        out_shape=pltpu.VMEM((2 * one.shape[0], one.shape[1]), F32),
        compiler_params=pltpu.CompilerParams(vmem_limit_bytes=4 * MIB),
        name="stacked",
    )(one, two)


def merged(own, other, width):
    if 2 * width <= LANE:
        return own + pltpu.roll(other, width, 1)
    return jnp.concatenate([own, other], axis=0)


def repack_kernel(width, edges, parcel, arrived, out):
    if edges:
        out[:edges, :] = parcel[:edges, :]
    out[edges:, :] = merged(parcel[PAD:, :], arrived[PAD:, :], width)


def repack(parcel, arrived, width, edges):
    height = (parcel.shape[0] - PAD) * (1 if 2 * width <= LANE else 2)
    return pl.pallas_call(
        functools.partial(repack_kernel, width, edges),
        in_specs=[VMEM] * 2,
        out_specs=VMEM,
        out_shape=pltpu.VMEM((edges + height, LANE), F32),
        compiler_params=pltpu.CompilerParams(vmem_limit_bytes=4 * MIB),
        name="repack",
    )(parcel, arrived)


def y_halos(ty, peers, first, second):
    one, two = first[:PAD, :], second[:PAD, :]
    even = (lax.rem(ty[0], 2) == 0).astype(F32)
    odd = 1.0 - even
    before = (two * even + one * odd) * (ty[0] > 0).astype(F32)
    after = (one * even + two * odd) * (ty[0] < peers - 1).astype(F32)
    low = lax.rem(lane_ids((PAD, LANE)), 2) == 0
    return jnp.where(low, pltpu.roll(before, 1, 1), pltpu.roll(after, LANE - 1, 1))


def outer_kernel(
    levels, peers, is_child, tx, ty, state, matrices, base, kappa, nudging, x_first, x_second,
    first, second, nest_x, nest_y, out, ahead, sides, wide, stack, group, sem,
):
    fields = matrices.shape[0]
    cols, _, rows = kappa.shape
    blocks = cols // 3
    lanes = lane_ids((PAD, LANE))
    turned = lax.rem(lanes + 1, LANE)
    copy = pltpu.make_async_copy(state.at[pl.ds(0, ahead.shape[0])], ahead, sem)
    copy.start()
    sides[...] = jnp.zeros_like(sides)
    halo = y_halos(ty, peers, first, second)

    def weighted(row_of_x):
        one = packed(lambda x: (row_of_x(x)[:, :LANE], row_of_x(x)[:, rows - LANE :]), cols)
        total = one
        for f in range(1, fields):
            total = total + pltpu.roll(one, 2 * f * cols, 1)
        return halo * total

    def fill_fix(value):
        for f in range(fields):
            fill_stack(stack.at[f], chunk(2), deepened(value))

    @pl.when(is_child[0] == 1)
    def _():
        fill_group(group)
        for f in range(fields):
            for n, side in enumerate(x_halos_of(tx, x_first, x_second, f)):
                x = (0, cols - 1)[n]
                at = (f * 2 + n) * DEPTH
                sides[at : at + levels, :] = side * (nudging[x : x + 1, :] * kappa[x])
        wide[:, :rows], wide[:, rows:] = halves(sides[...])
        value = grouped(wide[...], group[...])
        for f in range(fields):
            for n in range(2):
                at = (f * 2 + n) * DEPTH
                fill_stack(stack.at[f], chunk(n), value[at : at + DEPTH])
        part = weighted(lambda x: nudging[x : x + 1, :] * kappa[x])
        fill_fix(part + pltpu.roll(part, LANE - 2, 1) + pltpu.roll(part, LANE - 4, 1))

    @pl.when(is_child[0] == 0)
    def _():
        back = lax.rem(rows - nest_y[0], rows)
        reached = (nest_x[0] == 0, nest_x[0] + blocks == cols)
        for f in range(fields):
            for n, side in enumerate(x_halos_of(tx, x_first, x_second, f)):
                at = (f * 2 + n) * DEPTH
                weight = kappa[(0, cols - 1)[n]] * reached[n].astype(F32)
                sides[at : at + levels, :] = side * weight
                value = pltpu.roll(sides[at : at + DEPTH, :], back, 1)[:, :LANE]
                fill_stack(stack.at[f], chunk(n), value)
        starts = (nest_y[0] == 0).astype(F32)
        finals = (nest_y[0] == rows - LANE).astype(F32)
        part = weighted(lambda x: kappa[x])
        part = part * jnp.where(lax.rem(lanes, 2) == 0, starts, finals)
        value = jnp.zeros((PAD, LANE), F32)
        for b in range(blocks):
            shift = lax.rem(LANE + 4 * b - 2 * nest_x[0], LANE)
            here = lax.rem(turned, 2 * cols) // 2 == 3 * b
            value = jnp.where(here, pltpu.roll(part, shift, 1), value)
        fill_fix(value)

    fixes = jnp.zeros((PAD, LANE), F32)
    for f in range(fields):
        mixed = mix(matrices[f], stack[f])
        for n in range(2):
            at = pl.ds(f * (2 * levels) + n, levels, stride=2)
            out[at, :] = base[f, :levels, chunk(n)] + mixed[:levels, chunk(n)]
        fixes = jnp.where(turned // (2 * cols) == f, mixed[:PAD, chunk(2)], fixes)
    out[out.shape[0] - PAD :, :] = fixes
    copy.wait()


def outer(
    is_child, tx, ty, state2, matrices, base, kappa, nudging, x_halos, firsts, nests, dims, peers
):
    fields, levels, cols, chunks = dims
    rows = chunks * LANE
    height = -(-fields * 2 * levels // 8) * 8 + PAD
    return pl.pallas_call(
        functools.partial(outer_kernel, levels, peers),
        in_specs=[SMEM] * 3 + [HBM] + [VMEM] * 8 + [SMEM] * 2,
        out_specs=[VMEM] * 2,
        out_shape=[
            pltpu.VMEM((height, LANE), F32),
            pltpu.VMEM((state2.shape[0] // fields, LANE), F32),
        ],
        scratch_shapes=[
            pltpu.VMEM((fields * 2 * DEPTH, rows), F32),
            pltpu.VMEM((fields * 2 * DEPTH, 2 * rows), jnp.bfloat16),
            pltpu.VMEM((fields, 2 * DEPTH, 3 * LANE), jnp.bfloat16),
            pltpu.VMEM((2 * rows, LANE), jnp.bfloat16),
            pltpu.SemaphoreType.DMA,
        ],
        compiler_params=pltpu.CompilerParams(vmem_limit_bytes=12 * MIB),
        name="outer",
    )(is_child, tx, ty, in_hbm(state2), matrices, base, kappa, nudging, *x_halos, *firsts, *nests)


def tile_kernel(
    levels, peers, tx, ty, state, mask, matrices, kappa, x_first, x_second, first, second, ahead,
    out, buf, masked, sides, halo, stack, sems,
):
    cols, _, rows = masked.shape
    chunks = rows // LANE
    size = levels * cols * chunks
    fields = state.shape[0] // size

    def copy(f):
        at = pl.ds(f * size, size)
        return pltpu.make_async_copy(state.at[at], buf.at[at], sems.at[f])

    for f in range(1, fields):
        copy(f).start()
    sides[...] = jnp.zeros_like(sides)
    halo[...] = y_halos(ty, peers, first, second)
    pair = 2

    def field(f, carry, leading=False):
        if leading:
            fill_masked(levels, ahead, f, mask, masked)
        else:
            copy(f).wait()
            fill_masked(levels, buf, f, mask, masked)
        for n, side in enumerate(x_halos_of(tx, x_first, x_second, f)):
            sides[n, :levels, :] = side
        for x0 in range(0, cols, pair):
            for x in range(x0, x0 + pair):
                above = masked[x - 1] if x > 0 else sides[0]
                below = masked[x + 1] if x < cols - 1 else sides[1]
                shift = lax.rem(LANE - 2 * (f * cols + x), LANE)
                edge = pltpu.roll(halo[...], lax.rem(LANE + shift, LANE), 1)
                value = spread_of(masked[x], above, below, kappa[x], edge)
                part = slice((x - x0) * rows, (x - x0 + 1) * rows)
                fill_stack(stack, part, deepened(value))
            mixed = mix(matrices[f], stack[...])
            for n in range(pair * chunks):
                out[aligned((f * cols + x0) * chunks + n, PAD), :] = mixed[:PAD, chunk(n)]
        return carry

    field(0, 0, leading=True)
    lax.fori_loop(1, fields, field, 0, unroll=True)


def tile_of(tx, ty, state2, mask, matrices, kappa, x_halos, firsts, ahead, dims, peers):
    fields, levels, cols, chunks = dims
    rows = chunks * LANE
    return pl.pallas_call(
        functools.partial(tile_kernel, levels, peers),
        in_specs=[SMEM] * 2 + [HBM] + [VMEM] * 8,
        out_specs=VMEM,
        out_shape=pltpu.VMEM((fields * cols * chunks * PAD, LANE), F32),
        scratch_shapes=[
            pltpu.VMEM(state2.shape, F32),
            pltpu.VMEM((cols, PAD, rows), F32),
            pltpu.VMEM((2, PAD, rows), F32),
            pltpu.VMEM((PAD, LANE), F32),
            pltpu.VMEM((2 * DEPTH, 2 * rows), jnp.bfloat16),
            pltpu.SemaphoreType.DMA((fields,)),
        ],
        compiler_params=pltpu.CompilerParams(vmem_limit_bytes=16 * MIB),
        cost_estimate=COST,
        name="tile",
    )(tx, ty, in_hbm(state2), mask, matrices, kappa, *x_halos, *firsts, in_vmem(ahead))


def observe_kernel(dests, across, row, column, counts, places, mine, theirs, _, tile):
    lanes = lane_ids((1, LANE))
    slots = places.shape[1]
    ty, tx = row[0], column[0]
    me = ty * across + tx
    half = (mine.shape[0] - PAD) // slots * (LANE // dests)

    def source(turn, ref, g, carry):
        origin = (lax.div(g, across) ^ turn ^ ty) * across + (lax.rem(g, across) ^ tx)
        lane_in = lax.rem(g, LANE // dests) * dests + me
        block = PAD + lax.div(g, LANE // dests) * slots
        count = counts[0, origin]
        for k0 in range(0, slots, 4):
            ats, adds = [], []
            for m in range(k0, k0 + 4):
                place = places[origin, m]
                lane = place & (LANE - 1)
                value = pltpu.roll(ref[pl.ds(block + m, 1), :], (lane - lane_in) & (LANE - 1), 1)
                ats.append(place >> 7)
                adds.append(jnp.where(lanes == jnp.where(m < count, lane, LANE), value, 0.0))
            olds = [tile[pl.ds(at, 1), :] for at in ats]
            for k, (at, total) in enumerate(zip(ats, olds)):
                total = total + adds[k]
                for j in range(k):
                    total = total + jnp.where(ats[j] == at, adds[j], 0.0)
                tile[pl.ds(at, 1), :] = total
        return carry

    def both(n, carry):
        source(0, mine, n, carry)
        return source(3, theirs, n, carry)

    lax.fori_loop(0, half, both, 0)


def observe(row, column, places, counts, seen, tile, dests, across):
    return pl.pallas_call(
        functools.partial(observe_kernel, dests, across),
        in_specs=[SMEM] * 4 + [VMEM] * 3,
        out_specs=VMEM,
        out_shape=pltpu.VMEM(tile.shape, F32),
        input_output_aliases={6: 0},
        compiler_params=pltpu.CompilerParams(vmem_limit_bytes=4 * MIB),
        name="observe",
    )(row, column, counts, places, *seen, in_vmem(tile))


def finish_kernel(
    levels, is_child, nest_x, nest_y, tile, mask, in_arrived, out_arrived, in_sent, out_sent,
    out, buf, group, sems,
):
    cols = mask.shape[0]
    rows = mask.shape[2]
    chunks = rows // LANE
    step = cols * chunks
    size = levels * step
    fields = out.shape[0] // size
    blocks = cols // 3
    inner = blocks - 2
    lanes = lane_ids((levels, LANE))
    ends = jnp.logical_or(lanes == 0, lanes == LANE - 1)
    height = out_arrived.shape[0]

    def copy(f):
        at = pl.ds(f * size, size)
        return pltpu.make_async_copy(buf.at[at], out.at[at], sems.at[f])

    def piece_of(f, piece):
        return tile[pl.ds(pl.multiple_of((f * step + piece) * PAD, 8), levels), :]

    def payload(f, b, inner_ref, outer_ref):
        if b in (0, blocks - 1):
            value = outer_ref[pl.ds(f * (2 * levels) + min(b, 1), levels, stride=2), :]
        else:
            value = inner_ref[pl.ds(f * (levels * inner) + b - 1, levels, stride=inner), :]
        fixes = outer_ref[height - PAD : height - PAD + levels, :]
        shift = lax.rem(LANE - 2 * (f * cols + 3 * b), LANE)
        fixes = pltpu.roll(fixes, lax.rem(LANE + shift, LANE), 1)
        return value + jnp.where(ends, fixes, 0.0)

    def fill_child(f, carry):
        for b in range(blocks):
            high, low = halves(payload(f, b, in_arrived, out_arrived))
            both = jnp.concatenate([high, low], axis=1)
            value = jnp.dot(both, group[...], preferred_element_type=F32) * (1.0 / 9.0)
            for x in range(3 * b, 3 * b + 3):
                row = row_of(mask, x)
                for c in range(chunks):
                    piece = x * chunks + c
                    at = pl.ds(f * size + piece, levels, stride=step)
                    total = piece_of(f, piece) + value[:, chunk(c)]
                    buf[at, :] = total * row[:, chunk(c)]
        copy(f).start()
        return carry

    def fill_plain(f, carry):
        for x in range(cols):
            row = row_of(mask, x)
            for c in range(chunks):
                piece = x * chunks + c
                at = pl.ds(f * size + piece, levels, stride=step)
                buf[at, :] = piece_of(f, piece) * row[:, chunk(c)]
        return carry

    def fill_parent(f, carry):
        fill_plain(f, carry)
        for b in range(blocks):
            delta = payload(f, b, in_arrived, out_arrived) - payload(f, b, in_sent, out_sent)
            wide = jnp.concatenate([delta, jnp.zeros((levels, rows - LANE), F32)], 1)
            x = nest_x[0] + b
            value = pltpu.roll(wide, nest_y[0], 1) * row_of(mask, x)
            for c in range(chunks):
                at = pl.ds(f * size + x * chunks + c, levels, stride=step)
                buf[at, :] = buf[at, :] + value[:, chunk(c)]
        copy(f).start()
        return carry

    @pl.when(is_child[0] == 1)
    def _():
        ids = lax.broadcasted_iota(jnp.int32, group.shape, 0)
        ids = jnp.where(ids < LANE, ids, ids - LANE)
        group[...] = jnp.where(lane_ids(group.shape) // 3 == ids, 1.0, 0.0).astype(jnp.bfloat16)
        lax.fori_loop(0, fields, fill_child, 0)

    @pl.when(is_child[0] == 0)
    def _():
        lax.fori_loop(0, fields, fill_parent, 0)

    for f in range(fields):
        copy(f).wait()


def finish(is_child, nests, tile, mask, arrived, sent, dims):
    fields, levels, cols, chunks = dims
    rows = chunks * LANE
    size = (fields * levels * cols * chunks, LANE)
    return pl.pallas_call(
        functools.partial(finish_kernel, levels),
        in_specs=[SMEM] * 3 + [VMEM] * 6,
        out_specs=HBM,
        out_shape=pltpu.HBM(size, F32),
        scratch_shapes=[
            pltpu.VMEM(size, F32),
            pltpu.VMEM((2 * LANE, rows), jnp.bfloat16),
            pltpu.SemaphoreType.DMA((fields,)),
        ],
        compiler_params=pltpu.CompilerParams(vmem_limit_bytes=16 * MIB),
        cost_estimate=COST,
        name="finish",
    )(is_child, *nests, in_vmem(tile), mask, *arrived, *sent)


def from_neighbours(first, second, axis):
    size = lax.axis_size(axis)
    inner = [(i, i + 1) for i in range(1, size - 1, 2)]
    one = swapped(first, axis, 1)
    return one, lax.ppermute(second, axis, inner + [(j, i) for i, j in inner])


def swapped(value, axis, mask):
    return lax.ppermute(value, axis, [(i, i ^ mask) for i in range(lax.axis_size(axis))])


def local(
    adjoint_state,
    land_mask,
    diffusivity,
    mixing,
    nudging,
    nest_x,
    nest_y,
    obs_forcing,
    obs_cell,
    obs_count,
):
    _, fields, levels, cols, rows = adjoint_state.shape
    chunks = rows // LANE
    dims = (fields, levels, cols, chunks)
    state5 = adjoint_state.reshape(fields, levels, cols, 1, rows)
    state2 = adjoint_state.reshape(fields * levels * cols * chunks, LANE)
    mask = land_mask.reshape(cols, 1, rows)
    kappa = diffusivity.reshape(cols, 1, rows)
    mixing = mixing.reshape(fields, levels, 1, levels)
    peers, across = lax.axis_size("ty"), lax.axis_size("tx")
    assert peers == 4 and across & (across - 1) == 0 and 2 * fields * cols <= LANE
    assert levels <= PAD and cols % 3 == 0 and rows == 3 * LANE
    row = lax.axis_index("ty").astype(jnp.int32)
    column = lax.axis_index("tx").astype(jnp.int32)
    ty = row.reshape(1)
    is_child = (lax.axis_index("grp") == 0).astype(jnp.int32).reshape(1)
    nests = (nest_x, nest_y)

    forcing = obs_forcing[0, 0]
    dests = forcing.shape[1]
    counts = obs_count.reshape(1, -1)
    other = swapped(forcing, "tx", 1)
    pair = stacked(forcing, other)
    tx = column.reshape(1)
    *x_sent, ahead = x_edges(tx, nests, state5, mask)
    ahead = ahead.reshape(-1, LANE)
    pair, *x_sent = lax.optimization_barrier((pair, *x_sent))
    x_halos = from_neighbours(*x_sent, "tx")
    line = [forcing, other, swapped(pair, "tx", 2)]
    for n in range(2, across.bit_length() - 1):
        blocks = jnp.concatenate(line)
        line = [blocks, swapped(blocks, "tx", 1 << n)]
    masked, matrices, parcel, in_sent, places = front(
        is_child, state2, mask, kappa, nudging, mixing, nests, line, ahead,
        obs_cell[0, :, :, 0], dims,
    )
    first = swapped(parcel, "ty", 1)
    in_arrived = swapped(in_sent, "grp", 1)
    parcel = repack(parcel, first, across * dests, PAD)
    second = swapped(parcel, "ty", 3)
    firsts = (first, second)
    masked, x_halos, parcel = lax.optimization_barrier((masked, x_halos, parcel))
    base = base_of(is_child, nests, masked, matrices, kappa, nudging, dims)
    out_sent, ahead = outer(
        is_child, tx, ty, state2, matrices, base, kappa, nudging, x_halos, firsts, nests, dims, peers
    )
    out_arrived = swapped(out_sent, "grp", 1)
    tile = tile_of(tx, ty, state2, mask, matrices, kappa, x_halos, firsts, ahead, dims, peers)
    tile = observe(ty, tx, places, counts, (parcel, second), tile, dests, across)
    arrived, sent = (in_arrived, out_arrived), (in_sent, out_sent)
    out = finish(is_child, nests, tile, mask, arrived, sent, dims)
    return out.reshape(adjoint_state.shape)


def solution(mesh):
    in_specs = (
        P("grp", None, None, "tx", "ty"),
        P("grp", "tx", "ty"),
        P("grp", "tx", "ty"),
        P("grp", None, None, None),
        P("tx", "ty"),
        P(("ty", "tx")),
        P(("ty", "tx")),
        P("grp", ("ty", "tx"), None, None),
        P("grp", None, None, ("ty", "tx")),
        P("grp", None, ("ty", "tx")),
    )
    out_specs = P("grp", None, None, "tx", "ty")
    return jax.shard_map(local, mesh=mesh, in_specs=in_specs, out_specs=out_specs, check_vma=False)
```
